32 devices in a mesh: seq: 4 (over y, x), head: 8 (over z, core).
Axes of the slice: x: 2, y: 2, z: 4, core: 2. Of those that a mesh axis runs over, the one named last changes fastest.
Arguments:
- hidden: bfloat16 [8, 2048, 2048], P('head', 'seq'), may hold values from -6 to 6
- lengths: int32 [8], P('head'), may hold values from 512 to 2048, as said below
- out_grad: bfloat16 [8, 2048, 2048], P('head', 'seq'), may hold values from -6 to 6
- norm_gain: bfloat16 [2048], P('head'), may hold values from 0.5 to 1.5
- w_in: bfloat16 [2048, 8448], P('head'), may hold values from -0.125 to 0.125
- w_dt: bfloat16 [2048, 64], P('head'), may hold values from -0.125 to 0.125
- conv_weight: bfloat16 [4, 4352], P(None, 'head'), may hold values from -3 to 3
- conv_bias: bfloat16 [4352], P('head'), may hold values from -0.5 to 0.5
- dt_bias: bfloat16 [64], P('head'), may hold values from -4 to -2
- a_log: bfloat16 [64], P('head'), may hold values from -6 to 0
- skip_gain: bfloat16 [64], P('head'), may hold values from 0.5 to 1.5
- gate_gain: bfloat16 [4096], P('head'), may hold values from 0.5 to 1.5
- w_out: bfloat16 [4096, 2048], P('head'), may hold values from -0.09375 to 0.09375
Outputs:
- block_out: bfloat16 [8, 2048, 2048], P('head', 'seq')
- hidden_grad: float32 [8, 2048, 2048], P('head', 'seq')
- norm_gain_grad: float32 [2048], P('head')
- w_in_grad: float32 [2048, 8448], P('head')
- w_dt_grad: float32 [2048, 64], P('head')
- conv_weight_grad: float32 [4, 4352], P(None, 'head')
- conv_bias_grad: float32 [4352], P('head')
- dt_bias_grad: float32 [64], P('head')
- a_log_grad: float32 [64], P('head')
- skip_grad: float32 [64], P('head')
- gate_gain_grad: float32 [4096], P('head')
- w_out_grad: float32 [4096, 2048], P('head')
The draws below stay inside these ranges and needn't reach their ends.
Inputs may be any that keep to these rules, and one draw needn't show every extreme that they name: lengths of the buckets; some bucket has exactly 2048.
All inputs are finite; a program needn't handle non-finite values.
Results may differ from the reference program's by a relative error of at most 0.02.
Values may be sent and summed in bfloat16 or wider, within the bound.
A program may use at most 512 MiB of HBM per device.

```python
import jax
import jax.numpy as jnp
from jax import lax

D = 2048
HEADS = 64
HEAD_DIM = 64
STATE = 128
KERNEL = 4
SPAN = 256
LEN = 2048
DI = 4096
PROJ = 8448
CHANNELS = 4352
SEQS = 8


def draw_lengths(key, part):
    key = jax.random.fold_in(key, 11)
    key_one, key_two = jax.random.split(key)
    drawn = jax.random.randint(key_one, (SEQS,), LEN // 4, LEN + 1)
    chosen = jax.random.randint(key_two, (), 0, SEQS)
    return drawn.at[chosen].set(LEN).astype(jnp.int32)


def steps_of(stream_key, dims, cuts, smallest, high):
    factor_of = 1.0
    for position, blocks in cuts:
        heights = jax.random.uniform(jax.random.fold_in(jax.random.fold_in(stream_key, 6), position), (blocks,), jnp.float32, smallest / len(cuts), high / len(cuts))
        factor_of = factor_of * jnp.repeat(jnp.exp(heights), dims[position] // blocks).reshape((-1,) + (1,) * (len(dims) - 1 - position))
    return factor_of


def centred(key, extent, scale, limit, cuts=(), kind=jnp.bfloat16):
    values = scale * jax.random.normal(key, extent, jnp.float32)
    if cuts:
        values = values * steps_of(key, extent, cuts, -0.22, 0.18)
    return jnp.clip(values, -limit, limit).astype(kind)


def setup_inputs(seed: int = 0) -> dict:
    keys = jax.random.split(jax.random.key(seed), 14)
    return {
        "hidden": centred(keys[0], (SEQS, LEN, D), 1.0, 6.0, ((0, 8), (1, 4))),
        "lengths": draw_lengths(jax.random.fold_in(keys[13], 71), 0),
        "out_grad": centred(keys[2], (SEQS, LEN, D), 1.0, 6.0, ((0, 8), (1, 4))),
        "norm_gain": jnp.clip(1.0 + 0.1 * jax.random.normal(keys[3], (D,), jnp.float32), 0.5, 1.5).astype(jnp.bfloat16),
        "w_in": centred(keys[4], (D, PROJ), D ** -0.5, 0.125, ((0, 8),)),
        "w_dt": centred(keys[5], (D, HEADS), D ** -0.5, 0.125, ((0, 8),)),
        "conv_weight": centred(keys[6], (KERNEL, CHANNELS), KERNEL ** -0.5, 3.0, ((1, 8),)),
        "conv_bias": jnp.clip(jax.random.uniform(keys[7], (CHANNELS,), jnp.float32, -0.5, 0.5) * steps_of(keys[7], (CHANNELS,), ((0, 8),), -0.4, 0.0), -0.5, 0.5).astype(jnp.bfloat16),
        "dt_bias": jnp.clip(-4.0 + 2.0 * jax.random.uniform(keys[8], (HEADS,), jnp.float32) ** steps_of(keys[8], (HEADS,), ((0, 8),), -0.2, 0.2), -4.0, -2.0).astype(jnp.bfloat16),
        "a_log": jnp.clip(-6.0 + 6.0 * jax.random.uniform(keys[9], (HEADS,), jnp.float32) ** steps_of(keys[9], (HEADS,), ((0, 8),), -0.2, 0.2), -6.0, 0.0).astype(jnp.bfloat16),
        "skip_gain": jnp.clip(0.5 + 1.0 * jax.random.uniform(keys[10], (HEADS,), jnp.float32) ** steps_of(keys[10], (HEADS,), ((0, 8),), -0.2, 0.2), 0.5, 1.5).astype(jnp.bfloat16),
        "gate_gain": jnp.clip(1.0 + 0.1 * jax.random.normal(keys[11], (DI,), jnp.float32), 0.5, 1.5).astype(jnp.bfloat16),
        "w_out": centred(keys[12], (DI, D), DI ** -0.5, 0.09375, ((0, 8),)),
    }


EPS = 1e-05
HIGH = lax.Precision.HIGHEST

@jax.custom_vjp
def low(v):
    return lax.optimization_barrier(v.astype(jnp.bfloat16)).astype(jnp.float32)

@jax.custom_vjp
def low_back(v):
    return v

def low_keep(v):
    return (low(v), None)

def low_pass(kept, grad):
    return (grad,)

def back_keep(v):
    return (v, None)

def back_low(kept, grad):
    return (low(grad),)
low.defvjp(low_keep, low_pass)
low_back.defvjp(back_keep, back_low)

def rms_scale(values, gain):
    return values * lax.rsqrt(lax.optimization_barrier(jnp.mean(values * values, axis=-1, keepdims=True)) + EPS) * gain

def span_step(decay_rate, causal):

    def advance(state_in, pieces):
        x_block, dt_block, b_block, c_block = pieces
        cumulate = jnp.cumsum(dt_block * decay_rate, axis=0)
        spread = cumulate[:, None, :] - cumulate[None, :, :]
        weights = jnp.exp(jnp.where(causal[:, :, None], spread, -jnp.inf))
        scores = jnp.einsum('tn,sn->ts', c_block, b_block, precision=HIGH)
        scaled = x_block * dt_block[:, :, None]
        inner_part = jnp.einsum('tsh,shp->thp', scores[:, :, None] * weights, scaled, precision=HIGH)
        cross_part = jnp.einsum('tn,hnp->thp', c_block, state_in, precision=HIGH) * jnp.exp(cumulate)[:, :, None]
        tail_decay = jnp.exp(cumulate[-1:, :] - cumulate)
        state_add = jnp.einsum('sn,shp->hnp', b_block, scaled * tail_decay[:, :, None], precision=HIGH)
        renewed = jnp.exp(cumulate[-1, :])[:, None, None] * state_in + state_add
        return (renewed, inner_part + cross_part)
    return advance

def ssd_sequence(x_seq, dt_seq, b_seq, c_seq, a_log, skip_gain):
    seq_len, head_count, head_width = x_seq.shape
    span_count = seq_len // SPAN
    decay_rate = -jnp.exp(a_log)
    causal = jnp.tril(jnp.ones((SPAN, SPAN), dtype=jnp.bool_))
    blocks = (x_seq.reshape(span_count, SPAN, head_count, head_width), dt_seq.reshape(span_count, SPAN, head_count), b_seq.reshape(span_count, SPAN, b_seq.shape[1]), c_seq.reshape(span_count, SPAN, c_seq.shape[1]))
    zero_state = jnp.zeros((head_count, b_seq.shape[1], head_width), jnp.float32)
    _, outputs = lax.scan(jax.checkpoint(span_step(decay_rate, causal)), zero_state, blocks)
    return outputs.reshape(seq_len, head_count, head_width) + skip_gain[None, :, None] * x_seq

def layer_group(params, group_in, group_mask):
    norm_gain, w_in, w_dt, conv_weight, conv_bias, dt_bias, a_log, skip_gain, gate_gain, w_out = params
    groups = group_in.shape[0]
    normed = low(rms_scale(group_in, norm_gain))
    projected = low_back(jnp.einsum('gtd,de->gte', normed, w_in, precision=HIGH))
    dt_raw = low_back(jnp.einsum('gtd,dh->gth', normed, w_dt, precision=HIGH))
    gate_in = projected[..., :DI]
    conv_in = low(projected[..., DI:])
    padded = jnp.pad(conv_in, ((0, 0), (KERNEL - 1, 0), (0, 0)))
    conv_pre = conv_bias + jnp.zeros_like(conv_in)
    for shift_by in range(KERNEL):
        conv_pre = conv_pre + conv_weight[shift_by] * padded[:, shift_by:shift_by + LEN]
    activated = jax.nn.silu(conv_pre)
    x_part = low_back(low(activated[..., :DI]))
    b_part = low(activated[..., DI:DI + STATE])
    c_part = low(activated[..., DI + STATE:])
    dt_val = low_back(low(jax.nn.softplus(dt_raw + dt_bias)))
    scanned = jax.vmap(ssd_sequence, in_axes=(0, 0, 0, 0, None, None))(x_part.reshape(groups, LEN, HEADS, HEAD_DIM), dt_val, b_part, c_part, a_log, skip_gain)
    ssd_out = low_back(low(scanned.reshape(groups, LEN, DI)))
    gated_out = ssd_out * jax.nn.silu(gate_in)
    gate_normed = low(rms_scale(gated_out, gate_gain))
    branch = jnp.einsum('gtk,kd->gtd', gate_normed, w_out, precision=HIGH)
    return group_in + group_mask[..., None] * branch

def forward_all(params, hidden32, token_mask):
    seq_total = hidden32.shape[0]
    group_size = 2 if seq_total % 2 == 0 else 1
    stacked = hidden32.reshape(seq_total // group_size, group_size, LEN, D)
    masks = token_mask.reshape(seq_total // group_size, group_size, LEN)

    def one_group(carried, pieces):
        return (carried, layer_group(params, pieces[0], pieces[1]))
    _, outputs = lax.scan(jax.checkpoint(one_group), jnp.zeros((), jnp.float32), (stacked, masks))
    return outputs.reshape(seq_total, LEN, D)

def reference(hidden, lengths, out_grad, norm_gain, w_in, w_dt, conv_weight, conv_bias, dt_bias, a_log, skip_gain, gate_gain, w_out):
    params = (norm_gain.astype(jnp.float32), w_in.astype(jnp.float32), w_dt.astype(jnp.float32), conv_weight.astype(jnp.float32), conv_bias.astype(jnp.float32), dt_bias.astype(jnp.float32), a_log.astype(jnp.float32), skip_gain.astype(jnp.float32), gate_gain.astype(jnp.float32), w_out.astype(jnp.float32))
    positions = jnp.arange(LEN).astype(jnp.int32)
    token_mask = (positions[None, :] < lengths[:, None].astype(jnp.int32)).astype(jnp.float32)
    hidden32 = hidden.astype(jnp.float32)

    def whole_layer(values, weights):
        return forward_all(weights, values, token_mask)
    block32, pullback = jax.vjp(whole_layer, hidden32, params)
    hidden_grad, grad_list = pullback(out_grad.astype(jnp.float32))
    return (block32.astype(jnp.bfloat16), hidden_grad, grad_list[0], grad_list[1], grad_list[2], grad_list[3], grad_list[4], grad_list[5], grad_list[6], grad_list[7], grad_list[8], grad_list[9])
```

```python
import functools

import jax
import jax.numpy as jnp
from jax import lax
from jax.experimental import pallas as pl
from jax.experimental.pallas import tpu as pltpu
from jax.sharding import PartitionSpec as P

HEADS = 64
HEAD_DIM = 64
STATE = 128
KERNEL = 4
CHUNK = 256
DI = 4096
CHANNELS = 4352
PROJ = DI + CHANNELS
EPS = 1e-05
LANES = 128
EVERY = ("seq", "head")
F32 = jnp.float32
BF16 = jnp.bfloat16


def dot(a, b):
    return jnp.dot(a, b, preferred_element_type=F32)


def dot_t(a, b):
    return lax.dot_general(a, b, (((1,), (1,)), ((), ())), preferred_element_type=F32)


def t_dot(a, b):
    return lax.dot_general(a, b, (((0,), (0,)), ((), ())), preferred_element_type=F32)


def sigmoid(v):
    return 1.0 / (1.0 + jnp.exp(-v))


def project_kernel(h_ref, w_ref, cw_ref, cb_ref, dtb_ref, z_ref, u_ref, act_ref, slope_ref, aux_ref, ext, *, heads, wide):
    step = pl.program_id(0)
    rows = h_ref.shape[0]
    chans = u_ref.shape[1]
    h = h_ref[...]
    h32 = h.astype(F32)
    r0 = lax.rsqrt(jnp.mean(h32 * h32, axis=1, keepdims=True) + EPS)
    z_ref[...] = (dot(h, w_ref[:, :wide]) * r0).astype(BF16)
    u = (dot(h, w_ref[:, wide : wide + chans]) * r0).astype(BF16)
    dt_raw = dot(h, w_ref[:, wide + chans :]) * r0

    @pl.when(step == 0)
    def _():
        ext[0:8, :] = jnp.zeros((8, chans), F32)

    @pl.when(step > 0)
    def _():
        ext[0:8, :] = ext[rows : rows + 8, :]

    u_ref[...] = u
    ext[8 : rows + 8, :] = u.astype(F32)
    pre = cb_ref[0:1, :]
    for k in range(KERNEL):
        pre = pre + cw_ref[k : k + 1, :] * ext[pl.ds(8 - (KERNEL - 1) + k, rows), :]
    sig = sigmoid(pre)
    act_ref[...] = (pre * sig).astype(BF16)
    slope_ref[...] = (sig * (1.0 + pre * (1.0 - sig))).astype(BF16)
    v = dt_raw + dtb_ref[0:1, :]
    soft = jnp.maximum(v, 0.0) + jnp.log1p(jnp.exp(-jnp.abs(v)))
    soft = soft.astype(BF16).astype(F32)
    lane = lax.broadcasted_iota(jnp.int32, v.shape, 1)
    aux = jnp.where(lane < heads, soft, 0.0)
    sig_v = pltpu.roll(sigmoid(v), heads, 1)
    aux = jnp.where((lane >= heads) & (lane < 2 * heads), sig_v, aux)
    aux_ref[...] = jnp.where(lane == 2 * heads, r0, aux)


def decays(aux, heads, expand, rate_e, rate_row, rate_col):
    rows = aux.shape[0]
    lane = lax.broadcasted_iota(jnp.int32, aux.shape, 1)
    dt = jnp.where(lane < heads, aux, 0.0).astype(BF16)
    r = lax.broadcasted_iota(jnp.int32, (rows, rows), 0)
    c = lax.broadcasted_iota(jnp.int32, (rows, rows), 1)
    causal = c <= r
    lower = jnp.where(causal, 1.0, 0.0).astype(BF16)
    dt_e = dot(dt, expand)
    cum_e = dot(lower, dt_e.astype(BF16)) * rate_e
    cum_c = dot(lower, dt) * rate_row
    cum_t = lax.dot_general(dt, lower, (((0,), (1,)), ((), ())), preferred_element_type=F32) * rate_col
    return causal, dt_e, cum_e, cum_c, cum_t


def scan_kernel(act_ref, aux_ref, z_ref, d0_ref, exp_ref, rowp_ref, colp_ref, y_ref, gg_ref, st_ref, stat_ref, state, *, heads, wide):
    step = pl.program_id(0)

    @pl.when(step == 0)
    def _():
        state[...] = jnp.zeros_like(state)

    rows = act_ref.shape[0]
    x = act_ref[:, :wide]
    x32 = x.astype(F32)
    b = act_ref[:, wide : wide + STATE]
    c = act_ref[:, wide + STATE :]
    causal, dt_e, cum_e, cum_c, cum_t = decays(
        aux_ref[...], heads, exp_ref[...], rowp_ref[0:1, :], rowp_ref[3:4, :LANES], colp_ref[:, 0:1]
    )
    xdt = x32 * dt_e
    xdt16 = xdt.astype(BF16)
    scores = dot_t(c, b)
    st = state[...]
    st_ref[0] = st
    half = lax.broadcasted_iota(jnp.int32, (rows, LANES), 1) < HEAD_DIM
    parts = []
    for pair in range(heads // 2):
        x2 = xdt16[:, LANES * pair : LANES * (pair + 1)]
        got = []
        for h in (2 * pair, 2 * pair + 1):
            spread = cum_c[:, h : h + 1] - cum_t[h : h + 1, :]
            m = (scores * jnp.exp(jnp.where(causal, spread, -1e30))).astype(BF16)
            got.append(dot(m, x2))
        parts.append(jnp.where(half, got[0], got[1]))
    y = jnp.concatenate(parts, axis=1) + dot(c, st.astype(BF16)) * jnp.exp(cum_e)
    last = cum_e[rows - 1 : rows, :]
    tail = jnp.exp(last - cum_e)
    state[...] = jnp.exp(last) * st + t_dot(b, (xdt * tail).astype(BF16))
    y_ref[...] = y
    ssd = (y + rowp_ref[1:2, :] * x32).astype(BF16).astype(F32)
    z = z_ref[...].astype(F32)
    g = ssd * (z * sigmoid(z))
    gain = rowp_ref[2:3, :]
    gg = g * gain
    gg_ref[...] = gg.astype(BF16)
    ssq = jnp.sum(g * g, axis=1, keepdims=True)
    cross = jnp.sum(gg * d0_ref[...].astype(F32), axis=1, keepdims=True)
    lane = lax.broadcasted_iota(jnp.int32, (rows, LANES), 1)
    stat_ref[...] = jnp.where(lane == 0, ssq, jnp.where(lane == 1, cross, 0.0))


def seg_dot(v, seg):
    hi = v.astype(BF16)
    rest = v - hi.astype(F32)
    mid = rest.astype(BF16)
    low = (rest - mid.astype(F32)).astype(BF16)
    return dot(hi, seg) + dot(mid, seg) + dot(low, seg)


def back_kernel(
    act_ref, aux_ref, z_ref, d0_ref, y_ref, st_ref, slope_ref, u_ref, stat_ref,
    exp_ref, seg_ref, rowp_ref, colp_ref, cw_ref,
    dp_ref, sm_ref, adj, ext, *, heads, wide,
):
    step = pl.program_id(0)
    rows = act_ref.shape[0]
    chans = u_ref.shape[1]

    @pl.when(step == 0)
    def _():
        sm_ref[...] = jnp.zeros_like(sm_ref)
        adj[...] = jnp.zeros_like(adj)
        ext[rows : rows + 8, :] = jnp.zeros((8, chans), F32)

    @pl.when(step > 0)
    def _():
        ext[rows : rows + 8, :] = ext[0:8, :]

    x = act_ref[:, :wide]
    x32 = x.astype(F32)
    b = act_ref[:, wide : wide + STATE]
    c = act_ref[:, wide + STATE :]
    aux = aux_ref[...]
    stat = stat_ref[...]
    r1m = stat[:, 0:1]
    coef = stat[:, 1:2]
    r0 = aux[:, 2 * heads : 2 * heads + 1]
    skip_e = rowp_ref[1:2, :]
    gain = rowp_ref[2:3, :]

    y = y_ref[...]
    ssd = (y + skip_e * x32).astype(BF16).astype(F32)
    z = z_ref[...].astype(F32)
    sig = sigmoid(z)
    sz = z * sig
    d_gated = (r1m * gain) * d0_ref[...].astype(F32) - (ssd * sz) * coef
    dy16 = (d_gated * sz).astype(BF16)
    dy = dy16.astype(F32)
    dp_ref[:, :wide] = (r0 * (d_gated * ssd * (sig * (1.0 + z * (1.0 - sig))))).astype(BF16)

    causal, dt_e, cum_e, cum_c, cum_t = decays(
        aux, heads, exp_ref[...], rowp_ref[0:1, :], rowp_ref[3:4, :LANES], colp_ref[:, 0:1]
    )
    xdt = x32 * dt_e
    xdt16 = xdt.astype(BF16)
    scores = dot_t(c, b)
    st = st_ref[0]
    st16 = st.astype(BF16)
    q_in = adj[...]
    q16 = q_in.astype(BF16)
    last = cum_e[rows - 1 : rows, :]
    ecum = jnp.exp(cum_e)
    tail = jnp.exp(last - cum_e)
    half = lax.broadcasted_iota(jnp.int32, (rows, LANES), 1) < HEAD_DIM
    zero = jnp.zeros((rows, LANES), BF16)
    n_sum = None
    parts = []
    for pair in range(heads // 2):
        cut = slice(LANES * pair, LANES * (pair + 1))
        x2 = xdt16[:, cut]
        dy2 = dy16[:, cut]
        got = []
        for side in range(2):
            h = 2 * pair + side
            spread = cum_c[:, h : h + 1] - cum_t[h : h + 1, :]
            ell = jnp.exp(jnp.where(causal, spread, -1e30))
            m = (scores * ell).astype(BF16)
            got.append(t_dot(m, dy2))
            own = half if side == 0 else jnp.logical_not(half)
            n = dot_t(jnp.where(own, dy2, zero), x2) * ell
            n_sum = n if n_sum is None else n_sum + n
        parts.append(jnp.where(half, got[0], got[1]))
    out_part = dot(b, q16) * tail
    v = jnp.concatenate(parts, axis=1) + out_part
    n16 = n_sum.astype(BF16)
    dy_e = (dy * ecum).astype(BF16)
    x_tail = (xdt * tail).astype(BF16)
    d_b = t_dot(n16, c) + dot_t(x_tail, q16)
    d_c = dot(n16, b) + dot_t(dy_e, st16)
    elast = jnp.exp(last)
    adj[...] = elast * q_in + t_dot(c, dy_e)

    seg = seg_ref[...]
    flow = dy * y - xdt16.astype(F32) * v
    passed = jnp.sum(xdt16.astype(F32) * out_part, axis=0, keepdims=True)
    passed = passed + elast * jnp.sum(q_in * st, axis=0, keepdims=True)
    flow_h = seg_dot(flow, seg)
    passed_h = seg_dot(jnp.broadcast_to(passed, (8, wide)), seg)[0:1, :]
    upper = jnp.where(
        lax.broadcasted_iota(jnp.int32, (rows, rows), 1) >= lax.broadcasted_iota(jnp.int32, (rows, rows), 0), 1.0, 0.0
    ).astype(BF16)
    hi = flow_h.astype(BF16)
    rest = flow_h - hi.astype(F32)
    mid = rest.astype(BF16)
    low = (rest - mid.astype(F32)).astype(BF16)
    crossing = dot(upper, hi) + dot(upper, mid) + dot(upper, low) + passed_h
    rate_row = rowp_ref[3:4, :LANES]
    decay_grad = rate_row * crossing
    d_dt = seg_dot(x32 * v, seg) + decay_grad
    lane = lax.broadcasted_iota(jnp.int32, (rows, LANES), 1)
    sig_v = pltpu.roll(aux, LANES - heads, 1)
    d_pre = jnp.where(lane < heads, d_dt * sig_v, 0.0)
    dt = jnp.where(lane < heads, aux, 0.0)
    dp_ref[:, wide + chans :] = (r0 * d_pre).astype(BF16)

    d_act = jnp.concatenate([skip_e * dy + dt_e * v, d_b, d_c], axis=1)
    d_conv = d_act * slope_ref[...].astype(F32)
    ext[0:rows, :] = d_conv
    u = u_ref[...].astype(F32)
    d_u = None
    for k in range(KERNEL):
        moved = ext[pl.ds(KERNEL - 1 - k, rows), :]
        term = cw_ref[k : k + 1, :] * moved
        d_u = term if d_u is None else d_u + term
        sm_ref[k : k + 1, :] += jnp.sum(u * moved, axis=0, keepdims=True)
    dp_ref[:, wide : wide + chans] = (r0 * d_u).astype(BF16)
    sm_ref[4:5, :] += jnp.sum(d_conv, axis=0, keepdims=True)
    sm_ref[5:6, :wide] += jnp.sum(x32 * dy, axis=0, keepdims=True)
    sm_ref[6:7, :LANES] += jnp.sum(d_pre, axis=0, keepdims=True)
    sm_ref[7:8, :LANES] += jnp.sum(dt * decay_grad, axis=0, keepdims=True)


def local(hidden, lengths, out_grad, norm_gain, w_in, w_dt, conv_weight, conv_bias, dt_bias, a_log, skip_gain, gate_gain, w_out):
    ranks = lax.axis_size("seq")
    rank = lax.axis_index("seq")
    owners = lax.axis_size("head")
    owner = lax.axis_index("head")
    local_len, width = hidden.shape[1], hidden.shape[2]
    heads = HEADS // ranks
    wide = heads * HEAD_DIM
    chans = wide + 2 * STATE
    cols = wide + chans + LANES
    tokens = ranks * local_len
    chunk = min(CHUNK, local_len)
    steps = tokens // chunk
    shard = w_in.shape[0]

    small = jnp.concatenate([conv_weight.reshape(-1), conv_bias, dt_bias, a_log, skip_gain, gate_gain])
    small = lax.all_gather(small, "head")
    cs = CHANNELS // owners
    hs = HEADS // owners
    gs = DI // owners
    conv_w = small[:, : KERNEL * cs].reshape(owners, KERNEL, cs).swapaxes(0, 1).reshape(KERNEL, CHANNELS)
    at = KERNEL * cs
    conv_b = small[:, at : at + cs].reshape(CHANNELS)
    at += cs
    dt_b = small[:, at : at + hs].reshape(HEADS)
    at += hs
    a_all = small[:, at : at + hs].reshape(HEADS)
    at += hs
    skip_all = small[:, at : at + hs].reshape(HEADS)
    at += hs
    gain_all = small[:, at : at + gs].reshape(DI)

    def mine(v, size):
        return lax.dynamic_slice_in_dim(v, rank * size, size, v.ndim - 1)

    cw = jnp.concatenate([mine(conv_w[:, :DI], wide), conv_w[:, DI:]], axis=1).astype(F32)
    cb = jnp.concatenate([mine(conv_b[:DI], wide), conv_b[DI:]])[None].astype(F32)
    cw = jnp.concatenate([cw, jnp.zeros((8 - KERNEL, chans), F32)], axis=0)
    cb = jnp.broadcast_to(cb, (8, chans))
    dtb = jnp.broadcast_to(jnp.pad(mine(dt_b, heads).astype(F32), (0, LANES - heads))[None], (8, LANES))
    rate = -jnp.exp(mine(a_all, heads).astype(F32))
    rowp = jnp.stack(
        [
            jnp.repeat(rate, HEAD_DIM),
            jnp.repeat(mine(skip_all, heads).astype(F32), HEAD_DIM),
            mine(gain_all, wide).astype(F32),
            jnp.pad(rate, (0, wide - heads)),
        ]
        + [jnp.zeros((wide,), F32)] * 4
    )
    colp = jnp.broadcast_to(jnp.pad(rate, (0, LANES - heads))[:, None], (LANES, LANES))
    head_of = jnp.arange(wide, dtype=jnp.int32) // HEAD_DIM
    expand = (jnp.arange(LANES, dtype=jnp.int32)[:, None] == head_of[None]).astype(BF16)
    seg = expand.T

    gain_rows = norm_gain.astype(F32)[:, None]

    def scaled(v):
        return (v.astype(F32) * gain_rows).astype(BF16)

    sent = jnp.concatenate(
        [
            scaled(lax.dynamic_slice_in_dim(w_in, rank * wide, wide, 1)),
            scaled(lax.dynamic_slice_in_dim(w_in, DI + rank * wide, wide, 1)),
            scaled(w_in[:, 2 * DI :]),
            scaled(lax.dynamic_slice_in_dim(w_dt, rank * heads, heads, 1)),
            jnp.zeros((shard, LANES - heads), BF16),
        ],
        axis=1,
    )
    w_t = lax.all_gather(sent, "head", axis=0, tiled=True)
    w_o = lax.dynamic_slice_in_dim(lax.all_gather(w_out, "head", axis=0, tiled=True), rank * wide, wide, 0)
    h_all = lax.all_gather(hidden[0], "seq", axis=0, tiled=True)
    og_all = lax.all_gather(out_grad[0], "seq", axis=0, tiled=True)

    def forth(size):
        return pl.BlockSpec((chunk, size), lambda j: (j, 0))

    def back(size):
        return pl.BlockSpec((chunk, size), lambda j: (steps - 1 - j, 0))

    def whole(a):
        return pl.BlockSpec(a.shape, lambda j: (0,) * a.ndim, pipeline_mode=pl.Buffered(1))

    params = pltpu.CompilerParams(
        dimension_semantics=("arbitrary",), vmem_limit_bytes=56 * 1024 * 1024
    )
    grid = (steps,)

    def sds(shape, kind):
        return jax.ShapeDtypeStruct(shape, kind)

    z, u, act, slope, aux = pl.pallas_call(
        functools.partial(project_kernel, heads=heads, wide=wide),
        grid=grid,
        in_specs=[forth(width), whole(w_t), whole(cw), whole(cb), whole(dtb)],
        out_specs=[forth(wide), forth(chans), forth(chans), forth(chans), forth(LANES)],
        out_shape=[
            sds((tokens, wide), BF16),
            sds((tokens, chans), BF16),
            sds((tokens, chans), BF16),
            sds((tokens, chans), BF16),
            sds((tokens, LANES), F32),
        ],
        scratch_shapes=[pltpu.VMEM((chunk + 8, chans), F32)],
        compiler_params=params,
        cost_estimate=pl.CostEstimate(
            flops=2 * tokens * width * cols, bytes_accessed=2 * tokens * (width + 4 * chans), transcendentals=0
        ),
        name="project",
    )(h_all, w_t, cw, cb, dtb)

    d0 = dot_t(og_all, w_o).astype(BF16)

    y, gg, states, stat = pl.pallas_call(
        functools.partial(scan_kernel, heads=heads, wide=wide),
        grid=grid,
        in_specs=[forth(chans), forth(LANES), forth(wide), forth(wide), whole(expand), whole(rowp), whole(colp)],
        out_specs=[
            forth(wide),
            forth(wide),
            pl.BlockSpec((1, STATE, wide), lambda j: (j, 0, 0)),
            forth(LANES),
        ],
        out_shape=[
            sds((tokens, wide), F32),
            sds((tokens, wide), BF16),
            sds((steps, STATE, wide), F32),
            sds((tokens, LANES), F32),
        ],
        scratch_shapes=[pltpu.VMEM((STATE, wide), F32)],
        compiler_params=params,
        cost_estimate=pl.CostEstimate(
            flops=2 * tokens * wide * 6 * chunk, bytes_accessed=tokens * wide * 16, transcendentals=tokens * chunk * heads
        ),
        name="scan",
    )(act, aux, z, d0, expand, rowp, colp)

    sums = lax.psum(stat[:, :2].T.reshape(2, tokens // LANES, LANES), "seq").reshape(2, tokens)
    mask = (jnp.arange(tokens, dtype=jnp.int32) < lengths[0]).astype(F32)
    r1 = lax.rsqrt(sums[0] / DI + EPS)
    r1m = r1 * mask
    coef = r1m * r1 * r1 * sums[1] / DI
    lane = jnp.arange(LANES, dtype=jnp.int32)[None]
    stat2 = jnp.where(lane == 0, r1m[:, None], jnp.where(lane == 1, coef[:, None], 0.0))

    partial = dot(gg, w_o).astype(BF16)
    branch = lax.psum_scatter(partial, "seq", scatter_dimension=0, tiled=True)

    og_scaled = (og_all.astype(F32) * r1m[:, None]).astype(BF16)
    wog = t_dot(gg, og_scaled).astype(BF16)

    dp, sm = pl.pallas_call(
        functools.partial(back_kernel, heads=heads, wide=wide),
        grid=grid,
        in_specs=[
            back(chans), back(LANES), back(wide), back(wide), back(wide),
            pl.BlockSpec((1, STATE, wide), lambda j: (steps - 1 - j, 0, 0)),
            back(chans), back(chans), back(LANES),
            whole(expand), whole(seg), whole(rowp), whole(colp), whole(cw),
        ],
        out_specs=[back(cols), pl.BlockSpec((8, chans), lambda j: (0, 0))],
        out_shape=[sds((tokens, cols), BF16), sds((8, chans), F32)],
        scratch_shapes=[pltpu.VMEM((STATE, wide), F32), pltpu.VMEM((chunk + 8, chans), F32)],
        compiler_params=params,
        cost_estimate=pl.CostEstimate(
            flops=2 * tokens * wide * 12 * chunk, bytes_accessed=tokens * wide * 24, transcendentals=tokens * chunk * heads
        ),
        name="scan_back",
    )(act, aux, z, d0, y, states, slope, u, stat2, expand, seg, rowp, colp, cw)

    wig = t_dot(h_all, dp).astype(BF16)
    dn_part = dot_t(dp, w_t).astype(BF16)
    dn = lax.psum_scatter(dn_part, "seq", scatter_dimension=0, tiled=True).astype(F32)

    n_own = DI // owners
    if owners % ranks == 0 and n_own % owners == 0:
        pieces = wog.reshape(owners // ranks, owners, n_own // owners, width)
        pieces = lax.psum_scatter(pieces, "head", scatter_dimension=1, tiled=False)
        pieces = lax.all_gather(pieces, "seq", axis=0, tiled=True)
        w_out_grad = lax.all_to_all(pieces, "head", 0, 0, tiled=True).reshape(n_own, width).astype(F32)
    else:
        full = lax.all_gather(lax.psum(wog, "head"), "seq", axis=0, tiled=True)
        w_out_grad = lax.dynamic_slice_in_dim(full, owner * n_own, n_own, 0).astype(F32)
    gate_gain_grad = jnp.sum(w_out.astype(F32) * w_out_grad, axis=1) / gate_gain.astype(F32)

    rows_in = lax.psum_scatter(wig, "head", scatter_dimension=0, tiled=True)
    rows_in = lax.all_gather(rows_in, "seq")
    bc_cols = jnp.sum(rows_in[:, :, 2 * wide : wide + chans].astype(F32), axis=0)
    raw_in = jnp.concatenate(
        [rows_in[r, :, :wide].astype(F32) for r in range(ranks)]
        + [rows_in[r, :, wide : 2 * wide].astype(F32) for r in range(ranks)]
        + [bc_cols],
        axis=1,
    )
    raw_dt = jnp.concatenate(
        [rows_in[r, :, wide + chans : wide + chans + heads].astype(F32) for r in range(ranks)], axis=1
    )
    w_in_grad = raw_in * gain_rows
    w_dt_grad = raw_dt * gain_rows
    norm_gain_grad = jnp.sum(raw_in * w_in.astype(F32), axis=1) + jnp.sum(raw_dt * w_dt.astype(F32), axis=1)

    h32 = hidden[0].astype(F32)
    own_r1m = lax.dynamic_slice_in_dim(r1m, rank * local_len, local_len, 0)[:, None]
    block_out = (h32 + own_r1m * branch.astype(F32)).astype(BF16)[None]
    r0 = lax.rsqrt(jnp.mean(h32 * h32, axis=1, keepdims=True) + EPS)
    mixed = jnp.sum(dn * h32, axis=1, keepdims=True) / width
    hidden_grad = (out_grad[0].astype(F32) + dn - h32 * (r0 * r0 * mixed))[None]

    def laid(v, total, size):
        base = jnp.zeros(v.shape[:-1] + (total,), F32)
        return lax.dynamic_update_slice_in_dim(base, v, rank * size, v.ndim - 1)

    conv_all = jnp.concatenate([laid(sm[:5, :wide], DI, wide), sm[:5, wide:]], axis=1)
    skip_h = jnp.sum(sm[5, :wide].reshape(heads, HEAD_DIM), axis=1)
    vec = jnp.stack([sm[6, :heads], sm[7, :heads], skip_h])
    packed = jnp.concatenate([conv_all.reshape(-1), laid(vec, HEADS, heads).reshape(-1)])
    packed = lax.psum(packed, EVERY)
    n_conv = 5 * CHANNELS
    conv_all = packed[:n_conv].reshape(5, CHANNELS)
    vec = packed[n_conv:].reshape(3, HEADS)
    conv_own = lax.dynamic_slice_in_dim(conv_all, owner * cs, cs, 1)
    vec_own = lax.dynamic_slice_in_dim(vec, owner * hs, hs, 1)

    return (
        block_out,
        hidden_grad,
        norm_gain_grad,
        w_in_grad,
        w_dt_grad,
        conv_own[:KERNEL],
        conv_own[KERNEL],
        vec_own[0],
        vec_own[1],
        vec_own[2],
        gate_gain_grad,
        w_out_grad,
    )


def solution(mesh):
    rows = P("head", "seq", None)
    return jax.shard_map(
        local,
        mesh=mesh,
        in_specs=(
            rows, P("head"), rows, P("head"), P("head", None), P("head", None), P(None, "head"),
            P("head"), P("head"), P("head"), P("head"), P("head"), P("head", None),
        ),
        out_specs=(
            rows, rows, P("head"), P("head", None), P("head", None), P(None, "head"),
            P("head"), P("head"), P("head"), P("head"), P("head"), P("head", None),
        ),
        check_vma=False,
    )
```

```python
import functools

import jax
import jax.numpy as jnp
from jax import lax
from jax.experimental import pallas as pl
from jax.experimental.pallas import tpu as pltpu
from jax.sharding import PartitionSpec as P

HEADS = 64
HEAD_DIM = 64
STATE = 128
KERNEL = 4
CHUNK = 256
DI = 4096
CHANNELS = 4352
PROJ = DI + CHANNELS
EPS = 1e-05
LANES = 128
EVERY = ("seq", "head")
F32 = jnp.float32
BF16 = jnp.bfloat16


def dot(a, b):
    return jnp.dot(a, b, preferred_element_type=F32)


def dot_t(a, b):
    return lax.dot_general(a, b, (((1,), (1,)), ((), ())), preferred_element_type=F32)


def t_dot(a, b):
    return lax.dot_general(a, b, (((0,), (0,)), ((), ())), preferred_element_type=F32)


def sigmoid(v):
    return 1.0 / (1.0 + jnp.exp(-v))


def remote(src, dst, send, recv, target):
    return pltpu.make_async_remote_copy(
        src_ref=src, dst_ref=dst, send_sem=send, recv_sem=recv, device_id=target, device_id_type=pl.DeviceIdType.MESH
    )


def greet(peers, extra=()):
    barrier = pltpu.get_barrier_semaphore()
    count = len(peers)

    def hello(peer):
        pl.semaphore_signal(barrier, inc=1, device_id=peer, device_id_type=pl.DeviceIdType.MESH)

    for peer in peers:
        hello(peer)
    for there, peer in extra:
        pl.when(there)(functools.partial(hello, peer))
        count = count + jnp.where(there, 1, 0)
    pl.semaphore_wait(barrier, count)


def gather_kernel(
    hid_ref, og_ref, w_ref, wo_in_ref, gain_ref, dtw_ref,
    hall_ref, ogall_ref, wt_ref, wo_ref, z_ref, u_ref, d_ref, d0_ref,
    hv, ov, wv, wov, stage, zv, uv, dv, d0v,
    h_send, h_recv, o_send, o_recv, z_up, z_dn, z_recv, s_send, s_recv,
    c_up, c_dn, c_recv, t_send, t_recv, local_sem, out_sem, *, ring, wide,
):
    s = lax.axis_index("seq")
    q = hid_ref.shape[0]
    half = q // 2
    x_peer = s + 1 - 2 * lax.rem(s, 2)
    y_peer = lax.rem(s + 2, 4)
    far = 3 - s
    to_x, to_y = {"seq": x_peer}, {"seq": y_peer}
    chans = uv.shape[1]
    n_main = stage.shape[1]
    n = stage.shape[0]
    peers = [to_x, to_y]
    extra = []

    def block(ref, at, start, size):
        return ref.at[pl.ds(pl.multiple_of(at * q + start, 16), size), :]

    if ring:
        h = lax.axis_index("head")
        core = lax.rem(h, 2)
        r = h // 2
        last = lax.axis_size("head") // 2 - 1
        to_sib, to_up, to_down = {"head": h + 1 - 2 * core}, {"head": lax.rem(h + 2, 2 * last + 2)}, {"head": lax.rem(h + 2 * last, 2 * last + 2)}
        above, below = r < last, r > 0
        peers.append(to_sib)
        extra = [(above, to_up), (below, to_down)]
        first = pl.multiple_of(s * wide, LANES)
        second = pl.multiple_of(DI + s * wide, LANES)
        loads = [
            pltpu.make_async_copy(w_ref.at[:, pl.ds(first, wide)], stage.at[:, :wide], local_sem.at[0]),
            pltpu.make_async_copy(w_ref.at[:, pl.ds(second, wide)], stage.at[:, wide : 2 * wide], local_sem.at[1]),
            pltpu.make_async_copy(w_ref.at[:, 2 * DI :], stage.at[:, 2 * wide :], local_sem.at[2]),
        ]
        is_root = r == s
        n_o = wov.shape[0] // 2
        load_o = pltpu.make_async_copy(
            wo_in_ref, wov.at[pl.ds(pl.multiple_of(core * n_o, 16), n_o), :], local_sem.at[5]
        )
        pl.when(is_root)(load_o.start)
    else:
        loads = [
            pltpu.make_async_copy(w_ref, wv, local_sem.at[0]),
            pltpu.make_async_copy(wo_in_ref, wov, local_sem.at[5]),
        ]
    for copy in loads:
        copy.start()
    own_h = pltpu.make_async_copy(hid_ref, block(hv, s, 0, q), local_sem.at[3])
    own_o = pltpu.make_async_copy(og_ref, block(ov, s, 0, q), local_sem.at[4])
    own_h.start()
    own_o.start()
    greet(peers, extra)

    sent = []

    def send(src, dst, sems, i, target):
        copy = remote(src, dst, sems[0].at[i], sems[1].at[i], target)
        copy.start()
        sent.append(copy)
        return copy

    def open_exchange(src, buf, sems):
        return (
            send(src, block(buf, s, 0, q), sems, 0, to_x),
            send(src, block(buf, s, 0, q), sems, 1, to_y),
        )

    def relay(buf, sems, heads_in):
        heads_in[0].wait_recv()
        a = block(buf, x_peer, 0, half)
        first = send(a, a, sems, 2, to_y)
        heads_in[1].wait_recv()
        b = block(buf, y_peer, half, half)
        return first, send(b, b, sems, 3, to_x)

    h_sems, o_sems = (h_send, h_recv), (o_send, o_recv)
    h_open = open_exchange(hid_ref, hv, h_sems)

    closing = []
    if ring:
        def w_block(at):
            return wv.at[pl.ds(pl.multiple_of((2 * at + core) * n, 16), n), :]

        def w_copy(at, sems, target):
            return remote(w_block(at), w_block(at), sems.at[at], z_recv.at[at], target)

        def w_swap(at):
            return remote(w_block(at), w_block(at), s_send.at[at], s_recv.at[at], to_sib)

        def launch(there, make):
            @pl.when(there)
            def _():
                make().start()

            def finish():
                @pl.when(there)
                def _():
                    make().wait_send()

            closing.append(finish)

        always = r >= 0

        def w_step(k):
            lower, upper = r - k, r + k
            has_lower, has_upper = lower >= 0, upper <= last

            @pl.when(has_lower)
            def _():
                w_copy(lower, z_up, to_up).wait_recv()

            launch(has_lower & above, lambda: w_copy(lower, z_up, to_up))
            launch(has_lower, lambda: w_swap(lower))

            @pl.when(has_upper)
            def _():
                w_copy(upper, z_dn, to_down).wait_recv()

            launch(has_upper & below, lambda: w_copy(upper, z_dn, to_down))
            launch(has_upper, lambda: w_swap(upper))

        chunks = c_recv.shape[0]
        n_c = n_o // chunks
        dist = jnp.where(r > s, r - s, s - r)

        def o_block(i):
            return wov.at[pl.ds(pl.multiple_of(core * n_o + i * n_c, 16), n_c), :]

        def o_copy(i, sems, target):
            return remote(o_block(i), o_block(i), sems.at[i], c_recv.at[i], target)

        def o_swap(i):
            return remote(o_block(i), o_block(i), t_send.at[i], t_recv.at[i], to_sib)

        def o_root():
            @pl.when(is_root)
            def _():
                load_o.wait()

            for i in range(chunks):
                launch(is_root & above, lambda i=i: o_copy(i, c_up, to_up))
                launch(is_root & below, lambda i=i: o_copy(i, c_dn, to_down))
                launch(is_root, lambda i=i: o_swap(i))

        def o_tick(t):
            i = t - dist
            live = (dist >= 1) & (i >= 0) & (i < chunks)

            @pl.when(live)
            def _():
                o_copy(i, c_up, to_up).wait_recv()

            pl.when(live & (r > s) & above)(lambda: o_copy(i, c_up, to_up).start())
            pl.when(live & (r < s) & below)(lambda: o_copy(i, c_dn, to_down).start())
            pl.when(live)(lambda: o_swap(i).start())

        def o_finish():
            for i in range(chunks):
                pl.when((r > s) & above)(lambda: o_copy(i, c_up, to_up).wait_send())
                pl.when((r < s) & below)(lambda: o_copy(i, c_dn, to_down).wait_send())
                pl.when(dist >= 1)(lambda: o_swap(i).wait_send())

        closing.append(o_finish)
        for copy in loads:
            copy.wait()
        own = pl.ds(pl.multiple_of(h * n, 16), n)
        wv[own, :n_main] = (stage[...].astype(F32) * gain_ref[...]).astype(BF16)
        wv[own, n_main:] = dtw_ref[...]
        launch(above, lambda: w_copy(r, z_up, to_up))
        launch(below, lambda: w_copy(r, z_dn, to_down))
        launch(always, lambda: w_swap(r))
        w_step(1)
    else:
        for copy in loads:
            copy.wait()

    h_far = relay(hv, h_sems, h_open)
    if ring:
        w_step(2)
        o_root()
    for copy in h_far:
        copy.wait_recv()
    o_open = open_exchange(og_ref, ov, o_sems)
    if ring:
        o_tick(1)
        w_step(3)
        for at in range(4):
            w_swap(at).wait_recv()
    own_h.wait()
    own_o.wait()

    rows = min(CHUNK, q)

    def cut(at_block):
        return pl.ds(pl.multiple_of(at_block * q, 16), q)

    def project_outs(at_block, i):
        at = cut(at_block)
        pairs = ((hv, hall_ref), (zv, z_ref), (uv, u_ref), (dv, d_ref))
        return [
            pltpu.make_async_copy(src.at[at, :], dst.at[at, :], out_sem.at[4 * i + k])
            for k, (src, dst) in enumerate(pairs)
        ]

    def pull_outs(at_block, i):
        at = cut(at_block)
        pairs = ((ov, ogall_ref), (d0v, d0_ref))
        return [
            pltpu.make_async_copy(src.at[at, :], dst.at[at, :], out_sem.at[16 + 2 * i + k])
            for k, (src, dst) in enumerate(pairs)
        ]

    def nth(i):
        return jnp.where(i == 0, s, jnp.where(i == 1, x_peer, jnp.where(i == 2, y_peer, far)))

    w_out = pltpu.make_async_copy(wv, wt_ref, out_sem.at[24])
    o_out = pltpu.make_async_copy(wov, wo_ref, out_sem.at[25])
    w_out.start()

    def project(at_block):
        @pl.loop(0, q // rows)
        def _(j):
            at = pl.ds(pl.multiple_of(at_block * q + j * rows, 16), rows)
            hb = hv[at, :]
            h32 = hb.astype(F32)
            r0 = lax.rsqrt(jnp.mean(h32 * h32, axis=1, keepdims=True) + EPS)
            zv[at, :] = (dot(hb, wv[:, :wide]) * r0).astype(BF16)
            uv[at, :] = (dot(hb, wv[:, wide : wide + chans]) * r0).astype(BF16)
            raw = dot(hb, wv[:, wide + chans :]) * r0
            lane = lax.broadcasted_iota(jnp.int32, raw.shape, 1)
            dv[at, :] = jnp.where(lane == LANES - 1, r0, raw)

    def pull(at_block):
        at = cut(at_block)

        @pl.loop(0, wide // 256)
        def _(j):
            to = pl.ds(pl.multiple_of(j * 256, 256), 256)
            d0v[at, to] = dot_t(ov[at, :], wov[to, :]).astype(BF16)

    @pl.loop(0, 4)
    def _(i):
        at_block = nth(i)
        project(at_block)
        for copy in project_outs(at_block, i):
            copy.start()
        if ring:
            o_tick(2 + i)

    o_far = relay(ov, o_sems, o_open)
    if ring:
        o_tick(6)
        for i in range(chunks):
            o_swap(i).wait_recv()
    o_out.start()

    @pl.loop(0, 4)
    def _(i):
        at_block = nth(i)

        @pl.when(i == 3)
        def _():
            for copy in o_far:
                copy.wait_recv()

        pull(at_block)
        for copy in pull_outs(at_block, i):
            copy.start()

    for i, at_block in enumerate((s, x_peer, y_peer, far)):
        for copy in project_outs(at_block, i) + pull_outs(at_block, i):
            copy.wait()
    w_out.wait()
    o_out.wait()
    for copy in sent:
        copy.wait_send()
    for finish in closing:
        finish()


def decays(aux, heads, expand, rate_e, rate_row, rate_col):
    rows = aux.shape[0]
    lane = lax.broadcasted_iota(jnp.int32, aux.shape, 1)
    dt = jnp.where(lane < heads, aux, 0.0).astype(BF16)
    r = lax.broadcasted_iota(jnp.int32, (rows, rows), 0)
    c = lax.broadcasted_iota(jnp.int32, (rows, rows), 1)
    causal = c <= r
    lower = jnp.where(causal, 1.0, 0.0).astype(BF16)
    dt_e = dot(dt, expand)
    cum_e = dot(lower, dt_e.astype(BF16)) * rate_e
    cum_c = dot(lower, dt) * rate_row
    cum_t = lax.dot_general(dt, lower, (((0,), (1,)), ((), ())), preferred_element_type=F32) * rate_col
    return causal, dt_e, cum_e, cum_c, cum_t


def scan_kernel(
    u_ref, d_ref, z_ref, d0_ref, cw_ref, cb_ref, dtb_ref, exp_ref, rowp_ref, colp_ref,
    act_ref, slope_ref, aux_ref, y_ref, gg_ref, st_ref, sum_ref, state, ext, *, heads, wide,
):
    step = pl.program_id(0)
    rows = u_ref.shape[0]
    chans = u_ref.shape[1]

    @pl.when(step == 0)
    def _():
        state[...] = jnp.zeros_like(state)
        ext[0:8, :] = jnp.zeros((8, chans), F32)

    @pl.when(step > 0)
    def _():
        ext[0:8, :] = ext[rows : rows + 8, :]

    ext[8 : rows + 8, :] = u_ref[...].astype(F32)
    pre = cb_ref[0:1, :]
    for k in range(KERNEL):
        pre = pre + cw_ref[k : k + 1, :] * ext[pl.ds(8 - (KERNEL - 1) + k, rows), :]
    sig = sigmoid(pre)
    act = (pre * sig).astype(BF16)
    act_ref[...] = act
    slope_ref[...] = (sig * (1.0 + pre * (1.0 - sig))).astype(BF16)
    raw = d_ref[...]
    v = raw + dtb_ref[0:1, :]
    soft = jnp.maximum(v, 0.0) + jnp.log1p(jnp.exp(-jnp.abs(v)))
    soft = soft.astype(BF16).astype(F32)
    lane = lax.broadcasted_iota(jnp.int32, v.shape, 1)
    aux = jnp.where(lane < heads, soft, 0.0)
    sig_v = pltpu.roll(sigmoid(v), heads, 1)
    aux = jnp.where((lane >= heads) & (lane < 2 * heads), sig_v, aux)
    aux = jnp.where(lane == LANES - 1, raw, aux)
    aux_ref[...] = aux

    x = act[:, :wide]
    x32 = x.astype(F32)
    b = act[:, wide : wide + STATE]
    c = act[:, wide + STATE :]
    causal, dt_e, cum_e, cum_c, cum_t = decays(
        aux, heads, exp_ref[...], rowp_ref[0:1, :], rowp_ref[3:4, :LANES], colp_ref[:, 0:1]
    )
    xdt = x32 * dt_e
    xdt16 = xdt.astype(BF16)
    scores = dot_t(c, b)
    st = state[...]
    st_ref[0] = st
    half = lax.broadcasted_iota(jnp.int32, (rows, LANES), 1) < HEAD_DIM
    parts = []
    for pair in range(heads // 2):
        x2 = xdt16[:, LANES * pair : LANES * (pair + 1)]
        got = []
        for h in (2 * pair, 2 * pair + 1):
            spread = cum_c[:, h : h + 1] - cum_t[h : h + 1, :]
            m = (scores * jnp.exp(jnp.where(causal, spread, -1e30))).astype(BF16)
            got.append(dot(m, x2))
        parts.append(jnp.where(half, got[0], got[1]))
    y = jnp.concatenate(parts, axis=1) + dot(c, st.astype(BF16)) * jnp.exp(cum_e)
    last = cum_e[rows - 1 : rows, :]
    tail = jnp.exp(last - cum_e)
    state[...] = jnp.exp(last) * st + t_dot(b, (xdt * tail).astype(BF16))
    y_ref[...] = y
    ssd = (y + rowp_ref[1:2, :] * x32).astype(BF16).astype(F32)
    z = z_ref[...].astype(F32)
    g = ssd * (z * sigmoid(z))
    gg = g * rowp_ref[2:3, :]
    gg_ref[...] = gg.astype(BF16)
    ones = jnp.ones((8, wide), BF16)
    ssq = dot_t(ones, (g * g).astype(BF16))
    cross = dot_t(ones, (gg * d0_ref[...].astype(F32)).astype(BF16))
    sub = lax.broadcasted_iota(jnp.int32, ssq.shape, 0)
    sum_ref[...] = jnp.where(sub == 0, ssq, cross)


def seg_dot(v, seg):
    hi = v.astype(BF16)
    rest = v - hi.astype(F32)
    mid = rest.astype(BF16)
    low = (rest - mid.astype(F32)).astype(BF16)
    return dot(hi, seg) + dot(mid, seg) + dot(low, seg)


def back_kernel(
    act_ref, aux_ref, z_ref, d0_ref, y_ref, st_ref, slope_ref, u_ref, stat_ref,
    exp_ref, seg_ref, rowp_ref, colp_ref, cw_ref,
    dp_ref, sm_ref, adj, ext, *, heads, wide,
):
    step = pl.program_id(0)
    rows = act_ref.shape[0]
    chans = u_ref.shape[1]

    @pl.when(step == 0)
    def _():
        sm_ref[...] = jnp.zeros_like(sm_ref)
        adj[...] = jnp.zeros_like(adj)
        ext[rows : rows + 8, :] = jnp.zeros((8, chans), F32)

    @pl.when(step > 0)
    def _():
        ext[rows : rows + 8, :] = ext[0:8, :]

    x = act_ref[:, :wide]
    x32 = x.astype(F32)
    b = act_ref[:, wide : wide + STATE]
    c = act_ref[:, wide + STATE :]
    aux = aux_ref[...]
    stat = stat_ref[...]
    r1m = stat[:, 0:1]
    coef = stat[:, 1:2]
    r0 = aux[:, LANES - 1 : LANES]
    skip_e = rowp_ref[1:2, :]
    gain = rowp_ref[2:3, :]

    y = y_ref[...]
    ssd = (y + skip_e * x32).astype(BF16).astype(F32)
    z = z_ref[...].astype(F32)
    sig = sigmoid(z)
    sz = z * sig
    d_gated = (r1m * gain) * d0_ref[...].astype(F32) - (ssd * sz) * coef
    dy16 = (d_gated * sz).astype(BF16)
    dy = dy16.astype(F32)
    dp_ref[:, :wide] = (r0 * (d_gated * ssd * (sig * (1.0 + z * (1.0 - sig))))).astype(BF16)

    causal, dt_e, cum_e, cum_c, cum_t = decays(
        aux, heads, exp_ref[...], rowp_ref[0:1, :], rowp_ref[3:4, :LANES], colp_ref[:, 0:1]
    )
    xdt = x32 * dt_e
    xdt16 = xdt.astype(BF16)
    scores = dot_t(c, b)
    st = st_ref[0]
    st16 = st.astype(BF16)
    q_in = adj[...]
    q16 = q_in.astype(BF16)
    last = cum_e[rows - 1 : rows, :]
    ecum = jnp.exp(cum_e)
    tail = jnp.exp(last - cum_e)
    half = lax.broadcasted_iota(jnp.int32, (rows, LANES), 1) < HEAD_DIM
    zero = jnp.zeros((rows, LANES), BF16)
    n_sum = None
    parts = []
    for pair in range(heads // 2):
        cut = slice(LANES * pair, LANES * (pair + 1))
        x2 = xdt16[:, cut]
        dy2 = dy16[:, cut]
        got = []
        for side in range(2):
            h = 2 * pair + side
            spread = cum_c[:, h : h + 1] - cum_t[h : h + 1, :]
            ell = jnp.exp(jnp.where(causal, spread, -1e30))
            m = (scores * ell).astype(BF16)
            got.append(t_dot(m, dy2))
            own = half if side == 0 else jnp.logical_not(half)
            n = dot_t(jnp.where(own, dy2, zero), x2) * ell
            n_sum = n if n_sum is None else n_sum + n
        parts.append(jnp.where(half, got[0], got[1]))
    out_part = dot(b, q16) * tail
    v = jnp.concatenate(parts, axis=1) + out_part
    n16 = n_sum.astype(BF16)
    dy_e = (dy * ecum).astype(BF16)
    x_tail = (xdt * tail).astype(BF16)
    d_b = t_dot(n16, c) + dot_t(x_tail, q16)
    d_c = dot(n16, b) + dot_t(dy_e, st16)
    elast = jnp.exp(last)
    adj[...] = elast * q_in + t_dot(c, dy_e)

    seg = seg_ref[...]
    flow = dy * y - xdt16.astype(F32) * v
    passed = jnp.sum(xdt16.astype(F32) * out_part, axis=0, keepdims=True)
    passed = passed + elast * jnp.sum(q_in * st, axis=0, keepdims=True)
    flow_h = seg_dot(flow, seg)
    passed_h = seg_dot(jnp.broadcast_to(passed, (8, wide)), seg)[0:1, :]
    upper = jnp.where(
        lax.broadcasted_iota(jnp.int32, (rows, rows), 1) >= lax.broadcasted_iota(jnp.int32, (rows, rows), 0), 1.0, 0.0
    ).astype(BF16)
    hi = flow_h.astype(BF16)
    rest = flow_h - hi.astype(F32)
    mid = rest.astype(BF16)
    low = (rest - mid.astype(F32)).astype(BF16)
    crossing = dot(upper, hi) + dot(upper, mid) + dot(upper, low) + passed_h
    rate_row = rowp_ref[3:4, :LANES]
    decay_grad = rate_row * crossing
    d_dt = seg_dot(x32 * v, seg) + decay_grad
    lane = lax.broadcasted_iota(jnp.int32, (rows, LANES), 1)
    sig_v = pltpu.roll(aux, LANES - heads, 1)
    d_pre = jnp.where(lane < heads, d_dt * sig_v, 0.0)
    dt = jnp.where(lane < heads, aux, 0.0)
    dp_ref[:, wide + chans :] = (r0 * d_pre).astype(BF16)

    d_act = jnp.concatenate([skip_e * dy + dt_e * v, d_b, d_c], axis=1)
    d_conv = d_act * slope_ref[...].astype(F32)
    ext[0:rows, :] = d_conv
    u = u_ref[...].astype(F32)
    d_u = None
    for k in range(KERNEL):
        moved = ext[pl.ds(KERNEL - 1 - k, rows), :]
        term = cw_ref[k : k + 1, :] * moved
        d_u = term if d_u is None else d_u + term
        sm_ref[k : k + 1, :] += jnp.sum(u * moved, axis=0, keepdims=True)
    dp_ref[:, wide : wide + chans] = (r0 * d_u).astype(BF16)
    sm_ref[4:5, :] += jnp.sum(d_conv, axis=0, keepdims=True)
    sm_ref[5:6, :wide] += jnp.sum(x32 * dy, axis=0, keepdims=True)
    sm_ref[6:7, :LANES] += jnp.sum(d_pre, axis=0, keepdims=True)
    sm_ref[7:8, :LANES] += jnp.sum(dt * decay_grad, axis=0, keepdims=True)


def grads_kernel(
    dp_ref, w_ref, h_ref, piece_ref, tiny_ref,
    dn_ref, win_ref, wout_ref,
    dpv, wv, hb, far_p, y_p, x_p, far_a, far_b, y_f, x_f, dn_o, sib_s, mine_s, own_s, z_u, z_d, pv,
    load_sem, hb_sem, d_send, d_recv, s_send, s_recv, zu_send, zu_recv, zd_send, zd_recv,
    g_send, g_recv, p_send, p_recv, w_send, w_recv, out_sem,
):
    s = lax.axis_index("seq")
    h = lax.axis_index("head")
    owners = lax.axis_size("head")
    last = owners // 2 - 1
    core = lax.rem(h, 2)
    r = h // 2
    x_peer = s + 1 - 2 * lax.rem(s, 2)
    y_peer = lax.rem(s + 2, 4)
    far = 3 - s
    to_x, to_y = {"seq": x_peer}, {"seq": y_peer}
    to_sib = {"head": h + 1 - 2 * core}
    to_up, to_down = {"head": lax.rem(h + 2, owners)}, {"head": lax.rem(h + owners - 2, owners)}
    above, below = r < last, r > 0
    q = far_p.shape[0]
    half = q // 2
    n, cols = own_s.shape[1], own_s.shape[2]
    spare = LANES // 2
    tiles = cols // LANES
    edges = [LANES * (tiles * k // 4) for k in range(5)]
    spans = list(zip(edges[:-1], edges[1:]))
    sent = []
    closing = []

    def push(src, dst, sems, i, target):
        copy = remote(src, dst, sems[0].at[i], sems[1].at[i], target)
        copy.start()
        sent.append(copy)
        return copy

    def launch(there, make):
        @pl.when(there)
        def _():
            make().start()

        def finish():
            @pl.when(there)
            def _():
                make().wait_send()

        closing.append(finish)

    load_dp = pltpu.make_async_copy(dp_ref, dpv, load_sem.at[0])
    load_w = pltpu.make_async_copy(w_ref, wv, load_sem.at[1])
    load_dp.start()
    load_w.start()

    def chip(i):
        return jnp.where(lax.rem(i, 2) == 0, last - i // 2, i // 2)

    def load_h(i, other):
        at = 2 * chip(i) + (1 - core if other else core)
        slot = 0 if other else 1
        return pltpu.make_async_copy(
            h_ref.at[:, pl.ds(pl.multiple_of(at * n, LANES), n)], hb.at[slot], hb_sem.at[slot]
        )

    load_h(0, True).start()
    load_h(0, False).start()
    to_heads = [{"head": lax.rem(h + k, owners)} for k in range(1, owners)]
    greet([to_x, to_y] + to_heads)

    d_sems = (d_send, d_recv)
    g_sems = (g_send, g_recv)

    w_sems = (w_send, w_recv)
    own_piece = pltpu.make_async_copy(piece_ref, pv.at[s], load_sem.at[2])
    own_piece.start()
    w0 = push(piece_ref, pv.at[s], w_sems, 0, to_x)
    w1 = push(piece_ref, pv.at[s], w_sems, 1, to_y)
    tile = 256

    def part(block, out):
        at = pl.ds(pl.multiple_of(block * q, 16), q)

        @pl.loop(0, wv.shape[0] // tile)
        def _(j):
            to = pl.ds(pl.multiple_of(j * tile, tile), tile)
            out[:, to] = dot_t(dpv[at, :], wv[to, :]).astype(BF16)

    def add_to(out, at, extra):
        out[at, :] = (out[at, :].astype(F32) + extra.astype(F32)).astype(BF16)

    def swap(i):
        t = chip(i)
        return remote(sib_s.at[lax.rem(i, 2)], own_s.at[t], s_send.at[t], s_recv.at[t], to_sib)

    def rows_of(i):
        t = chip(i)
        slot = lax.rem(i, 2)

        @pl.when(i >= 2)
        def _():
            swap(i - 2).wait_send()

        load_h(i, True).wait()
        for lo, hi in spans:
            sib_s[slot, :, lo:hi] = t_dot(hb[0], dpv[:, lo:hi]).astype(BF16)
        sib_s[slot, :, cols - spare :] = tiny_ref[...]
        swap(i).start()

        @pl.when(i < 3)
        def _():
            load_h(i + 1, True).start()

        load_h(i, False).wait()
        for lo, hi in spans:
            mine_s[:, lo:hi] = t_dot(hb[1], dpv[:, lo:hi]).astype(BF16)
        mine_s[:, cols - spare :] = tiny_ref[...]

        @pl.when(i < 3)
        def _():
            load_h(i + 1, False).start()

        swap(i).wait_recv()
        join(t, mine_s)

    def join(t, extra):
        for lo, hi in spans:
            own_s[t, :, lo:hi] = (own_s[t, :, lo:hi].astype(F32) + extra[:, lo:hi].astype(F32)).astype(BF16)

    def up_copy(t):
        return remote(own_s.at[t], z_u.at[t - 1], zu_send.at[t], zu_recv.at[t], to_up)

    def down_copy(t):
        return remote(own_s.at[t], z_d.at[t], zd_send.at[t], zd_recv.at[t], to_down)

    def up_add(t):
        up_copy(t).wait_recv()
        join(t, z_u.at[t - 1])

    def down_add(t):
        down_copy(t).wait_recv()
        join(t, z_d.at[t])

    def pass_on(t, there, add, make):
        pl.when(there)(functools.partial(add, t))
        launch(there, lambda: make(t))

    def follow(t, there, make, before):
        @pl.when(there)
        def _():
            make(before).wait_send()
            make(t).start()

    def finish_later(t, there, make):
        def finish():
            @pl.when(there)
            def _():
                make(t).wait_send()

        closing.append(finish)

    load_dp.wait()
    load_w.wait()
    part(far, far_p)
    d0 = push(far_p.at[:half], far_a, d_sems, 0, to_x)
    d1 = push(far_p.at[half:], far_b, d_sems, 1, to_y)
    own_piece.wait()
    w0.wait_recv()
    piece_a = pv.at[x_peer, 0]
    w2 = push(piece_a, piece_a, w_sems, 2, to_y)
    w1.wait_recv()
    piece_b = pv.at[y_peer, 1]
    w3 = push(piece_b, piece_b, w_sems, 3, to_x)
    pl.loop(0, 2)(rows_of)
    @pl.when(r == 0)
    def _():
        up_copy(last).start()

    @pl.when(r == last)
    def _():
        down_copy(0).start()

    part(y_peer, y_p)
    d0.wait_recv()
    add_to(y_p, slice(0, half), far_a[...])
    d2 = push(y_p, y_f, d_sems, 2, to_y)
    part(x_peer, x_p)
    d1.wait_recv()
    add_to(x_p, slice(half, q), far_b[...])
    d3 = push(x_p, x_f, d_sems, 3, to_x)
    pl.loop(2, 4)(rows_of)

    follow(2, r == 0, up_copy, last)
    follow(1, r == last, down_copy, 0)
    pass_on(last, (r > 0) & above, up_add, up_copy)
    pass_on(0, (r < last) & below, down_add, down_copy)
    follow(1, r == 0, up_copy, 2)
    follow(2, r == last, down_copy, 1)
    pass_on(2, r == 1, up_add, up_copy)
    pass_on(1, r == 2, down_add, down_copy)
    finish_later(1, r == 0, up_copy)
    finish_later(2, r == last, down_copy)
    pl.when(r > 0)(lambda: up_add(r))
    pl.when(r < last)(lambda: down_add(r))

    red = own_s.at[r]
    g0 = push(red, win_ref.at[s], g_sems, 0, to_x)
    g1 = push(red, win_ref.at[s], g_sems, 1, to_y)
    own_win = pltpu.make_async_copy(red, win_ref.at[s], load_sem.at[3])
    own_win.start()
    w2.wait_recv()
    w3.wait_recv()
    per = owners // 4

    def piece_of(head):
        return pv.at[head // per, lax.rem(head, per)]

    pieces = []
    for k, peer in enumerate(to_heads):
        pieces.append(push(piece_of(peer["head"]), wout_ref.at[h], (p_send, p_recv), k, peer))
    own_piece = pltpu.make_async_copy(piece_of(h), wout_ref.at[h], load_sem.at[2])
    own_piece.start()

    d2.wait_recv()
    d3.wait_recv()

    def dn_out(j):
        to = pl.ds(pl.multiple_of(j * tile, tile), tile)
        return pltpu.make_async_copy(dn_o.at[lax.rem(j, 2)], dn_ref.at[:, to], out_sem.at[lax.rem(j, 2)])

    own_at = pl.ds(pl.multiple_of(s * q, 16), q)
    tiles_n = wv.shape[0] // tile

    @pl.loop(0, tiles_n)
    def _(j):
        to = pl.ds(pl.multiple_of(j * tile, tile), tile)
        got = dot_t(dpv[own_at, :], wv[to, :])

        @pl.when(j > 1)
        def _():
            dn_out(j - 2).wait()

        dn_o[lax.rem(j, 2)] = got + y_f[:, to].astype(F32) + x_f[:, to].astype(F32)
        dn_out(j).start()

    g0.wait_recv()
    part_a = win_ref.at[x_peer, : n // 2]
    g2 = push(part_a, part_a, g_sems, 2, to_y)
    g1.wait_recv()
    part_b = win_ref.at[y_peer, n // 2 :]
    g3 = push(part_b, part_b, g_sems, 3, to_x)
    dn_out(tiles_n - 2).wait()
    dn_out(tiles_n - 1).wait()
    own_win.wait()
    own_piece.wait()
    for copy in pieces:
        copy.wait_recv()
    g2.wait_recv()
    g3.wait_recv()
    for i in (2, 3):
        swap(i).wait_send()
    for copy in sent:
        copy.wait_send()
    for finish in closing:
        finish()


def local(hidden, lengths, out_grad, norm_gain, w_in, w_dt, conv_weight, conv_bias, dt_bias, a_log, skip_gain, gate_gain, w_out):
    ranks = lax.axis_size("seq")
    rank = lax.axis_index("seq")
    owners = lax.axis_size("head")
    owner = lax.axis_index("head")
    local_len, width = hidden.shape[1], hidden.shape[2]
    heads = HEADS // ranks
    wide = heads * HEAD_DIM
    chans = wide + 2 * STATE
    cols = wide + chans + LANES
    tokens = ranks * local_len
    chunk = min(CHUNK, local_len)
    steps = tokens // chunk
    shard = w_in.shape[0]

    gain_rows = norm_gain.astype(F32)[:, None]

    def scaled(v):
        return (v.astype(F32) * gain_rows).astype(BF16)

    spare = LANES // 2
    small = jnp.concatenate([conv_weight.reshape(-1), conv_bias, dt_bias, a_log, skip_gain, gate_gain])
    n_small = small.shape[0]
    small = jnp.pad(small, (0, shard * spare - n_small)).reshape(shard, spare)
    last_block = jnp.concatenate(
        [
            scaled(lax.dynamic_slice_in_dim(w_dt, rank * heads, heads, 1)),
            jnp.zeros((shard, LANES - spare - heads), BF16),
            small,
        ],
        axis=1,
    )
    ring = owners == 2 * ranks
    if ring:
        w_given, o_given = w_in, w_out
    else:
        w_given = lax.all_gather(
            jnp.concatenate(
                [
                    scaled(lax.dynamic_slice_in_dim(w_in, rank * wide, wide, 1)),
                    scaled(lax.dynamic_slice_in_dim(w_in, DI + rank * wide, wide, 1)),
                    scaled(w_in[:, 2 * DI :]),
                    last_block,
                ],
                axis=1,
            ),
            "head", axis=0, tiled=True,
        )
        o_given = lax.dynamic_slice_in_dim(lax.all_gather(w_out, "head", axis=0, tiled=True), rank * wide, wide, 0)

    def sds(shape, kind):
        return jax.ShapeDtypeStruct(shape, kind)

    hbm = pl.BlockSpec(memory_space=pl.ANY)
    vmem = pl.BlockSpec(memory_space=pltpu.VMEM)

    def dma(count):
        return pltpu.SemaphoreType.DMA((count,))

    h_all, og_all, w_t, w_o, z, u, d_raw, d0 = pl.pallas_call(
        functools.partial(gather_kernel, ring=ring, wide=wide),
        in_specs=[hbm, hbm, hbm, hbm, vmem, vmem],
        out_specs=[hbm] * 8,
        out_shape=[
            sds((tokens, width), BF16),
            sds((tokens, width), BF16),
            sds((width, cols), BF16),
            sds((wide, width), BF16),
            sds((tokens, wide), BF16),
            sds((tokens, chans), BF16),
            sds((tokens, LANES), F32),
            sds((tokens, wide), BF16),
        ],
        scratch_shapes=[
            pltpu.VMEM((tokens, width), BF16),
            pltpu.VMEM((tokens, width), BF16),
            pltpu.VMEM((width, cols), BF16),
            pltpu.VMEM((wide, width), BF16),
            pltpu.VMEM((shard, cols - LANES), BF16),
            pltpu.VMEM((tokens, wide), BF16),
            pltpu.VMEM((tokens, chans), BF16),
            pltpu.VMEM((tokens, LANES), F32),
            pltpu.VMEM((tokens, wide), BF16),
        ]
        + [dma(4)] * 14
        + [dma(6), dma(26)],
        compiler_params=pltpu.CompilerParams(
            collective_id=0, has_side_effects=True, vmem_limit_bytes=56 * 1024 * 1024
        ),
        cost_estimate=pl.CostEstimate(
            flops=2 * tokens * width * (cols + wide), bytes_accessed=4 * tokens * (width + cols), transcendentals=0
        ),
        name="gather_project",
    )(hidden[0], out_grad[0], w_given, o_given, gain_rows, last_block)

    small = w_t.reshape(owners, shard, cols)[:, :, cols - spare :].reshape(owners, shard * spare)
    cs = CHANNELS // owners
    hs = HEADS // owners
    gs = DI // owners
    conv_w = small[:, : KERNEL * cs].reshape(owners, KERNEL, cs).swapaxes(0, 1).reshape(KERNEL, CHANNELS)
    at = KERNEL * cs
    conv_b = small[:, at : at + cs].reshape(CHANNELS)
    at += cs
    dt_b = small[:, at : at + hs].reshape(HEADS)
    at += hs
    a_all = small[:, at : at + hs].reshape(HEADS)
    at += hs
    skip_all = small[:, at : at + hs].reshape(HEADS)
    at += hs
    gain_all = small[:, at : at + gs].reshape(DI)

    def mine(v, size):
        return lax.dynamic_slice_in_dim(v, rank * size, size, v.ndim - 1)

    cw = jnp.concatenate([mine(conv_w[:, :DI], wide), conv_w[:, DI:]], axis=1).astype(F32)
    cb = jnp.concatenate([mine(conv_b[:DI], wide), conv_b[DI:]])[None].astype(F32)
    cw = jnp.concatenate([cw, jnp.zeros((8 - KERNEL, chans), F32)], axis=0)
    cb = jnp.broadcast_to(cb, (8, chans))
    dtb = jnp.broadcast_to(jnp.pad(mine(dt_b, heads).astype(F32), (0, LANES - heads))[None], (8, LANES))
    rate = -jnp.exp(mine(a_all, heads).astype(F32))
    rowp = jnp.stack(
        [
            jnp.repeat(rate, HEAD_DIM),
            jnp.repeat(mine(skip_all, heads).astype(F32), HEAD_DIM),
            mine(gain_all, wide).astype(F32),
            jnp.pad(rate, (0, wide - heads)),
        ]
        + [jnp.zeros((wide,), F32)] * 4
    )
    colp = jnp.broadcast_to(jnp.pad(rate, (0, LANES - heads))[:, None], (LANES, LANES))
    head_of = jnp.arange(wide, dtype=jnp.int32) // HEAD_DIM
    expand = (jnp.arange(LANES, dtype=jnp.int32)[:, None] == head_of[None]).astype(BF16)
    seg = expand.T

    def forth(size):
        return pl.BlockSpec((chunk, size), lambda j: (j, 0))

    def back(size):
        return pl.BlockSpec((chunk, size), lambda j: (steps - 1 - j, 0))

    def whole(a):
        return pl.BlockSpec(a.shape, lambda j: (0,) * a.ndim, pipeline_mode=pl.Buffered(1))

    params = pltpu.CompilerParams(
        dimension_semantics=("arbitrary",), vmem_limit_bytes=56 * 1024 * 1024
    )
    grid = (steps,)

    act, slope, aux, y, gg, states, sums = pl.pallas_call(
        functools.partial(scan_kernel, heads=heads, wide=wide),
        grid=grid,
        in_specs=[
            forth(chans), forth(LANES), forth(wide), forth(wide),
            whole(cw), whole(cb), whole(dtb), whole(expand), whole(rowp), whole(colp),
        ],
        out_specs=[
            forth(chans), forth(chans), forth(LANES), forth(wide), forth(wide),
            pl.BlockSpec((1, STATE, wide), lambda j: (j, 0, 0)),
            pl.BlockSpec((8, chunk), lambda j: (0, j)),
        ],
        out_shape=[
            sds((tokens, chans), BF16),
            sds((tokens, chans), BF16),
            sds((tokens, LANES), F32),
            sds((tokens, wide), F32),
            sds((tokens, wide), BF16),
            sds((steps, STATE, wide), F32),
            sds((8, tokens), F32),
        ],
        scratch_shapes=[pltpu.VMEM((STATE, wide), F32), pltpu.VMEM((chunk + 8, chans), F32)],
        compiler_params=params,
        cost_estimate=pl.CostEstimate(
            flops=2 * tokens * wide * 12 * chunk, bytes_accessed=tokens * wide * 16, transcendentals=tokens * chunk * heads
        ),
        name="scan",
    )(u, d_raw, z, d0, cw, cb, dtb, expand, rowp, colp)

    sums = lax.psum(sums[:2].reshape(2, tokens // LANES, LANES), "seq").reshape(2, tokens)
    mask = (jnp.arange(tokens, dtype=jnp.int32) < lengths[0]).astype(F32)
    r1 = lax.rsqrt(sums[0] / DI + EPS)
    r1m = r1 * mask
    coef = r1m * r1 * r1 * sums[1] / DI
    lane = jnp.arange(LANES, dtype=jnp.int32)[None]
    stat2 = jnp.where(lane == 0, r1m[:, None], jnp.where(lane == 1, coef[:, None], 0.0))

    partial = dot(gg, w_o).astype(BF16)
    og_scaled = (og_all.astype(F32) * r1m[:, None]).astype(BF16)
    wog = t_dot(gg, og_scaled).astype(BF16)
    stat2, wog, partial = lax.optimization_barrier((stat2, wog, partial))
    branch = lax.psum_scatter(partial, "seq", scatter_dimension=0, tiled=True)

    dp, sm = pl.pallas_call(
        functools.partial(back_kernel, heads=heads, wide=wide),
        grid=grid,
        in_specs=[
            back(chans), back(LANES), back(wide), back(wide), back(wide),
            pl.BlockSpec((1, STATE, wide), lambda j: (steps - 1 - j, 0, 0)),
            back(chans), back(chans), back(LANES),
            whole(expand), whole(seg), whole(rowp), whole(colp), whole(cw),
        ],
        out_specs=[back(cols), pl.BlockSpec((8, chans), lambda j: (0, 0))],
        out_shape=[sds((tokens, cols), BF16), sds((8, chans), F32)],
        scratch_shapes=[pltpu.VMEM((STATE, wide), F32), pltpu.VMEM((chunk + 8, chans), F32)],
        compiler_params=params,
        cost_estimate=pl.CostEstimate(
            flops=2 * tokens * wide * 12 * chunk, bytes_accessed=tokens * wide * 24, transcendentals=tokens * chunk * heads
        ),
        name="scan_back",
    )(act, aux, z, d0, y, states, slope, u, stat2, expand, seg, rowp, colp, cw)

    skip_h = jnp.sum(sm[5, :wide].reshape(heads, HEAD_DIM), axis=1)
    tiny = jnp.concatenate([sm[:5].reshape(-1), sm[6, :heads], sm[7, :heads], skip_h])
    n_own = DI // owners
    if ring:
        piece = n_own // owners
        pieces = wog.reshape(owners // ranks, owners, piece, width).swapaxes(0, 1)
        pieces = lax.psum_scatter(pieces, "head", scatter_dimension=0, tiled=False)
        dp, pieces, branch = lax.optimization_barrier((dp, pieces, branch))
        laid = jnp.pad(tiny, (0, shard * spare - tiny.shape[0])).reshape(shard, spare).astype(BF16)
        dn, rows_in, w_out_grad = pl.pallas_call(
            grads_kernel,
            in_specs=[hbm, hbm, hbm, hbm, vmem],
            out_specs=[hbm] * 3,
            out_shape=[
                sds((local_len, width), F32),
                sds((ranks, shard, cols), BF16),
                sds((owners, piece, width), BF16),
            ],
            scratch_shapes=[
                pltpu.VMEM((tokens, cols), BF16),
                pltpu.VMEM((width, cols), BF16),
                pltpu.VMEM((2, tokens, shard), BF16),
            ]
            + [pltpu.VMEM((local_len, width), BF16)] * 3
            + [pltpu.VMEM((local_len // 2, width), BF16)] * 2
            + [pltpu.VMEM((local_len, width), BF16)] * 2
            + [
                pltpu.VMEM((2, local_len, 256), F32),
                pltpu.VMEM((2, shard, cols), BF16),
                pltpu.VMEM((shard, cols), BF16),
                pltpu.VMEM((4, shard, cols), BF16),
                pltpu.VMEM((3, shard, cols), BF16),
                pltpu.VMEM((3, shard, cols), BF16),
                pltpu.VMEM((ranks, owners // ranks, piece, width), BF16),
            ]
            + [dma(4), dma(2)]
            + [dma(4)] * 10
            + [dma(owners)] * 2
            + [dma(4)] * 2
            + [dma(2)],
            compiler_params=pltpu.CompilerParams(
                collective_id=1, has_side_effects=True, vmem_limit_bytes=56 * 1024 * 1024
            ),
            cost_estimate=pl.CostEstimate(
                flops=4 * tokens * width * cols, bytes_accessed=8 * tokens * cols, transcendentals=0
            ),
            name="weight_grads",
        )(dp, w_t, h_all, pieces, laid)
        w_out_grad = w_out_grad.reshape(n_own, width).astype(F32)
        tiny_all = rows_in[:, :, cols - spare :].reshape(ranks, shard * spare)[:, : tiny.shape[0]].astype(F32)
    else:
        full = lax.all_gather(lax.psum(wog, "head"), "seq", axis=0, tiled=True)
        w_out_grad = lax.dynamic_slice_in_dim(full, owner * n_own, n_own, 0).astype(F32)
        wig = t_dot(h_all, dp).astype(BF16)
        dn = lax.psum_scatter(dot_t(dp, w_t).astype(BF16), "seq", scatter_dimension=0, tiled=True).astype(F32)
        rows_in = lax.all_gather(lax.psum_scatter(wig, "head", scatter_dimension=0, tiled=True), "seq")
        tiny_all = lax.all_gather(lax.psum(tiny, "head"), "seq")
    gate_gain_grad = jnp.sum(w_out.astype(F32) * w_out_grad, axis=1) / gate_gain.astype(F32)

    bc_cols = jnp.sum(rows_in[:, :, 2 * wide : wide + chans].astype(F32), axis=0)
    raw_in = jnp.concatenate(
        [rows_in[r, :, :wide].astype(F32) for r in range(ranks)]
        + [rows_in[r, :, wide : 2 * wide].astype(F32) for r in range(ranks)]
        + [bc_cols],
        axis=1,
    )
    raw_dt = jnp.concatenate(
        [rows_in[r, :, wide + chans : wide + chans + heads].astype(F32) for r in range(ranks)], axis=1
    )
    w_in_grad = raw_in * gain_rows
    w_dt_grad = raw_dt * gain_rows
    norm_gain_grad = jnp.sum(raw_in * w_in.astype(F32), axis=1) + jnp.sum(raw_dt * w_dt.astype(F32), axis=1)

    h32 = hidden[0].astype(F32)
    own_r1m = lax.dynamic_slice_in_dim(r1m, rank * local_len, local_len, 0)[:, None]
    block_out = (h32 + own_r1m * branch.astype(F32)).astype(BF16)[None]
    r0 = lax.rsqrt(jnp.mean(h32 * h32, axis=1, keepdims=True) + EPS)
    mixed = jnp.sum(dn * h32, axis=1, keepdims=True) / width
    hidden_grad = (out_grad[0].astype(F32) + dn - h32 * (r0 * r0 * mixed))[None]

    n_conv = 5 * chans
    conv_all = tiny_all[:, :n_conv].reshape(ranks, 5, chans)
    conv_all = jnp.concatenate(
        [conv_all[:, :, :wide].swapaxes(0, 1).reshape(5, DI), jnp.sum(conv_all[:, :, wide:], axis=0)], axis=1
    )
    vec = tiny_all[:, n_conv:].reshape(ranks, 3, heads).swapaxes(0, 1).reshape(3, HEADS)
    conv_own = lax.dynamic_slice_in_dim(conv_all, owner * cs, cs, 1)
    vec_own = lax.dynamic_slice_in_dim(vec, owner * hs, hs, 1)

    return (
        block_out,
        hidden_grad,
        norm_gain_grad,
        w_in_grad,
        w_dt_grad,
        conv_own[:KERNEL],
        conv_own[KERNEL],
        vec_own[0],
        vec_own[1],
        vec_own[2],
        gate_gain_grad,
        w_out_grad,
    )


def solution(mesh):
    rows = P("head", "seq", None)
    return jax.shard_map(
        local,
        mesh=mesh,
        in_specs=(
            rows, P("head"), rows, P("head"), P("head", None), P("head", None), P(None, "head"),
            P("head"), P("head"), P("head"), P("head"), P("head"), P("head", None),
        ),
        out_specs=(
            rows, rows, P("head"), P("head", None), P("head", None), P(None, "head"),
            P("head"), P("head"), P("head"), P("head"), P("head"), P("head", None),
        ),
        check_vma=False,
    )
```

```python
import functools

import jax
import jax.numpy as jnp
from jax import lax
from jax.experimental import pallas as pl
from jax.experimental.pallas import tpu as pltpu
from jax.sharding import PartitionSpec as P

HEADS = 64
HEAD_DIM = 64
STATE = 128
KERNEL = 4
CHUNK = 256
DI = 4096
CHANNELS = 4352
PROJ = DI + CHANNELS
EPS = 1e-05
LANES = 128
EVERY = ("seq", "head")
F32 = jnp.float32
BF16 = jnp.bfloat16


def dot(a, b):
    return jnp.dot(a, b, preferred_element_type=F32)


def dot_t(a, b):
    return lax.dot_general(a, b, (((1,), (1,)), ((), ())), preferred_element_type=F32)


def t_dot(a, b):
    return lax.dot_general(a, b, (((0,), (0,)), ((), ())), preferred_element_type=F32)


def sigmoid(v):
    return 1.0 / (1.0 + jnp.exp(-v))


def remote(src, dst, send, recv, target):
    return pltpu.make_async_remote_copy(
        src_ref=src, dst_ref=dst, send_sem=send, recv_sem=recv, device_id=target, device_id_type=pl.DeviceIdType.MESH
    )


def greet(peers, extra=()):
    barrier = pltpu.get_barrier_semaphore()
    count = len(peers)

    def hello(peer):
        pl.semaphore_signal(barrier, inc=1, device_id=peer, device_id_type=pl.DeviceIdType.MESH)

    for peer in peers:
        hello(peer)
    for there, peer in extra:
        pl.when(there)(functools.partial(hello, peer))
        count = count + jnp.where(there, 1, 0)
    pl.semaphore_wait(barrier, count)


def gather_kernel(
    hid_ref, og_ref, w_ref, wo_in_ref, gain_ref, dtw_ref,
    hall_ref, ogall_ref, wt_ref, wo_ref, z_ref, u_ref, d_ref, d0_ref,
    hv, ov, wv, wov, stage, zv, uv, dv, d0v,
    h_send, h_recv, o_send, o_recv, z_up, z_dn, z_recv, s_send, s_recv,
    c_up, c_dn, c_recv, t_send, t_recv, local_sem, out_sem, *, ring, wide,
):
    s = lax.axis_index("seq")
    q = hid_ref.shape[0]
    half = q // 2
    x_peer = s + 1 - 2 * lax.rem(s, 2)
    y_peer = lax.rem(s + 2, 4)
    far = 3 - s
    to_x, to_y = {"seq": x_peer}, {"seq": y_peer}
    chans = uv.shape[1]
    n_main = stage.shape[1]
    n = stage.shape[0]
    peers = [to_x, to_y]
    extra = []

    def block(ref, at, start, size):
        return ref.at[pl.ds(pl.multiple_of(at * q + start, 16), size), :]

    if ring:
        h = lax.axis_index("head")
        core = lax.rem(h, 2)
        r = h // 2
        last = lax.axis_size("head") // 2 - 1
        to_sib, to_up, to_down = {"head": h + 1 - 2 * core}, {"head": lax.rem(h + 2, 2 * last + 2)}, {"head": lax.rem(h + 2 * last, 2 * last + 2)}
        above, below = r < last, r > 0
        peers.append(to_sib)
        extra = [(above, to_up), (below, to_down)]
        first = pl.multiple_of(s * wide, LANES)
        second = pl.multiple_of(DI + s * wide, LANES)
        loads = [
            pltpu.make_async_copy(w_ref.at[:, pl.ds(first, wide)], stage.at[:, :wide], local_sem.at[0]),
            pltpu.make_async_copy(w_ref.at[:, pl.ds(second, wide)], stage.at[:, wide : 2 * wide], local_sem.at[1]),
            pltpu.make_async_copy(w_ref.at[:, 2 * DI :], stage.at[:, 2 * wide :], local_sem.at[2]),
        ]
        is_root = r == s
        n_o = wov.shape[0] // 2
        load_o = pltpu.make_async_copy(
            wo_in_ref, wov.at[pl.ds(pl.multiple_of(core * n_o, 16), n_o), :], local_sem.at[5]
        )
        pl.when(is_root)(load_o.start)
    else:
        loads = [
            pltpu.make_async_copy(w_ref, wv, local_sem.at[0]),
            pltpu.make_async_copy(wo_in_ref, wov, local_sem.at[5]),
        ]
    for copy in loads:
        copy.start()
    own_h = pltpu.make_async_copy(hid_ref, block(hv, s, 0, q), local_sem.at[3])
    own_o = pltpu.make_async_copy(og_ref, block(ov, s, 0, q), local_sem.at[4])
    own_h.start()
    own_o.start()
    greet(peers, extra)

    sent = []

    def send(src, dst, sems, i, target):
        copy = remote(src, dst, sems[0].at[i], sems[1].at[i], target)
        copy.start()
        sent.append(copy)
        return copy

    def open_exchange(src, buf, sems):
        return (
            send(src, block(buf, s, 0, q), sems, 0, to_x),
            send(src, block(buf, s, 0, q), sems, 1, to_y),
        )

    def relay(buf, sems, heads_in):
        heads_in[0].wait_recv()
        a = block(buf, x_peer, 0, half)
        first = send(a, a, sems, 2, to_y)
        heads_in[1].wait_recv()
        b = block(buf, y_peer, half, half)
        return first, send(b, b, sems, 3, to_x)

    h_sems, o_sems = (h_send, h_recv), (o_send, o_recv)
    h_open = open_exchange(hid_ref, hv, h_sems)

    closing = []
    if ring:
        def w_block(at):
            return wv.at[pl.ds(pl.multiple_of((2 * at + core) * n, 16), n), :]

        def w_copy(at, sems, target):
            return remote(w_block(at), w_block(at), sems.at[at], z_recv.at[at], target)

        def w_swap(at):
            return remote(w_block(at), w_block(at), s_send.at[at], s_recv.at[at], to_sib)

        def launch(there, make):
            @pl.when(there)
            def _():
                make().start()

            def finish():
                @pl.when(there)
                def _():
                    make().wait_send()

            closing.append(finish)

        always = r >= 0

        def w_step(k):
            lower, upper = r - k, r + k
            has_lower, has_upper = lower >= 0, upper <= last

            @pl.when(has_lower)
            def _():
                w_copy(lower, z_up, to_up).wait_recv()

            launch(has_lower & above, lambda: w_copy(lower, z_up, to_up))
            launch(has_lower, lambda: w_swap(lower))

            @pl.when(has_upper)
            def _():
                w_copy(upper, z_dn, to_down).wait_recv()

            launch(has_upper & below, lambda: w_copy(upper, z_dn, to_down))
            launch(has_upper, lambda: w_swap(upper))

        chunks = c_recv.shape[0]
        n_c = n_o // chunks
        dist = jnp.where(r > s, r - s, s - r)

        def o_block(i):
            return wov.at[pl.ds(pl.multiple_of(core * n_o + i * n_c, 16), n_c), :]

        def o_copy(i, sems, target):
            return remote(o_block(i), o_block(i), sems.at[i], c_recv.at[i], target)

        def o_swap(i):
            return remote(o_block(i), o_block(i), t_send.at[i], t_recv.at[i], to_sib)

        def o_root():
            @pl.when(is_root)
            def _():
                load_o.wait()

            for i in range(chunks):
                launch(is_root & above, lambda i=i: o_copy(i, c_up, to_up))
                launch(is_root & below, lambda i=i: o_copy(i, c_dn, to_down))
                launch(is_root, lambda i=i: o_swap(i))

        def o_tick(t):
            i = t - dist
            live = (dist >= 1) & (i >= 0) & (i < chunks)

            @pl.when(live)
            def _():
                o_copy(i, c_up, to_up).wait_recv()

            pl.when(live & (r > s) & above)(lambda: o_copy(i, c_up, to_up).start())
            pl.when(live & (r < s) & below)(lambda: o_copy(i, c_dn, to_down).start())
            pl.when(live)(lambda: o_swap(i).start())

        def o_finish():
            for i in range(chunks):
                pl.when((r > s) & above)(lambda: o_copy(i, c_up, to_up).wait_send())
                pl.when((r < s) & below)(lambda: o_copy(i, c_dn, to_down).wait_send())
                pl.when(dist >= 1)(lambda: o_swap(i).wait_send())

        closing.append(o_finish)
        for copy in loads:
            copy.wait()
        own = pl.ds(pl.multiple_of(h * n, 16), n)
        wv[own, :n_main] = (stage[...].astype(F32) * gain_ref[...]).astype(BF16)
        wv[own, n_main:] = dtw_ref[...]
        launch(above, lambda: w_copy(r, z_up, to_up))
        launch(below, lambda: w_copy(r, z_dn, to_down))
        launch(always, lambda: w_swap(r))
        w_step(1)
    else:
        for copy in loads:
            copy.wait()

    h_far = relay(hv, h_sems, h_open)
    if ring:
        w_step(2)
        o_root()
    for copy in h_far:
        copy.wait_recv()
    o_open = open_exchange(og_ref, ov, o_sems)
    if ring:
        o_tick(1)
        w_step(3)
        for at in range(4):
            w_swap(at).wait_recv()
    own_h.wait()
    own_o.wait()

    rows = min(CHUNK, q)

    def cut(at_block):
        return pl.ds(pl.multiple_of(at_block * q, 16), q)

    def project_outs(at_block, i):
        at = cut(at_block)
        pairs = ((hv, hall_ref), (zv, z_ref), (uv, u_ref), (dv, d_ref))
        return [
            pltpu.make_async_copy(src.at[at, :], dst.at[at, :], out_sem.at[4 * i + k])
            for k, (src, dst) in enumerate(pairs)
        ]

    def pull_outs(at_block, i):
        at = cut(at_block)
        pairs = ((ov, ogall_ref), (d0v, d0_ref))
        return [
            pltpu.make_async_copy(src.at[at, :], dst.at[at, :], out_sem.at[16 + 2 * i + k])
            for k, (src, dst) in enumerate(pairs)
        ]

    def nth(i):
        return jnp.where(i == 0, s, jnp.where(i == 1, x_peer, jnp.where(i == 2, y_peer, far)))

    w_out = pltpu.make_async_copy(wv, wt_ref, out_sem.at[24])
    o_out = pltpu.make_async_copy(wov, wo_ref, out_sem.at[25])
    w_out.start()

    def project(at_block):
        @pl.loop(0, q // rows)
        def _(j):
            at = pl.ds(pl.multiple_of(at_block * q + j * rows, 16), rows)
            hb = hv[at, :]
            h32 = hb.astype(F32)
            r0 = lax.rsqrt(jnp.mean(h32 * h32, axis=1, keepdims=True) + EPS)
            zv[at, :] = (dot(hb, wv[:, :wide]) * r0).astype(BF16)
            uv[at, :] = (dot(hb, wv[:, wide : wide + chans]) * r0).astype(BF16)
            raw = dot(hb, wv[:, wide + chans :]) * r0
            lane = lax.broadcasted_iota(jnp.int32, raw.shape, 1)
            dv[at, :] = jnp.where(lane == LANES - 1, r0, raw)

    def pull(at_block):
        at = cut(at_block)

        @pl.loop(0, wide // 256)
        def _(j):
            to = pl.ds(pl.multiple_of(j * 256, 256), 256)
            d0v[at, to] = dot_t(ov[at, :], wov[to, :]).astype(BF16)

    @pl.loop(0, 4)
    def _(i):
        at_block = nth(i)
        project(at_block)
        for copy in project_outs(at_block, i):
            copy.start()
        if ring:
            o_tick(2 + i)

    o_far = relay(ov, o_sems, o_open)
    if ring:
        o_tick(6)
        for i in range(chunks):
            o_swap(i).wait_recv()
    o_out.start()

    @pl.loop(0, 4)
    def _(i):
        at_block = nth(i)

        @pl.when(i == 3)
        def _():
            for copy in o_far:
                copy.wait_recv()

        pull(at_block)
        for copy in pull_outs(at_block, i):
            copy.start()

    for i, at_block in enumerate((s, x_peer, y_peer, far)):
        for copy in project_outs(at_block, i) + pull_outs(at_block, i):
            copy.wait()
    w_out.wait()
    o_out.wait()
    for copy in sent:
        copy.wait_send()
    for finish in closing:
        finish()


def decays(aux, heads, expand, rate_e, rate_row, rate_col):
    rows = aux.shape[0]
    lane = lax.broadcasted_iota(jnp.int32, aux.shape, 1)
    dt = jnp.where(lane < heads, aux, 0.0).astype(BF16)
    r = lax.broadcasted_iota(jnp.int32, (rows, rows), 0)
    c = lax.broadcasted_iota(jnp.int32, (rows, rows), 1)
    causal = c <= r
    lower = jnp.where(causal, 1.0, 0.0).astype(BF16)
    dt_e = dot(dt, expand)
    cum_e = dot(lower, dt_e.astype(BF16)) * rate_e
    cum_c = dot(lower, dt) * rate_row
    cum_t = lax.dot_general(dt, lower, (((0,), (1,)), ((), ())), preferred_element_type=F32) * rate_col
    return causal, dt_e, cum_e, cum_c, cum_t


def scan_kernel(
    u_ref, d_ref, z_ref, d0_ref, cw_ref, cb_ref, dtb_ref, exp_ref, rowp_ref, colp_ref,
    act_ref, slope_ref, aux_ref, y_ref, gg_ref, st_ref, sum_ref, state, ext, *, heads, wide,
):
    step = pl.program_id(0)
    rows = u_ref.shape[0]
    chans = u_ref.shape[1]

    @pl.when(step == 0)
    def _():
        state[...] = jnp.zeros_like(state)
        ext[0:8, :] = jnp.zeros((8, chans), F32)

    @pl.when(step > 0)
    def _():
        ext[0:8, :] = ext[rows : rows + 8, :]

    ext[8 : rows + 8, :] = u_ref[...].astype(F32)
    pre = cb_ref[0:1, :]
    for k in range(KERNEL):
        pre = pre + cw_ref[k : k + 1, :] * ext[pl.ds(8 - (KERNEL - 1) + k, rows), :]
    sig = sigmoid(pre)
    act = (pre * sig).astype(BF16)
    act_ref[...] = act
    slope_ref[...] = (sig * (1.0 + pre * (1.0 - sig))).astype(BF16)
    raw = d_ref[...]
    v = raw + dtb_ref[0:1, :]
    soft = jnp.maximum(v, 0.0) + jnp.log1p(jnp.exp(-jnp.abs(v)))
    soft = soft.astype(BF16).astype(F32)
    lane = lax.broadcasted_iota(jnp.int32, v.shape, 1)
    aux = jnp.where(lane < heads, soft, 0.0)
    sig_v = pltpu.roll(sigmoid(v), heads, 1)
    aux = jnp.where((lane >= heads) & (lane < 2 * heads), sig_v, aux)
    aux = jnp.where(lane == LANES - 1, raw, aux)
    aux_ref[...] = aux

    x = act[:, :wide]
    x32 = x.astype(F32)
    b = act[:, wide : wide + STATE]
    c = act[:, wide + STATE :]
    causal, dt_e, cum_e, cum_c, cum_t = decays(
        aux, heads, exp_ref[...], rowp_ref[0:1, :], rowp_ref[3:4, :LANES], colp_ref[:, 0:1]
    )
    xdt = x32 * dt_e
    xdt16 = xdt.astype(BF16)
    scores = dot_t(c, b)
    st = state[...]
    st_ref[0] = st
    half = lax.broadcasted_iota(jnp.int32, (rows, LANES), 1) < HEAD_DIM
    parts = []
    for pair in range(heads // 2):
        x2 = xdt16[:, LANES * pair : LANES * (pair + 1)]
        got = []
        for h in (2 * pair, 2 * pair + 1):
            spread = cum_c[:, h : h + 1] - cum_t[h : h + 1, :]
            m = (scores * jnp.exp(jnp.where(causal, spread, -1e30))).astype(BF16)
            got.append(dot(m, x2))
        parts.append(jnp.where(half, got[0], got[1]))
    y = jnp.concatenate(parts, axis=1) + dot(c, st.astype(BF16)) * jnp.exp(cum_e)
    last = cum_e[rows - 1 : rows, :]
    tail = jnp.exp(last - cum_e)
    state[...] = jnp.exp(last) * st + t_dot(b, (xdt * tail).astype(BF16))
    y_ref[...] = y
    ssd = (y + rowp_ref[1:2, :] * x32).astype(BF16).astype(F32)
    z = z_ref[...].astype(F32)
    g = ssd * (z * sigmoid(z))
    gg = g * rowp_ref[2:3, :]
    gg_ref[...] = gg.astype(BF16)
    ones = jnp.ones((8, wide), BF16)
    ssq = dot_t(ones, (g * g).astype(BF16))
    cross = dot_t(ones, (gg * d0_ref[...].astype(F32)).astype(BF16))
    sub = lax.broadcasted_iota(jnp.int32, ssq.shape, 0)
    sum_ref[...] = jnp.where(sub == 0, ssq, cross)


def seg_dot(v, seg):
    hi = v.astype(BF16)
    rest = v - hi.astype(F32)
    mid = rest.astype(BF16)
    low = (rest - mid.astype(F32)).astype(BF16)
    return dot(hi, seg) + dot(mid, seg) + dot(low, seg)


def gate_kernel(x_ref, aux_ref, z_ref, d0_ref, y_ref, stat_ref, rowp_ref, dy_ref, dpg_ref):
    stat = stat_ref[...]
    r1m = stat[:, 0:1]
    coef = stat[:, 1:2]
    r0 = aux_ref[:, LANES - 1 : LANES]
    ssd = (y_ref[...] + rowp_ref[1:2, :] * x_ref[...].astype(F32)).astype(BF16).astype(F32)
    z = z_ref[...].astype(F32)
    sig = sigmoid(z)
    sz = z * sig
    d_gated = (r1m * rowp_ref[2:3, :]) * d0_ref[...].astype(F32) - (ssd * sz) * coef
    dy_ref[...] = (d_gated * sz).astype(BF16)
    dpg_ref[...] = (r0 * (d_gated * ssd * (sig * (1.0 + z * (1.0 - sig))))).astype(BF16)


def back_kernel(
    act_ref, aux_ref, dy_ref, y_ref, st_ref, slope_ref, u_ref, part_ref,
    exp_ref, seg_ref, rowp_ref, colp_ref, cw_ref,
    dp_ref, sm_ref, br_ref, adj, ext, y_b, x_b, own_b, far_a, far_b, y_f, x_f, br_o,
    b_send, b_recv, b_load, *, heads, wide,
):
    step = pl.program_id(0)
    steps = pl.num_programs(0)
    rows = act_ref.shape[0]
    chans = u_ref.shape[1]

    s = lax.axis_index("seq")
    q = y_b.shape[0]
    half = q // 2
    x_peer = s + 1 - 2 * lax.rem(s, 2)
    y_peer = lax.rem(s + 2, 4)
    to_x, to_y = {"seq": x_peer}, {"seq": y_peer}

    def at_rows(block, start, size):
        return part_ref.at[pl.ds(pl.multiple_of(block * q + start, 16), size), :]

    def b_copy(src, dst, i, target):
        return remote(src, dst, b_send.at[i], b_recv.at[i], target)

    out_a = b_copy(at_rows(3 - s, 0, half), far_a, 0, to_x)
    out_b = b_copy(at_rows(3 - s, half, half), far_b, 1, to_y)
    out_y = b_copy(y_b, y_f, 2, to_y)
    out_x = b_copy(x_b, x_f, 3, to_x)
    b_loads = [
        pltpu.make_async_copy(at_rows(y_peer, 0, q), y_b, b_load.at[0]),
        pltpu.make_async_copy(at_rows(x_peer, 0, q), x_b, b_load.at[1]),
        pltpu.make_async_copy(at_rows(s, 0, q), own_b, b_load.at[2]),
    ]

    @pl.when(step == 0)
    def _():
        greet([to_x, to_y])
        out_a.start()
        out_b.start()
        for copy in b_loads:
            copy.start()

    @pl.when(step == 3)
    def _():
        for copy in b_loads:
            copy.wait()
        out_a.wait_recv()
        y_b[:half, :] = (y_b[:half, :].astype(F32) + far_a[...].astype(F32)).astype(BF16)
        out_y.start()
        out_b.wait_recv()
        x_b[half:, :] = (x_b[half:, :].astype(F32) + far_b[...].astype(F32)).astype(BF16)
        out_x.start()

    @pl.when(step == 0)
    def _():
        sm_ref[...] = jnp.zeros_like(sm_ref)
        adj[...] = jnp.zeros_like(adj)
        ext[rows : rows + 8, :] = jnp.zeros((8, chans), F32)

    @pl.when(step > 0)
    def _():
        ext[rows : rows + 8, :] = ext[0:8, :]

    x = act_ref[:, :wide]
    x32 = x.astype(F32)
    b = act_ref[:, wide : wide + STATE]
    c = act_ref[:, wide + STATE :]
    aux = aux_ref[...]
    r0 = aux[:, LANES - 1 : LANES]
    skip_e = rowp_ref[1:2, :]
    y = y_ref[...]
    dy16 = dy_ref[...]
    dy = dy16.astype(F32)

    causal, dt_e, cum_e, cum_c, cum_t = decays(
        aux, heads, exp_ref[...], rowp_ref[0:1, :], rowp_ref[3:4, :LANES], colp_ref[:, 0:1]
    )
    xdt = x32 * dt_e
    xdt16 = xdt.astype(BF16)
    scores = dot_t(c, b)
    st = st_ref[0]
    st16 = st.astype(BF16)
    q_in = adj[...]
    q16 = q_in.astype(BF16)
    last = cum_e[rows - 1 : rows, :]
    ecum = jnp.exp(cum_e)
    tail = jnp.exp(last - cum_e)
    half = lax.broadcasted_iota(jnp.int32, (rows, LANES), 1) < HEAD_DIM
    zero = jnp.zeros((rows, LANES), BF16)
    n_sum = None
    parts = []
    for pair in range(heads // 2):
        cut = slice(LANES * pair, LANES * (pair + 1))
        x2 = xdt16[:, cut]
        dy2 = dy16[:, cut]
        got = []
        for side in range(2):
            h = 2 * pair + side
            spread = cum_c[:, h : h + 1] - cum_t[h : h + 1, :]
            ell = jnp.exp(jnp.where(causal, spread, -1e30))
            m = (scores * ell).astype(BF16)
            got.append(t_dot(m, dy2))
            own = half if side == 0 else jnp.logical_not(half)
            n = dot_t(jnp.where(own, dy2, zero), x2) * ell
            n_sum = n if n_sum is None else n_sum + n
        parts.append(jnp.where(half, got[0], got[1]))
    out_part = dot(b, q16) * tail
    v = jnp.concatenate(parts, axis=1) + out_part
    n16 = n_sum.astype(BF16)
    dy_e = (dy * ecum).astype(BF16)
    x_tail = (xdt * tail).astype(BF16)
    d_b = t_dot(n16, c) + dot_t(x_tail, q16)
    d_c = dot(n16, b) + dot_t(dy_e, st16)
    elast = jnp.exp(last)
    adj[...] = elast * q_in + t_dot(c, dy_e)

    seg = seg_ref[...]
    flow = dy * y - xdt16.astype(F32) * v
    passed = jnp.sum(xdt16.astype(F32) * out_part, axis=0, keepdims=True)
    passed = passed + elast * jnp.sum(q_in * st, axis=0, keepdims=True)
    flow_h = seg_dot(flow, seg)
    passed_h = seg_dot(jnp.broadcast_to(passed, (8, wide)), seg)[0:1, :]
    upper = jnp.where(
        lax.broadcasted_iota(jnp.int32, (rows, rows), 1) >= lax.broadcasted_iota(jnp.int32, (rows, rows), 0), 1.0, 0.0
    ).astype(BF16)
    hi = flow_h.astype(BF16)
    rest = flow_h - hi.astype(F32)
    mid = rest.astype(BF16)
    low = (rest - mid.astype(F32)).astype(BF16)
    crossing = dot(upper, hi) + dot(upper, mid) + dot(upper, low) + passed_h
    rate_row = rowp_ref[3:4, :LANES]
    decay_grad = rate_row * crossing
    d_dt = seg_dot(x32 * v, seg) + decay_grad
    lane = lax.broadcasted_iota(jnp.int32, (rows, LANES), 1)
    sig_v = pltpu.roll(aux, LANES - heads, 1)
    d_pre = jnp.where(lane < heads, d_dt * sig_v, 0.0)
    dt = jnp.where(lane < heads, aux, 0.0)
    dp_ref[:, chans:] = (r0 * d_pre).astype(BF16)

    d_act = jnp.concatenate([skip_e * dy + dt_e * v, d_b, d_c], axis=1)
    d_conv = d_act * slope_ref[...].astype(F32)
    ext[0:rows, :] = d_conv
    u = u_ref[...].astype(F32)
    d_u = None
    for k in range(KERNEL):
        moved = ext[pl.ds(KERNEL - 1 - k, rows), :]
        term = cw_ref[k : k + 1, :] * moved
        d_u = term if d_u is None else d_u + term
        sm_ref[k : k + 1, :] += jnp.sum(u * moved, axis=0, keepdims=True)
    dp_ref[:, :chans] = (r0 * d_u).astype(BF16)
    sm_ref[4:5, :] += jnp.sum(d_conv, axis=0, keepdims=True)
    sm_ref[5:6, :wide] += jnp.sum(x32 * dy, axis=0, keepdims=True)
    sm_ref[6:7, :LANES] += jnp.sum(d_pre, axis=0, keepdims=True)
    sm_ref[7:8, :LANES] += jnp.sum(dt * decay_grad, axis=0, keepdims=True)

    @pl.when(step == steps - 1)
    def _():
        out_y.wait_recv()
        out_x.wait_recv()
        br_o[...] = own_b[...].astype(F32) + y_f[...].astype(F32) + x_f[...].astype(F32)
        last_copy = pltpu.make_async_copy(br_o, br_ref, b_load.at[3])
        last_copy.start()
        for copy in (out_a, out_b, out_y, out_x):
            copy.wait_send()
        last_copy.wait()


def grads_kernel(
    dpg_ref, dp_ref, w_ref, h_ref, gate_ref, piece_ref, tiny_ref,
    dn_ref, wing_ref, win_ref, wout_ref,
    dpv, wv, hb, far_p, y_p, x_p, far_a, far_b, y_f, x_f, dn_o, sib_s, mine_s, own_s, z_u, z_d, pv,
    load_sem, hb_sem, d_send, d_recv, s_send, s_recv, zu_send, zu_recv, zd_send, zd_recv,
    g_send, g_recv, k_send, k_recv, p_send, p_recv, w_send, w_recv, out_sem,
):
    s = lax.axis_index("seq")
    h = lax.axis_index("head")
    owners = lax.axis_size("head")
    last = owners // 2 - 1
    core = lax.rem(h, 2)
    r = h // 2
    x_peer = s + 1 - 2 * lax.rem(s, 2)
    y_peer = lax.rem(s + 2, 4)
    far = 3 - s
    to_x, to_y = {"seq": x_peer}, {"seq": y_peer}
    to_sib = {"head": h + 1 - 2 * core}
    to_up, to_down = {"head": lax.rem(h + 2, owners)}, {"head": lax.rem(h + owners - 2, owners)}
    above, below = r < last, r > 0
    q = far_p.shape[0]
    half = q // 2
    n, cols = own_s.shape[1], own_s.shape[2]
    spare = LANES // 2
    tiles = cols // LANES
    edges = [LANES * (tiles * k // 4) for k in range(5)]
    spans = list(zip(edges[:-1], edges[1:]))
    sent = []
    closing = []

    def push(src, dst, sems, i, target):
        copy = remote(src, dst, sems[0].at[i], sems[1].at[i], target)
        copy.start()
        sent.append(copy)
        return copy

    def launch(there, make):
        @pl.when(there)
        def _():
            make().start()

        def finish():
            @pl.when(there)
            def _():
                make().wait_send()

        closing.append(finish)

    skip = dpv.shape[1] - cols
    load_dp = pltpu.make_async_copy(dp_ref, dpv.at[:, skip:], load_sem.at[0])
    load_w = pltpu.make_async_copy(w_ref, wv, load_sem.at[1])
    load_g = pltpu.make_async_copy(dpg_ref, dpv.at[:, :skip], load_sem.at[4])
    own_gate = pltpu.make_async_copy(gate_ref, wing_ref.at[s], load_sem.at[5])
    load_dp.start()
    load_g.start()
    load_w.start()
    own_gate.start()

    def chip(i):
        return jnp.where(lax.rem(i, 2) == 0, last - i // 2, i // 2)

    def load_h(i, other):
        at = 2 * chip(i) + (1 - core if other else core)
        slot = 0 if other else 1
        return pltpu.make_async_copy(
            h_ref.at[:, pl.ds(pl.multiple_of(at * n, LANES), n)], hb.at[slot], hb_sem.at[slot]
        )

    load_h(0, True).start()
    load_h(0, False).start()
    to_heads = [{"head": lax.rem(h + k, owners)} for k in range(1, owners)]
    greet([to_x, to_y] + to_heads)

    d_sems = (d_send, d_recv)
    g_sems = (g_send, g_recv)

    k_sems = (k_send, k_recv)
    k0 = push(gate_ref, wing_ref.at[s], k_sems, 0, to_x)
    k1 = push(gate_ref, wing_ref.at[s], k_sems, 1, to_y)
    w_sems = (w_send, w_recv)
    own_piece = pltpu.make_async_copy(piece_ref, pv.at[s], load_sem.at[2])
    own_piece.start()
    w0 = push(piece_ref, pv.at[s], w_sems, 0, to_x)
    w1 = push(piece_ref, pv.at[s], w_sems, 1, to_y)
    tile = 256

    def part(block, out):
        at = pl.ds(pl.multiple_of(block * q, 16), q)

        @pl.loop(0, wv.shape[0] // tile)
        def _(j):
            to = pl.ds(pl.multiple_of(j * tile, tile), tile)
            out[:, to] = dot_t(dpv[at, :], wv[to, :]).astype(BF16)

    def add_to(out, at, extra):
        out[at, :] = (out[at, :].astype(F32) + extra.astype(F32)).astype(BF16)

    def swap(i):
        t = chip(i)
        return remote(sib_s.at[lax.rem(i, 2)], own_s.at[t], s_send.at[t], s_recv.at[t], to_sib)

    def rows_of(i):
        t = chip(i)
        slot = lax.rem(i, 2)

        @pl.when(i >= 2)
        def _():
            swap(i - 2).wait_send()

        load_h(i, True).wait()
        for lo, hi in spans:
            sib_s[slot, :, lo:hi] = t_dot(hb[0], dpv[:, skip + lo : skip + hi]).astype(BF16)
        sib_s[slot, :, cols - spare :] = tiny_ref[...]
        swap(i).start()

        @pl.when(i < 3)
        def _():
            load_h(i + 1, True).start()

        load_h(i, False).wait()
        for lo, hi in spans:
            mine_s[:, lo:hi] = t_dot(hb[1], dpv[:, skip + lo : skip + hi]).astype(BF16)
        mine_s[:, cols - spare :] = tiny_ref[...]

        @pl.when(i < 3)
        def _():
            load_h(i + 1, False).start()

        swap(i).wait_recv()
        join(t, mine_s)

    def join(t, extra):
        for lo, hi in spans:
            own_s[t, :, lo:hi] = (own_s[t, :, lo:hi].astype(F32) + extra[:, lo:hi].astype(F32)).astype(BF16)

    def up_copy(t):
        return remote(own_s.at[t], z_u.at[t - 1], zu_send.at[t], zu_recv.at[t], to_up)

    def down_copy(t):
        return remote(own_s.at[t], z_d.at[t], zd_send.at[t], zd_recv.at[t], to_down)

    def up_add(t):
        up_copy(t).wait_recv()
        join(t, z_u.at[t - 1])

    def down_add(t):
        down_copy(t).wait_recv()
        join(t, z_d.at[t])

    def pass_on(t, there, add, make):
        pl.when(there)(functools.partial(add, t))
        launch(there, lambda: make(t))

    def follow(t, there, make, before):
        @pl.when(there)
        def _():
            make(before).wait_send()
            make(t).start()

    def finish_later(t, there, make):
        def finish():
            @pl.when(there)
            def _():
                make(t).wait_send()

        closing.append(finish)

    load_dp.wait()
    pl.loop(0, 2)(rows_of)

    @pl.when(r == 0)
    def _():
        up_copy(last).start()

    @pl.when(r == last)
    def _():
        down_copy(0).start()

    load_g.wait()
    load_w.wait()
    part(far, far_p)
    d0 = push(far_p.at[:half], far_a, d_sems, 0, to_x)
    d1 = push(far_p.at[half:], far_b, d_sems, 1, to_y)
    k0.wait_recv()
    gate_a = wing_ref.at[x_peer, : n // 2]
    k2 = push(gate_a, gate_a, k_sems, 2, to_y)
    k1.wait_recv()
    gate_b = wing_ref.at[y_peer, n // 2 :]
    k3 = push(gate_b, gate_b, k_sems, 3, to_x)
    own_piece.wait()
    w0.wait_recv()
    piece_a = pv.at[x_peer, 0]
    w2 = push(piece_a, piece_a, w_sems, 2, to_y)
    w1.wait_recv()
    piece_b = pv.at[y_peer, 1]
    w3 = push(piece_b, piece_b, w_sems, 3, to_x)
    pl.loop(2, 4)(rows_of)

    follow(2, r == 0, up_copy, last)
    follow(1, r == last, down_copy, 0)
    pass_on(last, (r > 0) & above, up_add, up_copy)
    pass_on(0, (r < last) & below, down_add, down_copy)
    part(y_peer, y_p)
    part(x_peer, x_p)
    follow(1, r == 0, up_copy, 2)
    follow(2, r == last, down_copy, 1)
    pass_on(2, r == 1, up_add, up_copy)
    pass_on(1, r == 2, down_add, down_copy)
    finish_later(1, r == 0, up_copy)
    finish_later(2, r == last, down_copy)
    d0.wait_recv()
    add_to(y_p, slice(0, half), far_a[...])
    d2 = push(y_p, y_f, d_sems, 2, to_y)
    d1.wait_recv()
    add_to(x_p, slice(half, q), far_b[...])
    d3 = push(x_p, x_f, d_sems, 3, to_x)
    pl.when(r > 0)(lambda: up_add(r))
    pl.when(r < last)(lambda: down_add(r))

    red = own_s.at[r]
    g0 = push(red, win_ref.at[s], g_sems, 0, to_x)
    g1 = push(red, win_ref.at[s], g_sems, 1, to_y)
    own_win = pltpu.make_async_copy(red, win_ref.at[s], load_sem.at[3])
    own_win.start()
    w2.wait_recv()
    w3.wait_recv()
    per = owners // 4

    def piece_of(head):
        return pv.at[head // per, lax.rem(head, per)]

    pieces = []
    for k, peer in enumerate(to_heads):
        pieces.append(push(piece_of(peer["head"]), wout_ref.at[h], (p_send, p_recv), k, peer))
    own_piece = pltpu.make_async_copy(piece_of(h), wout_ref.at[h], load_sem.at[2])
    own_piece.start()

    g0.wait_recv()
    part_a = win_ref.at[x_peer, : n // 2]
    g2 = push(part_a, part_a, g_sems, 2, to_y)
    g1.wait_recv()
    part_b = win_ref.at[y_peer, n // 2 :]
    g3 = push(part_b, part_b, g_sems, 3, to_x)

    d2.wait_recv()
    d3.wait_recv()

    def dn_out(j):
        to = pl.ds(pl.multiple_of(j * tile, tile), tile)
        return pltpu.make_async_copy(dn_o.at[lax.rem(j, 2)], dn_ref.at[:, to], out_sem.at[lax.rem(j, 2)])

    own_at = pl.ds(pl.multiple_of(s * q, 16), q)
    tiles_n = wv.shape[0] // tile

    @pl.loop(0, tiles_n)
    def _(j):
        to = pl.ds(pl.multiple_of(j * tile, tile), tile)
        got = dot_t(dpv[own_at, :], wv[to, :])

        @pl.when(j > 1)
        def _():
            dn_out(j - 2).wait()

        dn_o[lax.rem(j, 2)] = got + y_f[:, to].astype(F32) + x_f[:, to].astype(F32)
        dn_out(j).start()

    dn_out(tiles_n - 2).wait()
    dn_out(tiles_n - 1).wait()
    own_win.wait()
    own_gate.wait()
    own_piece.wait()
    k2.wait_recv()
    k3.wait_recv()
    for copy in pieces:
        copy.wait_recv()
    g2.wait_recv()
    g3.wait_recv()
    for i in (2, 3):
        swap(i).wait_send()
    for copy in sent:
        copy.wait_send()
    for finish in closing:
        finish()


def finish_kernel(gate_ref, rest_ref, w_ref, dtw_ref, gain_ref, win_ref, wdt_ref, norm_ref, *, heads, wide):
    ranks = gate_ref.shape[0]
    gain = gain_ref[...]
    norm = None

    def piece(at, raw):
        to = slice(at, at + raw.shape[1])
        win_ref[:, to] = raw * gain
        return jnp.sum(raw * w_ref[:, to].astype(F32), axis=1, keepdims=True)

    shared = None
    dt_parts = []
    for k in range(ranks):
        here = piece(k * wide, gate_ref[k].astype(F32)) + piece(DI + k * wide, rest_ref[k, :, :wide].astype(F32))
        norm = here if norm is None else norm + here
        bc = rest_ref[k, :, wide : wide + 2 * STATE].astype(F32)
        shared = bc if shared is None else shared + bc
        dt_parts.append(rest_ref[k, :, wide + 2 * STATE : wide + 2 * STATE + heads].astype(F32))
    norm = norm + piece(2 * DI, shared)
    raw = jnp.concatenate(dt_parts, axis=1)
    wdt_ref[...] = raw * gain
    norm_ref[...] = norm + jnp.sum(raw * dtw_ref[...].astype(F32), axis=1, keepdims=True)


def local(hidden, lengths, out_grad, norm_gain, w_in, w_dt, conv_weight, conv_bias, dt_bias, a_log, skip_gain, gate_gain, w_out):
    ranks = lax.axis_size("seq")
    rank = lax.axis_index("seq")
    owners = lax.axis_size("head")
    owner = lax.axis_index("head")
    local_len, width = hidden.shape[1], hidden.shape[2]
    heads = HEADS // ranks
    wide = heads * HEAD_DIM
    chans = wide + 2 * STATE
    cols = wide + chans + LANES
    tokens = ranks * local_len
    chunk = min(CHUNK, local_len)
    steps = tokens // chunk
    shard = w_in.shape[0]

    gain_rows = norm_gain.astype(F32)[:, None]

    def scaled(v):
        return (v.astype(F32) * gain_rows).astype(BF16)

    spare = LANES // 2
    small = jnp.concatenate([conv_weight.reshape(-1), conv_bias, dt_bias, a_log, skip_gain, gate_gain])
    n_small = small.shape[0]
    small = jnp.pad(small, (0, shard * spare - n_small)).reshape(shard, spare)
    last_block = jnp.concatenate(
        [
            scaled(lax.dynamic_slice_in_dim(w_dt, rank * heads, heads, 1)),
            jnp.zeros((shard, LANES - spare - heads), BF16),
            small,
        ],
        axis=1,
    )
    ring = owners == 2 * ranks
    if ring:
        w_given, o_given = w_in, w_out
    else:
        w_given = lax.all_gather(
            jnp.concatenate(
                [
                    scaled(lax.dynamic_slice_in_dim(w_in, rank * wide, wide, 1)),
                    scaled(lax.dynamic_slice_in_dim(w_in, DI + rank * wide, wide, 1)),
                    scaled(w_in[:, 2 * DI :]),
                    last_block,
                ],
                axis=1,
            ),
            "head", axis=0, tiled=True,
        )
        o_given = lax.dynamic_slice_in_dim(lax.all_gather(w_out, "head", axis=0, tiled=True), rank * wide, wide, 0)

    def sds(shape, kind):
        return jax.ShapeDtypeStruct(shape, kind)

    hbm = pl.BlockSpec(memory_space=pl.ANY)
    vmem = pl.BlockSpec(memory_space=pltpu.VMEM)

    def dma(count):
        return pltpu.SemaphoreType.DMA((count,))

    h_all, og_all, w_t, w_o, z, u, d_raw, d0 = pl.pallas_call(
        functools.partial(gather_kernel, ring=ring, wide=wide),
        in_specs=[hbm, hbm, hbm, hbm, vmem, vmem],
        out_specs=[hbm] * 8,
        out_shape=[
            sds((tokens, width), BF16),
            sds((tokens, width), BF16),
            sds((width, cols), BF16),
            sds((wide, width), BF16),
            sds((tokens, wide), BF16),
            sds((tokens, chans), BF16),
            sds((tokens, LANES), F32),
            sds((tokens, wide), BF16),
        ],
        scratch_shapes=[
            pltpu.VMEM((tokens, width), BF16),
            pltpu.VMEM((tokens, width), BF16),
            pltpu.VMEM((width, cols), BF16),
            pltpu.VMEM((wide, width), BF16),
            pltpu.VMEM((shard, cols - LANES), BF16),
            pltpu.VMEM((tokens, wide), BF16),
            pltpu.VMEM((tokens, chans), BF16),
            pltpu.VMEM((tokens, LANES), F32),
            pltpu.VMEM((tokens, wide), BF16),
        ]
        + [dma(4)] * 14
        + [dma(6), dma(26)],
        compiler_params=pltpu.CompilerParams(
            collective_id=0, has_side_effects=True, vmem_limit_bytes=56 * 1024 * 1024
        ),
        cost_estimate=pl.CostEstimate(
            flops=2 * tokens * width * (cols + wide), bytes_accessed=4 * tokens * (width + cols), transcendentals=0
        ),
        name="gather_project",
    )(hidden[0], out_grad[0], w_given, o_given, gain_rows, last_block)

    small = w_t.reshape(owners, shard, cols)[:, :, cols - spare :].reshape(owners, shard * spare)
    cs = CHANNELS // owners
    hs = HEADS // owners
    gs = DI // owners
    conv_w = small[:, : KERNEL * cs].reshape(owners, KERNEL, cs).swapaxes(0, 1).reshape(KERNEL, CHANNELS)
    at = KERNEL * cs
    conv_b = small[:, at : at + cs].reshape(CHANNELS)
    at += cs
    dt_b = small[:, at : at + hs].reshape(HEADS)
    at += hs
    a_all = small[:, at : at + hs].reshape(HEADS)
    at += hs
    skip_all = small[:, at : at + hs].reshape(HEADS)
    at += hs
    gain_all = small[:, at : at + gs].reshape(DI)

    def mine(v, size):
        return lax.dynamic_slice_in_dim(v, rank * size, size, v.ndim - 1)

    cw = jnp.concatenate([mine(conv_w[:, :DI], wide), conv_w[:, DI:]], axis=1).astype(F32)
    cb = jnp.concatenate([mine(conv_b[:DI], wide), conv_b[DI:]])[None].astype(F32)
    cw = jnp.concatenate([cw, jnp.zeros((8 - KERNEL, chans), F32)], axis=0)
    cb = jnp.broadcast_to(cb, (8, chans))
    dtb = jnp.broadcast_to(jnp.pad(mine(dt_b, heads).astype(F32), (0, LANES - heads))[None], (8, LANES))
    rate = -jnp.exp(mine(a_all, heads).astype(F32))
    rowp = jnp.stack(
        [
            jnp.repeat(rate, HEAD_DIM),
            jnp.repeat(mine(skip_all, heads).astype(F32), HEAD_DIM),
            mine(gain_all, wide).astype(F32),
            jnp.pad(rate, (0, wide - heads)),
        ]
        + [jnp.zeros((wide,), F32)] * 4
    )
    colp = jnp.broadcast_to(jnp.pad(rate, (0, LANES - heads))[:, None], (LANES, LANES))
    head_of = jnp.arange(wide, dtype=jnp.int32) // HEAD_DIM
    expand = (jnp.arange(LANES, dtype=jnp.int32)[:, None] == head_of[None]).astype(BF16)
    seg = expand.T

    def forth(size):
        return pl.BlockSpec((chunk, size), lambda j: (j, 0))

    def back(size):
        return pl.BlockSpec((chunk, size), lambda j: (steps - 1 - j, 0))

    def whole(a):
        return pl.BlockSpec(a.shape, lambda j: (0,) * a.ndim, pipeline_mode=pl.Buffered(1))

    params = pltpu.CompilerParams(
        dimension_semantics=("arbitrary",), vmem_limit_bytes=56 * 1024 * 1024
    )
    grid = (steps,)

    act, slope, aux, y, gg, states, sums = pl.pallas_call(
        functools.partial(scan_kernel, heads=heads, wide=wide),
        grid=grid,
        in_specs=[
            forth(chans), forth(LANES), forth(wide), forth(wide),
            whole(cw), whole(cb), whole(dtb), whole(expand), whole(rowp), whole(colp),
        ],
        out_specs=[
            forth(chans), forth(chans), forth(LANES), forth(wide), forth(wide),
            pl.BlockSpec((1, STATE, wide), lambda j: (j, 0, 0)),
            pl.BlockSpec((8, chunk), lambda j: (0, j)),
        ],
        out_shape=[
            sds((tokens, chans), BF16),
            sds((tokens, chans), BF16),
            sds((tokens, LANES), F32),
            sds((tokens, wide), F32),
            sds((tokens, wide), BF16),
            sds((steps, STATE, wide), F32),
            sds((8, tokens), F32),
        ],
        scratch_shapes=[pltpu.VMEM((STATE, wide), F32), pltpu.VMEM((chunk + 8, chans), F32)],
        compiler_params=params,
        cost_estimate=pl.CostEstimate(
            flops=2 * tokens * wide * 12 * chunk, bytes_accessed=tokens * wide * 16, transcendentals=tokens * chunk * heads
        ),
        name="scan",
    )(u, d_raw, z, d0, cw, cb, dtb, expand, rowp, colp)

    sums = lax.psum(sums[:2].reshape(2, tokens // LANES, LANES), "seq").reshape(2, tokens)
    mask = (jnp.arange(tokens, dtype=jnp.int32) < lengths[0]).astype(F32)
    r1 = lax.rsqrt(sums[0] / DI + EPS)
    r1m = r1 * mask
    coef = r1m * r1 * r1 * sums[1] / DI
    lane = jnp.arange(LANES, dtype=jnp.int32)[None]
    stat2 = jnp.where(lane == 0, r1m[:, None], jnp.where(lane == 1, coef[:, None], 0.0))

    partial = dot(gg, w_o).astype(BF16)
    dy, dpg = pl.pallas_call(
        gate_kernel,
        grid=grid,
        in_specs=[forth(wide), forth(LANES), forth(wide), forth(wide), forth(wide), forth(LANES), whole(rowp)],
        out_specs=[forth(wide), forth(wide)],
        out_shape=[sds((tokens, wide), BF16), sds((tokens, wide), BF16)],
        compiler_params=params,
        cost_estimate=pl.CostEstimate(
            flops=20 * tokens * wide, bytes_accessed=tokens * wide * 14, transcendentals=tokens * wide
        ),
        name="gate_back",
    )(act, aux, z, d0, y, stat2, rowp)

    og_scaled = (og_all.astype(F32) * r1m[:, None]).astype(BF16)
    wog = t_dot(gg, og_scaled).astype(BF16)
    wig_gate = t_dot(h_all, dpg).astype(BF16)
    dy, wog, wig_gate, partial = lax.optimization_barrier((dy, wog, wig_gate, partial))
    own_gate = lax.psum_scatter(wig_gate, "head", scatter_dimension=0, tiled=True)

    rest = chans + LANES
    dp, sm, branch = pl.pallas_call(
        functools.partial(back_kernel, heads=heads, wide=wide),
        grid=grid,
        in_specs=[
            back(chans), back(LANES), back(wide), back(wide),
            pl.BlockSpec((1, STATE, wide), lambda j: (steps - 1 - j, 0, 0)),
            back(chans), back(chans), hbm,
            whole(expand), whole(seg), whole(rowp), whole(colp), whole(cw),
        ],
        out_specs=[back(rest), pl.BlockSpec((8, chans), lambda j: (0, 0)), hbm],
        out_shape=[sds((tokens, rest), BF16), sds((8, chans), F32), sds((local_len, width), F32)],
        scratch_shapes=[pltpu.VMEM((STATE, wide), F32), pltpu.VMEM((chunk + 8, chans), F32)]
        + [pltpu.VMEM((local_len, width), BF16)] * 3
        + [pltpu.VMEM((local_len // 2, width), BF16)] * 2
        + [pltpu.VMEM((local_len, width), BF16)] * 2
        + [pltpu.VMEM((local_len, width), F32)]
        + [dma(4)] * 3,
        compiler_params=pltpu.CompilerParams(
            dimension_semantics=("arbitrary",), collective_id=2, has_side_effects=True,
            vmem_limit_bytes=56 * 1024 * 1024,
        ),
        cost_estimate=pl.CostEstimate(
            flops=2 * tokens * wide * 12 * chunk, bytes_accessed=tokens * wide * 24, transcendentals=tokens * chunk * heads
        ),
        name="scan_back",
    )(act, aux, dy, y, states, slope, u, partial, expand, seg, rowp, colp, cw)

    skip_h = jnp.sum(sm[5, :wide].reshape(heads, HEAD_DIM), axis=1)
    tiny = jnp.concatenate([sm[:5].reshape(-1), sm[6, :heads], sm[7, :heads], skip_h])
    n_own = DI // owners
    if ring:
        piece = n_own // owners
        pieces = wog.reshape(owners // ranks, owners, piece, width).swapaxes(0, 1)
        pieces = lax.psum_scatter(pieces, "head", scatter_dimension=0, tiled=False)
        laid = jnp.pad(tiny, (0, shard * spare - tiny.shape[0])).reshape(shard, spare).astype(BF16)
        dn, gate_rows, rest_rows, w_out_grad = pl.pallas_call(
            grads_kernel,
            in_specs=[hbm] * 6 + [vmem],
            out_specs=[hbm] * 4,
            out_shape=[
                sds((local_len, width), F32),
                sds((ranks, shard, wide), BF16),
                sds((ranks, shard, rest), BF16),
                sds((owners, piece, width), BF16),
            ],
            scratch_shapes=[
                pltpu.VMEM((tokens, cols), BF16),
                pltpu.VMEM((width, cols), BF16),
                pltpu.VMEM((2, tokens, shard), BF16),
            ]
            + [pltpu.VMEM((local_len, width), BF16)] * 3
            + [pltpu.VMEM((local_len // 2, width), BF16)] * 2
            + [pltpu.VMEM((local_len, width), BF16)] * 2
            + [
                pltpu.VMEM((2, local_len, 256), F32),
                pltpu.VMEM((2, shard, rest), BF16),
                pltpu.VMEM((shard, rest), BF16),
                pltpu.VMEM((4, shard, rest), BF16),
                pltpu.VMEM((3, shard, rest), BF16),
                pltpu.VMEM((3, shard, rest), BF16),
                pltpu.VMEM((ranks, owners // ranks, piece, width), BF16),
            ]
            + [dma(6), dma(2)]
            + [dma(4)] * 12
            + [dma(owners)] * 2
            + [dma(4)] * 2
            + [dma(2)],
            compiler_params=pltpu.CompilerParams(
                collective_id=1, has_side_effects=True, vmem_limit_bytes=56 * 1024 * 1024
            ),
            cost_estimate=pl.CostEstimate(
                flops=4 * tokens * width * cols, bytes_accessed=8 * tokens * cols, transcendentals=0
            ),
            name="weight_grads",
        )(dpg, dp, w_t, h_all, own_gate, pieces, laid)
        w_out_grad = w_out_grad.reshape(n_own, width).astype(F32)
        tiny_all = rest_rows[:, :, rest - spare :].reshape(ranks, shard * spare)[:, : tiny.shape[0]].astype(F32)
    else:
        full = lax.all_gather(lax.psum(wog, "head"), "seq", axis=0, tiled=True)
        w_out_grad = lax.dynamic_slice_in_dim(full, owner * n_own, n_own, 0).astype(F32)
        wig = t_dot(h_all, dp).astype(BF16)
        dn = (dot_t(dp, w_t[:, wide:]) + dot_t(dpg, w_t[:, :wide])).astype(BF16)
        dn = lax.psum_scatter(dn, "seq", scatter_dimension=0, tiled=True).astype(F32)
        gate_rows = lax.all_gather(own_gate, "seq")
        rest_rows = lax.all_gather(lax.psum_scatter(wig, "head", scatter_dimension=0, tiled=True), "seq")
        tiny_all = lax.all_gather(lax.psum(tiny, "head"), "seq")
    gate_gain_grad = jnp.sum(w_out.astype(F32) * w_out_grad, axis=1) / gate_gain.astype(F32)

    strip = min(32, shard)

    def rows_spec(size):
        return pl.BlockSpec((strip, size), lambda j: (j, 0))

    def ranks_spec(size):
        return pl.BlockSpec((ranks, strip, size), lambda j: (0, j, 0))

    w_in_grad, w_dt_grad, norm_gain_grad = pl.pallas_call(
        functools.partial(finish_kernel, heads=heads, wide=wide),
        grid=(shard // strip,),
        in_specs=[ranks_spec(wide), ranks_spec(rest), rows_spec(PROJ), rows_spec(HEADS), rows_spec(1)],
        out_specs=[rows_spec(PROJ), rows_spec(HEADS), rows_spec(1)],
        out_shape=[sds((shard, PROJ), F32), sds((shard, HEADS), F32), sds((shard, 1), F32)],
        compiler_params=params,
        cost_estimate=pl.CostEstimate(flops=6 * shard * PROJ, bytes_accessed=8 * shard * PROJ, transcendentals=0),
        name="w_in_finish",
    )(gate_rows, rest_rows, w_in, w_dt, gain_rows)
    norm_gain_grad = norm_gain_grad.reshape(shard)

    h32 = hidden[0].astype(F32)
    own_r1m = lax.dynamic_slice_in_dim(r1m, rank * local_len, local_len, 0)[:, None]
    block_out = (h32 + own_r1m * branch).astype(BF16)[None]
    r0 = lax.rsqrt(jnp.mean(h32 * h32, axis=1, keepdims=True) + EPS)
    mixed = jnp.sum(dn * h32, axis=1, keepdims=True) / width
    hidden_grad = (out_grad[0].astype(F32) + dn - h32 * (r0 * r0 * mixed))[None]

    n_conv = 5 * chans
    conv_all = tiny_all[:, :n_conv].reshape(ranks, 5, chans)
    conv_all = jnp.concatenate(
        [conv_all[:, :, :wide].swapaxes(0, 1).reshape(5, DI), jnp.sum(conv_all[:, :, wide:], axis=0)], axis=1
    )
    vec = tiny_all[:, n_conv:].reshape(ranks, 3, heads).swapaxes(0, 1).reshape(3, HEADS)
    conv_own = lax.dynamic_slice_in_dim(conv_all, owner * cs, cs, 1)
    vec_own = lax.dynamic_slice_in_dim(vec, owner * hs, hs, 1)

    return (
        block_out,
        hidden_grad,
        norm_gain_grad,
        w_in_grad,
        w_dt_grad,
        conv_own[:KERNEL],
        conv_own[KERNEL],
        vec_own[0],
        vec_own[1],
        vec_own[2],
        gate_gain_grad,
        w_out_grad,
    )


def solution(mesh):
    rows = P("head", "seq", None)
    return jax.shard_map(
        local,
        mesh=mesh,
        in_specs=(
            rows, P("head"), rows, P("head"), P("head", None), P("head", None), P(None, "head"),
            P("head"), P("head"), P("head"), P("head"), P("head"), P("head", None),
        ),
        out_specs=(
            rows, rows, P("head"), P("head", None), P("head", None), P(None, "head"),
            P("head"), P("head"), P("head"), P("head"), P("head"), P("head", None),
        ),
        check_vma=False,
    )
```

```python
import functools

import jax
import jax.numpy as jnp
from jax import lax
from jax.experimental import pallas as pl
from jax.experimental.pallas import tpu as pltpu
from jax.sharding import PartitionSpec as P

HEADS = 64
HEAD_DIM = 64
STATE = 128
KERNEL = 4
CHUNK = 256
DI = 4096
CHANNELS = 4352
PROJ = DI + CHANNELS
EPS = 1e-05
LANES = 128
EVERY = ("seq", "head")
F32 = jnp.float32
BF16 = jnp.bfloat16


def dot(a, b):
    return jnp.dot(a, b, preferred_element_type=F32)


def dot_t(a, b):
    return lax.dot_general(a, b, (((1,), (1,)), ((), ())), preferred_element_type=F32)


def t_dot(a, b):
    return lax.dot_general(a, b, (((0,), (0,)), ((), ())), preferred_element_type=F32)


def sigmoid(v):
    return 0.5 * jnp.tanh(0.5 * v) + 0.5


def remote(src, dst, send, recv, target):
    return pltpu.make_async_remote_copy(
        src_ref=src, dst_ref=dst, send_sem=send, recv_sem=recv, device_id=target, device_id_type=pl.DeviceIdType.MESH
    )


def greet(peers, extra=()):
    barrier = pltpu.get_barrier_semaphore()
    count = len(peers)

    def hello(peer):
        pl.semaphore_signal(barrier, inc=1, device_id=peer, device_id_type=pl.DeviceIdType.MESH)

    for peer in peers:
        hello(peer)
    for there, peer in extra:
        pl.when(there)(functools.partial(hello, peer))
        count = count + jnp.where(there, 1, 0)
    pl.semaphore_wait(barrier, count)


def gather_kernel(
    hid_ref, og_ref, w_ref, wo_in_ref, gain_ref, dtw_ref,
    hall_ref, ogall_ref, wt_ref, wo_ref, z_ref, u_ref, d_ref, d0_ref,
    hv, ov, wv, wov, stage, zv, uv, dv, d0v,
    h_send, h_recv, o_send, o_recv, z_up, z_dn, z_recv, s_send, s_recv,
    c_up, c_dn, c_recv, t_send, t_recv, local_sem, out_sem, *, ring, wide,
):
    s = lax.axis_index("seq")
    q = hid_ref.shape[0]
    half = q // 2
    x_peer = s + 1 - 2 * lax.rem(s, 2)
    y_peer = lax.rem(s + 2, 4)
    far = 3 - s
    to_x, to_y = {"seq": x_peer}, {"seq": y_peer}
    chans = uv.shape[1]
    n_main = stage.shape[1]
    n = stage.shape[0]
    peers = [to_x, to_y]
    extra = []

    def block(ref, at, start, size):
        return ref.at[pl.ds(pl.multiple_of(at * q + start, 16), size), :]

    if ring:
        h = lax.axis_index("head")
        core = lax.rem(h, 2)
        r = h // 2
        last = lax.axis_size("head") // 2 - 1
        to_sib, to_up, to_down = {"head": h + 1 - 2 * core}, {"head": lax.rem(h + 2, 2 * last + 2)}, {"head": lax.rem(h + 2 * last, 2 * last + 2)}
        above, below = r < last, r > 0
        peers.append(to_sib)
        extra = [(above, to_up), (below, to_down)]
        first = pl.multiple_of(s * wide, LANES)
        second = pl.multiple_of(DI + s * wide, LANES)
        loads = [
            pltpu.make_async_copy(w_ref.at[:, pl.ds(first, wide)], stage.at[:, :wide], local_sem.at[0]),
            pltpu.make_async_copy(w_ref.at[:, pl.ds(second, wide)], stage.at[:, wide : 2 * wide], local_sem.at[1]),
            pltpu.make_async_copy(w_ref.at[:, 2 * DI :], stage.at[:, 2 * wide :], local_sem.at[2]),
        ]
        is_root = r == s
        n_o = wov.shape[0] // 2
        load_o = pltpu.make_async_copy(
            wo_in_ref, wov.at[pl.ds(pl.multiple_of(core * n_o, 16), n_o), :], local_sem.at[5]
        )
        pl.when(is_root)(load_o.start)
    else:
        loads = [
            pltpu.make_async_copy(w_ref, wv, local_sem.at[0]),
            pltpu.make_async_copy(wo_in_ref, wov, local_sem.at[5]),
        ]
    for copy in loads:
        copy.start()
    own_h = pltpu.make_async_copy(hid_ref, block(hv, s, 0, q), local_sem.at[3])
    own_o = pltpu.make_async_copy(og_ref, block(ov, s, 0, q), local_sem.at[4])
    own_h.start()
    own_o.start()
    greet(peers, extra)

    sent = []

    def send(src, dst, sems, i, target):
        copy = remote(src, dst, sems[0].at[i], sems[1].at[i], target)
        copy.start()
        sent.append(copy)
        return copy

    def open_exchange(src, buf, sems):
        return (
            send(src, block(buf, s, 0, q), sems, 0, to_x),
            send(src, block(buf, s, 0, q), sems, 1, to_y),
        )

    def relay(buf, sems, heads_in):
        heads_in[0].wait_recv()
        a = block(buf, x_peer, 0, half)
        first = send(a, a, sems, 2, to_y)
        heads_in[1].wait_recv()
        b = block(buf, y_peer, half, half)
        return first, send(b, b, sems, 3, to_x)

    h_sems, o_sems = (h_send, h_recv), (o_send, o_recv)
    h_open = open_exchange(hid_ref, hv, h_sems)

    closing = []
    if ring:
        def w_block(at):
            return wv.at[pl.ds(pl.multiple_of((2 * at + core) * n, 16), n), :]

        def w_copy(at, sems, target):
            return remote(w_block(at), w_block(at), sems.at[at], z_recv.at[at], target)

        def w_swap(at):
            return remote(w_block(at), w_block(at), s_send.at[at], s_recv.at[at], to_sib)

        def launch(there, make):
            @pl.when(there)
            def _():
                make().start()

            def finish():
                @pl.when(there)
                def _():
                    make().wait_send()

            closing.append(finish)

        always = r >= 0

        def w_step(k):
            lower, upper = r - k, r + k
            has_lower, has_upper = lower >= 0, upper <= last

            @pl.when(has_lower)
            def _():
                w_copy(lower, z_up, to_up).wait_recv()

            launch(has_lower & above, lambda: w_copy(lower, z_up, to_up))
            launch(has_lower, lambda: w_swap(lower))

            @pl.when(has_upper)
            def _():
                w_copy(upper, z_dn, to_down).wait_recv()

            launch(has_upper & below, lambda: w_copy(upper, z_dn, to_down))
            launch(has_upper, lambda: w_swap(upper))

        chunks = c_recv.shape[0]
        n_c = n_o // chunks
        dist = jnp.where(r > s, r - s, s - r)

        def o_block(i):
            return wov.at[pl.ds(pl.multiple_of(core * n_o + i * n_c, 16), n_c), :]

        def o_copy(i, sems, target):
            return remote(o_block(i), o_block(i), sems.at[i], c_recv.at[i], target)

        def o_swap(i):
            return remote(o_block(i), o_block(i), t_send.at[i], t_recv.at[i], to_sib)

        def o_root():
            @pl.when(is_root)
            def _():
                load_o.wait()

            for i in range(chunks):
                launch(is_root & above, lambda i=i: o_copy(i, c_up, to_up))
                launch(is_root & below, lambda i=i: o_copy(i, c_dn, to_down))
                launch(is_root, lambda i=i: o_swap(i))

        def o_tick(t):
            i = t - dist
            live = (dist >= 1) & (i >= 0) & (i < chunks)

            @pl.when(live)
            def _():
                o_copy(i, c_up, to_up).wait_recv()

            pl.when(live & (r > s) & above)(lambda: o_copy(i, c_up, to_up).start())
            pl.when(live & (r < s) & below)(lambda: o_copy(i, c_dn, to_down).start())
            pl.when(live)(lambda: o_swap(i).start())

        def o_finish():
            for i in range(chunks):
                pl.when((r > s) & above)(lambda: o_copy(i, c_up, to_up).wait_send())
                pl.when((r < s) & below)(lambda: o_copy(i, c_dn, to_down).wait_send())
                pl.when(dist >= 1)(lambda: o_swap(i).wait_send())

        closing.append(o_finish)
        for copy in loads:
            copy.wait()
        own = pl.ds(pl.multiple_of(h * n, 16), n)
        wv[own, :n_main] = (stage[...].astype(F32) * gain_ref[...]).astype(BF16)
        wv[own, n_main:] = dtw_ref[...]
        launch(above, lambda: w_copy(r, z_up, to_up))
        launch(below, lambda: w_copy(r, z_dn, to_down))
        launch(always, lambda: w_swap(r))
        w_step(1)
    else:
        for copy in loads:
            copy.wait()

    h_far = relay(hv, h_sems, h_open)
    if ring:
        w_step(2)
        o_root()
    for copy in h_far:
        copy.wait_recv()
    o_open = open_exchange(og_ref, ov, o_sems)
    if ring:
        o_tick(1)
        w_step(3)
        for at in range(4):
            w_swap(at).wait_recv()
    own_h.wait()
    own_o.wait()

    rows = min(CHUNK, q)

    def cut(at_block):
        return pl.ds(pl.multiple_of(at_block * q, 16), q)

    def project_outs(at_block, i):
        at = cut(at_block)
        pairs = ((hv, hall_ref), (zv, z_ref), (uv, u_ref), (dv, d_ref))
        return [
            pltpu.make_async_copy(src.at[at, :], dst.at[at, :], out_sem.at[4 * i + k])
            for k, (src, dst) in enumerate(pairs)
        ]

    def pull_outs(at_block, i):
        at = cut(at_block)
        pairs = ((ov, ogall_ref), (d0v, d0_ref))
        return [
            pltpu.make_async_copy(src.at[at, :], dst.at[at, :], out_sem.at[16 + 2 * i + k])
            for k, (src, dst) in enumerate(pairs)
        ]

    def nth(i):
        return jnp.where(i == 0, s, jnp.where(i == 1, x_peer, jnp.where(i == 2, y_peer, far)))

    w_out = pltpu.make_async_copy(wv, wt_ref, out_sem.at[24])
    o_out = pltpu.make_async_copy(wov, wo_ref, out_sem.at[25])
    w_out.start()

    def project(at_block):
        @pl.loop(0, q // rows)
        def _(j):
            at = pl.ds(pl.multiple_of(at_block * q + j * rows, 16), rows)
            hb = hv[at, :]
            h32 = hb.astype(F32)
            r0 = lax.rsqrt(jnp.mean(h32 * h32, axis=1, keepdims=True) + EPS)
            zv[at, :] = (dot(hb, wv[:, :wide]) * r0).astype(BF16)
            uv[at, :] = (dot(hb, wv[:, wide : wide + chans]) * r0).astype(BF16)
            raw = dot(hb, wv[:, wide + chans :]) * r0
            lane = lax.broadcasted_iota(jnp.int32, raw.shape, 1)
            dv[at, :] = jnp.where(lane == LANES - 1, r0, raw)

    def pull(at_block):
        at = cut(at_block)

        @pl.loop(0, wide // 256)
        def _(j):
            to = pl.ds(pl.multiple_of(j * 256, 256), 256)
            d0v[at, to] = dot_t(ov[at, :], wov[to, :]).astype(BF16)

    @pl.loop(0, 4)
    def _(i):
        at_block = nth(i)
        project(at_block)
        for copy in project_outs(at_block, i):
            copy.start()
        if ring:
            o_tick(2 + i)

    if ring:
        o_tick(6)
    o_far = relay(ov, o_sems, o_open)
    if ring:
        for t in range(7, chunks + 3):
            o_tick(t)
        for i in range(chunks):
            o_swap(i).wait_recv()
    o_out.start()

    @pl.loop(0, 4)
    def _(i):
        at_block = nth(i)

        @pl.when(i == 3)
        def _():
            for copy in o_far:
                copy.wait_recv()

        pull(at_block)
        for copy in pull_outs(at_block, i):
            copy.start()

    for i, at_block in enumerate((s, x_peer, y_peer, far)):
        for copy in project_outs(at_block, i) + pull_outs(at_block, i):
            copy.wait()
    w_out.wait()
    o_out.wait()
    for copy in sent:
        copy.wait_send()
    for finish in closing:
        finish()


def decays(aux, heads, expand, rate_e, rate_row, rate_col):
    rows = aux.shape[0]
    lane = lax.broadcasted_iota(jnp.int32, aux.shape, 1)
    dt = jnp.where(lane < heads, aux, 0.0).astype(BF16)
    r = lax.broadcasted_iota(jnp.int32, (rows, rows), 0)
    c = lax.broadcasted_iota(jnp.int32, (rows, rows), 1)
    causal = c <= r
    lower = jnp.where(causal, 1.0, 0.0).astype(BF16)
    dt_e = dot(dt, expand)
    cum_e = dot(lower, dt_e.astype(BF16)) * rate_e
    cum_c = dot(lower, dt) * rate_row
    cum_t = lax.dot_general(dt, lower, (((0,), (1,)), ((), ())), preferred_element_type=F32) * rate_col
    return causal, dt_e, cum_e, cum_c, cum_t


def shift_matrix(rows, by):
    r = lax.broadcasted_iota(jnp.int32, (rows, rows), 0)
    c = lax.broadcasted_iota(jnp.int32, (rows, rows), 1)
    return jnp.where(c == r + by, 1.0, 0.0).astype(BF16)


def lower_parts(cum_c, cum_t, h, causal):
    mid = causal.shape[0] // 2
    near = causal[:mid, :mid]
    col, row = cum_c[:, h : h + 1], cum_t[h : h + 1, :]
    top = jnp.exp(jnp.where(near, col[:mid] - row[:, :mid], -1e30))
    low = jnp.exp(col[mid:] - row[:, :mid])
    right = jnp.exp(jnp.where(near, col[mid:] - row[:, mid:], -1e30))
    return top, low, right


def scan_kernel(
    u_ref, d_ref, z_ref, d0_ref, cw_ref, cb_ref, dtb_ref, exp_ref, rowp_ref, colp_ref,
    act_ref, slope_ref, aux_ref, y_ref, gg_ref, st_ref, sum_ref, state, ext, *, heads, wide,
):
    step = pl.program_id(0)
    rows = u_ref.shape[0]
    chans = u_ref.shape[1]

    @pl.when(step == 0)
    def _():
        state[...] = jnp.zeros_like(state)
        ext[...] = jnp.zeros_like(ext)

    u = u_ref[...]
    u32 = u.astype(F32)
    pre = cb_ref[0:1, :] + cw_ref[KERNEL - 1 : KERNEL, :] * u32
    before = jnp.zeros((8, chans), F32)
    for j in range(1, KERNEL):
        tap = cw_ref[KERNEL - 1 - j : KERNEL - j, :]
        pre = pre + tap * dot(shift_matrix(rows, -j), u)
        before = before + tap * ext[8 - j : 16 - j, :]
    pre = jnp.concatenate([pre[:8] + before, pre[8:]], axis=0)
    ext[0:8, :] = u32[rows - 8 :, :]
    sig = sigmoid(pre)
    act = (pre * sig).astype(BF16)
    act_ref[...] = act
    slope_ref[...] = (sig * (1.0 + pre * (1.0 - sig))).astype(BF16)
    raw = d_ref[...]
    v = raw + dtb_ref[0:1, :]
    soft = jnp.maximum(v, 0.0) + jnp.log1p(jnp.exp(-jnp.abs(v)))
    soft = soft.astype(BF16).astype(F32)
    lane = lax.broadcasted_iota(jnp.int32, v.shape, 1)
    aux = jnp.where(lane < heads, soft, 0.0)
    sig_v = pltpu.roll(sigmoid(v), heads, 1)
    aux = jnp.where((lane >= heads) & (lane < 2 * heads), sig_v, aux)
    aux = jnp.where(lane == LANES - 1, raw, aux)
    aux_ref[...] = aux

    x = act[:, :wide]
    x32 = x.astype(F32)
    b = act[:, wide : wide + STATE]
    c = act[:, wide + STATE :]
    causal, dt_e, cum_e, cum_c, cum_t = decays(
        aux, heads, exp_ref[...], rowp_ref[0:1, :], rowp_ref[3:4, :LANES], colp_ref[:, 0:1]
    )
    xdt = x32 * dt_e
    xdt16 = xdt.astype(BF16)
    scores = dot_t(c, b)
    st = state[...]
    st_ref[0] = st
    mid = rows // 2
    half = lax.broadcasted_iota(jnp.int32, (rows, LANES), 1) < HEAD_DIM
    parts = []
    for pair in range(heads // 2):
        x2 = xdt16[:, LANES * pair : LANES * (pair + 1)]
        got = []
        for h in (2 * pair, 2 * pair + 1):
            top, low, right = lower_parts(cum_c, cum_t, h, causal)
            m_top = (scores[:mid, :mid] * top).astype(BF16)
            m_low = (scores[mid:, :mid] * low).astype(BF16)
            m_right = (scores[mid:, mid:] * right).astype(BF16)
            y_low = dot(jnp.concatenate([m_low, m_right], axis=1), x2)
            got.append(jnp.concatenate([dot(m_top, x2[:mid]), y_low], axis=0))
        parts.append(jnp.where(half, got[0], got[1]))
    y = jnp.concatenate(parts, axis=1) + dot(c, st.astype(BF16)) * jnp.exp(cum_e)
    last = cum_e[rows - 1 : rows, :]
    tail = jnp.exp(last - cum_e)
    state[...] = jnp.exp(last) * st + t_dot(b, (xdt * tail).astype(BF16))
    y_ref[...] = y
    ssd = (y + rowp_ref[1:2, :] * x32).astype(BF16).astype(F32)
    z = z_ref[...].astype(F32)
    g = ssd * (z * sigmoid(z))
    gg = g * rowp_ref[2:3, :]
    gg_ref[...] = gg.astype(BF16)
    ones = jnp.ones((8, wide), BF16)
    ssq = dot_t(ones, (g * g).astype(BF16))
    cross = dot_t(ones, (gg * d0_ref[...].astype(F32)).astype(BF16))
    sub = lax.broadcasted_iota(jnp.int32, ssq.shape, 0)
    sum_ref[...] = jnp.where(sub == 0, ssq, cross)


def seg_dot(v, seg):
    hi = v.astype(BF16)
    rest = v - hi.astype(F32)
    mid = rest.astype(BF16)
    low = (rest - mid.astype(F32)).astype(BF16)
    return dot(hi, seg) + dot(mid, seg) + dot(low, seg)


def blend_kernel(
    gg_ref, wo_ref, og_ref, sums_ref, mask_ref,
    stat_ref, part_ref, wog_ref,
    ggv, wov, ogv, far_p, y_p, x_p, own_p, far_a, far_b, sv, staged,
    load_sem, d_send, d_recv, s_send, s_recv, out_sem, w_sem,
):
    s = lax.axis_index("seq")
    q = far_p.shape[0]
    half = q // 2
    rows = min(CHUNK, q)
    x_peer = s + 1 - 2 * lax.rem(s, 2)
    y_peer = lax.rem(s + 2, 4)
    far = 3 - s
    to_x, to_y, to_far = {"seq": x_peer}, {"seq": y_peer}, {"seq": far}
    loads = [
        pltpu.make_async_copy(src, dst, load_sem.at[i])
        for i, (src, dst) in enumerate(((gg_ref, ggv), (wo_ref, wov), (og_ref, ogv)))
    ]
    for copy in loads:
        copy.start()
    sv[s] = sums_ref[...]
    greet([to_x, to_y, to_far])
    sums = [
        remote(sums_ref, sv.at[s], s_send.at[i], s_recv.at[i], peer) for i, peer in enumerate((to_x, to_y, to_far))
    ]
    for copy in sums:
        copy.start()
    loads[0].wait()
    loads[1].wait()

    def part(block, out):
        @pl.loop(0, q // rows)
        def _(j):
            at = pl.ds(pl.multiple_of(block * q + j * rows, 16), rows)
            to = pl.ds(pl.multiple_of(j * rows, 16), rows)
            out[to, :] = dot(ggv[at, :], wov[...]).astype(BF16)

    part(far, far_p)
    d0 = remote(far_p.at[:half], far_a, d_send.at[0], d_recv.at[0], to_x)
    d1 = remote(far_p.at[half:], far_b, d_send.at[1], d_recv.at[1], to_y)
    d0.start()
    d1.start()
    part(y_peer, y_p)
    part(x_peer, x_p)
    part(s, own_p)
    own_out = pltpu.make_async_copy(own_p, part_ref.at[2], out_sem.at[2])
    own_out.start()

    for copy in sums:
        copy.wait_recv()
    total = (sv[0] + sv[1]) + (sv[2] + sv[3])
    r1 = lax.rsqrt(total[0:1] / DI + EPS)
    r1m = r1 * mask_ref[0:1]
    coef = r1m * r1 * r1 * total[1:2] / DI
    sub = lax.broadcasted_iota(jnp.int32, (LANES, r1.shape[1]), 0)
    stat = jnp.where(sub == 0, r1m, jnp.where(sub == 1, coef, 0.0)).T
    stat_ref[...] = stat

    @pl.loop(0, ggv.shape[0] // rows)
    def _(j):
        at = pl.ds(pl.multiple_of(j * rows, 16), rows)
        ggv[at, :] = (ggv[at, :].astype(F32) * stat_ref[at, 0:1]).astype(BF16)

    loads[2].wait()
    tile = 256
    ring = len(wog_ref.shape) == 4

    def w_out(m):
        slot = lax.rem(m, 2)
        if ring:
            per = tile // wog_ref.shape[2]
            groups = wov.shape[0] // 2 // tile
            to = wog_ref.at[pl.ds(lax.rem(m, groups) * per, per), m // groups]
            src = staged.at[slot].reshape(per, wog_ref.shape[2], wog_ref.shape[3])
        else:
            to = wog_ref.at[pl.ds(pl.multiple_of(m * tile, tile), tile), :]
            src = staged.at[slot]
        return pltpu.make_async_copy(src, to, w_sem.at[slot])

    count = wov.shape[0] // tile

    @pl.loop(0, count)
    def _(m):
        @pl.when(m >= 2)
        def _():
            w_out(m - 2).wait()

        at = pl.ds(pl.multiple_of(m * tile, tile), tile)
        staged[lax.rem(m, 2)] = t_dot(ggv[:, at], ogv[...]).astype(BF16)
        w_out(m).start()

    d0.wait_recv()
    y_p[:half, :] = (y_p[:half, :].astype(F32) + far_a[...].astype(F32)).astype(BF16)
    y_out = pltpu.make_async_copy(y_p, part_ref.at[0], out_sem.at[0])
    y_out.start()
    d1.wait_recv()
    x_p[half:, :] = (x_p[half:, :].astype(F32) + far_b[...].astype(F32)).astype(BF16)
    x_out = pltpu.make_async_copy(x_p, part_ref.at[1], out_sem.at[1])
    x_out.start()
    w_out(count - 2).wait()
    w_out(count - 1).wait()
    for copy in (own_out, y_out, x_out):
        copy.wait()
    for copy in sums + [d0, d1]:
        copy.wait_send()


def gate_kernel(x_ref, aux_ref, z_ref, d0_ref, y_ref, stat_ref, rowp_ref, dy_ref, dpg_ref):
    stat = stat_ref[...]
    r1m = stat[:, 0:1]
    coef = stat[:, 1:2]
    r0 = aux_ref[:, LANES - 1 : LANES]
    ssd = (y_ref[...] + rowp_ref[1:2, :] * x_ref[...].astype(F32)).astype(BF16).astype(F32)
    z = z_ref[...].astype(F32)
    sig = sigmoid(z)
    sz = z * sig
    d_gated = (r1m * rowp_ref[2:3, :]) * d0_ref[...].astype(F32) - (ssd * sz) * coef
    dy_ref[...] = (d_gated * sz).astype(BF16)
    dpg_ref[...] = (r0 * (d_gated * ssd * (sig * (1.0 + z * (1.0 - sig))))).astype(BF16)


def back_kernel(
    act_ref, aux_ref, dy_ref, y_ref, st_ref, slope_ref, u_ref, part_ref,
    exp_ref, seg_ref, rowp_ref, colp_ref, cw_ref,
    dp_ref, sm_ref, br_ref, adj, ext, own_b, y_f, x_f, br_o,
    b_send, b_recv, b_load, *, heads, wide,
):
    step = pl.program_id(0)
    steps = pl.num_programs(0)
    rows = act_ref.shape[0]
    chans = u_ref.shape[1]

    s = lax.axis_index("seq")
    x_peer = s + 1 - 2 * lax.rem(s, 2)
    y_peer = lax.rem(s + 2, 4)
    to_x, to_y = {"seq": x_peer}, {"seq": y_peer}
    out_y = remote(part_ref.at[0], y_f, b_send.at[0], b_recv.at[0], to_y)
    out_x = remote(part_ref.at[1], x_f, b_send.at[1], b_recv.at[1], to_x)
    own_load = pltpu.make_async_copy(part_ref.at[2], own_b, b_load.at[0])

    @pl.when(step == 0)
    def _():
        greet([to_x, to_y])
        out_y.start()
        out_x.start()
        own_load.start()

    @pl.when(step == 0)
    def _():
        sm_ref[...] = jnp.zeros_like(sm_ref)
        adj[...] = jnp.zeros_like(adj)
        ext[...] = jnp.zeros_like(ext)

    x = act_ref[:, :wide]
    x32 = x.astype(F32)
    b = act_ref[:, wide : wide + STATE]
    c = act_ref[:, wide + STATE :]
    aux = aux_ref[...]
    r0 = aux[:, LANES - 1 : LANES]
    skip_e = rowp_ref[1:2, :]
    y = y_ref[...]
    dy16 = dy_ref[...]
    dy = dy16.astype(F32)

    causal, dt_e, cum_e, cum_c, cum_t = decays(
        aux, heads, exp_ref[...], rowp_ref[0:1, :], rowp_ref[3:4, :LANES], colp_ref[:, 0:1]
    )
    xdt = x32 * dt_e
    xdt16 = xdt.astype(BF16)
    scores = dot_t(c, b)
    st = st_ref[0]
    st16 = st.astype(BF16)
    q_in = adj[...]
    q16 = q_in.astype(BF16)
    last = cum_e[rows - 1 : rows, :]
    ecum = jnp.exp(cum_e)
    tail = jnp.exp(last - cum_e)
    half = lax.broadcasted_iota(jnp.int32, (rows, LANES), 1) < HEAD_DIM
    zero = jnp.zeros((rows, LANES), BF16)
    mid = rows // 2
    n_sum = None
    parts = []
    for pair in range(heads // 2):
        cut = slice(LANES * pair, LANES * (pair + 1))
        x2 = xdt16[:, cut]
        dy2 = dy16[:, cut]
        got = []
        for side in range(2):
            h = 2 * pair + side
            top, low, right = lower_parts(cum_c, cum_t, h, causal)
            m_top = (scores[:mid, :mid] * top).astype(BF16)
            m_low = (scores[mid:, :mid] * low).astype(BF16)
            m_right = (scores[mid:, mid:] * right).astype(BF16)
            v_top = t_dot(jnp.concatenate([m_top, m_low], axis=0), dy2)
            got.append(jnp.concatenate([v_top, t_dot(m_right, dy2[mid:])], axis=0))
            own = half if side == 0 else jnp.logical_not(half)
            dy_own = jnp.where(own, dy2, zero)
            g_top = dot_t(dy_own[:mid], x2[:mid])
            g_low = dot_t(dy_own[mid:], x2)
            n = [g_top * top, g_low[:, :mid] * low, g_low[:, mid:] * right]
            n_sum = n if n_sum is None else [p + v for p, v in zip(n_sum, n)]
        parts.append(jnp.where(half, got[0], got[1]))
    n_low = jnp.concatenate([n_sum[1], n_sum[2]], axis=1).astype(BF16)
    n_top = n_sum[0].astype(BF16)
    out_part = dot(b, q16) * tail
    v = jnp.concatenate(parts, axis=1) + out_part
    dy_e = (dy * ecum).astype(BF16)
    x_tail = (xdt * tail).astype(BF16)
    d_b = jnp.concatenate([t_dot(jnp.concatenate([n_top, n_low[:, :mid]], axis=0), c), t_dot(n_low[:, mid:], c[mid:])], axis=0)
    d_b = d_b + dot_t(x_tail, q16)
    d_c = jnp.concatenate([dot(n_top, b[:mid]), dot(n_low, b)], axis=0) + dot_t(dy_e, st16)
    elast = jnp.exp(last)
    adj[...] = elast * q_in + t_dot(c, dy_e)

    seg = seg_ref[...]
    flow = dy * y - xdt16.astype(F32) * v
    passed = jnp.sum(xdt16.astype(F32) * out_part, axis=0, keepdims=True)
    passed = passed + elast * jnp.sum(q_in * st, axis=0, keepdims=True)
    flow_h = seg_dot(flow, seg)
    passed_h = seg_dot(jnp.broadcast_to(passed, (8, wide)), seg)[0:1, :]
    upper = jnp.where(
        lax.broadcasted_iota(jnp.int32, (rows, rows), 1) >= lax.broadcasted_iota(jnp.int32, (rows, rows), 0), 1.0, 0.0
    ).astype(BF16)
    hi = flow_h.astype(BF16)
    rest = flow_h - hi.astype(F32)
    mid = rest.astype(BF16)
    low = (rest - mid.astype(F32)).astype(BF16)
    crossing = dot(upper, hi) + dot(upper, mid) + dot(upper, low) + passed_h
    rate_row = rowp_ref[3:4, :LANES]
    decay_grad = rate_row * crossing
    d_dt = seg_dot(x32 * v, seg) + decay_grad
    lane = lax.broadcasted_iota(jnp.int32, (rows, LANES), 1)
    sig_v = pltpu.roll(aux, LANES - heads, 1)
    d_pre = jnp.where(lane < heads, d_dt * sig_v, 0.0)
    dt = jnp.where(lane < heads, aux, 0.0)
    dp_ref[:, chans:] = (r0 * d_pre).astype(BF16)

    d_act = jnp.concatenate([skip_e * dy + dt_e * v, d_b, d_c], axis=1)
    d_conv = d_act * slope_ref[...].astype(F32)
    d_conv16 = d_conv.astype(BF16)
    u = u_ref[...].astype(F32)
    d_u = cw_ref[KERNEL - 1 : KERNEL, :] * d_conv
    sm_ref[KERNEL - 1 : KERNEL, :] += jnp.sum(u * d_conv, axis=0, keepdims=True)
    for j in range(1, KERNEL):
        k = KERNEL - 1 - j
        moved = dot(shift_matrix(rows, j), d_conv16)
        moved = jnp.concatenate([moved[: rows - 8], moved[rows - 8 :] + ext[j : j + 8, :]], axis=0)
        d_u = d_u + cw_ref[k : k + 1, :] * moved
        sm_ref[k : k + 1, :] += jnp.sum(u * moved, axis=0, keepdims=True)
    ext[8:16, :] = d_conv[0:8, :]
    dp_ref[:, :chans] = (r0 * d_u).astype(BF16)
    sm_ref[4:5, :] += jnp.sum(d_conv, axis=0, keepdims=True)
    sm_ref[5:6, :wide] += jnp.sum(x32 * dy, axis=0, keepdims=True)
    sm_ref[6:7, :LANES] += jnp.sum(d_pre, axis=0, keepdims=True)
    sm_ref[7:8, :LANES] += jnp.sum(dt * decay_grad, axis=0, keepdims=True)

    @pl.when(step == steps - 1)
    def _():
        own_load.wait()
        out_y.wait_recv()
        out_x.wait_recv()
        br_o[...] = own_b[...].astype(F32) + y_f[...].astype(F32) + x_f[...].astype(F32)
        last_copy = pltpu.make_async_copy(br_o, br_ref, b_load.at[1])
        last_copy.start()
        for copy in (out_y, out_x):
            copy.wait_send()
        last_copy.wait()


def grads_kernel(
    dpg_ref, dp_ref, w_ref, h_ref, gate_ref, piece_ref, tiny_ref,
    dn_ref, wing_ref, win_ref, wout_ref,
    dpv, wv, hb, far_p, y_p, x_p, far_a, far_b, y_f, x_f, dn_o, sib_s, mine_s, own_s, z_u, z_d, pv,
    load_sem, hb_sem, d_send, d_recv, s_send, s_recv, zu_send, zu_recv, zd_send, zd_recv,
    g_send, g_recv, k_send, k_recv, p_send, p_recv, w_send, w_recv, out_sem,
):
    s = lax.axis_index("seq")
    h = lax.axis_index("head")
    owners = lax.axis_size("head")
    last = owners // 2 - 1
    core = lax.rem(h, 2)
    r = h // 2
    x_peer = s + 1 - 2 * lax.rem(s, 2)
    y_peer = lax.rem(s + 2, 4)
    far = 3 - s
    to_x, to_y = {"seq": x_peer}, {"seq": y_peer}
    to_sib = {"head": h + 1 - 2 * core}
    to_up, to_down = {"head": lax.rem(h + 2, owners)}, {"head": lax.rem(h + owners - 2, owners)}
    above, below = r < last, r > 0
    q = far_p.shape[0]
    half = q // 2
    n, cols = own_s.shape[1], own_s.shape[2]
    spare = LANES // 2
    tiles = cols // LANES
    edges = [LANES * (tiles * k // 4) for k in range(5)]
    spans = list(zip(edges[:-1], edges[1:]))
    sent = []
    closing = []

    def push(src, dst, sems, i, target):
        copy = remote(src, dst, sems[0].at[i], sems[1].at[i], target)
        copy.start()
        sent.append(copy)
        return copy

    def launch(there, make):
        @pl.when(there)
        def _():
            make().start()

        def finish():
            @pl.when(there)
            def _():
                make().wait_send()

        closing.append(finish)

    skip = dpv.shape[1] - cols
    load_dp = pltpu.make_async_copy(dp_ref, dpv.at[:, skip:], load_sem.at[0])
    load_w = pltpu.make_async_copy(w_ref, wv, load_sem.at[1])
    load_g = pltpu.make_async_copy(dpg_ref, dpv.at[:, :skip], load_sem.at[4])
    own_gate = pltpu.make_async_copy(gate_ref, wing_ref.at[s], load_sem.at[5])
    load_dp.start()
    load_g.start()
    load_w.start()
    own_gate.start()

    def chip(i):
        return jnp.where(lax.rem(i, 2) == 0, last - i // 2, i // 2)

    def load_h(i, other):
        at = 2 * chip(i) + (1 - core if other else core)
        slot = 0 if other else 1
        return pltpu.make_async_copy(
            h_ref.at[:, pl.ds(pl.multiple_of(at * n, LANES), n)], hb.at[slot], hb_sem.at[slot]
        )

    load_h(0, True).start()
    load_h(0, False).start()
    to_heads = [{"head": lax.rem(h + k, owners)} for k in range(1, owners)]
    greet([to_x, to_y] + to_heads)

    d_sems = (d_send, d_recv)
    g_sems = (g_send, g_recv)

    k_sems = (k_send, k_recv)
    k0 = push(gate_ref, wing_ref.at[s], k_sems, 0, to_x)
    k1 = push(gate_ref, wing_ref.at[s], k_sems, 1, to_y)
    w_sems = (w_send, w_recv)
    own_piece = pltpu.make_async_copy(piece_ref, pv.at[s], load_sem.at[2])
    own_piece.start()
    w0 = push(piece_ref, pv.at[s], w_sems, 0, to_x)
    w1 = push(piece_ref, pv.at[s], w_sems, 1, to_y)
    tile = 256

    def part(block, out):
        at = pl.ds(pl.multiple_of(block * q, 16), q)

        @pl.loop(0, wv.shape[0] // tile)
        def _(j):
            to = pl.ds(pl.multiple_of(j * tile, tile), tile)
            out[:, to] = dot_t(dpv[at, :], wv[to, :]).astype(BF16)

    def add_to(out, at, extra):
        out[at, :] = (out[at, :].astype(F32) + extra.astype(F32)).astype(BF16)

    def swap(i):
        t = chip(i)
        return remote(sib_s.at[lax.rem(i, 2)], own_s.at[t], s_send.at[t], s_recv.at[t], to_sib)

    def rows_of(i):
        t = chip(i)
        slot = lax.rem(i, 2)

        @pl.when(i >= 2)
        def _():
            swap(i - 2).wait_send()

        load_h(i, True).wait()
        for lo, hi in spans:
            sib_s[slot, :, lo:hi] = t_dot(hb[0], dpv[:, skip + lo : skip + hi]).astype(BF16)
        sib_s[slot, :, cols - spare :] = tiny_ref[...]
        swap(i).start()

        @pl.when(i < 3)
        def _():
            load_h(i + 1, True).start()

        load_h(i, False).wait()
        for lo, hi in spans:
            mine_s[:, lo:hi] = t_dot(hb[1], dpv[:, skip + lo : skip + hi]).astype(BF16)
        mine_s[:, cols - spare :] = tiny_ref[...]

        @pl.when(i < 3)
        def _():
            load_h(i + 1, False).start()

        swap(i).wait_recv()
        join(t, mine_s)

    def join(t, extra):
        for lo, hi in spans:
            own_s[t, :, lo:hi] = (own_s[t, :, lo:hi].astype(F32) + extra[:, lo:hi].astype(F32)).astype(BF16)

    def up_copy(t):
        return remote(own_s.at[t], z_u.at[t - 1], zu_send.at[t], zu_recv.at[t], to_up)

    def down_copy(t):
        return remote(own_s.at[t], z_d.at[t], zd_send.at[t], zd_recv.at[t], to_down)

    def up_add(t):
        up_copy(t).wait_recv()
        join(t, z_u.at[t - 1])

    def down_add(t):
        down_copy(t).wait_recv()
        join(t, z_d.at[t])

    def pass_on(t, there, add, make):
        pl.when(there)(functools.partial(add, t))
        launch(there, lambda: make(t))

    def follow(t, there, make, before):
        @pl.when(there)
        def _():
            make(before).wait_send()
            make(t).start()

    def finish_later(t, there, make):
        def finish():
            @pl.when(there)
            def _():
                make(t).wait_send()

        closing.append(finish)

    load_dp.wait()
    pl.loop(0, 2)(rows_of)

    @pl.when(r == 0)
    def _():
        up_copy(last).start()

    @pl.when(r == last)
    def _():
        down_copy(0).start()

    load_g.wait()
    load_w.wait()
    part(far, far_p)
    d0 = push(far_p.at[:half], far_a, d_sems, 0, to_x)
    d1 = push(far_p.at[half:], far_b, d_sems, 1, to_y)
    k0.wait_recv()
    gate_a = wing_ref.at[x_peer, : n // 2]
    k2 = push(gate_a, gate_a, k_sems, 2, to_y)
    k1.wait_recv()
    gate_b = wing_ref.at[y_peer, n // 2 :]
    k3 = push(gate_b, gate_b, k_sems, 3, to_x)
    own_piece.wait()
    w0.wait_recv()
    piece_a = pv.at[x_peer, 0]
    w2 = push(piece_a, piece_a, w_sems, 2, to_y)
    w1.wait_recv()
    piece_b = pv.at[y_peer, 1]
    w3 = push(piece_b, piece_b, w_sems, 3, to_x)
    pl.loop(2, 4)(rows_of)

    follow(2, r == 0, up_copy, last)
    follow(1, r == last, down_copy, 0)
    pass_on(last, (r > 0) & above, up_add, up_copy)
    pass_on(0, (r < last) & below, down_add, down_copy)
    part(y_peer, y_p)
    part(x_peer, x_p)
    follow(1, r == 0, up_copy, 2)
    follow(2, r == last, down_copy, 1)
    pass_on(2, r == 1, up_add, up_copy)
    pass_on(1, r == 2, down_add, down_copy)
    finish_later(1, r == 0, up_copy)
    finish_later(2, r == last, down_copy)
    d0.wait_recv()
    add_to(y_p, slice(0, half), far_a[...])
    d2 = push(y_p, y_f, d_sems, 2, to_y)
    d1.wait_recv()
    add_to(x_p, slice(half, q), far_b[...])
    d3 = push(x_p, x_f, d_sems, 3, to_x)
    pl.when(r > 0)(lambda: up_add(r))
    pl.when(r < last)(lambda: down_add(r))

    red = own_s.at[r]
    g0 = push(red, win_ref.at[s], g_sems, 0, to_x)
    g1 = push(red, win_ref.at[s], g_sems, 1, to_y)
    own_win = pltpu.make_async_copy(red, win_ref.at[s], load_sem.at[3])
    own_win.start()
    w2.wait_recv()
    w3.wait_recv()
    per = owners // 4

    def piece_of(head):
        return pv.at[head // per, lax.rem(head, per)]

    pieces = []
    for k, peer in enumerate(to_heads):
        pieces.append(push(piece_of(peer["head"]), wout_ref.at[h], (p_send, p_recv), k, peer))
    own_piece = pltpu.make_async_copy(piece_of(h), wout_ref.at[h], load_sem.at[2])
    own_piece.start()

    g0.wait_recv()
    part_a = win_ref.at[x_peer, : n // 2]
    g2 = push(part_a, part_a, g_sems, 2, to_y)
    g1.wait_recv()
    part_b = win_ref.at[y_peer, n // 2 :]
    g3 = push(part_b, part_b, g_sems, 3, to_x)

    d2.wait_recv()
    d3.wait_recv()

    def dn_out(j):
        to = pl.ds(pl.multiple_of(j * tile, tile), tile)
        return pltpu.make_async_copy(dn_o.at[lax.rem(j, 2)], dn_ref.at[:, to], out_sem.at[lax.rem(j, 2)])

    own_at = pl.ds(pl.multiple_of(s * q, 16), q)
    tiles_n = wv.shape[0] // tile

    @pl.loop(0, tiles_n)
    def _(j):
        to = pl.ds(pl.multiple_of(j * tile, tile), tile)
        got = dot_t(dpv[own_at, :], wv[to, :])

        @pl.when(j > 1)
        def _():
            dn_out(j - 2).wait()

        dn_o[lax.rem(j, 2)] = got + y_f[:, to].astype(F32) + x_f[:, to].astype(F32)
        dn_out(j).start()

    dn_out(tiles_n - 2).wait()
    dn_out(tiles_n - 1).wait()
    own_win.wait()
    own_gate.wait()
    own_piece.wait()
    k2.wait_recv()
    k3.wait_recv()
    for copy in pieces:
        copy.wait_recv()
    g2.wait_recv()
    g3.wait_recv()
    for i in (2, 3):
        swap(i).wait_send()
    for copy in sent:
        copy.wait_send()
    for finish in closing:
        finish()


def finish_kernel(gate_ref, rest_ref, w_ref, dtw_ref, gain_ref, win_ref, wdt_ref, norm_ref, *, heads, wide):
    ranks = gate_ref.shape[0]
    gain = gain_ref[...]
    norm = None

    def piece(at, raw):
        to = slice(at, at + raw.shape[1])
        win_ref[:, to] = raw * gain
        return jnp.sum(raw * w_ref[:, to].astype(F32), axis=1, keepdims=True)

    shared = None
    dt_parts = []
    for k in range(ranks):
        here = piece(k * wide, gate_ref[k].astype(F32)) + piece(DI + k * wide, rest_ref[k, :, :wide].astype(F32))
        norm = here if norm is None else norm + here
        bc = rest_ref[k, :, wide : wide + 2 * STATE].astype(F32)
        shared = bc if shared is None else shared + bc
        dt_parts.append(rest_ref[k, :, wide + 2 * STATE : wide + 2 * STATE + heads].astype(F32))
    norm = norm + piece(2 * DI, shared)
    raw = jnp.concatenate(dt_parts, axis=1)
    wdt_ref[...] = raw * gain
    norm_ref[...] = norm + jnp.sum(raw * dtw_ref[...].astype(F32), axis=1, keepdims=True)


def local(hidden, lengths, out_grad, norm_gain, w_in, w_dt, conv_weight, conv_bias, dt_bias, a_log, skip_gain, gate_gain, w_out):
    ranks = lax.axis_size("seq")
    rank = lax.axis_index("seq")
    owners = lax.axis_size("head")
    owner = lax.axis_index("head")
    local_len, width = hidden.shape[1], hidden.shape[2]
    heads = HEADS // ranks
    wide = heads * HEAD_DIM
    chans = wide + 2 * STATE
    cols = wide + chans + LANES
    tokens = ranks * local_len
    chunk = min(CHUNK, local_len)
    steps = tokens // chunk
    shard = w_in.shape[0]

    gain_rows = norm_gain.astype(F32)[:, None]

    def scaled(v):
        return (v.astype(F32) * gain_rows).astype(BF16)

    spare = LANES // 2
    small = jnp.concatenate([conv_weight.reshape(-1), conv_bias, dt_bias, a_log, skip_gain, gate_gain])
    n_small = small.shape[0]
    small = jnp.pad(small, (0, shard * spare - n_small)).reshape(shard, spare)
    last_block = jnp.concatenate(
        [
            scaled(lax.dynamic_slice_in_dim(w_dt, rank * heads, heads, 1)),
            jnp.zeros((shard, LANES - spare - heads), BF16),
            small,
        ],
        axis=1,
    )
    ring = owners == 2 * ranks
    if ring:
        w_given, o_given = w_in, w_out
    else:
        w_given = lax.all_gather(
            jnp.concatenate(
                [
                    scaled(lax.dynamic_slice_in_dim(w_in, rank * wide, wide, 1)),
                    scaled(lax.dynamic_slice_in_dim(w_in, DI + rank * wide, wide, 1)),
                    scaled(w_in[:, 2 * DI :]),
                    last_block,
                ],
                axis=1,
            ),
            "head", axis=0, tiled=True,
        )
        o_given = lax.dynamic_slice_in_dim(lax.all_gather(w_out, "head", axis=0, tiled=True), rank * wide, wide, 0)

    def sds(shape, kind):
        return jax.ShapeDtypeStruct(shape, kind)

    hbm = pl.BlockSpec(memory_space=pl.ANY)
    vmem = pl.BlockSpec(memory_space=pltpu.VMEM)

    def dma(count):
        return pltpu.SemaphoreType.DMA((count,))

    h_all, og_all, w_t, w_o, z, u, d_raw, d0 = pl.pallas_call(
        functools.partial(gather_kernel, ring=ring, wide=wide),
        in_specs=[hbm, hbm, hbm, hbm, vmem, vmem],
        out_specs=[hbm] * 8,
        out_shape=[
            sds((tokens, width), BF16),
            sds((tokens, width), BF16),
            sds((width, cols), BF16),
            sds((wide, width), BF16),
            sds((tokens, wide), BF16),
            sds((tokens, chans), BF16),
            sds((tokens, LANES), F32),
            sds((tokens, wide), BF16),
        ],
        scratch_shapes=[
            pltpu.VMEM((tokens, width), BF16),
            pltpu.VMEM((tokens, width), BF16),
            pltpu.VMEM((width, cols), BF16),
            pltpu.VMEM((wide, width), BF16),
            pltpu.VMEM((shard, cols - LANES), BF16),
            pltpu.VMEM((tokens, wide), BF16),
            pltpu.VMEM((tokens, chans), BF16),
            pltpu.VMEM((tokens, LANES), F32),
            pltpu.VMEM((tokens, wide), BF16),
        ]
        + [dma(4)] * 9
        + [dma(8)] * 5
        + [dma(6), dma(26)],
        compiler_params=pltpu.CompilerParams(
            collective_id=0, has_side_effects=True, vmem_limit_bytes=56 * 1024 * 1024
        ),
        cost_estimate=pl.CostEstimate(
            flops=2 * tokens * width * (cols + wide), bytes_accessed=4 * tokens * (width + cols), transcendentals=0
        ),
        name="gather_project",
    )(hidden[0], out_grad[0], w_given, o_given, gain_rows, last_block)

    small = w_t.reshape(owners, shard, cols)[:, :, cols - spare :].reshape(owners, shard * spare)
    cs = CHANNELS // owners
    hs = HEADS // owners
    gs = DI // owners
    conv_w = small[:, : KERNEL * cs].reshape(owners, KERNEL, cs).swapaxes(0, 1).reshape(KERNEL, CHANNELS)
    at = KERNEL * cs
    conv_b = small[:, at : at + cs].reshape(CHANNELS)
    at += cs
    dt_b = small[:, at : at + hs].reshape(HEADS)
    at += hs
    a_all = small[:, at : at + hs].reshape(HEADS)
    at += hs
    skip_all = small[:, at : at + hs].reshape(HEADS)
    at += hs
    gain_all = small[:, at : at + gs].reshape(DI)

    def mine(v, size):
        return lax.dynamic_slice_in_dim(v, rank * size, size, v.ndim - 1)

    cw = jnp.concatenate([mine(conv_w[:, :DI], wide), conv_w[:, DI:]], axis=1).astype(F32)
    cb = jnp.concatenate([mine(conv_b[:DI], wide), conv_b[DI:]])[None].astype(F32)
    cw = jnp.concatenate([cw, jnp.zeros((8 - KERNEL, chans), F32)], axis=0)
    cb = jnp.broadcast_to(cb, (8, chans))
    dtb = jnp.broadcast_to(jnp.pad(mine(dt_b, heads).astype(F32), (0, LANES - heads))[None], (8, LANES))
    rate = -jnp.exp(mine(a_all, heads).astype(F32))
    rowp = jnp.stack(
        [
            jnp.repeat(rate, HEAD_DIM),
            jnp.repeat(mine(skip_all, heads).astype(F32), HEAD_DIM),
            mine(gain_all, wide).astype(F32),
            jnp.pad(rate, (0, wide - heads)),
        ]
        + [jnp.zeros((wide,), F32)] * 4
    )
    colp = jnp.broadcast_to(jnp.pad(rate, (0, LANES - heads))[:, None], (LANES, LANES))
    head_of = jnp.arange(wide, dtype=jnp.int32) // HEAD_DIM
    expand = (jnp.arange(LANES, dtype=jnp.int32)[:, None] == head_of[None]).astype(BF16)
    seg = expand.T

    def forth(size):
        return pl.BlockSpec((chunk, size), lambda j: (j, 0))

    def back(size):
        return pl.BlockSpec((chunk, size), lambda j: (steps - 1 - j, 0))

    def whole(a):
        return pl.BlockSpec(a.shape, lambda j: (0,) * a.ndim, pipeline_mode=pl.Buffered(1))

    params = pltpu.CompilerParams(
        dimension_semantics=("arbitrary",), vmem_limit_bytes=56 * 1024 * 1024
    )
    grid = (steps,)

    act, slope, aux, y, gg, states, sums = pl.pallas_call(
        functools.partial(scan_kernel, heads=heads, wide=wide),
        grid=grid,
        in_specs=[
            forth(chans), forth(LANES), forth(wide), forth(wide),
            whole(cw), whole(cb), whole(dtb), whole(expand), whole(rowp), whole(colp),
        ],
        out_specs=[
            forth(chans), forth(chans), forth(LANES), forth(wide), forth(wide),
            pl.BlockSpec((1, STATE, wide), lambda j: (j, 0, 0)),
            pl.BlockSpec((8, chunk), lambda j: (0, j)),
        ],
        out_shape=[
            sds((tokens, chans), BF16),
            sds((tokens, chans), BF16),
            sds((tokens, LANES), F32),
            sds((tokens, wide), F32),
            sds((tokens, wide), BF16),
            sds((steps, STATE, wide), F32),
            sds((8, tokens), F32),
        ],
        scratch_shapes=[pltpu.VMEM((STATE, wide), F32), pltpu.VMEM((16, chans), F32)],
        compiler_params=params,
        cost_estimate=pl.CostEstimate(
            flops=2 * tokens * wide * 12 * chunk, bytes_accessed=tokens * wide * 16, transcendentals=tokens * chunk * heads
        ),
        name="scan",
    )(u, d_raw, z, d0, cw, cb, dtb, expand, rowp, colp)

    mask = (jnp.arange(tokens, dtype=jnp.int32) < lengths[0]).astype(F32)
    n_own = DI // owners
    piece = n_own // owners
    wog_shape = (owners, owners // ranks, piece, width) if ring else (wide, width)
    stat2, partial, wog = pl.pallas_call(
        blend_kernel,
        in_specs=[hbm, hbm, hbm, vmem, vmem],
        out_specs=[vmem, hbm, hbm],
        out_shape=[sds((tokens, LANES), F32), sds((3, local_len, width), BF16), sds(wog_shape, BF16)],
        scratch_shapes=[
            pltpu.VMEM((tokens, wide), BF16),
            pltpu.VMEM((wide, width), BF16),
            pltpu.VMEM((tokens, width), BF16),
        ]
        + [pltpu.VMEM((local_len, width), BF16)] * 4
        + [pltpu.VMEM((local_len // 2, width), BF16)] * 2
        + [pltpu.VMEM((ranks, 8, tokens), F32), pltpu.VMEM((2, 256, width), BF16)]
        + [dma(3), dma(2), dma(2), dma(3), dma(3), dma(3), dma(2)],
        compiler_params=pltpu.CompilerParams(
            collective_id=3, has_side_effects=True, vmem_limit_bytes=56 * 1024 * 1024
        ),
        cost_estimate=pl.CostEstimate(
            flops=4 * tokens * wide * width, bytes_accessed=4 * tokens * (width + wide), transcendentals=0
        ),
        name="blend",
    )(gg, w_o, og_all, sums, jnp.broadcast_to(mask[None], (8, tokens)))

    if ring:
        pieces = lax.psum_scatter(wog, "head", scatter_dimension=0, tiled=False)
    dy, dpg = pl.pallas_call(
        gate_kernel,
        grid=grid,
        in_specs=[forth(wide), forth(LANES), forth(wide), forth(wide), forth(wide), forth(LANES), whole(rowp)],
        out_specs=[forth(wide), forth(wide)],
        out_shape=[sds((tokens, wide), BF16), sds((tokens, wide), BF16)],
        compiler_params=params,
        cost_estimate=pl.CostEstimate(
            flops=20 * tokens * wide, bytes_accessed=tokens * wide * 14, transcendentals=tokens * wide
        ),
        name="gate_back",
    )(act, aux, z, d0, y, stat2, rowp)

    wig_gate = t_dot(h_all, dpg).astype(BF16)
    dy, wig_gate = lax.optimization_barrier((dy, wig_gate))
    own_gate = lax.psum_scatter(wig_gate, "head", scatter_dimension=0, tiled=True)

    rest = chans + LANES
    dp, sm, branch = pl.pallas_call(
        functools.partial(back_kernel, heads=heads, wide=wide),
        grid=grid,
        in_specs=[
            back(chans), back(LANES), back(wide), back(wide),
            pl.BlockSpec((1, STATE, wide), lambda j: (steps - 1 - j, 0, 0)),
            back(chans), back(chans), hbm,
            whole(expand), whole(seg), whole(rowp), whole(colp), whole(cw),
        ],
        out_specs=[back(rest), pl.BlockSpec((8, chans), lambda j: (0, 0)), hbm],
        out_shape=[sds((tokens, rest), BF16), sds((8, chans), F32), sds((local_len, width), F32)],
        scratch_shapes=[pltpu.VMEM((STATE, wide), F32), pltpu.VMEM((16, chans), F32)]
        + [pltpu.VMEM((local_len, width), BF16)] * 3
        + [pltpu.VMEM((local_len, width), F32)]
        + [dma(2)] * 3,
        compiler_params=pltpu.CompilerParams(
            dimension_semantics=("arbitrary",), collective_id=2, has_side_effects=True,
            vmem_limit_bytes=56 * 1024 * 1024,
        ),
        cost_estimate=pl.CostEstimate(
            flops=2 * tokens * wide * 12 * chunk, bytes_accessed=tokens * wide * 24, transcendentals=tokens * chunk * heads
        ),
        name="scan_back",
    )(act, aux, dy, y, states, slope, u, partial, expand, seg, rowp, colp, cw)

    skip_h = jnp.sum(sm[5, :wide].reshape(heads, HEAD_DIM), axis=1)
    tiny = jnp.concatenate([sm[:5].reshape(-1), sm[6, :heads], sm[7, :heads], skip_h])
    if ring:
        laid = jnp.pad(tiny, (0, shard * spare - tiny.shape[0])).reshape(shard, spare).astype(BF16)
        dn, gate_rows, rest_rows, w_out_grad = pl.pallas_call(
            grads_kernel,
            in_specs=[hbm] * 6 + [vmem],
            out_specs=[hbm] * 4,
            out_shape=[
                sds((local_len, width), F32),
                sds((ranks, shard, wide), BF16),
                sds((ranks, shard, rest), BF16),
                sds((owners, piece, width), BF16),
            ],
            scratch_shapes=[
                pltpu.VMEM((tokens, cols), BF16),
                pltpu.VMEM((width, cols), BF16),
                pltpu.VMEM((2, tokens, shard), BF16),
            ]
            + [pltpu.VMEM((local_len, width), BF16)] * 3
            + [pltpu.VMEM((local_len // 2, width), BF16)] * 2
            + [pltpu.VMEM((local_len, width), BF16)] * 2
            + [
                pltpu.VMEM((2, local_len, 256), F32),
                pltpu.VMEM((2, shard, rest), BF16),
                pltpu.VMEM((shard, rest), BF16),
                pltpu.VMEM((4, shard, rest), BF16),
                pltpu.VMEM((3, shard, rest), BF16),
                pltpu.VMEM((3, shard, rest), BF16),
                pltpu.VMEM((ranks, owners // ranks, piece, width), BF16),
            ]
            + [dma(6), dma(2)]
            + [dma(4)] * 12
            + [dma(owners)] * 2
            + [dma(4)] * 2
            + [dma(2)],
            compiler_params=pltpu.CompilerParams(
                collective_id=1, has_side_effects=True, vmem_limit_bytes=56 * 1024 * 1024
            ),
            cost_estimate=pl.CostEstimate(
                flops=4 * tokens * width * cols, bytes_accessed=8 * tokens * cols, transcendentals=0
            ),
            name="weight_grads",
        )(dpg, dp, w_t, h_all, own_gate, pieces, laid)
        w_out_grad = w_out_grad.reshape(n_own, width).astype(F32)
        tiny_all = rest_rows[:, :, rest - spare :].reshape(ranks, shard * spare)[:, : tiny.shape[0]].astype(F32)
    else:
        full = lax.all_gather(lax.psum(wog, "head"), "seq", axis=0, tiled=True)
        w_out_grad = lax.dynamic_slice_in_dim(full, owner * n_own, n_own, 0).astype(F32)
        wig = t_dot(h_all, dp).astype(BF16)
        dn = (dot_t(dp, w_t[:, wide:]) + dot_t(dpg, w_t[:, :wide])).astype(BF16)
        dn = lax.psum_scatter(dn, "seq", scatter_dimension=0, tiled=True).astype(F32)
        gate_rows = lax.all_gather(own_gate, "seq")
        rest_rows = lax.all_gather(lax.psum_scatter(wig, "head", scatter_dimension=0, tiled=True), "seq")
        tiny_all = lax.all_gather(lax.psum(tiny, "head"), "seq")
    gate_gain_grad = jnp.sum(w_out.astype(F32) * w_out_grad, axis=1) / gate_gain.astype(F32)

    strip = min(32, shard)

    def rows_spec(size):
        return pl.BlockSpec((strip, size), lambda j: (j, 0))

    def ranks_spec(size):
        return pl.BlockSpec((ranks, strip, size), lambda j: (0, j, 0))

    w_in_grad, w_dt_grad, norm_gain_grad = pl.pallas_call(
        functools.partial(finish_kernel, heads=heads, wide=wide),
        grid=(shard // strip,),
        in_specs=[ranks_spec(wide), ranks_spec(rest), rows_spec(PROJ), rows_spec(HEADS), rows_spec(1)],
        out_specs=[rows_spec(PROJ), rows_spec(HEADS), rows_spec(1)],
        out_shape=[sds((shard, PROJ), F32), sds((shard, HEADS), F32), sds((shard, 1), F32)],
        compiler_params=params,
        cost_estimate=pl.CostEstimate(flops=6 * shard * PROJ, bytes_accessed=8 * shard * PROJ, transcendentals=0),
        name="w_in_finish",
    )(gate_rows, rest_rows, w_in, w_dt, gain_rows)
    norm_gain_grad = norm_gain_grad.reshape(shard)

    h32 = hidden[0].astype(F32)
    own_r1m = lax.dynamic_slice_in_dim(stat2[:, 0:1], rank * local_len, local_len, 0)
    block_out = (h32 + own_r1m * branch).astype(BF16)[None]
    r0 = lax.rsqrt(jnp.mean(h32 * h32, axis=1, keepdims=True) + EPS)
    mixed = jnp.sum(dn * h32, axis=1, keepdims=True) / width
    hidden_grad = (out_grad[0].astype(F32) + dn - h32 * (r0 * r0 * mixed))[None]

    n_conv = 5 * chans
    conv_all = tiny_all[:, :n_conv].reshape(ranks, 5, chans)
    conv_all = jnp.concatenate(
        [conv_all[:, :, :wide].swapaxes(0, 1).reshape(5, DI), jnp.sum(conv_all[:, :, wide:], axis=0)], axis=1
    )
    vec = tiny_all[:, n_conv:].reshape(ranks, 3, heads).swapaxes(0, 1).reshape(3, HEADS)
    conv_own = lax.dynamic_slice_in_dim(conv_all, owner * cs, cs, 1)
    vec_own = lax.dynamic_slice_in_dim(vec, owner * hs, hs, 1)

    return (
        block_out,
        hidden_grad,
        norm_gain_grad,
        w_in_grad,
        w_dt_grad,
        conv_own[:KERNEL],
        conv_own[KERNEL],
        vec_own[0],
        vec_own[1],
        vec_own[2],
        gate_gain_grad,
        w_out_grad,
    )


def solution(mesh):
    rows = P("head", "seq", None)
    return jax.shard_map(
        local,
        mesh=mesh,
        in_specs=(
            rows, P("head"), rows, P("head"), P("head", None), P("head", None), P(None, "head"),
            P("head"), P("head"), P("head"), P("head"), P("head"), P("head", None),
        ),
        out_specs=(
            rows, rows, P("head"), P("head", None), P("head", None), P(None, "head"),
            P("head"), P("head"), P("head"), P("head"), P("head"), P("head", None),
        ),
        check_vma=False,
    )
```

```python
import functools

import jax
import jax.numpy as jnp
from jax import lax
from jax.experimental import pallas as pl
from jax.experimental.pallas import tpu as pltpu
from jax.sharding import PartitionSpec as P

HEADS = 64
HEAD_DIM = 64
STATE = 128
KERNEL = 4
CHUNK = 256
DI = 4096
CHANNELS = 4352
PROJ = DI + CHANNELS
EPS = 1e-05
LANES = 128
EVERY = ("seq", "head")
F32 = jnp.float32
BF16 = jnp.bfloat16


def dot(a, b):
    return jnp.dot(a, b, preferred_element_type=F32)


def dot_t(a, b):
    return lax.dot_general(a, b, (((1,), (1,)), ((), ())), preferred_element_type=F32)


def t_dot(a, b):
    return lax.dot_general(a, b, (((0,), (0,)), ((), ())), preferred_element_type=F32)


def sigmoid(v):
    return 0.5 * jnp.tanh(0.5 * v) + 0.5


def remote(src, dst, send, recv, target):
    return pltpu.make_async_remote_copy(
        src_ref=src, dst_ref=dst, send_sem=send, recv_sem=recv, device_id=target, device_id_type=pl.DeviceIdType.MESH
    )


def greet(peers, extra=()):
    barrier = pltpu.get_barrier_semaphore()
    count = len(peers)

    def hello(peer):
        pl.semaphore_signal(barrier, inc=1, device_id=peer, device_id_type=pl.DeviceIdType.MESH)

    for peer in peers:
        hello(peer)
    for there, peer in extra:
        pl.when(there)(functools.partial(hello, peer))
        count = count + jnp.where(there, 1, 0)
    pl.semaphore_wait(barrier, count)


def gather_kernel(
    hid_ref, og_ref, w_ref, wo_in_ref, gain_ref, dtw_ref,
    hall_ref, ogall_ref, wt_ref, wo_ref, z_ref, u_ref, d_ref, d0_ref,
    hv, ov, wv, wov, stage, zv, uv, dv, d0v,
    h_send, h_recv, o_send, o_recv, z_up, z_dn, z_recv, s_send, s_recv,
    c_up, c_dn, c_recv, t_send, t_recv, local_sem, out_sem, *, ring, wide,
):
    s = lax.axis_index("seq")
    q = hid_ref.shape[0]
    half = q // 2
    x_peer = s + 1 - 2 * lax.rem(s, 2)
    y_peer = lax.rem(s + 2, 4)
    far = 3 - s
    to_x, to_y = {"seq": x_peer}, {"seq": y_peer}
    chans = uv.shape[1]
    n_main = stage.shape[1]
    n = stage.shape[0]
    peers = [to_x, to_y]
    extra = []

    def block(ref, at, start, size):
        return ref.at[pl.ds(pl.multiple_of(at * q + start, 16), size), :]

    if ring:
        h = lax.axis_index("head")
        core = lax.rem(h, 2)
        r = h // 2
        last = lax.axis_size("head") // 2 - 1
        to_sib, to_up, to_down = {"head": h + 1 - 2 * core}, {"head": lax.rem(h + 2, 2 * last + 2)}, {"head": lax.rem(h + 2 * last, 2 * last + 2)}
        above, below = r < last, r > 0
        peers.append(to_sib)
        extra = [(above, to_up), (below, to_down)]
        first = pl.multiple_of(s * wide, LANES)
        second = pl.multiple_of(DI + s * wide, LANES)
        loads = [
            pltpu.make_async_copy(w_ref.at[:, pl.ds(first, wide)], stage.at[:, :wide], local_sem.at[0]),
            pltpu.make_async_copy(w_ref.at[:, pl.ds(second, wide)], stage.at[:, wide : 2 * wide], local_sem.at[1]),
            pltpu.make_async_copy(w_ref.at[:, 2 * DI :], stage.at[:, 2 * wide :], local_sem.at[2]),
        ]
        is_root = r == s
        n_o = wov.shape[0] // 2
        load_o = pltpu.make_async_copy(
            wo_in_ref, wov.at[pl.ds(pl.multiple_of(core * n_o, 16), n_o), :], local_sem.at[5]
        )
        pl.when(is_root)(load_o.start)
    else:
        loads = [
            pltpu.make_async_copy(w_ref, wv, local_sem.at[0]),
            pltpu.make_async_copy(wo_in_ref, wov, local_sem.at[5]),
        ]
    for copy in loads:
        copy.start()
    own_h = pltpu.make_async_copy(hid_ref, block(hv, s, 0, q), local_sem.at[3])
    own_o = pltpu.make_async_copy(og_ref, block(ov, s, 0, q), local_sem.at[4])
    own_h.start()
    own_o.start()
    greet(peers, extra)

    sent = []

    def send(src, dst, sems, i, target):
        copy = remote(src, dst, sems[0].at[i], sems[1].at[i], target)
        copy.start()
        sent.append(copy)
        return copy

    def open_exchange(src, buf, sems):
        return (
            send(src, block(buf, s, 0, q), sems, 0, to_x),
            send(src, block(buf, s, 0, q), sems, 1, to_y),
        )

    def relay(buf, sems, heads_in):
        heads_in[0].wait_recv()
        a = block(buf, x_peer, 0, half)
        first = send(a, a, sems, 2, to_y)
        heads_in[1].wait_recv()
        b = block(buf, y_peer, half, half)
        return first, send(b, b, sems, 3, to_x)

    h_sems, o_sems = (h_send, h_recv), (o_send, o_recv)
    h_open = open_exchange(hid_ref, hv, h_sems)

    closing = []
    if ring:
        def w_block(at):
            return wv.at[pl.ds(pl.multiple_of((2 * at + core) * n, 16), n), :]

        def w_copy(at, sems, target):
            return remote(w_block(at), w_block(at), sems.at[at], z_recv.at[at], target)

        def w_swap(at):
            return remote(w_block(at), w_block(at), s_send.at[at], s_recv.at[at], to_sib)

        def launch(there, make):
            @pl.when(there)
            def _():
                make().start()

            def finish():
                @pl.when(there)
                def _():
                    make().wait_send()

            closing.append(finish)

        always = r >= 0

        def w_step(k):
            lower, upper = r - k, r + k
            has_lower, has_upper = lower >= 0, upper <= last

            @pl.when(has_lower)
            def _():
                w_copy(lower, z_up, to_up).wait_recv()

            launch(has_lower & above, lambda: w_copy(lower, z_up, to_up))
            launch(has_lower, lambda: w_swap(lower))

            @pl.when(has_upper)
            def _():
                w_copy(upper, z_dn, to_down).wait_recv()

            launch(has_upper & below, lambda: w_copy(upper, z_dn, to_down))
            launch(has_upper, lambda: w_swap(upper))

        chunks = c_recv.shape[0]
        n_c = n_o // chunks
        dist = jnp.where(r > s, r - s, s - r)

        def o_block(i):
            return wov.at[pl.ds(pl.multiple_of(core * n_o + i * n_c, 16), n_c), :]

        def o_copy(i, sems, target):
            return remote(o_block(i), o_block(i), sems.at[i], c_recv.at[i], target)

        def o_swap(i):
            return remote(o_block(i), o_block(i), t_send.at[i], t_recv.at[i], to_sib)

        def o_root():
            @pl.when(is_root)
            def _():
                load_o.wait()

            for i in range(chunks):
                launch(is_root & above, lambda i=i: o_copy(i, c_up, to_up))
                launch(is_root & below, lambda i=i: o_copy(i, c_dn, to_down))
                launch(is_root, lambda i=i: o_swap(i))

        def o_tick(t):
            i = t - dist
            live = (dist >= 1) & (i >= 0) & (i < chunks)

            @pl.when(live)
            def _():
                o_copy(i, c_up, to_up).wait_recv()

            pl.when(live & (r > s) & above)(lambda: o_copy(i, c_up, to_up).start())
            pl.when(live & (r < s) & below)(lambda: o_copy(i, c_dn, to_down).start())
            pl.when(live)(lambda: o_swap(i).start())

        def o_finish():
            for i in range(chunks):
                pl.when((r > s) & above)(lambda: o_copy(i, c_up, to_up).wait_send())
                pl.when((r < s) & below)(lambda: o_copy(i, c_dn, to_down).wait_send())
                pl.when(dist >= 1)(lambda: o_swap(i).wait_send())

        closing.append(o_finish)
        for copy in loads:
            copy.wait()
        own = pl.ds(pl.multiple_of(h * n, 16), n)
        wv[own, :n_main] = (stage[...].astype(F32) * gain_ref[...]).astype(BF16)
        wv[own, n_main:] = dtw_ref[...]
        launch(above, lambda: w_copy(r, z_up, to_up))
        launch(below, lambda: w_copy(r, z_dn, to_down))
        launch(always, lambda: w_swap(r))
        w_step(1)
    else:
        for copy in loads:
            copy.wait()

    h_far = relay(hv, h_sems, h_open)
    if ring:
        w_step(2)
        o_root()
    for copy in h_far:
        copy.wait_recv()
    o_open = open_exchange(og_ref, ov, o_sems)
    if ring:
        o_tick(1)
        w_step(3)
        for at in range(4):
            w_swap(at).wait_recv()
    own_h.wait()
    own_o.wait()

    rows = min(CHUNK, q)

    def cut(at_block):
        return pl.ds(pl.multiple_of(at_block * q, 16), q)

    def project_outs(at_block, i):
        at = cut(at_block)
        pairs = ((hv, hall_ref), (zv, z_ref), (uv, u_ref), (dv, d_ref))
        return [
            pltpu.make_async_copy(src.at[at, :], dst.at[at, :], out_sem.at[4 * i + k])
            for k, (src, dst) in enumerate(pairs)
        ]

    def pull_outs(at_block, i):
        at = cut(at_block)
        pairs = ((ov, ogall_ref), (d0v, d0_ref))
        return [
            pltpu.make_async_copy(src.at[at, :], dst.at[at, :], out_sem.at[16 + 2 * i + k])
            for k, (src, dst) in enumerate(pairs)
        ]

    def nth(i):
        return jnp.where(i == 0, s, jnp.where(i == 1, x_peer, jnp.where(i == 2, y_peer, far)))

    w_out = pltpu.make_async_copy(wv, wt_ref, out_sem.at[24])
    o_out = pltpu.make_async_copy(wov, wo_ref, out_sem.at[25])
    w_out.start()

    def project(at_block):
        @pl.loop(0, q // rows)
        def _(j):
            at = pl.ds(pl.multiple_of(at_block * q + j * rows, 16), rows)
            hb = hv[at, :]
            h32 = hb.astype(F32)
            r0 = lax.rsqrt(jnp.mean(h32 * h32, axis=1, keepdims=True) + EPS)
            zv[at, :] = (dot(hb, wv[:, :wide]) * r0).astype(BF16)
            uv[at, :] = (dot(hb, wv[:, wide : wide + chans]) * r0).astype(BF16)
            raw = dot(hb, wv[:, wide + chans :]) * r0
            lane = lax.broadcasted_iota(jnp.int32, raw.shape, 1)
            dv[at, :] = jnp.where(lane == LANES - 1, r0, raw)

    def pull(at_block):
        at = cut(at_block)

        @pl.loop(0, wide // 256)
        def _(j):
            to = pl.ds(pl.multiple_of(j * 256, 256), 256)
            d0v[at, to] = dot_t(ov[at, :], wov[to, :]).astype(BF16)

    @pl.loop(0, 4)
    def _(i):
        at_block = nth(i)
        project(at_block)
        for copy in project_outs(at_block, i):
            copy.start()
        if ring:
            o_tick(2 + i)

    if ring:
        o_tick(6)
    o_far = relay(ov, o_sems, o_open)
    if ring:
        for t in range(7, chunks + 3):
            o_tick(t)
        for i in range(chunks):
            o_swap(i).wait_recv()
    o_out.start()

    @pl.loop(0, 4)
    def _(i):
        at_block = nth(i)

        @pl.when(i == 3)
        def _():
            for copy in o_far:
                copy.wait_recv()

        pull(at_block)
        for copy in pull_outs(at_block, i):
            copy.start()

    for i, at_block in enumerate((s, x_peer, y_peer, far)):
        for copy in project_outs(at_block, i) + pull_outs(at_block, i):
            copy.wait()
    w_out.wait()
    o_out.wait()
    for copy in sent:
        copy.wait_send()
    for finish in closing:
        finish()


def decays(aux, heads, expand, rate_e, rate_row, rate_col):
    rows = aux.shape[0]
    lane = lax.broadcasted_iota(jnp.int32, aux.shape, 1)
    dt = jnp.where(lane < heads, aux, 0.0).astype(BF16)
    r = lax.broadcasted_iota(jnp.int32, (rows, rows), 0)
    c = lax.broadcasted_iota(jnp.int32, (rows, rows), 1)
    causal = c <= r
    lower = jnp.where(causal, 1.0, 0.0).astype(BF16)
    dt_e = dot(dt, expand)
    cum_e = dot(lower, dt_e.astype(BF16)) * rate_e
    cum_c = dot(lower, dt) * rate_row
    cum_t = lax.dot_general(dt, lower, (((0,), (1,)), ((), ())), preferred_element_type=F32) * rate_col
    return causal, dt_e, cum_e, cum_c, cum_t


def shift_matrix(rows, by):
    r = lax.broadcasted_iota(jnp.int32, (rows, rows), 0)
    c = lax.broadcasted_iota(jnp.int32, (rows, rows), 1)
    return jnp.where(c == r + by, 1.0, 0.0).astype(BF16)


def lower_parts(cum_c, cum_t, h, causal):
    mid = causal.shape[0] // 2
    near = causal[:mid, :mid]
    col, row = cum_c[:, h : h + 1], cum_t[h : h + 1, :]
    top = jnp.exp(jnp.where(near, col[:mid] - row[:, :mid], -1e30))
    low = jnp.exp(col[mid:] - row[:, :mid])
    right = jnp.exp(jnp.where(near, col[mid:] - row[:, mid:], -1e30))
    return top, low, right


def scan_kernel(
    u_ref, d_ref, z_ref, d0_ref, cw_ref, cb_ref, dtb_ref, exp_ref, rowp_ref, colp_ref,
    act_ref, slope_ref, aux_ref, y_ref, gg_ref, st_ref, sum_ref, state, ext, *, heads, wide,
):
    step = pl.program_id(0)
    rows = u_ref.shape[0]
    chans = u_ref.shape[1]

    @pl.when(step == 0)
    def _():
        state[...] = jnp.zeros_like(state)
        ext[...] = jnp.zeros_like(ext)

    u = u_ref[...]
    u32 = u.astype(F32)
    pre = cb_ref[0:1, :] + cw_ref[KERNEL - 1 : KERNEL, :] * u32
    before = jnp.zeros((8, chans), F32)
    for j in range(1, KERNEL):
        tap = cw_ref[KERNEL - 1 - j : KERNEL - j, :]
        pre = pre + tap * dot(shift_matrix(rows, -j), u)
        before = before + tap * ext[8 - j : 16 - j, :]
    pre = jnp.concatenate([pre[:8] + before, pre[8:]], axis=0)
    ext[0:8, :] = u32[rows - 8 :, :]
    sig = sigmoid(pre)
    act = (pre * sig).astype(BF16)
    act_ref[...] = act
    slope_ref[...] = (sig * (1.0 + pre * (1.0 - sig))).astype(BF16)
    raw = d_ref[...]
    v = raw + dtb_ref[0:1, :]
    soft = jnp.maximum(v, 0.0) + jnp.log1p(jnp.exp(-jnp.abs(v)))
    soft = soft.astype(BF16).astype(F32)
    lane = lax.broadcasted_iota(jnp.int32, v.shape, 1)
    aux = jnp.where(lane < heads, soft, 0.0)
    sig_v = pltpu.roll(sigmoid(v), heads, 1)
    aux = jnp.where((lane >= heads) & (lane < 2 * heads), sig_v, aux)
    aux = jnp.where(lane == LANES - 1, raw, aux)
    aux_ref[...] = aux

    x = act[:, :wide]
    x32 = x.astype(F32)
    b = act[:, wide : wide + STATE]
    c = act[:, wide + STATE :]
    causal, dt_e, cum_e, cum_c, cum_t = decays(
        aux, heads, exp_ref[...], rowp_ref[0:1, :], rowp_ref[3:4, :LANES], colp_ref[:, 0:1]
    )
    xdt = x32 * dt_e
    xdt16 = xdt.astype(BF16)
    scores = dot_t(c, b)
    st = state[...]
    st_ref[0] = st
    mid = rows // 2
    half = lax.broadcasted_iota(jnp.int32, (rows, LANES), 1) < HEAD_DIM
    parts = []
    for pair in range(heads // 2):
        x2 = xdt16[:, LANES * pair : LANES * (pair + 1)]
        got = []
        for h in (2 * pair, 2 * pair + 1):
            top, low, right = lower_parts(cum_c, cum_t, h, causal)
            m_top = (scores[:mid, :mid] * top).astype(BF16)
            m_low = (scores[mid:, :mid] * low).astype(BF16)
            m_right = (scores[mid:, mid:] * right).astype(BF16)
            y_low = dot(jnp.concatenate([m_low, m_right], axis=1), x2)
            got.append(jnp.concatenate([dot(m_top, x2[:mid]), y_low], axis=0))
        parts.append(jnp.where(half, got[0], got[1]))
    y = jnp.concatenate(parts, axis=1) + dot(c, st.astype(BF16)) * jnp.exp(cum_e)
    last = cum_e[rows - 1 : rows, :]
    tail = jnp.exp(last - cum_e)
    state[...] = jnp.exp(last) * st + t_dot(b, (xdt * tail).astype(BF16))
    y16 = y.astype(BF16)
    y_ref[...] = y16
    ssd = (y16.astype(F32) + rowp_ref[1:2, :] * x32).astype(BF16).astype(F32)
    z = z_ref[...].astype(F32)
    g = ssd * (z * sigmoid(z))
    gg = g * rowp_ref[2:3, :]
    gg_ref[...] = gg.astype(BF16)
    ones = jnp.ones((8, wide), BF16)
    ssq = dot_t(ones, (g * g).astype(BF16))
    cross = dot_t(ones, (gg * d0_ref[...].astype(F32)).astype(BF16))
    sub = lax.broadcasted_iota(jnp.int32, ssq.shape, 0)
    sum_ref[...] = jnp.where(sub == 0, ssq, cross)


def seg_dot(v, seg):
    hi = v.astype(BF16)
    rest = v - hi.astype(F32)
    mid = rest.astype(BF16)
    low = (rest - mid.astype(F32)).astype(BF16)
    return dot(hi, seg) + dot(mid, seg) + dot(low, seg)


def line_sum(own, z_u, z_d, sems, r, last, to_up, to_down, join, closing):
    zu_send, zu_recv, zd_send, zd_recv = sems

    def up_copy(t):
        return remote(own.at[t], z_u.at[t - 1], zu_send.at[t], zu_recv.at[t], to_up)

    def down_copy(t):
        return remote(own.at[t], z_d.at[t], zd_send.at[t], zd_recv.at[t], to_down)

    def up_add(t):
        up_copy(t).wait_recv()
        join(t, z_u.at[t - 1])

    def down_add(t):
        down_copy(t).wait_recv()
        join(t, z_d.at[t])

    def sent_later(t, there, make):
        closing.append(lambda: pl.when(there)(lambda: make(t).wait_send()))

    def pass_on(t, there, add, make):
        @pl.when(there)
        def _():
            add(t)
            make(t).start()

        sent_later(t, there, make)

    def follow(t, there, make, before):
        @pl.when(there)
        def _():
            make(before).wait_send()
            make(t).start()

    def start():
        pl.when(r == 0)(lambda: up_copy(last).start())
        pl.when(r == last)(lambda: down_copy(0).start())

    def second():
        follow(2, r == 0, up_copy, last)
        follow(1, r == last, down_copy, 0)
        pass_on(last, r == 1, up_add, up_copy)
        pass_on(0, r == 2, down_add, down_copy)

    def across():
        pass_on(last, r == 2, up_add, up_copy)
        pass_on(0, r == 1, down_add, down_copy)

    def third():
        follow(1, r == 0, up_copy, 2)
        follow(2, r == last, down_copy, 1)
        pass_on(2, r == 1, up_add, up_copy)
        pass_on(1, r == 2, down_add, down_copy)
        sent_later(1, r == 0, up_copy)
        sent_later(2, r == last, down_copy)

    def final():
        pl.when(r > 0)(lambda: up_add(r))
        pl.when(r < last)(lambda: down_add(r))

    return start, second, across, third, final


def mid_kernel(
    gg_ref, wo_ref, og_ref, h_ref, act_ref, aux_ref, z_ref, d0_ref, y_ref, sums_ref, mask_ref, rowp_ref,
    br_ref, wog_ref, dy_ref, dpg_ref, gate_ref,
    stat_v, ggv, wov, ogv, far_p, y_p, x_p, own_p, far_a, far_b, y_f, x_f, sv,
    ow, other, other_in, z_u, z_d, part_s, xin, zin, din, yin, ain, dyo, hb, rows_s,
    load_sem, d_send, d_recv, s_send, s_recv, c_send, c_recv, zu_send, zu_recv, zd_send, zd_recv,
    in_sem, dy_sem, hb_sem, rows_sem, out_sem, *, ring,
):
    s = lax.axis_index("seq")
    tokens, wide = ggv.shape
    width = wov.shape[1]
    q = far_p.shape[0]
    half = q // 2
    rows = min(CHUNK, q)
    tile = 256
    x_peer = s + 1 - 2 * lax.rem(s, 2)
    y_peer = lax.rem(s + 2, 4)
    far = 3 - s
    to_x, to_y, to_far = {"seq": x_peer}, {"seq": y_peer}, {"seq": far}
    load_gg = pltpu.make_async_copy(gg_ref, ggv, load_sem.at[0])
    load_wo = pltpu.make_async_copy(wo_ref, wov, load_sem.at[1])
    cut = ogv.shape[1]

    def load_og(d):
        return pltpu.make_async_copy(og_ref.at[:, d * cut : (d + 1) * cut], ogv, load_sem.at[2])

    def load_chunk(i):
        at = pl.ds(pl.multiple_of(i * rows, 16), rows)
        slot = lax.rem(i, 2)
        pairs = ((act_ref.at[at, :wide], xin), (z_ref.at[at, :], zin), (d0_ref.at[at, :], din), (y_ref.at[at, :], yin), (aux_ref.at[at, :], ain))
        return [pltpu.make_async_copy(src, dst.at[slot], in_sem.at[slot, k]) for k, (src, dst) in enumerate(pairs)]

    def load_h(i):
        slot = lax.rem(i, 2)
        return pltpu.make_async_copy(h_ref.at[:, pl.ds(pl.multiple_of(i * tile, tile), tile)], hb.at[slot], hb_sem.at[slot])

    load_gg.start()
    load_wo.start()
    load_og(0).start()
    peers = [to_x, to_y, to_far]
    extra = []
    closing = []
    if ring:
        h = lax.axis_index("head")
        owners = lax.axis_size("head")
        last = owners // 2 - 1
        core = lax.rem(h, 2)
        r = h // 2
        to_sib = {"head": h + 1 - 2 * core}
        to_up, to_down = {"head": lax.rem(h + 2, owners)}, {"head": lax.rem(h + owners - 2, owners)}
        peers.append(to_sib)
        extra = [(r < last, to_up), (r > 0, to_down)]

        def join(t, more):
            ow[t] = (ow[t].astype(F32) + more[...].astype(F32)).astype(BF16)

        start, second, across, third, final = line_sum(
            ow, z_u, z_d, (zu_send, zu_recv, zd_send, zd_recv), r, last, to_up, to_down, join, closing
        )
    sv[s] = sums_ref[...]
    greet(peers, extra)
    sums = [
        remote(sums_ref, sv.at[s], s_send.at[i], s_recv.at[i], peer) for i, peer in enumerate((to_x, to_y, to_far))
    ]
    for copy in sums:
        copy.start()
    for i in (0, 1):
        for copy in load_chunk(i):
            copy.start()
    load_h(0).start()
    load_h(1).start()
    load_gg.wait()
    for copy in sums:
        copy.wait_recv()
    total = (sv[0] + sv[1]) + (sv[2] + sv[3])
    r1 = lax.rsqrt(total[0:1] / DI + EPS)
    r1m = r1 * mask_ref[0:1]
    coef = r1m * r1 * r1 * total[1:2] / DI
    sub = lax.broadcasted_iota(jnp.int32, (LANES, tokens), 0)
    stat_v[...] = jnp.where(sub == 0, r1m, jnp.where(sub == 1, coef, 0.0)).T

    @pl.loop(0, tokens // rows)
    def _(j):
        at = pl.ds(pl.multiple_of(j * rows, 16), rows)
        ggv[at, :] = (ggv[at, :].astype(F32) * stat_v[at, 0:1]).astype(BF16)

    load_wo.wait()

    def part(block, out):
        @pl.loop(0, q // rows)
        def _(j):
            at = pl.ds(pl.multiple_of(block * q + j * rows, 16), rows)
            to = pl.ds(pl.multiple_of(j * rows, 16), rows)
            out[to, :] = dot(ggv[at, :], wov[...]).astype(BF16)

    def d_copy(src, dst, i, target):
        copy = remote(src, dst, d_send.at[i], d_recv.at[i], target)
        copy.start()
        return copy

    part(far, far_p)
    d0 = d_copy(far_p.at[:half], far_a, 0, to_x)
    d1 = d_copy(far_p.at[half:], far_b, 1, to_y)
    part(y_peer, y_p)
    d2 = d_copy(y_p.at[half:], y_f.at[half:], 2, to_y)
    part(x_peer, x_p)
    d3 = d_copy(x_p.at[:half], x_f.at[:half], 3, to_x)
    part(s, own_p)

    def w_rows(d):
        to = slice(d * cut, (d + 1) * cut)

        @pl.loop(0, wide // tile)
        def _(m):
            at = pl.ds(pl.multiple_of(m * tile, tile), tile)
            got = t_dot(ggv[:, at], ogv[...]).astype(BF16)
            if ring:
                piece = ow.shape[2]
                chips = tile // (2 * piece)
                groups = wide // 2 // tile
                part_s[...] = got.reshape(part_s.shape)
                first = pl.ds(lax.rem(m, groups) * chips, chips)
                ow[first, m // groups, :, to] = part_s[:, core]
                other[first, m // groups, :, to] = part_s[:, 1 - core]
            else:
                rows_s[0, :, : got.shape[1]] = got
                copy = pltpu.make_async_copy(rows_s.at[0], wog_ref.at[at, to], out_sem.at[0])
                copy.start()
                copy.wait()

    load_og(0).wait()
    w_rows(0)
    load_og(1).start()
    load_og(1).wait()
    w_rows(1)
    if ring:
        swap = remote(other, other_in, c_send.at[0], c_recv.at[0], to_sib)
        swap.start()
        swap.wait_recv()

        @pl.loop(0, 4)
        def _(t):
            join(t, other_in.at[t])

        start()
    d0.wait_recv()
    y_p[:half, :] = (y_p[:half, :].astype(F32) + far_a[...].astype(F32)).astype(BF16)
    d4 = d_copy(y_p.at[:half], y_f.at[:half], 4, to_y)
    d1.wait_recv()
    x_p[half:, :] = (x_p[half:, :].astype(F32) + far_b[...].astype(F32)).astype(BF16)
    d5 = d_copy(x_p.at[half:], x_f.at[half:], 5, to_x)

    def dy_out(i):
        at = pl.ds(pl.multiple_of(i * rows, 16), rows)
        return pltpu.make_async_copy(dyo.at[lax.rem(i, 2)], dy_ref.at[at, :], dy_sem.at[lax.rem(i, 2)])

    chunks = tokens // rows

    def gate_chunk(i):
        slot = lax.rem(i, 2)
        at = pl.ds(pl.multiple_of(i * rows, 16), rows)
        for copy in load_chunk(i):
            copy.wait()
        r0 = ain[slot, :, LANES - 1 : LANES]
        ssd = (yin[slot].astype(F32) + rowp_ref[1:2, :] * xin[slot].astype(F32)).astype(BF16).astype(F32)
        z = zin[slot].astype(F32)
        sig = sigmoid(z)
        sz = z * sig
        d_gated = (stat_v[at, 0:1] * rowp_ref[2:3, :]) * din[slot].astype(F32) - (ssd * sz) * stat_v[at, 1:2]

        @pl.when(i >= 2)
        def _():
            dy_out(i - 2).wait()

        dyo[slot] = (d_gated * sz).astype(BF16)
        dy_out(i).start()
        ggv[at, :] = (r0 * (d_gated * ssd * (sig * (1.0 + z * (1.0 - sig))))).astype(BF16)

        @pl.when(i + 2 < chunks)
        def _():
            for copy in load_chunk(i + 2):
                copy.start()

    pl.loop(0, chunks - 1)(gate_chunk)
    if ring:
        second()
    pl.loop(chunks - 1, chunks)(gate_chunk)
    dpg_out = pltpu.make_async_copy(ggv, dpg_ref, out_sem.at[1])
    dpg_out.start()

    def rows_out(i):
        slot = lax.rem(i, 2)
        at = pl.ds(pl.multiple_of(i * tile, tile), tile)
        return pltpu.make_async_copy(rows_s.at[slot], gate_ref.at[at, :], rows_sem.at[slot])

    blocks = width // tile

    def gate_rows(i):
        slot = lax.rem(i, 2)
        load_h(i).wait()
        got = t_dot(hb[slot], ggv[...]).astype(BF16)

        @pl.when(i >= 2)
        def _():
            rows_out(i - 2).wait()

        rows_s[slot] = got
        rows_out(i).start()

        @pl.when(i + 2 < blocks)
        def _():
            load_h(i + 2).start()

    pl.loop(0, blocks // 2)(gate_rows)
    if ring:
        across()
        third()
    pl.loop(blocks // 2, blocks)(gate_rows)
    if ring:
        final()
        wog_out = pltpu.make_async_copy(ow.at[r], wog_ref, out_sem.at[0])
        wog_out.start()
    for copy in (d2, d3, d4, d5):
        copy.wait_recv()
    own_p[...] = (own_p[...].astype(F32) + y_f[...].astype(F32) + x_f[...].astype(F32)).astype(BF16)
    br_out = pltpu.make_async_copy(own_p, br_ref, out_sem.at[2])
    br_out.start()
    for i in (chunks - 2, chunks - 1):
        dy_out(i).wait()
    for i in (blocks - 2, blocks - 1):
        rows_out(i).wait()
    dpg_out.wait()
    br_out.wait()
    for copy in sums + [d0, d1, d2, d3, d4, d5]:
        copy.wait_send()
    if ring:
        wog_out.wait()
        swap.wait_send()
    for finish in closing:
        finish()


def back_kernel(
    act_ref, aux_ref, dy_ref, y_ref, st_ref, slope_ref, u_ref, piece_ref,
    exp_ref, seg_ref, rowp_ref, colp_ref, cw_ref,
    dp_ref, sm_ref, all_ref, adj, ext, b_send, b_recv, b_load, *, heads, wide, ring,
):
    step = pl.program_id(0)
    steps = pl.num_programs(0)
    rows = act_ref.shape[0]
    chans = u_ref.shape[1]

    if ring:
        s = lax.axis_index("seq")
        x_peer = s + 1 - 2 * lax.rem(s, 2)
        y_peer = lax.rem(s + 2, 4)
        to_x, to_y = {"seq": x_peer}, {"seq": y_peer}
        from_x, from_y = all_ref.at[x_peer, 0], all_ref.at[y_peer, 1]
        moves = [
            remote(piece_ref, all_ref.at[s], b_send.at[0], b_recv.at[0], to_x),
            remote(piece_ref, all_ref.at[s], b_send.at[1], b_recv.at[1], to_y),
            remote(from_x, from_x, b_send.at[2], b_recv.at[2], to_y),
            remote(from_y, from_y, b_send.at[3], b_recv.at[3], to_x),
        ]
        own_piece = pltpu.make_async_copy(piece_ref, all_ref.at[s], b_load.at[0])

        @pl.when(step == 0)
        def _():
            greet([to_x, to_y])
            moves[0].start()
            moves[1].start()
            own_piece.start()

        @pl.when(step == 3)
        def _():
            moves[0].wait_recv()
            moves[2].start()
            moves[1].wait_recv()
            moves[3].start()

    @pl.when(step == 0)
    def _():
        sm_ref[...] = jnp.zeros_like(sm_ref)
        adj[...] = jnp.zeros_like(adj)
        ext[...] = jnp.zeros_like(ext)

    x = act_ref[:, :wide]
    x32 = x.astype(F32)
    b = act_ref[:, wide : wide + STATE]
    c = act_ref[:, wide + STATE :]
    aux = aux_ref[...]
    r0 = aux[:, LANES - 1 : LANES]
    skip_e = rowp_ref[1:2, :]
    y = y_ref[...].astype(F32)
    dy16 = dy_ref[...]
    dy = dy16.astype(F32)

    causal, dt_e, cum_e, cum_c, cum_t = decays(
        aux, heads, exp_ref[...], rowp_ref[0:1, :], rowp_ref[3:4, :LANES], colp_ref[:, 0:1]
    )
    xdt = x32 * dt_e
    xdt16 = xdt.astype(BF16)
    scores = dot_t(c, b)
    st = st_ref[0]
    st16 = st.astype(BF16)
    q_in = adj[...]
    q16 = q_in.astype(BF16)
    last = cum_e[rows - 1 : rows, :]
    ecum = jnp.exp(cum_e)
    tail = jnp.exp(last - cum_e)
    half = lax.broadcasted_iota(jnp.int32, (rows, LANES), 1) < HEAD_DIM
    zero = jnp.zeros((rows, LANES), BF16)
    mid = rows // 2
    n_sum = None
    parts = []
    for pair in range(heads // 2):
        cut = slice(LANES * pair, LANES * (pair + 1))
        x2 = xdt16[:, cut]
        dy2 = dy16[:, cut]
        got = []
        for side in range(2):
            h = 2 * pair + side
            top, low, right = lower_parts(cum_c, cum_t, h, causal)
            m_top = (scores[:mid, :mid] * top).astype(BF16)
            m_low = (scores[mid:, :mid] * low).astype(BF16)
            m_right = (scores[mid:, mid:] * right).astype(BF16)
            v_top = t_dot(jnp.concatenate([m_top, m_low], axis=0), dy2)
            got.append(jnp.concatenate([v_top, t_dot(m_right, dy2[mid:])], axis=0))
            own = half if side == 0 else jnp.logical_not(half)
            dy_own = jnp.where(own, dy2, zero)
            g_top = dot_t(dy_own[:mid], x2[:mid])
            g_low = dot_t(dy_own[mid:], x2)
            n = [g_top * top, g_low[:, :mid] * low, g_low[:, mid:] * right]
            n_sum = n if n_sum is None else [p + v for p, v in zip(n_sum, n)]
        parts.append(jnp.where(half, got[0], got[1]))
    n_low = jnp.concatenate([n_sum[1], n_sum[2]], axis=1).astype(BF16)
    n_top = n_sum[0].astype(BF16)
    out_part = dot(b, q16) * tail
    v = jnp.concatenate(parts, axis=1) + out_part
    dy_e = (dy * ecum).astype(BF16)
    x_tail = (xdt * tail).astype(BF16)
    d_b = jnp.concatenate([t_dot(jnp.concatenate([n_top, n_low[:, :mid]], axis=0), c), t_dot(n_low[:, mid:], c[mid:])], axis=0)
    d_b = d_b + dot_t(x_tail, q16)
    d_c = jnp.concatenate([dot(n_top, b[:mid]), dot(n_low, b)], axis=0) + dot_t(dy_e, st16)
    elast = jnp.exp(last)
    adj[...] = elast * q_in + t_dot(c, dy_e)

    seg = seg_ref[...]
    flow = dy * y - xdt16.astype(F32) * v
    passed = jnp.sum(xdt16.astype(F32) * out_part, axis=0, keepdims=True)
    passed = passed + elast * jnp.sum(q_in * st, axis=0, keepdims=True)
    flow_h = seg_dot(flow, seg)
    passed_h = seg_dot(jnp.broadcast_to(passed, (8, wide)), seg)[0:1, :]
    upper = jnp.where(
        lax.broadcasted_iota(jnp.int32, (rows, rows), 1) >= lax.broadcasted_iota(jnp.int32, (rows, rows), 0), 1.0, 0.0
    ).astype(BF16)
    hi = flow_h.astype(BF16)
    rest = flow_h - hi.astype(F32)
    mid = rest.astype(BF16)
    low = (rest - mid.astype(F32)).astype(BF16)
    crossing = dot(upper, hi) + dot(upper, mid) + dot(upper, low) + passed_h
    rate_row = rowp_ref[3:4, :LANES]
    decay_grad = rate_row * crossing
    d_dt = seg_dot(x32 * v, seg) + decay_grad
    lane = lax.broadcasted_iota(jnp.int32, (rows, LANES), 1)
    sig_v = pltpu.roll(aux, LANES - heads, 1)
    d_pre = jnp.where(lane < heads, d_dt * sig_v, 0.0)
    dt = jnp.where(lane < heads, aux, 0.0)
    dp_ref[:, chans:] = (r0 * d_pre).astype(BF16)

    d_act = jnp.concatenate([skip_e * dy + dt_e * v, d_b, d_c], axis=1)
    d_conv = d_act * slope_ref[...].astype(F32)
    d_conv16 = d_conv.astype(BF16)
    u = u_ref[...].astype(F32)
    d_u = cw_ref[KERNEL - 1 : KERNEL, :] * d_conv
    sm_ref[KERNEL - 1 : KERNEL, :] += jnp.sum(u * d_conv, axis=0, keepdims=True)
    for j in range(1, KERNEL):
        k = KERNEL - 1 - j
        moved = dot(shift_matrix(rows, j), d_conv16)
        moved = jnp.concatenate([moved[: rows - 8], moved[rows - 8 :] + ext[j : j + 8, :]], axis=0)
        d_u = d_u + cw_ref[k : k + 1, :] * moved
        sm_ref[k : k + 1, :] += jnp.sum(u * moved, axis=0, keepdims=True)
    ext[8:16, :] = d_conv[0:8, :]
    dp_ref[:, :chans] = (r0 * d_u).astype(BF16)
    sm_ref[4:5, :] += jnp.sum(d_conv, axis=0, keepdims=True)
    sm_ref[5:6, :wide] += jnp.sum(x32 * dy, axis=0, keepdims=True)
    sm_ref[6:7, :LANES] += jnp.sum(d_pre, axis=0, keepdims=True)
    sm_ref[7:8, :LANES] += jnp.sum(dt * decay_grad, axis=0, keepdims=True)

    if ring:
        @pl.when(step == steps - 1)
        def _():
            moves[2].wait_recv()
            moves[3].wait_recv()
            for copy in moves:
                copy.wait_send()
            own_piece.wait()


def grads_kernel(
    dpg_ref, dp_ref, w_ref, h_ref, gate_ref, piece_ref, tiny_ref,
    dn_ref, wing_ref, win_ref, wout_ref,
    dpv, wv, hb, far_p, y_p, x_p, far_a, far_b, y_f, x_f, sib_s, mine_s, own_s, z_u, z_d,
    load_sem, hb_sem, d_send, d_recv, s_send, s_recv, zu_send, zu_recv, zd_send, zd_recv,
    g_send, g_recv, k_send, k_recv, p_send, p_recv, out_sem,
):
    s = lax.axis_index("seq")
    h = lax.axis_index("head")
    owners = lax.axis_size("head")
    last = owners // 2 - 1
    core = lax.rem(h, 2)
    r = h // 2
    x_peer = s + 1 - 2 * lax.rem(s, 2)
    y_peer = lax.rem(s + 2, 4)
    far = 3 - s
    to_x, to_y = {"seq": x_peer}, {"seq": y_peer}
    to_sib = {"head": h + 1 - 2 * core}
    to_up, to_down = {"head": lax.rem(h + 2, owners)}, {"head": lax.rem(h + owners - 2, owners)}
    above, below = r < last, r > 0
    q = far_p.shape[0]
    half = q // 2
    n, cols = own_s.shape[1], own_s.shape[2]
    spare = LANES // 2
    tiles = cols // LANES
    edges = [LANES * (tiles * k // 4) for k in range(5)]
    spans = list(zip(edges[:-1], edges[1:]))
    sent = []
    closing = []

    def push(src, dst, sems, i, target):
        copy = remote(src, dst, sems[0].at[i], sems[1].at[i], target)
        copy.start()
        sent.append(copy)
        return copy

    def launch(there, make):
        @pl.when(there)
        def _():
            make().start()

        def finish():
            @pl.when(there)
            def _():
                make().wait_send()

        closing.append(finish)

    skip = dpv.shape[1] - cols
    load_dp = pltpu.make_async_copy(dp_ref, dpv.at[:, skip:], load_sem.at[0])
    load_w = pltpu.make_async_copy(w_ref, wv, load_sem.at[1])
    load_g = pltpu.make_async_copy(dpg_ref, dpv.at[:, :skip], load_sem.at[4])
    own_gate = pltpu.make_async_copy(gate_ref, wing_ref.at[s], load_sem.at[5])
    load_dp.start()
    load_g.start()
    load_w.start()
    own_gate.start()

    def chip(i):
        return jnp.where(lax.rem(i, 2) == 0, last - i // 2, i // 2)

    def load_h(i, other):
        at = 2 * chip(i) + (1 - core if other else core)
        slot = 0 if other else 1
        return pltpu.make_async_copy(
            h_ref.at[:, pl.ds(pl.multiple_of(at * n, LANES), n)], hb.at[slot], hb_sem.at[slot]
        )

    load_h(0, True).start()
    load_h(0, False).start()
    to_heads = [{"head": lax.rem(h + k, owners)} for k in range(1, owners)]
    greet([to_x, to_y] + to_heads)

    d_sems = (d_send, d_recv)
    g_sems = (g_send, g_recv)

    k_sems = (k_send, k_recv)
    k0 = push(gate_ref, wing_ref.at[s], k_sems, 0, to_x)
    k1 = push(gate_ref, wing_ref.at[s], k_sems, 1, to_y)
    tile = 256

    def part(block, out):
        at = pl.ds(pl.multiple_of(block * q, 16), q)

        @pl.loop(0, wv.shape[0] // tile)
        def _(j):
            to = pl.ds(pl.multiple_of(j * tile, tile), tile)
            out[:, to] = dot_t(dpv[at, :], wv[to, :]).astype(BF16)

    def add_to(out, at, extra):
        out[at, :] = (out[at, :].astype(F32) + extra.astype(F32)).astype(BF16)

    def swap(i):
        t = chip(i)
        return remote(sib_s.at[lax.rem(i, 2)], own_s.at[t], s_send.at[t], s_recv.at[t], to_sib)

    def rows_of(i):
        t = chip(i)
        slot = lax.rem(i, 2)

        @pl.when(i >= 2)
        def _():
            swap(i - 2).wait_send()

        load_h(i, True).wait()
        for lo, hi in spans:
            sib_s[slot, :, lo:hi] = t_dot(hb[0], dpv[:, skip + lo : skip + hi]).astype(BF16)
        sib_s[slot, :, cols - spare :] = tiny_ref[...]
        swap(i).start()

        @pl.when(i < 3)
        def _():
            load_h(i + 1, True).start()

        load_h(i, False).wait()
        for lo, hi in spans:
            mine_s[:, lo:hi] = t_dot(hb[1], dpv[:, skip + lo : skip + hi]).astype(BF16)
        mine_s[:, cols - spare :] = tiny_ref[...]

        @pl.when(i < 3)
        def _():
            load_h(i + 1, False).start()

        swap(i).wait_recv()
        join(t, mine_s)

    def join(t, extra):
        for lo, hi in spans:
            own_s[t, :, lo:hi] = (own_s[t, :, lo:hi].astype(F32) + extra[:, lo:hi].astype(F32)).astype(BF16)

    start, second, across, third, final = line_sum(
        own_s, z_u, z_d, (zu_send, zu_recv, zd_send, zd_recv), r, last, to_up, to_down, join, closing
    )

    load_dp.wait()
    load_g.wait()
    load_w.wait()
    part(far, far_p)
    d0 = push(far_p.at[:half], far_a, d_sems, 0, to_x)
    d1 = push(far_p.at[half:], far_b, d_sems, 1, to_y)
    pl.loop(0, 2)(rows_of)
    start()
    k0.wait_recv()
    gate_a = wing_ref.at[x_peer, : n // 2]
    k2 = push(gate_a, gate_a, k_sems, 2, to_y)
    k1.wait_recv()
    gate_b = wing_ref.at[y_peer, n // 2 :]
    k3 = push(gate_b, gate_b, k_sems, 3, to_x)
    pl.loop(2, 4)(rows_of)
    part(y_peer, y_p)
    d2 = push(y_p.at[half:], y_f.at[half:], d_sems, 2, to_y)
    second()
    part(x_peer, x_p)
    d3 = push(x_p.at[:half], x_f.at[:half], d_sems, 3, to_x)
    d0.wait_recv()
    add_to(y_p, slice(0, half), far_a[...])
    d4 = push(y_p.at[:half], y_f.at[:half], d_sems, 4, to_y)
    d1.wait_recv()
    add_to(x_p, slice(half, q), far_b[...])
    d5 = push(x_p.at[half:], x_f.at[half:], d_sems, 5, to_x)
    across()
    third()
    d0.wait_send()
    d1.wait_send()
    part(s, far_p)
    final()

    red = own_s.at[r]
    g0 = push(red, win_ref.at[s], g_sems, 0, to_x)
    g1 = push(red, win_ref.at[s], g_sems, 1, to_y)
    own_win = pltpu.make_async_copy(red, win_ref.at[s], load_sem.at[3])
    own_win.start()
    per = owners // 4

    def piece_of(head):
        return piece_ref.at[head // per, lax.rem(head, per)]

    pieces = []
    for k, peer in enumerate(to_heads):
        pieces.append(push(piece_of(peer["head"]), wout_ref.at[h], (p_send, p_recv), k, peer))
    own_piece = pltpu.make_async_copy(piece_of(h), wout_ref.at[h], load_sem.at[2])
    own_piece.start()

    g0.wait_recv()
    part_a = win_ref.at[x_peer, : n // 2]
    g2 = push(part_a, part_a, g_sems, 2, to_y)
    g1.wait_recv()
    part_b = win_ref.at[y_peer, n // 2 :]
    g3 = push(part_b, part_b, g_sems, 3, to_x)

    for copy in (d2, d3, d4, d5):
        copy.wait_recv()
    far_p[...] = (far_p[...].astype(F32) + y_f[...].astype(F32) + x_f[...].astype(F32)).astype(BF16)
    dn_out = pltpu.make_async_copy(far_p, dn_ref, out_sem.at[0])
    dn_out.start()
    dn_out.wait()
    own_win.wait()
    own_gate.wait()
    own_piece.wait()
    k2.wait_recv()
    k3.wait_recv()
    for copy in pieces:
        copy.wait_recv()
    g2.wait_recv()
    g3.wait_recv()
    for i in (2, 3):
        swap(i).wait_send()
    for copy in sent:
        if copy is not d0 and copy is not d1:
            copy.wait_send()
    for finish in closing:
        finish()


def finish_kernel(
    gate_ref, rest_ref, w_ref, dtw_ref, gain_ref, wog_ref, wo_ref, ggain_ref, hid_ref, og_ref, dn_ref, br_ref,
    win_ref, wdt_ref, norm_ref, wout_ref, gg_ref, blk_ref, hg_ref, *, heads, wide,
):
    ranks = gate_ref.shape[0]
    wog = wog_ref[...].astype(F32)
    wout_ref[...] = wog
    gg_ref[...] = jnp.sum(wog * wo_ref[...].astype(F32), axis=1, keepdims=True) / ggain_ref[...]
    h32 = hid_ref[...].astype(F32)
    blk_ref[...] = (h32 + br_ref[...].astype(F32)).astype(BF16)
    dn = dn_ref[...].astype(F32)
    count = h32.shape[1]
    r0 = lax.rsqrt(jnp.sum(h32 * h32, axis=1, keepdims=True) / count + EPS)
    mixed = jnp.sum(dn * h32, axis=1, keepdims=True) / count
    hg_ref[...] = og_ref[...].astype(F32) + dn - h32 * (r0 * r0 * mixed)

    gain = gain_ref[...]
    norm = None

    def piece(at, raw):
        to = slice(at, at + raw.shape[1])
        win_ref[:, to] = raw * gain
        return jnp.sum(raw * w_ref[:, to].astype(F32), axis=1, keepdims=True)

    shared = None
    dt_parts = []
    for k in range(ranks):
        here = piece(k * wide, gate_ref[k].astype(F32)) + piece(DI + k * wide, rest_ref[k, :, :wide].astype(F32))
        norm = here if norm is None else norm + here
        bc = rest_ref[k, :, wide : wide + 2 * STATE].astype(F32)
        shared = bc if shared is None else shared + bc
        dt_parts.append(rest_ref[k, :, wide + 2 * STATE : wide + 2 * STATE + heads].astype(F32))
    norm = norm + piece(2 * DI, shared)
    raw = jnp.concatenate(dt_parts, axis=1)
    wdt_ref[...] = raw * gain
    norm_ref[...] = norm + jnp.sum(raw * dtw_ref[...].astype(F32), axis=1, keepdims=True)


def local(hidden, lengths, out_grad, norm_gain, w_in, w_dt, conv_weight, conv_bias, dt_bias, a_log, skip_gain, gate_gain, w_out):
    ranks = lax.axis_size("seq")
    rank = lax.axis_index("seq")
    owners = lax.axis_size("head")
    owner = lax.axis_index("head")
    local_len, width = hidden.shape[1], hidden.shape[2]
    heads = HEADS // ranks
    wide = heads * HEAD_DIM
    chans = wide + 2 * STATE
    cols = wide + chans + LANES
    tokens = ranks * local_len
    chunk = min(CHUNK, local_len)
    steps = tokens // chunk
    shard = w_in.shape[0]

    gain_rows = norm_gain.astype(F32)[:, None]

    def scaled(v):
        return (v.astype(F32) * gain_rows).astype(BF16)

    spare = LANES // 2
    small = jnp.concatenate([conv_weight.reshape(-1), conv_bias, dt_bias, a_log, skip_gain, gate_gain])
    n_small = small.shape[0]
    small = jnp.pad(small, (0, shard * spare - n_small)).reshape(shard, spare)
    last_block = jnp.concatenate(
        [
            scaled(lax.dynamic_slice_in_dim(w_dt, rank * heads, heads, 1)),
            jnp.zeros((shard, LANES - spare - heads), BF16),
            small,
        ],
        axis=1,
    )
    ring = owners == 2 * ranks
    if ring:
        w_given, o_given = w_in, w_out
    else:
        w_given = lax.all_gather(
            jnp.concatenate(
                [
                    scaled(lax.dynamic_slice_in_dim(w_in, rank * wide, wide, 1)),
                    scaled(lax.dynamic_slice_in_dim(w_in, DI + rank * wide, wide, 1)),
                    scaled(w_in[:, 2 * DI :]),
                    last_block,
                ],
                axis=1,
            ),
            "head", axis=0, tiled=True,
        )
        o_given = lax.dynamic_slice_in_dim(lax.all_gather(w_out, "head", axis=0, tiled=True), rank * wide, wide, 0)

    def sds(shape, kind):
        return jax.ShapeDtypeStruct(shape, kind)

    hbm = pl.BlockSpec(memory_space=pl.ANY)
    vmem = pl.BlockSpec(memory_space=pltpu.VMEM)

    def dma(count):
        return pltpu.SemaphoreType.DMA((count,))

    h_all, og_all, w_t, w_o, z, u, d_raw, d0 = pl.pallas_call(
        functools.partial(gather_kernel, ring=ring, wide=wide),
        in_specs=[hbm, hbm, hbm, hbm, vmem, vmem],
        out_specs=[hbm] * 8,
        out_shape=[
            sds((tokens, width), BF16),
            sds((tokens, width), BF16),
            sds((width, cols), BF16),
            sds((wide, width), BF16),
            sds((tokens, wide), BF16),
            sds((tokens, chans), BF16),
            sds((tokens, LANES), F32),
            sds((tokens, wide), BF16),
        ],
        scratch_shapes=[
            pltpu.VMEM((tokens, width), BF16),
            pltpu.VMEM((tokens, width), BF16),
            pltpu.VMEM((width, cols), BF16),
            pltpu.VMEM((wide, width), BF16),
            pltpu.VMEM((shard, cols - LANES), BF16),
            pltpu.VMEM((tokens, wide), BF16),
            pltpu.VMEM((tokens, chans), BF16),
            pltpu.VMEM((tokens, LANES), F32),
            pltpu.VMEM((tokens, wide), BF16),
        ]
        + [dma(4)] * 9
        + [dma(8)] * 5
        + [dma(6), dma(26)],
        compiler_params=pltpu.CompilerParams(
            collective_id=0, has_side_effects=True, vmem_limit_bytes=56 * 1024 * 1024
        ),
        cost_estimate=pl.CostEstimate(
            flops=2 * tokens * width * (cols + wide), bytes_accessed=4 * tokens * (width + cols), transcendentals=0
        ),
        name="gather_project",
    )(hidden[0], out_grad[0], w_given, o_given, gain_rows, last_block)

    small = w_t.reshape(owners, shard, cols)[:, :, cols - spare :].reshape(owners, shard * spare)
    cs = CHANNELS // owners
    hs = HEADS // owners
    gs = DI // owners
    conv_w = small[:, : KERNEL * cs].reshape(owners, KERNEL, cs).swapaxes(0, 1).reshape(KERNEL, CHANNELS)
    at = KERNEL * cs
    conv_b = small[:, at : at + cs].reshape(CHANNELS)
    at += cs
    dt_b = small[:, at : at + hs].reshape(HEADS)
    at += hs
    a_all = small[:, at : at + hs].reshape(HEADS)
    at += hs
    skip_all = small[:, at : at + hs].reshape(HEADS)
    at += hs
    gain_all = small[:, at : at + gs].reshape(DI)

    def mine(v, size):
        return lax.dynamic_slice_in_dim(v, rank * size, size, v.ndim - 1)

    cw = jnp.concatenate([mine(conv_w[:, :DI], wide), conv_w[:, DI:]], axis=1).astype(F32)
    cb = jnp.concatenate([mine(conv_b[:DI], wide), conv_b[DI:]])[None].astype(F32)
    cw = jnp.concatenate([cw, jnp.zeros((8 - KERNEL, chans), F32)], axis=0)
    cb = jnp.broadcast_to(cb, (8, chans))
    dtb = jnp.broadcast_to(jnp.pad(mine(dt_b, heads).astype(F32), (0, LANES - heads))[None], (8, LANES))
    rate = -jnp.exp(mine(a_all, heads).astype(F32))
    rowp = jnp.stack(
        [
            jnp.repeat(rate, HEAD_DIM),
            jnp.repeat(mine(skip_all, heads).astype(F32), HEAD_DIM),
            mine(gain_all, wide).astype(F32),
            jnp.pad(rate, (0, wide - heads)),
        ]
        + [jnp.zeros((wide,), F32)] * 4
    )
    colp = jnp.broadcast_to(jnp.pad(rate, (0, LANES - heads))[:, None], (LANES, LANES))
    head_of = jnp.arange(wide, dtype=jnp.int32) // HEAD_DIM
    expand = (jnp.arange(LANES, dtype=jnp.int32)[:, None] == head_of[None]).astype(BF16)
    seg = expand.T

    def forth(size):
        return pl.BlockSpec((chunk, size), lambda j: (j, 0))

    def back(size):
        return pl.BlockSpec((chunk, size), lambda j: (steps - 1 - j, 0))

    def whole(a):
        return pl.BlockSpec(a.shape, lambda j: (0,) * a.ndim, pipeline_mode=pl.Buffered(1))

    params = pltpu.CompilerParams(
        dimension_semantics=("arbitrary",), vmem_limit_bytes=56 * 1024 * 1024
    )
    grid = (steps,)

    act, slope, aux, y, gg, states, sums = pl.pallas_call(
        functools.partial(scan_kernel, heads=heads, wide=wide),
        grid=grid,
        in_specs=[
            forth(chans), forth(LANES), forth(wide), forth(wide),
            whole(cw), whole(cb), whole(dtb), whole(expand), whole(rowp), whole(colp),
        ],
        out_specs=[
            forth(chans), forth(chans), forth(LANES), forth(wide), forth(wide),
            pl.BlockSpec((1, STATE, wide), lambda j: (j, 0, 0)),
            pl.BlockSpec((8, chunk), lambda j: (0, j)),
        ],
        out_shape=[
            sds((tokens, chans), BF16),
            sds((tokens, chans), BF16),
            sds((tokens, LANES), F32),
            sds((tokens, wide), BF16),
            sds((tokens, wide), BF16),
            sds((steps, STATE, wide), F32),
            sds((8, tokens), F32),
        ],
        scratch_shapes=[pltpu.VMEM((STATE, wide), F32), pltpu.VMEM((16, chans), F32)],
        compiler_params=params,
        cost_estimate=pl.CostEstimate(
            flops=2 * tokens * wide * 12 * chunk, bytes_accessed=tokens * wide * 16, transcendentals=tokens * chunk * heads
        ),
        name="scan",
    )(u, d_raw, z, d0, cw, cb, dtb, expand, rowp, colp)

    mask = (jnp.arange(tokens, dtype=jnp.int32) < lengths[0]).astype(F32)
    n_own = DI // owners
    piece = n_own // owners
    per = owners // ranks
    wog_shape = (per, piece, width) if ring else (wide, width)
    line_shape = (4, per, piece, width) if ring else (1, 1, 16, LANES)
    in_chunk = min(CHUNK, local_len)
    branch, wog, dy, dpg, wig_gate = pl.pallas_call(
        functools.partial(mid_kernel, ring=ring),
        in_specs=[hbm] * 9 + [vmem] * 3,
        out_specs=[hbm] * 5,
        out_shape=[
            sds((local_len, width), BF16),
            sds(wog_shape, BF16),
            sds((tokens, wide), BF16),
            sds((tokens, wide), BF16),
            sds((width, wide), BF16),
        ],
        scratch_shapes=[
            pltpu.VMEM((tokens, LANES), F32),
            pltpu.VMEM((tokens, wide), BF16),
            pltpu.VMEM((wide, width), BF16),
            pltpu.VMEM((tokens, width // 2), BF16),
        ]
        + [pltpu.VMEM((local_len, width), BF16)] * 4
        + [pltpu.VMEM((local_len // 2, width), BF16)] * 2
        + [pltpu.VMEM((local_len, width), BF16)] * 2
        + [pltpu.VMEM((ranks, 8, tokens), F32)]
        + [pltpu.VMEM(line_shape, BF16)] * 3
        + [pltpu.VMEM((3,) + line_shape[1:], BF16)] * 2
        + [pltpu.VMEM((256 // (2 * piece), 2, piece, width // 2) if ring else (16, LANES), BF16)]
        + [pltpu.VMEM((2, in_chunk, wide), BF16)] * 4
        + [
            pltpu.VMEM((2, in_chunk, LANES), F32),
            pltpu.VMEM((2, in_chunk, wide), BF16),
            pltpu.VMEM((2, tokens, 256), BF16),
            pltpu.VMEM((2, 256, wide), BF16),
        ]
        + [dma(3)]
        + [dma(6)] * 2
        + [dma(3)] * 2
        + [dma(1)] * 2
        + [dma(4)] * 4
        + [pltpu.SemaphoreType.DMA((2, 5)), dma(2), dma(2), dma(2), dma(3)],
        compiler_params=pltpu.CompilerParams(
            collective_id=3, has_side_effects=True, vmem_limit_bytes=56 * 1024 * 1024
        ),
        cost_estimate=pl.CostEstimate(
            flops=6 * tokens * wide * width, bytes_accessed=4 * tokens * (width + 5 * wide), transcendentals=0
        ),
        name="mid",
    )(gg, w_o, og_all, h_all, act, aux, z, d0, y, sums, jnp.broadcast_to(mask[None], (8, tokens)), rowp)
    own_gate = lax.psum_scatter(wig_gate, "head", scatter_dimension=0, tiled=True)

    rest = chans + LANES
    dp, sm, pieces = pl.pallas_call(
        functools.partial(back_kernel, heads=heads, wide=wide, ring=ring),
        grid=grid,
        in_specs=[
            back(chans), back(LANES), back(wide), back(wide),
            pl.BlockSpec((1, STATE, wide), lambda j: (steps - 1 - j, 0, 0)),
            back(chans), back(chans), hbm,
            whole(expand), whole(seg), whole(rowp), whole(colp), whole(cw),
        ],
        out_specs=[back(rest), pl.BlockSpec((8, chans), lambda j: (0, 0)), hbm],
        out_shape=[sds((tokens, rest), BF16), sds((8, chans), F32), sds((ranks,) + wog_shape, BF16)],
        scratch_shapes=[pltpu.VMEM((STATE, wide), F32), pltpu.VMEM((16, chans), F32)]
        + [dma(4)] * 2
        + [dma(1)],
        compiler_params=pltpu.CompilerParams(
            dimension_semantics=("arbitrary",), collective_id=2, has_side_effects=True,
            vmem_limit_bytes=56 * 1024 * 1024,
        )
        if ring
        else params,
        cost_estimate=pl.CostEstimate(
            flops=2 * tokens * wide * 12 * chunk, bytes_accessed=tokens * wide * 24, transcendentals=tokens * chunk * heads
        ),
        name="scan_back",
    )(act, aux, dy, y, states, slope, u, wog, expand, seg, rowp, colp, cw)

    skip_h = jnp.sum(sm[5, :wide].reshape(heads, HEAD_DIM), axis=1)
    tiny = jnp.concatenate([sm[:5].reshape(-1), sm[6, :heads], sm[7, :heads], skip_h])
    if ring:
        laid = jnp.pad(tiny, (0, shard * spare - tiny.shape[0])).reshape(shard, spare).astype(BF16)
        dn, gate_rows, rest_rows, w_out_grad = pl.pallas_call(
            grads_kernel,
            in_specs=[hbm] * 6 + [vmem],
            out_specs=[hbm] * 4,
            out_shape=[
                sds((local_len, width), BF16),
                sds((ranks, shard, wide), BF16),
                sds((ranks, shard, rest), BF16),
                sds((owners, piece, width), BF16),
            ],
            scratch_shapes=[
                pltpu.VMEM((tokens, cols), BF16),
                pltpu.VMEM((width, cols), BF16),
                pltpu.VMEM((2, tokens, shard), BF16),
            ]
            + [pltpu.VMEM((local_len, width), BF16)] * 3
            + [pltpu.VMEM((local_len // 2, width), BF16)] * 2
            + [pltpu.VMEM((local_len, width), BF16)] * 2
            + [
                pltpu.VMEM((2, shard, rest), BF16),
                pltpu.VMEM((shard, rest), BF16),
                pltpu.VMEM((4, shard, rest), BF16),
                pltpu.VMEM((3, shard, rest), BF16),
                pltpu.VMEM((3, shard, rest), BF16),
            ]
            + [dma(6), dma(2)]
            + [dma(6)] * 2
            + [dma(4)] * 10
            + [dma(owners)] * 2
            + [dma(2)],
            compiler_params=pltpu.CompilerParams(
                collective_id=1, has_side_effects=True, vmem_limit_bytes=56 * 1024 * 1024
            ),
            cost_estimate=pl.CostEstimate(
                flops=4 * tokens * width * cols, bytes_accessed=8 * tokens * cols, transcendentals=0
            ),
            name="weight_grads",
        )(dpg, dp, w_t, h_all, own_gate, pieces, laid)
        w_out_grad = w_out_grad.reshape(n_own, width)
        tiny_all = rest_rows[:, :, rest - spare :].reshape(ranks, shard * spare)[:, : tiny.shape[0]].astype(F32)
    else:
        full = lax.all_gather(lax.psum(wog, "head"), "seq", axis=0, tiled=True)
        w_out_grad = lax.dynamic_slice_in_dim(full, owner * n_own, n_own, 0)
        wig = t_dot(h_all, dp).astype(BF16)
        dn = (dot_t(dp, w_t[:, wide:]) + dot_t(dpg, w_t[:, :wide])).astype(BF16)
        dn = lax.psum_scatter(dn, "seq", scatter_dimension=0, tiled=True)
        gate_rows = lax.all_gather(own_gate, "seq")
        rest_rows = lax.all_gather(lax.psum_scatter(wig, "head", scatter_dimension=0, tiled=True), "seq")
        tiny_all = lax.all_gather(lax.psum(tiny, "head"), "seq")
    strips = min(8, shard // 16)

    def strip(total, size):
        return pl.BlockSpec((total // strips, size), lambda j: (j, 0))

    def ranks_strip(size):
        return pl.BlockSpec((ranks, shard // strips, size), lambda j: (0, j, 0))

    w_in_grad, w_dt_grad, norm_gain_grad, w_out_grad, gate_gain_grad, block_out, hidden_grad = pl.pallas_call(
        functools.partial(finish_kernel, heads=heads, wide=wide),
        grid=(strips,),
        in_specs=[
            ranks_strip(wide), ranks_strip(rest), strip(shard, PROJ), strip(shard, HEADS), strip(shard, 1),
            strip(n_own, width), strip(n_own, width), strip(n_own, 1),
            strip(local_len, width), strip(local_len, width), strip(local_len, width), strip(local_len, width),
        ],
        out_specs=[
            strip(shard, PROJ), strip(shard, HEADS), strip(shard, 1), strip(n_own, width), strip(n_own, 1),
            strip(local_len, width), strip(local_len, width),
        ],
        out_shape=[
            sds((shard, PROJ), F32),
            sds((shard, HEADS), F32),
            sds((shard, 1), F32),
            sds((n_own, width), F32),
            sds((n_own, 1), F32),
            sds((local_len, width), BF16),
            sds((local_len, width), F32),
        ],
        compiler_params=params,
        cost_estimate=pl.CostEstimate(flops=6 * shard * PROJ, bytes_accessed=16 * shard * PROJ, transcendentals=0),
        name="finish",
    )(
        gate_rows, rest_rows, w_in, w_dt, gain_rows, w_out_grad, w_out, gate_gain.astype(F32)[:, None],
        hidden[0], out_grad[0], dn, branch,
    )

    n_conv = 5 * chans
    conv_all = tiny_all[:, :n_conv].reshape(ranks, 5, chans)
    conv_all = jnp.concatenate(
        [conv_all[:, :, :wide].swapaxes(0, 1).reshape(5, DI), jnp.sum(conv_all[:, :, wide:], axis=0)], axis=1
    )
    vec = tiny_all[:, n_conv:].reshape(ranks, 3, heads).swapaxes(0, 1).reshape(3, HEADS)
    conv_own = lax.dynamic_slice_in_dim(conv_all, owner * cs, cs, 1)
    vec_own = lax.dynamic_slice_in_dim(vec, owner * hs, hs, 1)

    return (
        block_out[None],
        hidden_grad[None],
        norm_gain_grad.reshape(shard),
        w_in_grad,
        w_dt_grad,
        conv_own[:KERNEL],
        conv_own[KERNEL],
        vec_own[0],
        vec_own[1],
        vec_own[2],
        gate_gain_grad.reshape(n_own),
        w_out_grad,
    )


def solution(mesh):
    rows = P("head", "seq", None)
    return jax.shard_map(
        local,
        mesh=mesh,
        in_specs=(
            rows, P("head"), rows, P("head"), P("head", None), P("head", None), P(None, "head"),
            P("head"), P("head"), P("head"), P("head"), P("head"), P("head", None),
        ),
        out_specs=(
            rows, rows, P("head"), P("head", None), P("head", None), P(None, "head"),
            P("head"), P("head"), P("head"), P("head"), P("head"), P("head", None),
        ),
        check_vma=False,
    )
```

```python
import functools

import jax
import jax.numpy as jnp
from jax import lax
from jax.experimental import pallas as pl
from jax.experimental.pallas import tpu as pltpu
from jax.sharding import PartitionSpec as P

HEADS = 64
HEAD_DIM = 64
STATE = 128
KERNEL = 4
CHUNK = 256
DI = 4096
CHANNELS = 4352
PROJ = DI + CHANNELS
EPS = 1e-05
LANES = 128
EVERY = ("seq", "head")
F32 = jnp.float32
BF16 = jnp.bfloat16


def dot(a, b):
    return jnp.dot(a, b, preferred_element_type=F32)


def dot_t(a, b):
    return lax.dot_general(a, b, (((1,), (1,)), ((), ())), preferred_element_type=F32)


def t_dot(a, b):
    return lax.dot_general(a, b, (((0,), (0,)), ((), ())), preferred_element_type=F32)


def sigmoid(v):
    return 0.5 * jnp.tanh(0.5 * v) + 0.5


def remote(src, dst, send, recv, target):
    return pltpu.make_async_remote_copy(
        src_ref=src, dst_ref=dst, send_sem=send, recv_sem=recv, device_id=target, device_id_type=pl.DeviceIdType.MESH
    )


def greet(peers, extra=()):
    barrier = pltpu.get_barrier_semaphore()
    count = len(peers)

    def hello(peer):
        pl.semaphore_signal(barrier, inc=1, device_id=peer, device_id_type=pl.DeviceIdType.MESH)

    for peer in peers:
        hello(peer)
    for there, peer in extra:
        pl.when(there)(functools.partial(hello, peer))
        count = count + jnp.where(there, 1, 0)
    pl.semaphore_wait(barrier, count)


def decays(aux, heads, expand, rate_e, rate_row, rate_col):
    rows = aux.shape[0]
    lane = lax.broadcasted_iota(jnp.int32, aux.shape, 1)
    dt = jnp.where(lane < heads, aux, 0.0).astype(BF16)
    r = lax.broadcasted_iota(jnp.int32, (rows, rows), 0)
    c = lax.broadcasted_iota(jnp.int32, (rows, rows), 1)
    causal = c <= r
    lower = jnp.where(causal, 1.0, 0.0).astype(BF16)
    dt_e = dot(dt, expand)
    cum_e = dot(lower, dt_e.astype(BF16)) * rate_e
    cum_c = dot(lower, dt) * rate_row
    cum_t = lax.dot_general(dt, lower, (((0,), (1,)), ((), ())), preferred_element_type=F32) * rate_col
    return causal, dt_e, cum_e, cum_c, cum_t


def head_matrix(wide, turned=False):
    shape = (wide, LANES) if turned else (LANES, wide)
    channel = lax.broadcasted_iota(jnp.int32, shape, 0 if turned else 1)
    head = lax.broadcasted_iota(jnp.int32, shape, 1 if turned else 0)
    return jnp.where(channel // HEAD_DIM == head, 1.0, 0.0).astype(BF16)


def shift_matrix(rows, by):
    r = lax.broadcasted_iota(jnp.int32, (rows, rows), 0)
    c = lax.broadcasted_iota(jnp.int32, (rows, rows), 1)
    return jnp.where(c == r + by, 1.0, 0.0).astype(BF16)


def lower_parts(cum_c, cum_t, h, causal):
    mid = causal.shape[0] // 2
    near = causal[:mid, :mid]
    col, row = cum_c[:, h : h + 1], cum_t[h : h + 1, :]
    top = jnp.exp(jnp.where(near, col[:mid] - row[:, :mid], -1e30))
    low = jnp.exp(col[mid:] - row[:, :mid])
    right = jnp.exp(jnp.where(near, col[mid:] - row[:, mid:], -1e30))
    return top, low, right


def scan_chunk(u, raw, z, taps, bias, dtb, expand, rowp, rate_col, state, ext, st_out, heads):
    rows, chans = u.shape
    wide = expand.shape[1]
    u32 = u.astype(F32)
    pre = bias + taps[KERNEL - 1 : KERNEL] * u32
    before = jnp.zeros((8, chans), F32)
    for j in range(1, KERNEL):
        tap = taps[KERNEL - 1 - j : KERNEL - j]
        pre = pre + tap * dot(shift_matrix(rows, -j), u)
        before = before + tap * ext[8 - j : 16 - j, :]
    pre = jnp.concatenate([pre[:8] + before, pre[8:]], axis=0)
    ext[0:8, :] = u32[rows - 8 :, :]
    sig = sigmoid(pre)
    act = (pre * sig).astype(BF16)
    slope = (sig * (1.0 + pre * (1.0 - sig))).astype(BF16)
    v = raw + dtb
    soft = jnp.maximum(v, 0.0) + jnp.log1p(jnp.exp(-jnp.abs(v)))
    soft = soft.astype(BF16).astype(F32)
    lane = lax.broadcasted_iota(jnp.int32, v.shape, 1)
    aux = jnp.where(lane < heads, soft, 0.0)
    sig_v = pltpu.roll(sigmoid(v), heads, 1)
    aux = jnp.where((lane >= heads) & (lane < 2 * heads), sig_v, aux)
    aux = jnp.where(lane == LANES - 1, raw, aux)

    x32 = act[:, :wide].astype(F32)
    b = act[:, wide : wide + STATE]
    c = act[:, wide + STATE :]
    causal, dt_e, cum_e, cum_c, cum_t = decays(aux, heads, expand, rowp[0:1], rowp[3:4, :LANES], rate_col)
    xdt = x32 * dt_e
    xdt16 = xdt.astype(BF16)
    scores = dot_t(c, b)
    st = state[...]
    st_out[...] = st
    mid = rows // 2
    half = lax.broadcasted_iota(jnp.int32, (rows, LANES), 1) < HEAD_DIM
    parts = []
    for pair in range(heads // 2):
        x2 = xdt16[:, LANES * pair : LANES * (pair + 1)]
        got = []
        for h in (2 * pair, 2 * pair + 1):
            top, low, right = lower_parts(cum_c, cum_t, h, causal)
            m_top = (scores[:mid, :mid] * top).astype(BF16)
            m_low = (scores[mid:, :mid] * low).astype(BF16)
            m_right = (scores[mid:, mid:] * right).astype(BF16)
            y_low = dot(jnp.concatenate([m_low, m_right], axis=1), x2)
            got.append(jnp.concatenate([dot(m_top, x2[:mid]), y_low], axis=0))
        parts.append(jnp.where(half, got[0], got[1]))
    y = jnp.concatenate(parts, axis=1) + dot(c, st.astype(BF16)) * jnp.exp(cum_e)
    last = cum_e[rows - 1 : rows, :]
    tail = jnp.exp(last - cum_e)
    state[...] = jnp.exp(last) * st + t_dot(b, (xdt * tail).astype(BF16))
    y16 = y.astype(BF16)
    ssd = (y16.astype(F32) + rowp[1:2] * x32).astype(BF16).astype(F32)
    z = z.astype(F32)
    g = ssd * (z * sigmoid(z))
    gg = (g * rowp[2:3]).astype(BF16)
    ssq = dot_t(jnp.ones((8, wide), BF16), (g * g).astype(BF16))
    return act, slope, aux, y16, gg, ssq


def with_cross(ssq, gg, d0):
    cross = dot_t(jnp.ones((8, gg.shape[1]), BF16), (gg.astype(F32) * d0.astype(F32)).astype(BF16))
    return jnp.where(lax.broadcasted_iota(jnp.int32, ssq.shape, 0) == 0, ssq, cross)


def scan_kernel(
    u_ref, d_ref, z_ref, d0_ref, cw_ref, dtb_ref, rowp_ref, colp_ref,
    act_ref, slope_ref, aux_ref, y_ref, gg_ref, st_ref, sum_ref, state, ext, *, heads,
):
    @pl.when(pl.program_id(0) == 0)
    def _():
        state[...] = jnp.zeros_like(state)
        ext[...] = jnp.zeros_like(ext)

    act, slope, aux, y16, gg, ssq = scan_chunk(
        u_ref[...], d_ref[...], z_ref[...], cw_ref[0:KERNEL, :], cw_ref[KERNEL : KERNEL + 1, :], dtb_ref[0:1, :],
        head_matrix(z_ref.shape[1]), rowp_ref[...], colp_ref[:, 0:1], state, ext, st_ref.at[0], heads,
    )
    act_ref[...] = act
    slope_ref[...] = slope
    aux_ref[...] = aux
    y_ref[...] = y16
    gg_ref[...] = gg
    sum_ref[...] = with_cross(ssq, gg, d0_ref[...])


def seg_dot(v, seg):
    hi = v.astype(BF16)
    return dot(hi, seg) + dot((v - hi.astype(F32)).astype(BF16), seg)


def rank_params(par, s, cw_ref, dtb_ref, rowp_ref, colp_ref, heads, wide):
    owners, _, lanes = par.shape
    chans = cw_ref.shape[1]
    share = CHANNELS // owners
    gains = DI // owners
    per = HEADS // owners

    def iota(shape, dim):
        return lax.broadcasted_iota(jnp.int32, shape, dim)

    def chosen(there):
        return jnp.where(there, 1.0, 0.0).astype(BF16)

    cw_ref[...] = jnp.zeros_like(cw_ref)
    at = iota((1, chans), 1)
    wanted = jnp.where(at < wide, s * wide + at, DI + at - wide)

    @pl.loop(0, owners)
    def _(j):
        i = iota((lanes, chans), 0)
        cw_ref[...] += dot(par[j], chosen((i + j * share == wanted) & (i < share)))

    count = heads // per
    a_e, skip_e, a_row, dt_row, a_col, gain = 0.0, 0.0, 0.0, 0.0, 0.0, []
    head_of = iota((LANES, wide), 1) // HEAD_DIM
    lane_e = iota((LANES, wide), 0)
    lane = iota((LANES, LANES), 0)
    to = iota((LANES, LANES), 1)
    for k in range(count):
        block = par[s * count + k]
        few = block[:, :LANES]
        gain.append(block[5:6, :gains].astype(F32))

        def spread(first):
            return chosen((lane_e - first + per * k == head_of) & (lane_e >= first) & (lane_e < first + per))

        def placed(first):
            return chosen((lane - first + per * k == to) & (lane >= first) & (lane < first + per))

        a_e = a_e + dot(few, spread(per))
        skip_e = skip_e + dot(few, spread(2 * per))
        dt_row = dt_row + dot(few, placed(0))
        a_row = a_row + dot(few, placed(per))
        a_col = a_col + lax.dot_general(placed(per), few, (((0,), (1,)), ((), ())), preferred_element_type=F32)
    rowp_ref[0:1, :] = -jnp.exp(a_e[6:7])
    rowp_ref[1:2, :] = skip_e[6:7]
    rowp_ref[2:3, :] = jnp.concatenate(gain, axis=1)
    rowp_ref[3:8, :] = jnp.zeros((5, wide), F32)
    rowp_ref[3:4, :LANES] = jnp.where(iota((1, LANES), 1) < heads, -jnp.exp(a_row[6:7]), 0.0)
    dtb_ref[...] = jnp.broadcast_to(dt_row[6:7], dtb_ref.shape)
    col = jnp.where(iota((LANES, 1), 0) < heads, -jnp.exp(a_col[:, 6:7]), 0.0)
    colp_ref[...] = jnp.broadcast_to(col, colp_ref.shape)


def gather_kernel(
    hid_ref, og_ref, w_ref, wo_in_ref, gain_ref, dtw_ref, cwt_ref, cbi_ref, ggn_ref, hds_ref,
    hall_ref, ogall_ref, wt_ref, wo_ref, z_ref, u_ref, d0_ref, act_ref, slope_ref, aux_ref, y_ref, gg_ref, st_ref,
    sum_ref, cw_ref, dtb_ref, rowp_ref, colp_ref,
    hv, ov, wv, wov, stage, zv, uv, dv, par, par_f, state, ext, st_v,
    h_send, h_recv, o_send, o_recv, z_up, z_dn, z_recv, s_send, s_recv,
    c_up, c_dn, c_recv, t_send, t_recv, a_send, a_recv, local_sem, out_sem, scan_sem, st_sem, *, heads, wide,
):
    ring = True
    s = lax.axis_index("seq")
    q = hid_ref.shape[0]
    half = q // 2
    x_peer = s + 1 - 2 * lax.rem(s, 2)
    y_peer = lax.rem(s + 2, 4)
    far = 3 - s
    to_x, to_y = {"seq": x_peer}, {"seq": y_peer}
    chans = uv.shape[1]
    n_main = stage.shape[1]
    n = stage.shape[0]
    peers = [to_x, to_y]

    def block(ref, at, start, size):
        return ref.at[pl.ds(pl.multiple_of(at * q + start, 16), size), :]

    if ring:
        h = lax.axis_index("head")
        core = lax.rem(h, 2)
        r = h // 2
        last = lax.axis_size("head") // 2 - 1
        to_sib, to_up, to_down = {"head": h + 1 - 2 * core}, {"head": lax.rem(h + 2, 2 * last + 2)}, {"head": lax.rem(h + 2 * last, 2 * last + 2)}
        above, below = r < last, r > 0
        owners = lax.axis_size("head")
        to_heads = [{"head": lax.rem(h + k, owners)} for k in range(1, owners)]
        peers += to_heads
        first = pl.multiple_of(s * wide, LANES)
        second = pl.multiple_of(DI + s * wide, LANES)
        loads = [
            pltpu.make_async_copy(w_ref.at[:, pl.ds(first, wide)], stage.at[:, :wide], local_sem.at[0]),
            pltpu.make_async_copy(w_ref.at[:, pl.ds(second, wide)], stage.at[:, wide : 2 * wide], local_sem.at[1]),
            pltpu.make_async_copy(w_ref.at[:, 2 * DI :], stage.at[:, 2 * wide :], local_sem.at[2]),
        ]
        is_root = r == s
        n_o = wov.shape[0] // 2
        load_o = pltpu.make_async_copy(
            wo_in_ref, wov.at[pl.ds(pl.multiple_of(core * n_o, 16), n_o), :], local_sem.at[5]
        )
        pl.when(is_root)(load_o.start)
    for copy in loads:
        copy.start()
    own_h = pltpu.make_async_copy(hid_ref, block(hv, s, 0, q), local_sem.at[3])
    own_o = pltpu.make_async_copy(og_ref, block(ov, s, 0, q), local_sem.at[4])
    own_h.start()
    own_o.start()
    par_f[...] = jnp.zeros_like(par_f)
    par_f[0:KERNEL, : cwt_ref.shape[1]] = cwt_ref[...].astype(F32)
    for k, row in enumerate((cbi_ref, ggn_ref, hds_ref)):
        par_f[KERNEL + k : KERNEL + k + 1, : row.shape[1]] = row[...].astype(F32)
    par[h] = par_f[...].astype(BF16)
    greet(peers)

    sent = []

    def send(src, dst, sems, i, target):
        copy = remote(src, dst, sems[0].at[i], sems[1].at[i], target)
        copy.start()
        sent.append(copy)
        return copy

    def open_exchange(src, buf, sems):
        return (
            send(src, block(buf, s, 0, q), sems, 0, to_x),
            send(src, block(buf, s, 0, q), sems, 1, to_y),
        )

    def relay(buf, sems, heads_in):
        heads_in[0].wait_recv()
        a = block(buf, x_peer, 0, half)
        first = send(a, a, sems, 2, to_y)
        heads_in[1].wait_recv()
        b = block(buf, y_peer, half, half)
        return first, send(b, b, sems, 3, to_x)

    h_sems, o_sems = (h_send, h_recv), (o_send, o_recv)
    h_open = open_exchange(hid_ref, hv, h_sems)
    pars = [send(par.at[h], par.at[h], (a_send, a_recv), k, peer) for k, peer in enumerate(to_heads)]

    closing = []
    if ring:
        def w_block(at):
            return wv.at[pl.ds(pl.multiple_of((2 * at + core) * n, 16), n), :]

        def w_copy(at, sems, target):
            return remote(w_block(at), w_block(at), sems.at[at], z_recv.at[at], target)

        def w_swap(at):
            return remote(w_block(at), w_block(at), s_send.at[at], s_recv.at[at], to_sib)

        def launch(there, make):
            @pl.when(there)
            def _():
                make().start()

            def finish():
                @pl.when(there)
                def _():
                    make().wait_send()

            closing.append(finish)

        always = r >= 0

        def w_step(k):
            lower, upper = r - k, r + k
            has_lower, has_upper = lower >= 0, upper <= last

            @pl.when(has_lower)
            def _():
                w_copy(lower, z_up, to_up).wait_recv()

            launch(has_lower & above, lambda: w_copy(lower, z_up, to_up))
            launch(has_lower, lambda: w_swap(lower))

            @pl.when(has_upper)
            def _():
                w_copy(upper, z_dn, to_down).wait_recv()

            launch(has_upper & below, lambda: w_copy(upper, z_dn, to_down))
            launch(has_upper, lambda: w_swap(upper))

        chunks = c_recv.shape[0]
        n_c = n_o // chunks
        dist = jnp.where(r > s, r - s, s - r)
        ending = (r == 0) | (r == last)

        def o_block(i):
            return wov.at[pl.ds(pl.multiple_of(core * n_o + i * n_c, 16), n_c), :]

        def o_copy(i, sems, target):
            return remote(o_block(i), o_block(i), sems.at[i], c_recv.at[i], target)

        def o_swap(i):
            return remote(o_block(i), o_block(i), t_send.at[i], t_recv.at[i], to_sib)

        def o_root():
            @pl.when(is_root)
            def _():
                load_o.wait()

            for i in range(chunks):
                pl.when(is_root & above & (r != 2))(lambda i=i: o_copy(i, c_up, to_up).start())
                pl.when(is_root & below & (r != 1))(lambda i=i: o_copy(i, c_dn, to_down).start())
                pl.when(is_root)(lambda i=i: o_swap(i).start())

        def o_root_late():
            for i in range(chunks):
                pl.when(is_root & (r == 2))(lambda i=i: o_copy(i, c_up, to_up).start())
                pl.when(is_root & (r == 1))(lambda i=i: o_copy(i, c_dn, to_down).start())

        def o_tick(t):
            i = t - dist
            live = (dist >= 1) & (i >= 0) & (i < chunks) & jnp.logical_not(ending)

            @pl.when(live)
            def _():
                o_copy(i, c_up, to_up).wait_recv()

            pl.when(live & (r > s) & above)(lambda: o_copy(i, c_up, to_up).start())
            pl.when(live & (r < s) & below)(lambda: o_copy(i, c_dn, to_down).start())
            pl.when(live)(lambda: o_swap(i).start())

        def o_rest():
            @pl.when(ending & (dist >= 1))
            def _():
                for i in range(chunks):
                    o_copy(i, c_up, to_up).wait_recv()
                    o_swap(i).start()

        def o_finish():
            for i in range(chunks):
                pl.when((r >= s) & above)(lambda: o_copy(i, c_up, to_up).wait_send())
                pl.when((r <= s) & below)(lambda: o_copy(i, c_dn, to_down).wait_send())
                o_swap(i).wait_send()

        for copy in loads:
            copy.wait()
        own = pl.ds(pl.multiple_of(h * n, 16), n)
        wv[own, :n_main] = (stage[...].astype(F32) * gain_ref[...].astype(F32)).astype(BF16)
        shape = (dtw_ref.shape[1], LANES)
        place = lax.broadcasted_iota(jnp.int32, shape, 1)
        taken = (lax.broadcasted_iota(jnp.int32, shape, 0) == place + s * heads) & (place < heads)
        own_dt = dot(dtw_ref[...], jnp.where(taken, 1.0, 0.0).astype(BF16))
        wv[own, n_main:] = (own_dt * gain_ref[...].astype(F32)).astype(BF16)
        launch(above, lambda: w_copy(r, z_up, to_up))
        launch(below, lambda: w_copy(r, z_dn, to_down))
        launch(always, lambda: w_swap(r))
        w_step(1)

    rows = min(CHUNK, q)

    def cut(at_block):
        return pl.ds(pl.multiple_of(at_block * q, 16), q)

    def project_outs(at_block, i):
        at = cut(at_block)
        pairs = ((hv, hall_ref), (zv, z_ref), (uv, u_ref))
        return [
            pltpu.make_async_copy(src.at[at, :], dst.at[at, :], out_sem.at[3 * i + k])
            for k, (src, dst) in enumerate(pairs)
        ]

    act_at, y_at = slice(0, chans), slice(chans, chans + wide)
    gg_at, d0_at = slice(0, wide), slice(wide, 2 * wide)

    def scan_outs(j):
        at = pl.ds(pl.multiple_of(j * rows, 16), rows)
        slot = lax.rem(j, 2)
        pairs = (
            (wv.at[at, act_at], act_ref), (wv.at[at, y_at], y_ref), (uv.at[at, :], slope_ref),
            (dv.at[at, :], aux_ref), (hv.at[at, gg_at], gg_ref),
        )
        copies = [pltpu.make_async_copy(src, dst.at[at, :], scan_sem.at[j, k]) for k, (src, dst) in enumerate(pairs)]
        return copies, pltpu.make_async_copy(st_v.at[slot], st_ref.at[j], st_sem.at[slot])

    def pull_outs(at_block, i):
        at = cut(at_block)
        pairs = ((ov.at[at, :], ogall_ref), (hv.at[at, d0_at], d0_ref))
        return [
            pltpu.make_async_copy(src, dst.at[at, :], out_sem.at[12 + 2 * i + k])
            for k, (src, dst) in enumerate(pairs)
        ]

    def nth(i):
        return jnp.where(i == 0, s, jnp.where(i == 1, x_peer, jnp.where(i == 2, y_peer, far)))

    w_out = pltpu.make_async_copy(wv, wt_ref, out_sem.at[20])
    o_out = pltpu.make_async_copy(wov, wo_ref, out_sem.at[21])

    width = wv.shape[0]
    strip = width // 4
    late_chip = jnp.where(r < 2, last, 0)
    early_k = pl.ds(pl.multiple_of(jnp.where(late_chip == 0, strip, 0), strip), 3 * strip)
    late_k = pl.ds(pl.multiple_of(late_chip * strip, strip), strip)

    def project(at_block, k, ahead):
        @pl.loop(0, q // rows)
        def _(j):
            at = pl.ds(pl.multiple_of(at_block * q + j * rows, 16), rows)
            hb = hv[at, k]
            z = dot(hb, wv[k, :wide])
            u = dot(hb, wv[k, wide : wide + chans])
            raw = dot(hb, wv[k, wide + chans :])
            if ahead:
                zv[at, :] = z.astype(BF16)
                uv[at, :] = u.astype(BF16)
                dv[at, :] = raw
            else:
                h32 = hv[at, :].astype(F32)
                r0 = lax.rsqrt(jnp.mean(h32 * h32, axis=1, keepdims=True) + EPS)
                zv[at, :] = ((z + zv[at, :].astype(F32)) * r0).astype(BF16)
                uv[at, :] = ((u + uv[at, :].astype(F32)) * r0).astype(BF16)
                raw = (raw + dv[at, :]) * r0
                lane = lax.broadcasted_iota(jnp.int32, raw.shape, 1)
                dv[at, :] = jnp.where(lane == LANES - 1, r0, raw)

    def pull(at_block):
        at = cut(at_block)

        @pl.loop(0, wide // 256)
        def _(j):
            from_o = pl.ds(pl.multiple_of(j * 256, 256), 256)
            to = pl.ds(pl.multiple_of(wide + j * 256, 256), 256)
            hv[at, to] = dot_t(ov[at, :], wov[from_o, :]).astype(BF16)

        @pl.loop(0, q // rows)
        def _(j):
            some = pl.ds(pl.multiple_of(at_block * q + j * rows, 16), rows)
            lanes = pl.ds(pl.multiple_of(at_block * q + j * rows, LANES), rows)
            sum_ref[:, lanes] = with_cross(sum_ref[:, lanes], hv[some, gg_at], hv[some, d0_at])

    h_far = relay(hv, h_sems, h_open)
    own_h.wait()
    own_o.wait()
    for copy in pars:
        copy.wait_recv()
    rank_params(par, s, cw_ref, dtb_ref, rowp_ref, colp_ref, heads, wide)
    w_step(2)
    o_root()
    for k in range(1, 4):
        w_swap(lax.rem(late_chip + k, 4)).wait_recv()
    project(s, early_k, True)
    project(x_peer, early_k, True)
    for copy in h_far:
        copy.wait_recv()
    o_open = open_exchange(og_ref, ov, o_sems)
    o_tick(1)

    @pl.loop(2, 4)
    def _(i):
        project(nth(i), early_k, True)
        o_tick(i)

    o_root_late()
    w_step(3)
    w_swap(late_chip).wait_recv()
    w_out.start()

    @pl.loop(0, 4)
    def _(i):
        at_block = nth(i)
        project(at_block, late_k, False)
        for copy in project_outs(at_block, i):
            copy.start()
        pl.when(i < 3)(lambda: o_tick(4 + i))

    for i, at_block in enumerate((s, x_peer, y_peer, far)):
        for copy in project_outs(at_block, i):
            copy.wait()
    w_out.wait()
    for copy in h_far:
        copy.wait_send()
    sent[:] = [copy for copy in sent if copy is not h_far[0] and copy is not h_far[1]]
    for finish in closing:
        finish()
    o_a, o_b = block(ov, x_peer, 0, half), block(ov, y_peer, half, half)
    o_far = [
        remote(o_a, o_a, o_send.at[2], o_recv.at[2], to_y),
        remote(o_b, o_b, o_send.at[3], o_recv.at[3], to_x),
    ]
    sent += o_far
    state[...] = jnp.zeros_like(state)
    ext[...] = jnp.zeros_like(ext)
    expand = head_matrix(wide)
    steps = 4 * q // rows

    @pl.loop(0, steps)
    def _(j):
        at = pl.ds(pl.multiple_of(j * rows, 16), rows)
        slot = lax.rem(j, 2)

        @pl.when(j >= 2)
        def _():
            scan_outs(j - 2)[1].wait()

        @pl.when(j == steps - 2)
        def _():
            for opened, copy in zip(o_open, o_far):
                opened.wait_recv()
                copy.start()

        act, slope, aux, y16, gg, ssq = scan_chunk(
            uv[at, :], dv[at, :], zv[at, :], cw_ref[0:KERNEL, :], cw_ref[KERNEL : KERNEL + 1, :], dtb_ref[0:1, :],
            expand, rowp_ref[...], colp_ref[:, 0:1], state, ext, st_v.at[slot], heads,
        )
        wv[at, act_at] = act
        wv[at, y_at] = y16
        uv[at, :] = slope
        dv[at, :] = aux
        hv[at, gg_at] = gg
        sum_ref[:, pl.ds(pl.multiple_of(j * rows, LANES), rows)] = ssq
        copies, st_copy = scan_outs(j)
        for copy in copies:
            copy.start()
        st_copy.start()
        pl.when(lax.rem(j, 2) == 0)(lambda: o_tick(7 + j // 2))

    o_rest()
    for i in range(chunks):
        o_swap(i).wait_recv()
    o_out.start()

    @pl.loop(0, 4)
    def _(i):
        at_block = nth(i)

        @pl.when(i == 3)
        def _():
            for copy in o_far:
                copy.wait_recv()

        pull(at_block)
        for copy in pull_outs(at_block, i):
            copy.start()

    for i, at_block in enumerate((s, x_peer, y_peer, far)):
        for copy in pull_outs(at_block, i):
            copy.wait()

    @pl.loop(0, steps)
    def _(j):
        for copy in scan_outs(j)[0]:
            copy.wait()

    for j in (steps - 2, steps - 1):
        scan_outs(j)[1].wait()
    o_out.wait()
    for copy in sent:
        copy.wait_send()
    o_finish()


def line_sum(own, z_u, z_d, sems, r, last, to_up, to_down, join, closing):
    zu_send, zu_recv, zd_send, zd_recv = sems

    def up_copy(t):
        return remote(own.at[t], z_u.at[t - 1], zu_send.at[t], zu_recv.at[t], to_up)

    def down_copy(t):
        return remote(own.at[t], z_d.at[t], zd_send.at[t], zd_recv.at[t], to_down)

    def up_add(t):
        up_copy(t).wait_recv()
        join(t, z_u.at[t - 1])

    def down_add(t):
        down_copy(t).wait_recv()
        join(t, z_d.at[t])

    def sent_later(t, there, make):
        closing.append(lambda: pl.when(there)(lambda: make(t).wait_send()))

    def pass_on(t, there, add, make):
        @pl.when(there)
        def _():
            add(t)
            make(t).start()

        sent_later(t, there, make)

    def follow(t, there, make, before):
        @pl.when(there)
        def _():
            make(before).wait_send()
            make(t).start()

    def start():
        pl.when(r == 0)(lambda: up_copy(last).start())
        pl.when(r == last)(lambda: down_copy(0).start())

    def second():
        follow(2, r == 0, up_copy, last)
        follow(1, r == last, down_copy, 0)
        pass_on(last, r == 1, up_add, up_copy)
        pass_on(0, r == 2, down_add, down_copy)

    def across():
        pass_on(last, r == 2, up_add, up_copy)
        pass_on(0, r == 1, down_add, down_copy)

    def third():
        follow(1, r == 0, up_copy, 2)
        follow(2, r == last, down_copy, 1)
        pass_on(2, r == 1, up_add, up_copy)
        pass_on(1, r == 2, down_add, down_copy)
        sent_later(1, r == 0, up_copy)
        sent_later(2, r == last, down_copy)

    def final():
        pl.when(r > 0)(lambda: up_add(r))
        pl.when(r < last)(lambda: down_add(r))

    return start, second, across, third, final


def mid_kernel(
    gg_ref, wo_ref, og_ref, h_ref, act_ref, aux_ref, z_ref, d0_ref, y_ref, sums_ref, mask_ref, rowp_ref,
    br_ref, wog_ref, dy_ref, dpg_ref, gate_ref,
    stat_v, ggv, wov, ogv, far_p, y_p, x_p, own_p, far_a, far_b, y_f, x_f, sv,
    ow, other, other_in, z_u, z_d, part_s, xin, zin, din, yin, ain, dyo, hb, rows_s,
    load_sem, d_send, d_recv, s_send, s_recv, c_send, c_recv, zu_send, zu_recv, zd_send, zd_recv,
    in_sem, dy_sem, hb_sem, rows_sem, out_sem, *, ring,
):
    s = lax.axis_index("seq")
    tokens, wide = ggv.shape
    width = wov.shape[1]
    q = far_p.shape[0]
    half = q // 2
    rows = min(CHUNK, q)
    tile = 256
    x_peer = s + 1 - 2 * lax.rem(s, 2)
    y_peer = lax.rem(s + 2, 4)
    far = 3 - s
    to_x, to_y, to_far = {"seq": x_peer}, {"seq": y_peer}, {"seq": far}
    load_gg = pltpu.make_async_copy(gg_ref, ggv, load_sem.at[0])
    load_wo = pltpu.make_async_copy(wo_ref, wov, load_sem.at[1])
    cut = ogv.shape[1]

    def load_og(d):
        return pltpu.make_async_copy(og_ref.at[:, d * cut : (d + 1) * cut], ogv, load_sem.at[2])

    def load_chunk(i):
        at = pl.ds(pl.multiple_of(i * rows, 16), rows)
        slot = lax.rem(i, 2)
        pairs = ((act_ref.at[at, :wide], xin), (z_ref.at[at, :], zin), (d0_ref.at[at, :], din), (y_ref.at[at, :], yin), (aux_ref.at[at, :], ain))
        return [pltpu.make_async_copy(src, dst.at[slot], in_sem.at[slot, k]) for k, (src, dst) in enumerate(pairs)]

    def load_h(i):
        slot = lax.rem(i, 2)
        return pltpu.make_async_copy(h_ref.at[:, pl.ds(pl.multiple_of(i * tile, tile), tile)], hb.at[slot], hb_sem.at[slot])

    load_gg.start()
    load_wo.start()
    load_og(0).start()
    peers = [to_x, to_y, to_far]
    extra = []
    closing = []
    if ring:
        h = lax.axis_index("head")
        owners = lax.axis_size("head")
        last = owners // 2 - 1
        core = lax.rem(h, 2)
        r = h // 2
        to_sib = {"head": h + 1 - 2 * core}
        to_up, to_down = {"head": lax.rem(h + 2, owners)}, {"head": lax.rem(h + owners - 2, owners)}
        peers.append(to_sib)
        extra = [(r < last, to_up), (r > 0, to_down)]

        def join(t, more):
            ow[t] = (ow[t].astype(F32) + more[...].astype(F32)).astype(BF16)

        start, second, across, third, final = line_sum(
            ow, z_u, z_d, (zu_send, zu_recv, zd_send, zd_recv), r, last, to_up, to_down, join, closing
        )
    sv[s] = sums_ref[...]
    greet(peers, extra)
    sums = [
        remote(sums_ref, sv.at[s], s_send.at[i], s_recv.at[i], peer) for i, peer in enumerate((to_x, to_y, to_far))
    ]
    for copy in sums:
        copy.start()
    for i in (0, 1):
        for copy in load_chunk(i):
            copy.start()
    load_h(0).start()
    load_h(1).start()
    load_gg.wait()
    load_wo.wait()

    def part(block, out):
        @pl.loop(0, q // rows)
        def _(j):
            at = pl.ds(pl.multiple_of(block * q + j * rows, 16), rows)
            to = pl.ds(pl.multiple_of(j * rows, 16), rows)
            out[to, :] = dot(ggv[at, :], wov[...]).astype(BF16)

    def d_copy(src, dst, i, target):
        copy = remote(src, dst, d_send.at[i], d_recv.at[i], target)
        copy.start()
        return copy

    part(far, far_p)
    d0 = d_copy(far_p.at[:half], far_a, 0, to_x)
    d1 = d_copy(far_p.at[half:], far_b, 1, to_y)
    part(y_peer, y_p)
    d2 = d_copy(y_p.at[half:], y_f.at[half:], 2, to_y)
    part(x_peer, x_p)
    d3 = d_copy(x_p.at[:half], x_f.at[:half], 3, to_x)
    part(s, own_p)

    for copy in sums:
        copy.wait_recv()
    total = (sv[0] + sv[1]) + (sv[2] + sv[3])
    r1 = lax.rsqrt(total[0:1] / DI + EPS)
    r1m = r1 * mask_ref[0:1]
    coef = r1m * r1 * r1 * total[1:2] / DI
    sub = lax.broadcasted_iota(jnp.int32, (LANES, tokens), 0)
    stat_v[...] = jnp.where(sub == 0, r1m, jnp.where(sub == 1, coef, 0.0)).T

    @pl.loop(0, tokens // rows)
    def _(j):
        at = pl.ds(pl.multiple_of(j * rows, 16), rows)
        ggv[at, :] = (ggv[at, :].astype(F32) * stat_v[at, 0:1]).astype(BF16)

    def w_rows(d):
        to = slice(d * cut, (d + 1) * cut)

        @pl.loop(0, wide // tile)
        def _(m):
            at = pl.ds(pl.multiple_of(m * tile, tile), tile)
            got = t_dot(ggv[:, at], ogv[...]).astype(BF16)
            if ring:
                piece = ow.shape[2]
                chips = tile // (2 * piece)
                groups = wide // 2 // tile
                part_s[...] = got.reshape(part_s.shape)
                first = pl.ds(lax.rem(m, groups) * chips, chips)
                ow[first, m // groups, :, to] = part_s[:, core]
                other[first, m // groups, :, to] = part_s[:, 1 - core]
            else:
                rows_s[0, :, : got.shape[1]] = got
                copy = pltpu.make_async_copy(rows_s.at[0], wog_ref.at[at, to], out_sem.at[0])
                copy.start()
                copy.wait()

    load_og(0).wait()
    w_rows(0)
    load_og(1).start()
    load_og(1).wait()
    w_rows(1)
    if ring:
        swap = remote(other, other_in, c_send.at[0], c_recv.at[0], to_sib)
        swap.start()
        swap.wait_recv()

        @pl.loop(0, 4)
        def _(t):
            join(t, other_in.at[t])

        start()
    d0.wait_recv()
    y_p[:half, :] = (y_p[:half, :].astype(F32) + far_a[...].astype(F32)).astype(BF16)
    d4 = d_copy(y_p.at[:half], y_f.at[:half], 4, to_y)
    d1.wait_recv()
    x_p[half:, :] = (x_p[half:, :].astype(F32) + far_b[...].astype(F32)).astype(BF16)
    d5 = d_copy(x_p.at[half:], x_f.at[half:], 5, to_x)

    def dy_out(i):
        at = pl.ds(pl.multiple_of(i * rows, 16), rows)
        return pltpu.make_async_copy(dyo.at[lax.rem(i, 2)], dy_ref.at[at, :], dy_sem.at[lax.rem(i, 2)])

    chunks = tokens // rows

    def gate_chunk(i):
        slot = lax.rem(i, 2)
        at = pl.ds(pl.multiple_of(i * rows, 16), rows)
        for copy in load_chunk(i):
            copy.wait()
        r0 = ain[slot, :, LANES - 1 : LANES]
        ssd = (yin[slot].astype(F32) + rowp_ref[1:2, :] * xin[slot].astype(F32)).astype(BF16).astype(F32)
        z = zin[slot].astype(F32)
        sig = sigmoid(z)
        sz = z * sig
        d_gated = (stat_v[at, 0:1] * rowp_ref[2:3, :]) * din[slot].astype(F32) - (ssd * sz) * stat_v[at, 1:2]

        @pl.when(i >= 2)
        def _():
            dy_out(i - 2).wait()

        dyo[slot] = (d_gated * sz).astype(BF16)
        dy_out(i).start()
        ggv[at, :] = (r0 * (d_gated * ssd * (sig * (1.0 + z * (1.0 - sig))))).astype(BF16)

        @pl.when(i + 2 < chunks)
        def _():
            for copy in load_chunk(i + 2):
                copy.start()

    pl.loop(0, chunks - 1)(gate_chunk)
    if ring:
        second()
    pl.loop(chunks - 1, chunks)(gate_chunk)
    dpg_out = pltpu.make_async_copy(ggv, dpg_ref, out_sem.at[1])
    dpg_out.start()

    def rows_out(i):
        slot = lax.rem(i, 2)
        at = pl.ds(pl.multiple_of(i * tile, tile), tile)
        return pltpu.make_async_copy(rows_s.at[slot], gate_ref.at[at, :], rows_sem.at[slot])

    blocks = width // tile

    def gate_rows(i):
        slot = lax.rem(i, 2)
        load_h(i).wait()
        got = t_dot(hb[slot], ggv[...]).astype(BF16)

        @pl.when(i >= 2)
        def _():
            rows_out(i - 2).wait()

        rows_s[slot] = got
        rows_out(i).start()

        @pl.when(i + 2 < blocks)
        def _():
            load_h(i + 2).start()

    pl.loop(0, blocks // 2)(gate_rows)
    if ring:
        across()
        third()
    pl.loop(blocks // 2, blocks)(gate_rows)
    if ring:
        final()
        wog_out = pltpu.make_async_copy(ow.at[r], wog_ref, out_sem.at[0])
        wog_out.start()
    for copy in (d2, d3, d4, d5):
        copy.wait_recv()

    @pl.loop(0, q // 128)
    def _(j):
        at = pl.ds(pl.multiple_of(j * 128, 128), 128)
        whole = own_p[at, :].astype(F32) + y_f[at, :].astype(F32) + x_f[at, :].astype(F32)
        own_p[at, :] = (whole * stat_v[pl.ds(pl.multiple_of(s * q + j * 128, 128), 128), 0:1]).astype(BF16)

    br_out = pltpu.make_async_copy(own_p, br_ref, out_sem.at[2])
    br_out.start()
    for i in (chunks - 2, chunks - 1):
        dy_out(i).wait()
    for i in (blocks - 2, blocks - 1):
        rows_out(i).wait()
    dpg_out.wait()
    br_out.wait()
    for copy in sums + [d0, d1, d2, d3, d4, d5]:
        copy.wait_send()
    if ring:
        wog_out.wait()
        swap.wait_send()
    for finish in closing:
        finish()


def back_kernel(
    act_ref, aux_ref, dy_ref, y_ref, st_ref, slope_ref, u_ref, piece_ref,
    rowp_ref, colp_ref, cw_ref,
    dp_ref, sm_ref, all_ref, adj, ext, exp_v, seg_v, b_send, b_recv, b_load, *, heads, wide, ring,
):
    step = pl.program_id(0)
    steps = pl.num_programs(0)
    rows = act_ref.shape[0]
    chans = u_ref.shape[1]

    if ring:
        s = lax.axis_index("seq")
        x_peer = s + 1 - 2 * lax.rem(s, 2)
        y_peer = lax.rem(s + 2, 4)
        to_x, to_y = {"seq": x_peer}, {"seq": y_peer}
        from_x, from_y = all_ref.at[x_peer, 0], all_ref.at[y_peer, 1]
        moves = [
            remote(piece_ref, all_ref.at[s], b_send.at[0], b_recv.at[0], to_x),
            remote(piece_ref, all_ref.at[s], b_send.at[1], b_recv.at[1], to_y),
            remote(from_x, from_x, b_send.at[2], b_recv.at[2], to_y),
            remote(from_y, from_y, b_send.at[3], b_recv.at[3], to_x),
        ]
        own_piece = pltpu.make_async_copy(piece_ref, all_ref.at[s], b_load.at[0])

        @pl.when(step == 0)
        def _():
            greet([to_x, to_y])
            moves[0].start()
            moves[1].start()
            own_piece.start()

        @pl.when(step == 3)
        def _():
            moves[0].wait_recv()
            moves[2].start()
            moves[1].wait_recv()
            moves[3].start()

    @pl.when(step == 0)
    def _():
        sm_ref[...] = jnp.zeros_like(sm_ref)
        adj[...] = jnp.zeros_like(adj)
        exp_v[...] = head_matrix(wide)
        seg_v[...] = head_matrix(wide, True)
        ext[...] = jnp.zeros_like(ext)

    x = act_ref[:, :wide]
    x32 = x.astype(F32)
    b = act_ref[:, wide : wide + STATE]
    c = act_ref[:, wide + STATE :]
    aux = aux_ref[...]
    r0 = aux[:, LANES - 1 : LANES]
    skip_e = rowp_ref[1:2, :]
    y = y_ref[...].astype(F32)
    dy16 = dy_ref[...]
    dy = dy16.astype(F32)

    causal, dt_e, cum_e, cum_c, cum_t = decays(
        aux, heads, exp_v[...], rowp_ref[0:1, :], rowp_ref[3:4, :LANES], colp_ref[:, 0:1]
    )
    xdt = x32 * dt_e
    xdt16 = xdt.astype(BF16)
    scores = dot_t(c, b)
    st = st_ref[0]
    st16 = st.astype(BF16)
    q_in = adj[...]
    q16 = q_in.astype(BF16)
    last = cum_e[rows - 1 : rows, :]
    ecum = jnp.exp(cum_e)
    tail = jnp.exp(last - cum_e)
    half = lax.broadcasted_iota(jnp.int32, (rows, LANES), 1) < HEAD_DIM
    zero = jnp.zeros((rows, LANES), BF16)
    mid = rows // 2
    n_sum = None
    parts = []
    for pair in range(heads // 2):
        cut = slice(LANES * pair, LANES * (pair + 1))
        x2 = xdt16[:, cut]
        dy2 = dy16[:, cut]
        got = []
        for side in range(2):
            h = 2 * pair + side
            top, low, right = lower_parts(cum_c, cum_t, h, causal)
            m_top = (scores[:mid, :mid] * top).astype(BF16)
            m_low = (scores[mid:, :mid] * low).astype(BF16)
            m_right = (scores[mid:, mid:] * right).astype(BF16)
            v_top = t_dot(jnp.concatenate([m_top, m_low], axis=0), dy2)
            got.append(jnp.concatenate([v_top, t_dot(m_right, dy2[mid:])], axis=0))
            own = half if side == 0 else jnp.logical_not(half)
            dy_own = jnp.where(own, dy2, zero)
            g_top = dot_t(dy_own[:mid], x2[:mid])
            g_low = dot_t(dy_own[mid:], x2)
            n = [g_top * top, g_low[:, :mid] * low, g_low[:, mid:] * right]
            n_sum = n if n_sum is None else [p + v for p, v in zip(n_sum, n)]
        parts.append(jnp.where(half, got[0], got[1]))
    n_low = jnp.concatenate([n_sum[1], n_sum[2]], axis=1).astype(BF16)
    n_top = n_sum[0].astype(BF16)
    out_part = dot(b, q16) * tail
    v = jnp.concatenate(parts, axis=1) + out_part
    dy_e = (dy * ecum).astype(BF16)
    x_tail = (xdt * tail).astype(BF16)
    d_b = jnp.concatenate([t_dot(jnp.concatenate([n_top, n_low[:, :mid]], axis=0), c), t_dot(n_low[:, mid:], c[mid:])], axis=0)
    d_b = d_b + dot_t(x_tail, q16)
    d_c = jnp.concatenate([dot(n_top, b[:mid]), dot(n_low, b)], axis=0) + dot_t(dy_e, st16)
    elast = jnp.exp(last)
    adj[...] = elast * q_in + t_dot(c, dy_e)

    seg = seg_v[...]
    flow = dy * y - xdt16.astype(F32) * v
    passed = jnp.sum(xdt16.astype(F32) * out_part, axis=0, keepdims=True)
    passed = passed + elast * jnp.sum(q_in * st, axis=0, keepdims=True)
    flow_h = seg_dot(flow, seg)
    passed_h = seg_dot(jnp.broadcast_to(passed, (8, wide)), seg)[0:1, :]
    upper = jnp.where(
        lax.broadcasted_iota(jnp.int32, (rows, rows), 1) >= lax.broadcasted_iota(jnp.int32, (rows, rows), 0), 1.0, 0.0
    ).astype(BF16)
    hi = flow_h.astype(BF16)
    rest = flow_h - hi.astype(F32)
    mid = rest.astype(BF16)
    low = (rest - mid.astype(F32)).astype(BF16)
    crossing = dot(upper, hi) + dot(upper, mid) + dot(upper, low) + passed_h
    rate_row = rowp_ref[3:4, :LANES]
    decay_grad = rate_row * crossing
    d_dt = dot((x32 * v).astype(BF16), seg) + decay_grad
    lane = lax.broadcasted_iota(jnp.int32, (rows, LANES), 1)
    sig_v = pltpu.roll(aux, LANES - heads, 1)
    d_pre = jnp.where(lane < heads, d_dt * sig_v, 0.0)
    dt = jnp.where(lane < heads, aux, 0.0)
    dp_ref[:, chans:] = (r0 * d_pre).astype(BF16)

    d_act = jnp.concatenate([skip_e * dy + dt_e * v, d_b, d_c], axis=1)
    d_conv = d_act * slope_ref[...].astype(F32)
    d_conv16 = d_conv.astype(BF16)
    u = u_ref[...].astype(F32)
    d_u = cw_ref[KERNEL - 1 : KERNEL, :] * d_conv
    sm_ref[KERNEL - 1 : KERNEL, :] += jnp.sum(u * d_conv, axis=0, keepdims=True)
    for j in range(1, KERNEL):
        k = KERNEL - 1 - j
        moved = dot(shift_matrix(rows, j), d_conv16)
        moved = jnp.concatenate([moved[: rows - 8], moved[rows - 8 :] + ext[j : j + 8, :]], axis=0)
        d_u = d_u + cw_ref[k : k + 1, :] * moved
        sm_ref[k : k + 1, :] += jnp.sum(u * moved, axis=0, keepdims=True)
    ext[8:16, :] = d_conv[0:8, :]
    dp_ref[:, :chans] = (r0 * d_u).astype(BF16)
    sm_ref[4:5, :] += jnp.sum(d_conv, axis=0, keepdims=True)
    sm_ref[5:6, :wide] += jnp.sum(x32 * dy, axis=0, keepdims=True)
    sm_ref[6:7, :LANES] += jnp.sum(d_pre, axis=0, keepdims=True)
    sm_ref[7:8, :LANES] += jnp.sum(dt * decay_grad, axis=0, keepdims=True)

    if ring:
        @pl.when(step == steps - 1)
        def _():
            moves[2].wait_recv()
            moves[3].wait_recv()
            for copy in moves:
                copy.wait_send()
            own_piece.wait()


def grads_kernel(
    dpg_ref, dp_ref, w_ref, h_ref, gate_ref, piece_ref, sm_ref,
    dn_ref, wing_ref, win_ref, wout_ref,
    dpv, wv, hb, tiny_f, tiny_v, far_p, y_p, x_p, far_a, far_b, y_f, x_f, sib_s, mine_s, own_s, z_u, z_d,
    load_sem, hb_sem, d_send, d_recv, s_send, s_recv, zu_send, zu_recv, zd_send, zd_recv,
    g_send, g_recv, k_send, k_recv, p_send, p_recv, out_sem,
):
    s = lax.axis_index("seq")
    h = lax.axis_index("head")
    owners = lax.axis_size("head")
    last = owners // 2 - 1
    core = lax.rem(h, 2)
    r = h // 2
    x_peer = s + 1 - 2 * lax.rem(s, 2)
    y_peer = lax.rem(s + 2, 4)
    far = 3 - s
    to_x, to_y = {"seq": x_peer}, {"seq": y_peer}
    to_sib = {"head": h + 1 - 2 * core}
    to_up, to_down = {"head": lax.rem(h + 2, owners)}, {"head": lax.rem(h + owners - 2, owners)}
    above, below = r < last, r > 0
    q = far_p.shape[0]
    half = q // 2
    n, cols = own_s.shape[1], own_s.shape[2]
    spare = LANES // 2
    tiles = cols // LANES
    edges = [LANES * (tiles * k // 4) for k in range(5)]
    spans = list(zip(edges[:-1], edges[1:]))
    sent = []
    closing = []

    def push(src, dst, sems, i, target):
        copy = remote(src, dst, sems[0].at[i], sems[1].at[i], target)
        copy.start()
        sent.append(copy)
        return copy

    def launch(there, make):
        @pl.when(there)
        def _():
            make().start()

        def finish():
            @pl.when(there)
            def _():
                make().wait_send()

        closing.append(finish)

    skip = dpv.shape[1] - cols
    load_dp = pltpu.make_async_copy(dp_ref, dpv.at[:, skip:], load_sem.at[0])
    load_w = pltpu.make_async_copy(w_ref, wv, load_sem.at[1])
    load_g = pltpu.make_async_copy(dpg_ref, dpv.at[:, :skip], load_sem.at[4])
    own_gate = pltpu.make_async_copy(gate_ref, wing_ref.at[s], load_sem.at[5])
    load_dp.start()
    load_g.start()
    load_w.start()
    own_gate.start()

    def chip(i):
        return jnp.where(lax.rem(i, 2) == 0, last - i // 2, i // 2)

    def load_h(i, other):
        at = 2 * chip(i) + (1 - core if other else core)
        slot = 0 if other else 1
        return pltpu.make_async_copy(
            h_ref.at[:, pl.ds(pl.multiple_of(at * n, LANES), n)], hb.at[slot], hb_sem.at[slot]
        )

    load_h(0, True).start()
    load_h(0, False).start()

    tiny_f[...] = jnp.zeros_like(tiny_f)
    for k in range(sm_ref.shape[1] // spare):
        tiny_f[8 * k : 8 * k + 8, :] = sm_ref[:, spare * k : spare * (k + 1)]
    tiny_v[...] = tiny_f[...].astype(BF16)
    to_heads = [{"head": lax.rem(h + k, owners)} for k in range(1, owners)]
    greet([to_x, to_y] + to_heads)

    d_sems = (d_send, d_recv)
    g_sems = (g_send, g_recv)

    k_sems = (k_send, k_recv)
    k0 = push(gate_ref, wing_ref.at[s], k_sems, 0, to_x)
    k1 = push(gate_ref, wing_ref.at[s], k_sems, 1, to_y)
    tile = 256

    def part(block, out):
        at = pl.ds(pl.multiple_of(block * q, 16), q)

        @pl.loop(0, wv.shape[0] // tile)
        def _(j):
            to = pl.ds(pl.multiple_of(j * tile, tile), tile)
            out[:, to] = dot_t(dpv[at, :], wv[to, :]).astype(BF16)

    def add_to(out, at, extra):
        out[at, :] = (out[at, :].astype(F32) + extra.astype(F32)).astype(BF16)

    def swap(i):
        t = chip(i)
        return remote(sib_s.at[lax.rem(i, 2)], own_s.at[t], s_send.at[t], s_recv.at[t], to_sib)

    def rows_of(i):
        t = chip(i)
        slot = lax.rem(i, 2)

        @pl.when(i >= 2)
        def _():
            swap(i - 2).wait_send()

        load_h(i, True).wait()
        for lo, hi in spans:
            sib_s[slot, :, lo:hi] = t_dot(hb[0], dpv[:, skip + lo : skip + hi]).astype(BF16)
        sib_s[slot, :, cols - spare :] = tiny_v[...]
        swap(i).start()

        @pl.when(i < 3)
        def _():
            load_h(i + 1, True).start()

        load_h(i, False).wait()
        for lo, hi in spans:
            mine_s[:, lo:hi] = t_dot(hb[1], dpv[:, skip + lo : skip + hi]).astype(BF16)
        mine_s[:, cols - spare :] = tiny_v[...]

        @pl.when(i < 3)
        def _():
            load_h(i + 1, False).start()

        swap(i).wait_recv()
        join(t, mine_s)

    def join(t, extra):
        for lo, hi in spans:
            own_s[t, :, lo:hi] = (own_s[t, :, lo:hi].astype(F32) + extra[:, lo:hi].astype(F32)).astype(BF16)

    start, second, across, third, final = line_sum(
        own_s, z_u, z_d, (zu_send, zu_recv, zd_send, zd_recv), r, last, to_up, to_down, join, closing
    )

    load_dp.wait()
    load_g.wait()
    load_w.wait()
    part(far, far_p)
    d0 = push(far_p.at[:half], far_a, d_sems, 0, to_x)
    d1 = push(far_p.at[half:], far_b, d_sems, 1, to_y)
    pl.loop(0, 2)(rows_of)
    start()
    k0.wait_recv()
    gate_a = wing_ref.at[x_peer, : n // 2]
    k2 = push(gate_a, gate_a, k_sems, 2, to_y)
    k1.wait_recv()
    gate_b = wing_ref.at[y_peer, n // 2 :]
    k3 = push(gate_b, gate_b, k_sems, 3, to_x)
    pl.loop(2, 4)(rows_of)
    part(y_peer, y_p)
    d2 = push(y_p.at[half:], y_f.at[half:], d_sems, 2, to_y)
    second()
    part(x_peer, x_p)
    d3 = push(x_p.at[:half], x_f.at[:half], d_sems, 3, to_x)
    d0.wait_recv()
    add_to(y_p, slice(0, half), far_a[...])
    d4 = push(y_p.at[:half], y_f.at[:half], d_sems, 4, to_y)
    d1.wait_recv()
    add_to(x_p, slice(half, q), far_b[...])
    d5 = push(x_p.at[half:], x_f.at[half:], d_sems, 5, to_x)
    across()
    third()
    d0.wait_send()
    d1.wait_send()
    part(s, far_p)
    final()

    red = own_s.at[r]
    g0 = push(red, win_ref.at[s], g_sems, 0, to_x)
    g1 = push(red, win_ref.at[s], g_sems, 1, to_y)
    own_win = pltpu.make_async_copy(red, win_ref.at[s], load_sem.at[3])
    own_win.start()
    per = owners // 4

    def piece_of(head):
        return piece_ref.at[head // per, lax.rem(head, per)]

    pieces = []
    for k, peer in enumerate(to_heads):
        pieces.append(push(piece_of(peer["head"]), wout_ref.at[h], (p_send, p_recv), k, peer))
    own_piece = pltpu.make_async_copy(piece_of(h), wout_ref.at[h], load_sem.at[2])
    own_piece.start()

    g0.wait_recv()
    part_a = win_ref.at[x_peer, : n // 2]
    g2 = push(part_a, part_a, g_sems, 2, to_y)
    g1.wait_recv()
    part_b = win_ref.at[y_peer, n // 2 :]
    g3 = push(part_b, part_b, g_sems, 3, to_x)

    for copy in (d2, d3, d4, d5):
        copy.wait_recv()
    far_p[...] = (far_p[...].astype(F32) + y_f[...].astype(F32) + x_f[...].astype(F32)).astype(BF16)
    dn_out = pltpu.make_async_copy(far_p, dn_ref, out_sem.at[0])
    dn_out.start()
    dn_out.wait()
    own_win.wait()
    own_gate.wait()
    own_piece.wait()
    k2.wait_recv()
    k3.wait_recv()
    for copy in pieces:
        copy.wait_recv()
    g2.wait_recv()
    g3.wait_recv()
    for i in (2, 3):
        swap(i).wait_send()
    for copy in sent:
        if copy is not d0 and copy is not d1:
            copy.wait_send()
    for finish in closing:
        finish()


def finish_kernel(
    gate_ref, rest_ref, w_ref, dtw_ref, gain_ref, wog_ref, wo_ref, hid_ref, og_ref, dn_ref, br_ref,
    win_ref, wdt_ref, norm_ref, wout_ref, gg_ref, blk_ref, hg_ref, *, heads, wide,
):
    ranks = gate_ref.shape[0]
    wog = wog_ref[...].astype(F32)
    wout_ref[...] = wog
    step = pl.program_id(0)

    @pl.when(step == 0)
    def _():
        gg_ref[...] = jnp.zeros_like(gg_ref)
        norm_ref[...] = jnp.zeros_like(norm_ref)

    def lay(ref, col):
        shape = (col.shape[0], ref.shape[1])
        place = lax.broadcasted_iota(jnp.int32, shape, 0) + step * col.shape[0]
        there = lax.broadcasted_iota(jnp.int32, shape, 1) == place
        ref[...] += jnp.sum(jnp.where(there, col, 0.0), axis=0, keepdims=True)

    lay(gg_ref, jnp.sum(wog * wo_ref[...].astype(F32), axis=1, keepdims=True))
    h32 = hid_ref[...].astype(F32)
    blk_ref[...] = (h32 + br_ref[...].astype(F32)).astype(BF16)
    dn = dn_ref[...].astype(F32)
    count = h32.shape[1]
    r0 = lax.rsqrt(jnp.sum(h32 * h32, axis=1, keepdims=True) / count + EPS)
    mixed = jnp.sum(dn * h32, axis=1, keepdims=True) / count
    hg_ref[...] = og_ref[...].astype(F32) + dn - h32 * (r0 * r0 * mixed)

    gain = gain_ref[...].astype(F32)
    norm = None

    def piece(at, raw):
        to = slice(at, at + raw.shape[1])
        win_ref[:, to] = raw * gain
        return jnp.sum(raw * w_ref[:, to].astype(F32), axis=1, keepdims=True)

    shared = None
    dt_parts = []
    for k in range(ranks):
        here = piece(k * wide, gate_ref[k].astype(F32)) + piece(DI + k * wide, rest_ref[k, :, :wide].astype(F32))
        norm = here if norm is None else norm + here
        bc = rest_ref[k, :, wide : wide + 2 * STATE].astype(F32)
        shared = bc if shared is None else shared + bc
        dt_parts.append(rest_ref[k, :, wide + 2 * STATE : wide + 2 * STATE + heads].astype(F32))
    norm = norm + piece(2 * DI, shared)
    raw = jnp.concatenate(dt_parts, axis=1)
    wdt_ref[...] = raw * gain
    lay(norm_ref, norm + jnp.sum(raw * dtw_ref[...].astype(F32), axis=1, keepdims=True))


def local(hidden, lengths, out_grad, norm_gain, w_in, w_dt, conv_weight, conv_bias, dt_bias, a_log, skip_gain, gate_gain, w_out):
    ranks = lax.axis_size("seq")
    rank = lax.axis_index("seq")
    owners = lax.axis_size("head")
    owner = lax.axis_index("head")
    local_len, width = hidden.shape[1], hidden.shape[2]
    heads = HEADS // ranks
    wide = heads * HEAD_DIM
    chans = wide + 2 * STATE
    cols = wide + chans + LANES
    tokens = ranks * local_len
    chunk = min(CHUNK, local_len)
    steps = tokens // chunk
    shard = w_in.shape[0]

    gain_rows = norm_gain[:, None]

    def scaled(v):
        return (v.astype(F32) * gain_rows.astype(F32)).astype(BF16)

    spare = LANES // 2
    ring = owners == 2 * ranks

    def sds(shape, kind):
        return jax.ShapeDtypeStruct(shape, kind)

    hbm = pl.BlockSpec(memory_space=pl.ANY)
    vmem = pl.BlockSpec(memory_space=pltpu.VMEM)

    def dma(count):
        return pltpu.SemaphoreType.DMA((count,))

    def forth(size):
        return pl.BlockSpec((chunk, size), lambda j: (j, 0))

    def back(size):
        return pl.BlockSpec((chunk, size), lambda j: (steps - 1 - j, 0))

    def whole(a):
        return pl.BlockSpec(a.shape, lambda j: (0,) * a.ndim, pipeline_mode=pl.Buffered(1))

    params = pltpu.CompilerParams(
        dimension_semantics=("arbitrary",), vmem_limit_bytes=56 * 1024 * 1024
    )
    grid = (steps,)
    cs = CHANNELS // owners
    hs = HEADS // owners
    scan_out = [
        sds((tokens, chans), BF16),
        sds((tokens, chans), BF16),
        sds((tokens, LANES), F32),
        sds((tokens, wide), BF16),
        sds((tokens, wide), BF16),
        sds((steps, STATE, wide), F32),
        sds((8, tokens), F32),
    ]

    if ring:
        lanes = -(-max(cs, DI // owners) // LANES) * LANES

        (
            h_all, og_all, w_t, w_o, z, u, d0, act, slope, aux, y, gg, states, sums, cw, dtb, rowp, colp,
        ) = pl.pallas_call(
            functools.partial(gather_kernel, heads=heads, wide=wide),
            in_specs=[hbm] * 4 + [vmem] * 6,
            out_specs=[hbm] * 13 + [vmem] * 5,
            out_shape=[
                sds((tokens, width), BF16),
                sds((tokens, width), BF16),
                sds((width, cols), BF16),
                sds((wide, width), BF16),
                sds((tokens, wide), BF16),
                sds((tokens, chans), BF16),
                sds((tokens, wide), BF16),
            ]
            + scan_out
            + [sds((16, chans), F32), sds((8, LANES), F32), sds((8, wide), F32), sds((LANES, LANES), F32)],
            scratch_shapes=[
                pltpu.VMEM((tokens, width), BF16),
                pltpu.VMEM((tokens, width), BF16),
                pltpu.VMEM((width, cols), BF16),
                pltpu.VMEM((wide, width), BF16),
                pltpu.VMEM((shard, cols - LANES), BF16),
                pltpu.VMEM((tokens, wide), BF16),
                pltpu.VMEM((tokens, chans), BF16),
                pltpu.VMEM((tokens, LANES), F32),
                pltpu.VMEM((owners, 16, lanes), BF16),
                pltpu.VMEM((16, lanes), F32),
                pltpu.VMEM((STATE, wide), F32),
                pltpu.VMEM((16, chans), F32),
                pltpu.VMEM((2, STATE, wide), F32),
            ]
            + [dma(4)] * 9
            + [dma(8)] * 5
            + [dma(owners)] * 2
            + [dma(6), dma(22), pltpu.SemaphoreType.DMA((steps, 5)), dma(2)],
            compiler_params=pltpu.CompilerParams(
                collective_id=0, has_side_effects=True, vmem_limit_bytes=56 * 1024 * 1024
            ),
            cost_estimate=pl.CostEstimate(
                flops=2 * tokens * width * (cols + wide), bytes_accessed=4 * tokens * (width + cols), transcendentals=0
            ),
            name="gather_scan",
        )(
            hidden[0], out_grad[0], w_in, w_out, gain_rows, w_dt, conv_weight, conv_bias[None], gate_gain[None],
            jnp.concatenate([dt_bias, a_log, skip_gain])[None],
        )
    else:
        dt_block = jnp.pad(scaled(lax.dynamic_slice_in_dim(w_dt, rank * heads, heads, 1)), ((0, 0), (0, LANES - heads)))
        w_t = lax.all_gather(
            jnp.concatenate(
                [
                    scaled(lax.dynamic_slice_in_dim(w_in, rank * wide, wide, 1)),
                    scaled(lax.dynamic_slice_in_dim(w_in, DI + rank * wide, wide, 1)),
                    scaled(w_in[:, 2 * DI :]),
                    dt_block,
                ],
                axis=1,
            ),
            "head", axis=0, tiled=True,
        )
        w_o = lax.dynamic_slice_in_dim(lax.all_gather(w_out, "head", axis=0, tiled=True), rank * wide, wide, 0)
        h_all = lax.all_gather(hidden[0], "seq", axis=0, tiled=True)
        og_all = lax.all_gather(out_grad[0], "seq", axis=0, tiled=True)
        h32 = h_all.astype(F32)
        r0 = lax.rsqrt(jnp.mean(h32 * h32, axis=1, keepdims=True) + EPS)
        projected = dot(h_all, w_t) * r0
        z = projected[:, :wide].astype(BF16)
        u = projected[:, wide : wide + chans].astype(BF16)
        d_raw = jnp.concatenate([projected[:, wide + chans : cols - 1], r0], axis=1)
        d0 = dot_t(og_all, w_o).astype(BF16)

        def mine(v, size):
            return lax.dynamic_slice_in_dim(v, rank * size, size, v.ndim - 1)

        conv_w = lax.all_gather(conv_weight, "head", axis=1, tiled=True)
        conv_b = lax.all_gather(conv_bias, "head", axis=0, tiled=True)
        cw = jnp.concatenate([conv_w, conv_b[None]], axis=0)
        cw = jnp.concatenate([mine(cw[:, :DI], wide), cw[:, DI:]], axis=1).astype(F32)
        cw = jnp.pad(cw, ((0, 16 - KERNEL - 1), (0, 0)))
        rate = -jnp.exp(mine(lax.all_gather(a_log, "head", axis=0, tiled=True), heads).astype(F32))
        dtb = jnp.pad(mine(lax.all_gather(dt_bias, "head", axis=0, tiled=True), heads).astype(F32), (0, LANES - heads))
        dtb = jnp.broadcast_to(dtb[None], (8, LANES))
        rowp = jnp.stack(
            [
                jnp.repeat(rate, HEAD_DIM),
                jnp.repeat(mine(lax.all_gather(skip_gain, "head", axis=0, tiled=True), heads).astype(F32), HEAD_DIM),
                mine(lax.all_gather(gate_gain, "head", axis=0, tiled=True), wide).astype(F32),
                jnp.pad(rate, (0, wide - heads)),
            ]
            + [jnp.zeros((wide,), F32)] * 4
        )
        colp = jnp.broadcast_to(jnp.pad(rate, (0, LANES - heads))[:, None], (LANES, LANES))
        act, slope, aux, y, gg, states, sums = pl.pallas_call(
            functools.partial(scan_kernel, heads=heads),
            grid=grid,
            in_specs=[
                forth(chans), forth(LANES), forth(wide), forth(wide),
                whole(cw), whole(dtb), whole(rowp), whole(colp),
            ],
            out_specs=[
                forth(chans), forth(chans), forth(LANES), forth(wide), forth(wide),
                pl.BlockSpec((1, STATE, wide), lambda j: (j, 0, 0)),
                pl.BlockSpec((8, chunk), lambda j: (0, j)),
            ],
            out_shape=scan_out,
            scratch_shapes=[pltpu.VMEM((STATE, wide), F32), pltpu.VMEM((16, chans), F32)],
            compiler_params=params,
            name="scan",
        )(u, d_raw, z, d0, cw, dtb, rowp, colp)

    mask = (jnp.arange(tokens, dtype=jnp.int32) < lengths[0]).astype(F32)
    n_own = DI // owners
    piece = n_own // owners
    per = owners // ranks
    wog_shape = (per, piece, width) if ring else (wide, width)
    line_shape = (4, per, piece, width) if ring else (1, 1, 16, LANES)
    in_chunk = min(CHUNK, local_len)
    branch, wog, dy, dpg, wig_gate = pl.pallas_call(
        functools.partial(mid_kernel, ring=ring),
        in_specs=[hbm] * 9 + [vmem] * 3,
        out_specs=[hbm] * 5,
        out_shape=[
            sds((local_len, width), BF16),
            sds(wog_shape, BF16),
            sds((tokens, wide), BF16),
            sds((tokens, wide), BF16),
            sds((width, wide), BF16),
        ],
        scratch_shapes=[
            pltpu.VMEM((tokens, LANES), F32),
            pltpu.VMEM((tokens, wide), BF16),
            pltpu.VMEM((wide, width), BF16),
            pltpu.VMEM((tokens, width // 2), BF16),
        ]
        + [pltpu.VMEM((local_len, width), BF16)] * 4
        + [pltpu.VMEM((local_len // 2, width), BF16)] * 2
        + [pltpu.VMEM((local_len, width), BF16)] * 2
        + [pltpu.VMEM((ranks, 8, tokens), F32)]
        + [pltpu.VMEM(line_shape, BF16)] * 3
        + [pltpu.VMEM((3,) + line_shape[1:], BF16)] * 2
        + [pltpu.VMEM((256 // (2 * piece), 2, piece, width // 2) if ring else (16, LANES), BF16)]
        + [pltpu.VMEM((2, in_chunk, wide), BF16)] * 4
        + [
            pltpu.VMEM((2, in_chunk, LANES), F32),
            pltpu.VMEM((2, in_chunk, wide), BF16),
            pltpu.VMEM((2, tokens, 256), BF16),
            pltpu.VMEM((2, 256, wide), BF16),
        ]
        + [dma(3)]
        + [dma(6)] * 2
        + [dma(3)] * 2
        + [dma(1)] * 2
        + [dma(4)] * 4
        + [pltpu.SemaphoreType.DMA((2, 5)), dma(2), dma(2), dma(2), dma(3)],
        compiler_params=pltpu.CompilerParams(
            collective_id=3, has_side_effects=True, vmem_limit_bytes=56 * 1024 * 1024
        ),
        cost_estimate=pl.CostEstimate(
            flops=6 * tokens * wide * width, bytes_accessed=4 * tokens * (width + 5 * wide), transcendentals=0
        ),
        name="mid",
    )(gg, w_o, og_all, h_all, act, aux, z, d0, y, sums, jnp.broadcast_to(mask[None], (8, tokens)), rowp)
    own_gate = lax.psum_scatter(wig_gate, "head", scatter_dimension=0, tiled=True)

    rest = chans + LANES
    dp, sm, pieces = pl.pallas_call(
        functools.partial(back_kernel, heads=heads, wide=wide, ring=ring),
        grid=grid,
        in_specs=[
            back(chans), back(LANES), back(wide), back(wide),
            pl.BlockSpec((1, STATE, wide), lambda j: (steps - 1 - j, 0, 0)),
            back(chans), back(chans), hbm,
            whole(rowp), whole(colp), whole(cw),
        ],
        out_specs=[back(rest), pl.BlockSpec((8, chans), lambda j: (0, 0)), hbm],
        out_shape=[sds((tokens, rest), BF16), sds((8, chans), F32), sds((ranks,) + wog_shape, BF16)],
        scratch_shapes=[
            pltpu.VMEM((STATE, wide), F32),
            pltpu.VMEM((16, chans), F32),
            pltpu.VMEM((LANES, wide), BF16),
            pltpu.VMEM((wide, LANES), BF16),
        ]
        + [dma(4)] * 2
        + [dma(1)],
        compiler_params=pltpu.CompilerParams(
            dimension_semantics=("arbitrary",), collective_id=2, has_side_effects=True,
            vmem_limit_bytes=56 * 1024 * 1024,
        )
        if ring
        else params,
        cost_estimate=pl.CostEstimate(
            flops=2 * tokens * wide * 12 * chunk, bytes_accessed=tokens * wide * 24, transcendentals=tokens * chunk * heads
        ),
        name="scan_back",
    )(act, aux, dy, y, states, slope, u, wog, rowp, colp, cw)

    if ring:
        dn, gate_rows, rest_rows, w_out_grad = pl.pallas_call(
            grads_kernel,
            in_specs=[hbm] * 6 + [vmem],
            out_specs=[hbm] * 4,
            out_shape=[
                sds((local_len, width), BF16),
                sds((ranks, shard, wide), BF16),
                sds((ranks, shard, rest), BF16),
                sds((owners, piece, width), BF16),
            ],
            scratch_shapes=[
                pltpu.VMEM((tokens, cols), BF16),
                pltpu.VMEM((width, cols), BF16),
                pltpu.VMEM((2, tokens, shard), BF16),
                pltpu.VMEM((shard, spare), F32),
                pltpu.VMEM((shard, spare), BF16),
            ]
            + [pltpu.VMEM((local_len, width), BF16)] * 3
            + [pltpu.VMEM((local_len // 2, width), BF16)] * 2
            + [pltpu.VMEM((local_len, width), BF16)] * 2
            + [
                pltpu.VMEM((2, shard, rest), BF16),
                pltpu.VMEM((shard, rest), BF16),
                pltpu.VMEM((4, shard, rest), BF16),
                pltpu.VMEM((3, shard, rest), BF16),
                pltpu.VMEM((3, shard, rest), BF16),
            ]
            + [dma(6), dma(2)]
            + [dma(6)] * 2
            + [dma(4)] * 10
            + [dma(owners)] * 2
            + [dma(2)],
            compiler_params=pltpu.CompilerParams(
                collective_id=1, has_side_effects=True, vmem_limit_bytes=56 * 1024 * 1024
            ),
            cost_estimate=pl.CostEstimate(
                flops=4 * tokens * width * cols, bytes_accessed=8 * tokens * cols, transcendentals=0
            ),
            name="weight_grads",
        )(dpg, dp, w_t, h_all, own_gate, pieces, sm)
        w_out_grad = w_out_grad.reshape(n_own, width)
        groups = chans // spare
        tiny_all = rest_rows[:, : 8 * groups, rest - spare :].astype(F32).reshape(ranks, groups, 8, spare)
        tiny_all = tiny_all.swapaxes(1, 2).reshape(ranks, 8, chans)
    else:
        full = lax.all_gather(lax.psum(wog, "head"), "seq", axis=0, tiled=True)
        w_out_grad = lax.dynamic_slice_in_dim(full, owner * n_own, n_own, 0)
        wig = t_dot(h_all, dp).astype(BF16)
        dn = (dot_t(dp, w_t[:, wide:]) + dot_t(dpg, w_t[:, :wide])).astype(BF16)
        dn = lax.psum_scatter(dn, "seq", scatter_dimension=0, tiled=True)
        gate_rows = lax.all_gather(own_gate, "seq")
        rest_rows = lax.all_gather(lax.psum_scatter(wig, "head", scatter_dimension=0, tiled=True), "seq")
        tiny_all = lax.all_gather(lax.psum(sm, "head"), "seq")
    strips = min(8, shard // 16)

    def strip(total, size):
        return pl.BlockSpec((total // strips, size), lambda j: (j, 0))

    def ranks_strip(size):
        return pl.BlockSpec((ranks, shard // strips, size), lambda j: (0, j, 0))

    w_in_grad, w_dt_grad, norm_gain_grad, w_out_grad, gate_gain_grad, block_out, hidden_grad = pl.pallas_call(
        functools.partial(finish_kernel, heads=heads, wide=wide),
        grid=(strips,),
        in_specs=[
            ranks_strip(wide), ranks_strip(rest), strip(shard, PROJ), strip(shard, HEADS), strip(shard, 1),
            strip(n_own, width), strip(n_own, width),
            strip(local_len, width), strip(local_len, width), strip(local_len, width), strip(local_len, width),
        ],
        out_specs=[
            strip(shard, PROJ), strip(shard, HEADS), pl.BlockSpec((1, shard), lambda j: (0, 0)),
            strip(n_own, width), pl.BlockSpec((1, n_own), lambda j: (0, 0)),
            strip(local_len, width), strip(local_len, width),
        ],
        out_shape=[
            sds((shard, PROJ), F32),
            sds((shard, HEADS), F32),
            sds((1, shard), F32),
            sds((n_own, width), F32),
            sds((1, n_own), F32),
            sds((local_len, width), BF16),
            sds((local_len, width), F32),
        ],
        compiler_params=params,
        cost_estimate=pl.CostEstimate(flops=6 * shard * PROJ, bytes_accessed=16 * shard * PROJ, transcendentals=0),
        name="finish",
    )(
        gate_rows, rest_rows, w_in, w_dt, gain_rows, w_out_grad, w_out,
        hidden[0], out_grad[0], dn, branch,
    )

    conv_all = jnp.concatenate(
        [tiny_all[:, :5, :wide].swapaxes(0, 1).reshape(5, DI), jnp.sum(tiny_all[:, :5, wide:], axis=0)], axis=1
    )
    skip_all = jnp.sum(tiny_all[:, 5, :wide].reshape(ranks, heads, HEAD_DIM), axis=2)
    vec = jnp.stack([tiny_all[:, 6, :heads], tiny_all[:, 7, :heads], skip_all]).reshape(3, HEADS)
    conv_own = lax.dynamic_slice_in_dim(conv_all, owner * cs, cs, 1)
    vec_own = lax.dynamic_slice_in_dim(vec, owner * hs, hs, 1)

    return (
        block_out[None],
        hidden_grad[None],
        norm_gain_grad.reshape(shard),
        w_in_grad,
        w_dt_grad,
        conv_own[:KERNEL],
        conv_own[KERNEL],
        vec_own[0],
        vec_own[1],
        vec_own[2],
        gate_gain_grad.reshape(n_own) / gate_gain.astype(F32),
        w_out_grad,
    )


def solution(mesh):
    rows = P("head", "seq", None)
    return jax.shard_map(
        local,
        mesh=mesh,
        in_specs=(
            rows, P("head"), rows, P("head"), P("head", None), P("head", None), P(None, "head"),
            P("head"), P("head"), P("head"), P("head"), P("head"), P("head", None),
        ),
        out_specs=(
            rows, rows, P("head"), P("head", None), P("head", None), P(None, "head"),
            P("head"), P("head"), P("head"), P("head"), P("head"), P("head", None),
        ),
        check_vma=False,
    )
```

```python
import functools

import jax
import jax.numpy as jnp
from jax import lax
from jax.experimental import pallas as pl
from jax.experimental.pallas import tpu as pltpu
from jax.sharding import PartitionSpec as P

HEADS = 64
HEAD_DIM = 64
STATE = 128
KERNEL = 4
CHUNK = 256
DI = 4096
CHANNELS = 4352
PROJ = DI + CHANNELS
EPS = 1e-05
LANES = 128
EVERY = ("seq", "head")
F32 = jnp.float32
BF16 = jnp.bfloat16


def dot(a, b):
    return jnp.dot(a, b, preferred_element_type=F32)


def dot_t(a, b):
    return lax.dot_general(a, b, (((1,), (1,)), ((), ())), preferred_element_type=F32)


def t_dot(a, b):
    return lax.dot_general(a, b, (((0,), (0,)), ((), ())), preferred_element_type=F32)


def sigmoid(v):
    return 0.5 * jnp.tanh(0.5 * v) + 0.5


def remote(src, dst, send, recv, target):
    return pltpu.make_async_remote_copy(
        src_ref=src, dst_ref=dst, send_sem=send, recv_sem=recv, device_id=target, device_id_type=pl.DeviceIdType.MESH
    )


def greet(peers, extra=()):
    barrier = pltpu.get_barrier_semaphore()
    count = len(peers)

    def hello(peer):
        pl.semaphore_signal(barrier, inc=1, device_id=peer, device_id_type=pl.DeviceIdType.MESH)

    for peer in peers:
        hello(peer)
    for there, peer in extra:
        pl.when(there)(functools.partial(hello, peer))
        count = count + jnp.where(there, 1, 0)
    pl.semaphore_wait(barrier, count)


def decays(aux, heads, expand, rate_e, rate_row, rate_col):
    rows = aux.shape[0]
    lane = lax.broadcasted_iota(jnp.int32, aux.shape, 1)
    dt = jnp.where(lane < heads, aux, 0.0).astype(BF16)
    r = lax.broadcasted_iota(jnp.int32, (rows, rows), 0)
    c = lax.broadcasted_iota(jnp.int32, (rows, rows), 1)
    causal = c <= r
    lower = jnp.where(causal, 1.0, 0.0).astype(BF16)
    dt_e = dot(dt, expand)
    cum_e = dot(lower, dt_e.astype(BF16)) * rate_e
    cum_c = dot(lower, dt) * rate_row
    cum_t = lax.dot_general(dt, lower, (((0,), (1,)), ((), ())), preferred_element_type=F32) * rate_col
    return causal, dt_e, cum_e, cum_c, cum_t


def head_matrix(wide, turned=False):
    shape = (wide, LANES) if turned else (LANES, wide)
    channel = lax.broadcasted_iota(jnp.int32, shape, 0 if turned else 1)
    head = lax.broadcasted_iota(jnp.int32, shape, 1 if turned else 0)
    return jnp.where(channel // HEAD_DIM == head, 1.0, 0.0).astype(BF16)


def shift_matrix(rows, by):
    r = lax.broadcasted_iota(jnp.int32, (rows, rows), 0)
    c = lax.broadcasted_iota(jnp.int32, (rows, rows), 1)
    return jnp.where(c == r + by, 1.0, 0.0).astype(BF16)


def lower_parts(cum_c, cum_t, h, causal):
    mid = causal.shape[0] // 2
    near = causal[:mid, :mid]
    col, row = cum_c[:, h : h + 1], cum_t[h : h + 1, :]
    top = jnp.exp(jnp.where(near, col[:mid] - row[:, :mid], -1e30))
    low = jnp.exp(col[mid:] - row[:, :mid])
    right = jnp.exp(jnp.where(near, col[mid:] - row[:, mid:], -1e30))
    return top, low, right


def scan_chunk(u, raw, z, taps, bias, dtb, expand, rowp, rate_col, state, ext, st_out, heads):
    rows, chans = u.shape
    wide = expand.shape[1]
    u32 = u.astype(F32)
    pre = bias + taps[KERNEL - 1 : KERNEL] * u32
    before = jnp.zeros((8, chans), F32)
    for j in range(1, KERNEL):
        tap = taps[KERNEL - 1 - j : KERNEL - j]
        pre = pre + tap * dot(shift_matrix(rows, -j), u)
        before = before + tap * ext[8 - j : 16 - j, :]
    pre = jnp.concatenate([pre[:8] + before, pre[8:]], axis=0)
    ext[0:8, :] = u32[rows - 8 :, :]
    sig = sigmoid(pre)
    act = (pre * sig).astype(BF16)
    slope = (sig * (1.0 + pre * (1.0 - sig))).astype(BF16)
    v = raw + dtb
    soft = jnp.maximum(v, 0.0) + jnp.log1p(jnp.exp(-jnp.abs(v)))
    soft = soft.astype(BF16).astype(F32)
    lane = lax.broadcasted_iota(jnp.int32, v.shape, 1)
    aux = jnp.where(lane < heads, soft, 0.0)
    sig_v = pltpu.roll(sigmoid(v), heads, 1)
    aux = jnp.where((lane >= heads) & (lane < 2 * heads), sig_v, aux)
    aux = jnp.where(lane == LANES - 1, raw, aux)

    x32 = act[:, :wide].astype(F32)
    b = act[:, wide : wide + STATE]
    c = act[:, wide + STATE :]
    causal, dt_e, cum_e, cum_c, cum_t = decays(aux, heads, expand, rowp[0:1], rowp[3:4, :LANES], rate_col)
    xdt = x32 * dt_e
    xdt16 = xdt.astype(BF16)
    scores = dot_t(c, b)
    st = state[...]
    st_out[...] = st
    mid = rows // 2
    half = lax.broadcasted_iota(jnp.int32, (rows, LANES), 1) < HEAD_DIM
    parts = []
    for pair in range(heads // 2):
        x2 = xdt16[:, LANES * pair : LANES * (pair + 1)]
        got = []
        for h in (2 * pair, 2 * pair + 1):
            top, low, right = lower_parts(cum_c, cum_t, h, causal)
            m_top = (scores[:mid, :mid] * top).astype(BF16)
            m_low = (scores[mid:, :mid] * low).astype(BF16)
            m_right = (scores[mid:, mid:] * right).astype(BF16)
            y_low = dot(jnp.concatenate([m_low, m_right], axis=1), x2)
            got.append(jnp.concatenate([dot(m_top, x2[:mid]), y_low], axis=0))
        parts.append(jnp.where(half, got[0], got[1]))
    y = jnp.concatenate(parts, axis=1) + dot(c, st.astype(BF16)) * jnp.exp(cum_e)
    last = cum_e[rows - 1 : rows, :]
    tail = jnp.exp(last - cum_e)
    state[...] = jnp.exp(last) * st + t_dot(b, (xdt * tail).astype(BF16))
    y16 = y.astype(BF16)
    ssd = (y16.astype(F32) + rowp[1:2] * x32).astype(BF16).astype(F32)
    z = z.astype(F32)
    g = ssd * (z * sigmoid(z))
    gg = (g * rowp[2:3]).astype(BF16)
    ssq = dot_t(jnp.ones((8, wide), BF16), (g * g).astype(BF16))
    return act, slope, aux, y16, gg, ssq


def with_cross(ssq, gg, d0):
    cross = dot_t(jnp.ones((8, gg.shape[1]), BF16), (gg.astype(F32) * d0.astype(F32)).astype(BF16))
    return jnp.where(lax.broadcasted_iota(jnp.int32, ssq.shape, 0) == 0, ssq, cross)


def scan_kernel(
    u_ref, d_ref, z_ref, d0_ref, cw_ref, dtb_ref, rowp_ref, colp_ref,
    act_ref, slope_ref, aux_ref, y_ref, gg_ref, st_ref, sum_ref, state, ext, *, heads,
):
    @pl.when(pl.program_id(0) == 0)
    def _():
        state[...] = jnp.zeros_like(state)
        ext[...] = jnp.zeros_like(ext)

    act, slope, aux, y16, gg, ssq = scan_chunk(
        u_ref[...], d_ref[...], z_ref[...], cw_ref[0:KERNEL, :], cw_ref[KERNEL : KERNEL + 1, :], dtb_ref[0:1, :],
        head_matrix(z_ref.shape[1]), rowp_ref[...], colp_ref[:, 0:1], state, ext, st_ref.at[0], heads,
    )
    act_ref[...] = act
    slope_ref[...] = slope
    aux_ref[...] = aux
    y_ref[...] = y16
    gg_ref[...] = gg
    sum_ref[...] = with_cross(ssq, gg, d0_ref[...])


def seg_dot(v, seg):
    hi = v.astype(BF16)
    return dot(hi, seg) + dot((v - hi.astype(F32)).astype(BF16), seg)


def rank_params(par, s, cw_ref, dtb_ref, rowp_ref, colp_ref, heads, wide):
    owners, _, lanes = par.shape
    chans = cw_ref.shape[1]
    share = CHANNELS // owners
    gains = DI // owners
    per = HEADS // owners

    def iota(shape, dim):
        return lax.broadcasted_iota(jnp.int32, shape, dim)

    def chosen(there):
        return jnp.where(there, 1.0, 0.0).astype(BF16)

    cw_ref[...] = jnp.zeros_like(cw_ref)
    at = iota((1, chans), 1)
    wanted = jnp.where(at < wide, s * wide + at, DI + at - wide)

    @pl.loop(0, owners)
    def _(j):
        i = iota((lanes, chans), 0)
        cw_ref[...] += dot(par[j], chosen((i + j * share == wanted) & (i < share)))

    count = heads // per
    a_e, skip_e, a_row, dt_row, a_col, gain = 0.0, 0.0, 0.0, 0.0, 0.0, []
    head_of = iota((LANES, wide), 1) // HEAD_DIM
    lane_e = iota((LANES, wide), 0)
    lane = iota((LANES, LANES), 0)
    to = iota((LANES, LANES), 1)
    for k in range(count):
        block = par[s * count + k]
        few = block[:, :LANES]
        gain.append(block[5:6, :gains].astype(F32))

        def spread(first):
            return chosen((lane_e - first + per * k == head_of) & (lane_e >= first) & (lane_e < first + per))

        def placed(first):
            return chosen((lane - first + per * k == to) & (lane >= first) & (lane < first + per))

        a_e = a_e + dot(few, spread(per))
        skip_e = skip_e + dot(few, spread(2 * per))
        dt_row = dt_row + dot(few, placed(0))
        a_row = a_row + dot(few, placed(per))
        a_col = a_col + lax.dot_general(placed(per), few, (((0,), (1,)), ((), ())), preferred_element_type=F32)
    rowp_ref[0:1, :] = -jnp.exp(a_e[6:7])
    rowp_ref[1:2, :] = skip_e[6:7]
    rowp_ref[2:3, :] = jnp.concatenate(gain, axis=1)
    rowp_ref[3:8, :] = jnp.zeros((5, wide), F32)
    rowp_ref[3:4, :LANES] = jnp.where(iota((1, LANES), 1) < heads, -jnp.exp(a_row[6:7]), 0.0)
    dtb_ref[...] = jnp.broadcast_to(dt_row[6:7], dtb_ref.shape)
    col = jnp.where(iota((LANES, 1), 0) < heads, -jnp.exp(a_col[:, 6:7]), 0.0)
    colp_ref[...] = jnp.broadcast_to(col, colp_ref.shape)


def gather_kernel(
    hid_ref, og_ref, w_ref, wo_in_ref, gain_ref, dtw_ref, cwt_ref, cbi_ref, ggn_ref, hds_ref,
    hall_ref, ogall_ref, wt_ref, wo_ref, z_ref, u_ref, d0_ref, act_ref, slope_ref, aux_ref, y_ref, gg_ref, st_ref,
    sum_ref, cw_ref, dtb_ref, rowp_ref, colp_ref,
    hv, ov, wv, wov, stage, zv, uv, dv, par, par_f, state, ext, st_v,
    h_send, h_recv, o_send, o_recv, z_up, z_dn, z_recv, s_send, s_recv,
    c_up, c_dn, c_recv, t_send, t_recv, a_send, a_recv, local_sem, out_sem, scan_sem, st_sem, *, heads, wide,
):
    ring = True
    s = lax.axis_index("seq")
    q = hid_ref.shape[0]
    half = q // 2
    x_peer = s + 1 - 2 * lax.rem(s, 2)
    y_peer = lax.rem(s + 2, 4)
    far = 3 - s
    to_x, to_y = {"seq": x_peer}, {"seq": y_peer}
    chans = uv.shape[1]
    n_main = stage.shape[1]
    n = stage.shape[0]
    peers = [to_x, to_y]

    def block(ref, at, start, size):
        return ref.at[pl.ds(pl.multiple_of(at * q + start, 16), size), :]

    if ring:
        h = lax.axis_index("head")
        core = lax.rem(h, 2)
        r = h // 2
        last = lax.axis_size("head") // 2 - 1
        to_sib, to_up, to_down = {"head": h + 1 - 2 * core}, {"head": lax.rem(h + 2, 2 * last + 2)}, {"head": lax.rem(h + 2 * last, 2 * last + 2)}
        above, below = r < last, r > 0
        owners = lax.axis_size("head")
        to_heads = [{"head": lax.rem(h + k, owners)} for k in range(1, owners)]
        peers += to_heads
        first = pl.multiple_of(s * wide, LANES)
        second = pl.multiple_of(DI + s * wide, LANES)
        loads = [
            pltpu.make_async_copy(w_ref.at[:, pl.ds(first, wide)], stage.at[:, :wide], local_sem.at[0]),
            pltpu.make_async_copy(w_ref.at[:, pl.ds(second, wide)], stage.at[:, wide : 2 * wide], local_sem.at[1]),
            pltpu.make_async_copy(w_ref.at[:, 2 * DI :], stage.at[:, 2 * wide :], local_sem.at[2]),
        ]
        is_root = r == s
        n_o = wov.shape[0] // 2
        load_o = pltpu.make_async_copy(
            wo_in_ref, wov.at[pl.ds(pl.multiple_of(core * n_o, 16), n_o), :], local_sem.at[5]
        )
        pl.when(is_root)(load_o.start)
    for copy in loads:
        copy.start()
    own_h = pltpu.make_async_copy(hid_ref, block(hv, s, 0, q), local_sem.at[3])
    own_o = pltpu.make_async_copy(og_ref, block(ov, s, 0, q), local_sem.at[4])
    own_h.start()
    own_o.start()
    par_f[...] = jnp.zeros_like(par_f)
    par_f[0:KERNEL, : cwt_ref.shape[1]] = cwt_ref[...].astype(F32)
    for k, row in enumerate((cbi_ref, ggn_ref, hds_ref)):
        par_f[KERNEL + k : KERNEL + k + 1, : row.shape[1]] = row[...].astype(F32)
    par[h] = par_f[...].astype(BF16)
    greet(peers)

    sent = []

    def send(src, dst, sems, i, target):
        copy = remote(src, dst, sems[0].at[i], sems[1].at[i], target)
        copy.start()
        sent.append(copy)
        return copy

    def open_exchange(src, buf, sems):
        return (
            send(src, block(buf, s, 0, q), sems, 0, to_x),
            send(src, block(buf, s, 0, q), sems, 1, to_y),
        )

    def relay(buf, sems, heads_in):
        heads_in[0].wait_recv()
        a = block(buf, x_peer, 0, half)
        first = send(a, a, sems, 2, to_y)
        heads_in[1].wait_recv()
        b = block(buf, y_peer, half, half)
        return first, send(b, b, sems, 3, to_x)

    h_sems, o_sems = (h_send, h_recv), (o_send, o_recv)
    h_open = open_exchange(hid_ref, hv, h_sems)
    pars = [send(par.at[h], par.at[h], (a_send, a_recv), k, peer) for k, peer in enumerate(to_heads)]

    closing = []
    if ring:
        def w_block(at):
            return wv.at[pl.ds(pl.multiple_of((2 * at + core) * n, 16), n), :]

        def w_copy(at, sems, target):
            return remote(w_block(at), w_block(at), sems.at[at], z_recv.at[at], target)

        def w_swap(at):
            return remote(w_block(at), w_block(at), s_send.at[at], s_recv.at[at], to_sib)

        def launch(there, make):
            @pl.when(there)
            def _():
                make().start()

            def finish():
                @pl.when(there)
                def _():
                    make().wait_send()

            closing.append(finish)

        always = r >= 0

        def w_step(k):
            lower, upper = r - k, r + k
            has_lower, has_upper = lower >= 0, upper <= last

            @pl.when(has_lower)
            def _():
                w_copy(lower, z_up, to_up).wait_recv()

            launch(has_lower & above, lambda: w_copy(lower, z_up, to_up))
            launch(has_lower, lambda: w_swap(lower))

            @pl.when(has_upper)
            def _():
                w_copy(upper, z_dn, to_down).wait_recv()

            launch(has_upper & below, lambda: w_copy(upper, z_dn, to_down))
            launch(has_upper, lambda: w_swap(upper))

        chunks = c_recv.shape[0]
        n_c = n_o // chunks
        dist = jnp.where(r > s, r - s, s - r)
        ending = (r == 0) | (r == last)

        def o_block(i):
            return wov.at[pl.ds(pl.multiple_of(core * n_o + i * n_c, 16), n_c), :]

        def o_copy(i, sems, target):
            return remote(o_block(i), o_block(i), sems.at[i], c_recv.at[i], target)

        def o_swap(i):
            return remote(o_block(i), o_block(i), t_send.at[i], t_recv.at[i], to_sib)

        def o_root():
            @pl.when(is_root)
            def _():
                load_o.wait()

            for i in range(chunks):
                pl.when(is_root & above & (r != 2))(lambda i=i: o_copy(i, c_up, to_up).start())
                pl.when(is_root & below & (r != 1))(lambda i=i: o_copy(i, c_dn, to_down).start())
                pl.when(is_root)(lambda i=i: o_swap(i).start())

        def o_root_late():
            for i in range(chunks):
                pl.when(is_root & (r == 2))(lambda i=i: o_copy(i, c_up, to_up).start())
                pl.when(is_root & (r == 1))(lambda i=i: o_copy(i, c_dn, to_down).start())

        def o_tick(t):
            i = t - dist
            live = (dist >= 1) & (i >= 0) & (i < chunks) & jnp.logical_not(ending)

            @pl.when(live)
            def _():
                o_copy(i, c_up, to_up).wait_recv()

            pl.when(live & (r > s) & above)(lambda: o_copy(i, c_up, to_up).start())
            pl.when(live & (r < s) & below)(lambda: o_copy(i, c_dn, to_down).start())
            pl.when(live)(lambda: o_swap(i).start())

        def o_rest():
            @pl.when(ending & (dist >= 1))
            def _():
                for i in range(chunks):
                    o_copy(i, c_up, to_up).wait_recv()
                    o_swap(i).start()

        def o_finish():
            for i in range(chunks):
                pl.when((r >= s) & above)(lambda: o_copy(i, c_up, to_up).wait_send())
                pl.when((r <= s) & below)(lambda: o_copy(i, c_dn, to_down).wait_send())
                o_swap(i).wait_send()

        for copy in loads:
            copy.wait()
        own = pl.ds(pl.multiple_of(h * n, 16), n)
        wv[own, :n_main] = (stage[...].astype(F32) * gain_ref[...].astype(F32)).astype(BF16)
        shape = (dtw_ref.shape[1], LANES)
        place = lax.broadcasted_iota(jnp.int32, shape, 1)
        taken = (lax.broadcasted_iota(jnp.int32, shape, 0) == place + s * heads) & (place < heads)
        own_dt = dot(dtw_ref[...], jnp.where(taken, 1.0, 0.0).astype(BF16))
        wv[own, n_main:] = (own_dt * gain_ref[...].astype(F32)).astype(BF16)
        launch(above, lambda: w_copy(r, z_up, to_up))
        launch(below, lambda: w_copy(r, z_dn, to_down))
        launch(always, lambda: w_swap(r))
        w_step(1)

    rows = min(CHUNK, q)

    def cut(at_block):
        return pl.ds(pl.multiple_of(at_block * q, 16), q)

    def project_outs(at_block, i):
        at = cut(at_block)
        pairs = ((hv, hall_ref), (zv, z_ref), (uv, u_ref))
        return [
            pltpu.make_async_copy(src.at[at, :], dst.at[at, :], out_sem.at[3 * i + k])
            for k, (src, dst) in enumerate(pairs)
        ]

    act_at, y_at = slice(0, chans), slice(chans, chans + wide)
    gg_at, d0_at = slice(0, wide), slice(wide, 2 * wide)

    def scan_outs(j):
        at = pl.ds(pl.multiple_of(j * rows, 16), rows)
        slot = lax.rem(j, 2)
        pairs = (
            (wv.at[at, act_at], act_ref), (wv.at[at, y_at], y_ref), (uv.at[at, :], slope_ref),
            (dv.at[at, :], aux_ref), (hv.at[at, gg_at], gg_ref),
        )
        copies = [pltpu.make_async_copy(src, dst.at[at, :], scan_sem.at[j, k]) for k, (src, dst) in enumerate(pairs)]
        return copies, pltpu.make_async_copy(st_v.at[slot], st_ref.at[j], st_sem.at[slot])

    def pull_outs(at_block, i):
        at = cut(at_block)
        pairs = ((ov.at[at, :], ogall_ref), (hv.at[at, d0_at], d0_ref))
        return [
            pltpu.make_async_copy(src, dst.at[at, :], out_sem.at[12 + 2 * i + k])
            for k, (src, dst) in enumerate(pairs)
        ]

    def nth(i):
        return jnp.where(i == 0, s, jnp.where(i == 1, x_peer, jnp.where(i == 2, y_peer, far)))

    w_out = pltpu.make_async_copy(wv, wt_ref, out_sem.at[20])
    o_out = pltpu.make_async_copy(wov, wo_ref, out_sem.at[21])

    width = wv.shape[0]
    strip = width // 4
    late_chip = jnp.where(r < 2, last, 0)
    early_k = pl.ds(pl.multiple_of(jnp.where(late_chip == 0, strip, 0), strip), 3 * strip)
    late_k = pl.ds(pl.multiple_of(late_chip * strip, strip), strip)

    def project(at_block, k, ahead):
        @pl.loop(0, q // rows)
        def _(j):
            at = pl.ds(pl.multiple_of(at_block * q + j * rows, 16), rows)
            hb = hv[at, k]
            z = dot(hb, wv[k, :wide])
            u = dot(hb, wv[k, wide : wide + chans])
            raw = dot(hb, wv[k, wide + chans :])
            if ahead:
                zv[at, :] = z.astype(BF16)
                uv[at, :] = u.astype(BF16)
                dv[at, :] = raw
            else:
                h32 = hv[at, :].astype(F32)
                r0 = lax.rsqrt(jnp.mean(h32 * h32, axis=1, keepdims=True) + EPS)
                zv[at, :] = ((z + zv[at, :].astype(F32)) * r0).astype(BF16)
                uv[at, :] = ((u + uv[at, :].astype(F32)) * r0).astype(BF16)
                raw = (raw + dv[at, :]) * r0
                lane = lax.broadcasted_iota(jnp.int32, raw.shape, 1)
                dv[at, :] = jnp.where(lane == LANES - 1, r0, raw)

    def pull(at_block):
        at = cut(at_block)

        @pl.loop(0, wide // 256)
        def _(j):
            from_o = pl.ds(pl.multiple_of(j * 256, 256), 256)
            to = pl.ds(pl.multiple_of(wide + j * 256, 256), 256)
            hv[at, to] = dot_t(ov[at, :], wov[from_o, :]).astype(BF16)

        @pl.loop(0, q // rows)
        def _(j):
            some = pl.ds(pl.multiple_of(at_block * q + j * rows, 16), rows)
            lanes = pl.ds(pl.multiple_of(at_block * q + j * rows, LANES), rows)
            sum_ref[:, lanes] = with_cross(sum_ref[:, lanes], hv[some, gg_at], hv[some, d0_at])

    h_far = relay(hv, h_sems, h_open)
    own_h.wait()
    own_o.wait()
    for copy in pars:
        copy.wait_recv()
    rank_params(par, s, cw_ref, dtb_ref, rowp_ref, colp_ref, heads, wide)
    w_step(2)
    o_root()
    for k in range(1, 4):
        w_swap(lax.rem(late_chip + k, 4)).wait_recv()
    project(s, early_k, True)
    project(x_peer, early_k, True)
    for copy in h_far:
        copy.wait_recv()
    o_open = open_exchange(og_ref, ov, o_sems)
    o_tick(1)

    @pl.loop(2, 4)
    def _(i):
        project(nth(i), early_k, True)
        o_tick(i)

    o_root_late()
    w_step(3)
    w_swap(late_chip).wait_recv()
    w_out.start()

    @pl.loop(0, 4)
    def _(i):
        at_block = nth(i)
        project(at_block, late_k, False)
        for copy in project_outs(at_block, i):
            copy.start()
        pl.when(i < 3)(lambda: o_tick(4 + i))

    for i, at_block in enumerate((s, x_peer, y_peer, far)):
        for copy in project_outs(at_block, i):
            copy.wait()
    w_out.wait()
    for copy in h_far:
        copy.wait_send()
    sent[:] = [copy for copy in sent if copy is not h_far[0] and copy is not h_far[1]]
    for finish in closing:
        finish()
    o_a, o_b = block(ov, x_peer, 0, half), block(ov, y_peer, half, half)
    o_far = [
        remote(o_a, o_a, o_send.at[2], o_recv.at[2], to_y),
        remote(o_b, o_b, o_send.at[3], o_recv.at[3], to_x),
    ]
    sent += o_far
    state[...] = jnp.zeros_like(state)
    ext[...] = jnp.zeros_like(ext)
    expand = head_matrix(wide)
    steps = 4 * q // rows

    @pl.loop(0, steps)
    def _(j):
        at = pl.ds(pl.multiple_of(j * rows, 16), rows)
        slot = lax.rem(j, 2)

        @pl.when(j >= 2)
        def _():
            scan_outs(j - 2)[1].wait()

        @pl.when(j == steps - 2)
        def _():
            for opened, copy in zip(o_open, o_far):
                opened.wait_recv()
                copy.start()

        act, slope, aux, y16, gg, ssq = scan_chunk(
            uv[at, :], dv[at, :], zv[at, :], cw_ref[0:KERNEL, :], cw_ref[KERNEL : KERNEL + 1, :], dtb_ref[0:1, :],
            expand, rowp_ref[...], colp_ref[:, 0:1], state, ext, st_v.at[slot], heads,
        )
        wv[at, act_at] = act
        wv[at, y_at] = y16
        uv[at, :] = slope
        dv[at, :] = aux
        hv[at, gg_at] = gg
        sum_ref[:, pl.ds(pl.multiple_of(j * rows, LANES), rows)] = ssq
        copies, st_copy = scan_outs(j)
        for copy in copies:
            copy.start()
        st_copy.start()
        pl.when(lax.rem(j, 2) == 0)(lambda: o_tick(7 + j // 2))

    o_rest()
    for i in range(chunks):
        o_swap(i).wait_recv()
    o_out.start()

    @pl.loop(0, 4)
    def _(i):
        at_block = nth(i)

        @pl.when(i == 3)
        def _():
            for copy in o_far:
                copy.wait_recv()

        pull(at_block)
        for copy in pull_outs(at_block, i):
            copy.start()

    for i, at_block in enumerate((s, x_peer, y_peer, far)):
        for copy in pull_outs(at_block, i):
            copy.wait()

    @pl.loop(0, steps)
    def _(j):
        for copy in scan_outs(j)[0]:
            copy.wait()

    for j in (steps - 2, steps - 1):
        scan_outs(j)[1].wait()
    o_out.wait()
    for copy in sent:
        copy.wait_send()
    o_finish()


def line_sum(own, z_u, z_d, sems, r, last, to_up, to_down, join, closing):
    zu_send, zu_recv, zd_send, zd_recv = sems

    def up_copy(t):
        return remote(own.at[t], z_u.at[t - 1], zu_send.at[t], zu_recv.at[t], to_up)

    def down_copy(t):
        return remote(own.at[t], z_d.at[t], zd_send.at[t], zd_recv.at[t], to_down)

    def up_add(t):
        up_copy(t).wait_recv()
        join(t, z_u.at[t - 1])

    def down_add(t):
        down_copy(t).wait_recv()
        join(t, z_d.at[t])

    def sent_later(t, there, make):
        closing.append(lambda: pl.when(there)(lambda: make(t).wait_send()))

    def pass_on(t, there, add, make):
        @pl.when(there)
        def _():
            add(t)
            make(t).start()

        sent_later(t, there, make)

    def follow(t, there, make, before):
        @pl.when(there)
        def _():
            make(before).wait_send()
            make(t).start()

    def start():
        pl.when(r == 0)(lambda: up_copy(last).start())
        pl.when(r == last)(lambda: down_copy(0).start())

    def second():
        follow(2, r == 0, up_copy, last)
        follow(1, r == last, down_copy, 0)
        pass_on(last, r == 1, up_add, up_copy)
        pass_on(0, r == 2, down_add, down_copy)

    def across():
        pass_on(last, r == 2, up_add, up_copy)
        pass_on(0, r == 1, down_add, down_copy)

    def third():
        follow(1, r == 0, up_copy, 2)
        follow(2, r == last, down_copy, 1)
        pass_on(2, r == 1, up_add, up_copy)
        pass_on(1, r == 2, down_add, down_copy)
        sent_later(1, r == 0, up_copy)
        sent_later(2, r == last, down_copy)

    def final():
        pl.when(r > 0)(lambda: up_add(r))
        pl.when(r < last)(lambda: down_add(r))

    return start, second, across, third, final


def mid_kernel(
    gg_ref, wo_ref, og_ref, h_ref, act_ref, aux_ref, z_ref, d0_ref, y_ref, sums_ref, mask_ref, rowp_ref,
    br_ref, wog_ref, dy_ref, dpg_ref, gate_ref,
    stat_v, ggv, wov, ogv, far_p, y_p, x_p, own_p, far_a, far_b, y_f, x_f, sv,
    ow, other, other_in, z_u, z_d, part_s, xin, zin, din, yin, ain, dyo, hb, rows_s,
    load_sem, d_send, d_recv, s_send, s_recv, c_send, c_recv, zu_send, zu_recv, zd_send, zd_recv,
    in_sem, dy_sem, hb_sem, rows_sem, out_sem, *, ring,
):
    s = lax.axis_index("seq")
    tokens, wide = ggv.shape
    width = wov.shape[1]
    q = far_p.shape[0]
    half = q // 2
    rows = min(CHUNK, q)
    tile = 256
    x_peer = s + 1 - 2 * lax.rem(s, 2)
    y_peer = lax.rem(s + 2, 4)
    far = 3 - s
    to_x, to_y, to_far = {"seq": x_peer}, {"seq": y_peer}, {"seq": far}
    load_gg = pltpu.make_async_copy(gg_ref, ggv, load_sem.at[0])
    load_wo = pltpu.make_async_copy(wo_ref, wov, load_sem.at[1])
    cut = ogv.shape[1]

    def load_og(d):
        return pltpu.make_async_copy(og_ref.at[:, d * cut : (d + 1) * cut], ogv, load_sem.at[2])

    def load_chunk(i):
        at = pl.ds(pl.multiple_of(i * rows, 16), rows)
        slot = lax.rem(i, 2)
        pairs = ((act_ref.at[at, :wide], xin), (z_ref.at[at, :], zin), (d0_ref.at[at, :], din), (y_ref.at[at, :], yin), (aux_ref.at[at, :], ain))
        return [pltpu.make_async_copy(src, dst.at[slot], in_sem.at[slot, k]) for k, (src, dst) in enumerate(pairs)]

    def load_h(i):
        slot = lax.rem(i, 2)
        return pltpu.make_async_copy(h_ref.at[:, pl.ds(pl.multiple_of(i * tile, tile), tile)], hb.at[slot], hb_sem.at[slot])

    load_gg.start()
    load_wo.start()
    load_og(0).start()
    peers = [to_x, to_y, to_far]
    extra = []
    closing = []
    if ring:
        h = lax.axis_index("head")
        owners = lax.axis_size("head")
        last = owners // 2 - 1
        core = lax.rem(h, 2)
        r = h // 2
        to_sib = {"head": h + 1 - 2 * core}
        to_up, to_down = {"head": lax.rem(h + 2, owners)}, {"head": lax.rem(h + owners - 2, owners)}
        peers.append(to_sib)
        extra = [(r < last, to_up), (r > 0, to_down)]

        def join(t, more):
            ow[t] = (ow[t].astype(F32) + more[...].astype(F32)).astype(BF16)

        start, second, across, third, final = line_sum(
            ow, z_u, z_d, (zu_send, zu_recv, zd_send, zd_recv), r, last, to_up, to_down, join, closing
        )
    sv[s] = sums_ref[...]
    greet(peers, extra)
    sums = [
        remote(sums_ref, sv.at[s], s_send.at[i], s_recv.at[i], peer) for i, peer in enumerate((to_x, to_y, to_far))
    ]
    for copy in sums:
        copy.start()
    for i in (0, 1):
        for copy in load_chunk(i):
            copy.start()
    load_h(0).start()
    load_h(1).start()
    load_gg.wait()
    load_wo.wait()

    def part(block, out):
        @pl.loop(0, q // rows)
        def _(j):
            at = pl.ds(pl.multiple_of(block * q + j * rows, 16), rows)
            to = pl.ds(pl.multiple_of(j * rows, 16), rows)
            out[to, :] = dot(ggv[at, :], wov[...]).astype(BF16)

    def d_copy(src, dst, i, target):
        copy = remote(src, dst, d_send.at[i], d_recv.at[i], target)
        copy.start()
        return copy

    part(far, far_p)
    d0 = d_copy(far_p.at[:half], far_a, 0, to_x)
    d1 = d_copy(far_p.at[half:], far_b, 1, to_y)
    part(y_peer, y_p)
    d2 = d_copy(y_p.at[half:], y_f.at[half:], 2, to_y)
    part(x_peer, x_p)
    d3 = d_copy(x_p.at[:half], x_f.at[:half], 3, to_x)
    part(s, own_p)

    for copy in sums:
        copy.wait_recv()
    total = (sv[0] + sv[1]) + (sv[2] + sv[3])
    r1 = lax.rsqrt(total[0:1] / DI + EPS)
    r1m = r1 * mask_ref[0:1]
    coef = r1m * r1 * r1 * total[1:2] / DI
    sub = lax.broadcasted_iota(jnp.int32, (LANES, tokens), 0)
    stat_v[...] = jnp.where(sub == 0, r1m, jnp.where(sub == 1, coef, 0.0)).T

    @pl.loop(0, tokens // rows)
    def _(j):
        at = pl.ds(pl.multiple_of(j * rows, 16), rows)
        ggv[at, :] = (ggv[at, :].astype(F32) * stat_v[at, 0:1]).astype(BF16)

    def w_rows(d):
        to = slice(d * cut, (d + 1) * cut)

        @pl.loop(0, wide // tile)
        def _(m):
            at = pl.ds(pl.multiple_of(m * tile, tile), tile)
            got = t_dot(ggv[:, at], ogv[...]).astype(BF16)
            if ring:
                piece = ow.shape[2]
                chips = tile // (2 * piece)
                groups = wide // 2 // tile
                part_s[...] = got.reshape(part_s.shape)
                first = pl.ds(lax.rem(m, groups) * chips, chips)
                ow[first, m // groups, :, to] = part_s[:, core]
                other[first, m // groups, :, to] = part_s[:, 1 - core]
            else:
                rows_s[0, :, : got.shape[1]] = got
                copy = pltpu.make_async_copy(rows_s.at[0], wog_ref.at[at, to], out_sem.at[0])
                copy.start()
                copy.wait()

    load_og(0).wait()
    w_rows(0)
    load_og(1).start()
    load_og(1).wait()
    w_rows(1)
    if ring:
        swap = remote(other, other_in, c_send.at[0], c_recv.at[0], to_sib)
        swap.start()
        swap.wait_recv()

        @pl.loop(0, 4)
        def _(t):
            join(t, other_in.at[t])

        start()
    d0.wait_recv()
    y_p[:half, :] = (y_p[:half, :].astype(F32) + far_a[...].astype(F32)).astype(BF16)
    d4 = d_copy(y_p.at[:half], y_f.at[:half], 4, to_y)
    d1.wait_recv()
    x_p[half:, :] = (x_p[half:, :].astype(F32) + far_b[...].astype(F32)).astype(BF16)
    d5 = d_copy(x_p.at[half:], x_f.at[half:], 5, to_x)

    def dy_out(i):
        at = pl.ds(pl.multiple_of(i * rows, 16), rows)
        return pltpu.make_async_copy(dyo.at[lax.rem(i, 2)], dy_ref.at[at, :], dy_sem.at[lax.rem(i, 2)])

    chunks = tokens // rows

    def gate_chunk(i):
        slot = lax.rem(i, 2)
        at = pl.ds(pl.multiple_of(i * rows, 16), rows)
        for copy in load_chunk(i):
            copy.wait()
        r0 = ain[slot, :, LANES - 1 : LANES]
        ssd = (yin[slot].astype(F32) + rowp_ref[1:2, :] * xin[slot].astype(F32)).astype(BF16).astype(F32)
        z = zin[slot].astype(F32)
        sig = sigmoid(z)
        sz = z * sig
        d_gated = (stat_v[at, 0:1] * rowp_ref[2:3, :]) * din[slot].astype(F32) - (ssd * sz) * stat_v[at, 1:2]

        @pl.when(i >= 2)
        def _():
            dy_out(i - 2).wait()

        dyo[slot] = (d_gated * sz).astype(BF16)
        dy_out(i).start()
        ggv[at, :] = (r0 * (d_gated * ssd * (sig * (1.0 + z * (1.0 - sig))))).astype(BF16)

        @pl.when(i + 2 < chunks)
        def _():
            for copy in load_chunk(i + 2):
                copy.start()

    pl.loop(0, chunks - 1)(gate_chunk)
    if ring:
        second()
    pl.loop(chunks - 1, chunks)(gate_chunk)
    dpg_out = pltpu.make_async_copy(ggv, dpg_ref, out_sem.at[1])
    dpg_out.start()

    def rows_out(i):
        slot = lax.rem(i, 2)
        at = pl.ds(pl.multiple_of(i * tile, tile), tile)
        return pltpu.make_async_copy(rows_s.at[slot], gate_ref.at[at, :], rows_sem.at[slot])

    blocks = width // tile

    def gate_rows(i):
        slot = lax.rem(i, 2)
        load_h(i).wait()
        got = t_dot(hb[slot], ggv[...]).astype(BF16)

        @pl.when(i >= 2)
        def _():
            rows_out(i - 2).wait()

        rows_s[slot] = got
        rows_out(i).start()

        @pl.when(i + 2 < blocks)
        def _():
            load_h(i + 2).start()

    pl.loop(0, blocks // 2)(gate_rows)
    if ring:
        across()
        third()
    pl.loop(blocks // 2, blocks)(gate_rows)
    if ring:
        final()
        wog_out = pltpu.make_async_copy(ow.at[r], wog_ref, out_sem.at[0])
        wog_out.start()
    for copy in (d2, d3, d4, d5):
        copy.wait_recv()

    @pl.loop(0, q // 128)
    def _(j):
        at = pl.ds(pl.multiple_of(j * 128, 128), 128)
        whole = own_p[at, :].astype(F32) + y_f[at, :].astype(F32) + x_f[at, :].astype(F32)
        own_p[at, :] = (whole * stat_v[pl.ds(pl.multiple_of(s * q + j * 128, 128), 128), 0:1]).astype(BF16)

    br_out = pltpu.make_async_copy(own_p, br_ref, out_sem.at[2])
    br_out.start()
    for i in (chunks - 2, chunks - 1):
        dy_out(i).wait()
    for i in (blocks - 2, blocks - 1):
        rows_out(i).wait()
    dpg_out.wait()
    br_out.wait()
    for copy in sums + [d0, d1, d2, d3, d4, d5]:
        copy.wait_send()
    if ring:
        wog_out.wait()
        swap.wait_send()
    for finish in closing:
        finish()


def back_kernel(
    act_ref, aux_ref, dy_ref, y_ref, st_ref, slope_ref, u_ref, piece_ref,
    rowp_ref, colp_ref, cw_ref,
    dp_ref, sm_ref, all_ref, adj, ext, exp_v, seg_v, b_send, b_recv, b_load, *, heads, wide, ring,
):
    step = pl.program_id(0)
    steps = pl.num_programs(0)
    rows = act_ref.shape[0]
    chans = u_ref.shape[1]

    if ring:
        s = lax.axis_index("seq")
        x_peer = s + 1 - 2 * lax.rem(s, 2)
        y_peer = lax.rem(s + 2, 4)
        to_x, to_y = {"seq": x_peer}, {"seq": y_peer}
        from_x, from_y = all_ref.at[x_peer, 0], all_ref.at[y_peer, 1]
        moves = [
            remote(piece_ref, all_ref.at[s], b_send.at[0], b_recv.at[0], to_x),
            remote(piece_ref, all_ref.at[s], b_send.at[1], b_recv.at[1], to_y),
            remote(from_x, from_x, b_send.at[2], b_recv.at[2], to_y),
            remote(from_y, from_y, b_send.at[3], b_recv.at[3], to_x),
        ]
        own_piece = pltpu.make_async_copy(piece_ref, all_ref.at[s], b_load.at[0])

        @pl.when(step == 0)
        def _():
            greet([to_x, to_y])
            moves[0].start()
            moves[1].start()
            own_piece.start()

        @pl.when(step == 3)
        def _():
            moves[0].wait_recv()
            moves[2].start()
            moves[1].wait_recv()
            moves[3].start()

    @pl.when(step == 0)
    def _():
        sm_ref[...] = jnp.zeros_like(sm_ref)
        adj[...] = jnp.zeros_like(adj)
        exp_v[...] = head_matrix(wide)
        seg_v[...] = head_matrix(wide, True)
        ext[...] = jnp.zeros_like(ext)

    x = act_ref[:, :wide]
    x32 = x.astype(F32)
    b = act_ref[:, wide : wide + STATE]
    c = act_ref[:, wide + STATE :]
    aux = aux_ref[...]
    r0 = aux[:, LANES - 1 : LANES]
    skip_e = rowp_ref[1:2, :]
    y = y_ref[...].astype(F32)
    dy16 = dy_ref[...]
    dy = dy16.astype(F32)

    causal, dt_e, cum_e, cum_c, cum_t = decays(
        aux, heads, exp_v[...], rowp_ref[0:1, :], rowp_ref[3:4, :LANES], colp_ref[:, 0:1]
    )
    xdt = x32 * dt_e
    xdt16 = xdt.astype(BF16)
    scores = dot_t(c, b)
    st = st_ref[0]
    st16 = st.astype(BF16)
    q_in = adj[...]
    q16 = q_in.astype(BF16)
    last = cum_e[rows - 1 : rows, :]
    ecum = jnp.exp(cum_e)
    tail = jnp.exp(last - cum_e)
    half = lax.broadcasted_iota(jnp.int32, (rows, LANES), 1) < HEAD_DIM
    zero = jnp.zeros((rows, LANES), BF16)
    mid = rows // 2
    n_sum = None
    parts = []
    for pair in range(heads // 2):
        cut = slice(LANES * pair, LANES * (pair + 1))
        x2 = xdt16[:, cut]
        dy2 = dy16[:, cut]
        got = []
        for side in range(2):
            h = 2 * pair + side
            top, low, right = lower_parts(cum_c, cum_t, h, causal)
            m_top = (scores[:mid, :mid] * top).astype(BF16)
            m_low = (scores[mid:, :mid] * low).astype(BF16)
            m_right = (scores[mid:, mid:] * right).astype(BF16)
            v_top = t_dot(jnp.concatenate([m_top, m_low], axis=0), dy2)
            got.append(jnp.concatenate([v_top, t_dot(m_right, dy2[mid:])], axis=0))
            own = half if side == 0 else jnp.logical_not(half)
            dy_own = jnp.where(own, dy2, zero)
            g_top = dot_t(dy_own[:mid], x2[:mid])
            g_low = dot_t(dy_own[mid:], x2)
            n = [g_top * top, g_low[:, :mid] * low, g_low[:, mid:] * right]
            n_sum = n if n_sum is None else [p + v for p, v in zip(n_sum, n)]
        parts.append(jnp.where(half, got[0], got[1]))
    n_low = jnp.concatenate([n_sum[1], n_sum[2]], axis=1).astype(BF16)
    n_top = n_sum[0].astype(BF16)
    out_part = dot(b, q16) * tail
    v = jnp.concatenate(parts, axis=1) + out_part
    dy_e = (dy * ecum).astype(BF16)
    x_tail = (xdt * tail).astype(BF16)
    d_b = jnp.concatenate([t_dot(jnp.concatenate([n_top, n_low[:, :mid]], axis=0), c), t_dot(n_low[:, mid:], c[mid:])], axis=0)
    d_b = d_b + dot_t(x_tail, q16)
    d_c = jnp.concatenate([dot(n_top, b[:mid]), dot(n_low, b)], axis=0) + dot_t(dy_e, st16)
    elast = jnp.exp(last)
    adj[...] = elast * q_in + t_dot(c, dy_e)

    seg = seg_v[...]
    flow = dy * y - xdt16.astype(F32) * v
    passed = jnp.sum(xdt16.astype(F32) * out_part, axis=0, keepdims=True)
    passed = passed + elast * jnp.sum(q_in * st, axis=0, keepdims=True)
    flow_h = seg_dot(flow, seg)
    passed_h = seg_dot(jnp.broadcast_to(passed, (8, wide)), seg)[0:1, :]
    upper = jnp.where(
        lax.broadcasted_iota(jnp.int32, (rows, rows), 1) >= lax.broadcasted_iota(jnp.int32, (rows, rows), 0), 1.0, 0.0
    ).astype(BF16)
    hi = flow_h.astype(BF16)
    rest = flow_h - hi.astype(F32)
    mid = rest.astype(BF16)
    low = (rest - mid.astype(F32)).astype(BF16)
    crossing = dot(upper, hi) + dot(upper, mid) + dot(upper, low) + passed_h
    rate_row = rowp_ref[3:4, :LANES]
    decay_grad = rate_row * crossing
    d_dt = dot((x32 * v).astype(BF16), seg) + decay_grad
    lane = lax.broadcasted_iota(jnp.int32, (rows, LANES), 1)
    sig_v = pltpu.roll(aux, LANES - heads, 1)
    d_pre = jnp.where(lane < heads, d_dt * sig_v, 0.0)
    dt = jnp.where(lane < heads, aux, 0.0)
    dp_ref[:, chans:] = (r0 * d_pre).astype(BF16)

    d_act = jnp.concatenate([skip_e * dy + dt_e * v, d_b, d_c], axis=1)
    d_conv = d_act * slope_ref[...].astype(F32)
    d_conv16 = d_conv.astype(BF16)
    u = u_ref[...].astype(F32)
    d_u = cw_ref[KERNEL - 1 : KERNEL, :] * d_conv
    sm_ref[KERNEL - 1 : KERNEL, :] += jnp.sum(u * d_conv, axis=0, keepdims=True)
    for j in range(1, KERNEL):
        k = KERNEL - 1 - j
        moved = dot(shift_matrix(rows, j), d_conv16)
        moved = jnp.concatenate([moved[: rows - 8], moved[rows - 8 :] + ext[j : j + 8, :]], axis=0)
        d_u = d_u + cw_ref[k : k + 1, :] * moved
        sm_ref[k : k + 1, :] += jnp.sum(u * moved, axis=0, keepdims=True)
    ext[8:16, :] = d_conv[0:8, :]
    dp_ref[:, :chans] = (r0 * d_u).astype(BF16)
    sm_ref[4:5, :] += jnp.sum(d_conv, axis=0, keepdims=True)
    sm_ref[5:6, :wide] += jnp.sum(x32 * dy, axis=0, keepdims=True)
    sm_ref[6:7, :LANES] += jnp.sum(d_pre, axis=0, keepdims=True)
    sm_ref[7:8, :LANES] += jnp.sum(dt * decay_grad, axis=0, keepdims=True)

    if ring:
        @pl.when(step == steps - 1)
        def _():
            moves[2].wait_recv()
            moves[3].wait_recv()
            for copy in moves:
                copy.wait_send()
            own_piece.wait()


def grads_kernel(
    dpg_ref, dp_ref, w_ref, h_ref, gate_ref, piece_ref, sm_ref,
    dn_ref, wing_ref, win_ref, wout_ref,
    dpv, wv, hb, tiny_f, tiny_v, far_p, y_p, x_p, far_a, far_b, y_f, x_f, sib_s, mine_s, own_s, z_u, z_d,
    load_sem, hb_sem, d_send, d_recv, s_send, s_recv, zu_send, zu_recv, zd_send, zd_recv,
    g_send, g_recv, k_send, k_recv, p_send, p_recv, out_sem,
):
    s = lax.axis_index("seq")
    h = lax.axis_index("head")
    owners = lax.axis_size("head")
    last = owners // 2 - 1
    core = lax.rem(h, 2)
    r = h // 2
    x_peer = s + 1 - 2 * lax.rem(s, 2)
    y_peer = lax.rem(s + 2, 4)
    far = 3 - s
    to_x, to_y = {"seq": x_peer}, {"seq": y_peer}
    to_sib = {"head": h + 1 - 2 * core}
    to_up, to_down = {"head": lax.rem(h + 2, owners)}, {"head": lax.rem(h + owners - 2, owners)}
    above, below = r < last, r > 0
    q = far_p.shape[0]
    half = q // 2
    n, cols = own_s.shape[1], own_s.shape[2]
    spare = LANES // 2
    tiles = cols // LANES
    edges = [LANES * (tiles * k // 4) for k in range(5)]
    spans = list(zip(edges[:-1], edges[1:]))
    sent = []
    closing = []

    def push(src, dst, sems, i, target):
        copy = remote(src, dst, sems[0].at[i], sems[1].at[i], target)
        copy.start()
        sent.append(copy)
        return copy

    def launch(there, make):
        @pl.when(there)
        def _():
            make().start()

        def finish():
            @pl.when(there)
            def _():
                make().wait_send()

        closing.append(finish)

    skip = dpv.shape[1] - cols
    load_dp = pltpu.make_async_copy(dp_ref, dpv.at[:, skip:], load_sem.at[0])
    load_w = pltpu.make_async_copy(w_ref, wv, load_sem.at[1])
    load_g = pltpu.make_async_copy(dpg_ref, dpv.at[:, :skip], load_sem.at[4])
    own_gate = pltpu.make_async_copy(gate_ref, wing_ref.at[s], load_sem.at[5])
    load_dp.start()
    load_g.start()
    load_w.start()
    own_gate.start()

    def chip(i):
        return jnp.where(lax.rem(i, 2) == 0, last - i // 2, i // 2)

    def load_h(i, other):
        at = 2 * chip(i) + (1 - core if other else core)
        slot = 0 if other else 1
        return pltpu.make_async_copy(
            h_ref.at[:, pl.ds(pl.multiple_of(at * n, LANES), n)], hb.at[slot], hb_sem.at[slot]
        )

    load_h(0, True).start()
    load_h(0, False).start()

    tiny_f[...] = jnp.zeros_like(tiny_f)
    for k in range(sm_ref.shape[1] // spare):
        tiny_f[8 * k : 8 * k + 8, :] = sm_ref[:, spare * k : spare * (k + 1)]
    tiny_v[...] = tiny_f[...].astype(BF16)
    to_heads = [{"head": lax.rem(h + k, owners)} for k in range(1, owners)]
    greet([to_x, to_y] + to_heads)

    d_sems = (d_send, d_recv)
    g_sems = (g_send, g_recv)

    k_sems = (k_send, k_recv)
    k0 = push(gate_ref, wing_ref.at[s], k_sems, 0, to_x)
    k1 = push(gate_ref, wing_ref.at[s], k_sems, 1, to_y)
    tile = 256

    def part(block, out):
        at = pl.ds(pl.multiple_of(block * q, 16), q)

        @pl.loop(0, wv.shape[0] // tile)
        def _(j):
            to = pl.ds(pl.multiple_of(j * tile, tile), tile)
            out[:, to] = dot_t(dpv[at, :], wv[to, :]).astype(BF16)

    def add_to(out, at, extra):
        out[at, :] = (out[at, :].astype(F32) + extra.astype(F32)).astype(BF16)

    def swap(i):
        t = chip(i)
        return remote(sib_s.at[lax.rem(i, 2)], own_s.at[t], s_send.at[t], s_recv.at[t], to_sib)

    def rows_of(i):
        t = chip(i)
        slot = lax.rem(i, 2)

        @pl.when(i >= 2)
        def _():
            swap(i - 2).wait_send()

        load_h(i, True).wait()
        for lo, hi in spans:
            sib_s[slot, :, lo:hi] = t_dot(hb[0], dpv[:, skip + lo : skip + hi]).astype(BF16)
        sib_s[slot, :, cols - spare :] = tiny_v[...]
        swap(i).start()

        @pl.when(i < 3)
        def _():
            load_h(i + 1, True).start()

        load_h(i, False).wait()
        for lo, hi in spans:
            mine_s[:, lo:hi] = t_dot(hb[1], dpv[:, skip + lo : skip + hi]).astype(BF16)
        mine_s[:, cols - spare :] = tiny_v[...]

        @pl.when(i < 3)
        def _():
            load_h(i + 1, False).start()

        swap(i).wait_recv()
        join(t, mine_s)

    def join(t, extra):
        for lo, hi in spans:
            own_s[t, :, lo:hi] = (own_s[t, :, lo:hi].astype(F32) + extra[:, lo:hi].astype(F32)).astype(BF16)

    start, second, across, third, final = line_sum(
        own_s, z_u, z_d, (zu_send, zu_recv, zd_send, zd_recv), r, last, to_up, to_down, join, closing
    )

    load_dp.wait()
    load_g.wait()
    load_w.wait()
    part(far, far_p)
    d0 = push(far_p.at[:half], far_a, d_sems, 0, to_x)
    d1 = push(far_p.at[half:], far_b, d_sems, 1, to_y)
    pl.loop(0, 2)(rows_of)
    start()
    k0.wait_recv()
    gate_a = wing_ref.at[x_peer, : n // 2]
    k2 = push(gate_a, gate_a, k_sems, 2, to_y)
    k1.wait_recv()
    gate_b = wing_ref.at[y_peer, n // 2 :]
    k3 = push(gate_b, gate_b, k_sems, 3, to_x)
    pl.loop(2, 4)(rows_of)
    part(y_peer, y_p)
    d2 = push(y_p.at[half:], y_f.at[half:], d_sems, 2, to_y)
    second()
    part(x_peer, x_p)
    d3 = push(x_p.at[:half], x_f.at[:half], d_sems, 3, to_x)
    d0.wait_recv()
    add_to(y_p, slice(0, half), far_a[...])
    d4 = push(y_p.at[:half], y_f.at[:half], d_sems, 4, to_y)
    d1.wait_recv()
    add_to(x_p, slice(half, q), far_b[...])
    d5 = push(x_p.at[half:], x_f.at[half:], d_sems, 5, to_x)
    across()
    third()
    d0.wait_send()
    d1.wait_send()
    part(s, far_p)
    final()

    red = own_s.at[r]
    g0 = push(red, win_ref.at[s], g_sems, 0, to_x)
    g1 = push(red, win_ref.at[s], g_sems, 1, to_y)
    own_win = pltpu.make_async_copy(red, win_ref.at[s], load_sem.at[3])
    own_win.start()
    per = owners // 4

    def piece_of(head):
        return piece_ref.at[head // per, lax.rem(head, per)]

    pieces = []
    for k, peer in enumerate(to_heads):
        pieces.append(push(piece_of(peer["head"]), wout_ref.at[h], (p_send, p_recv), k, peer))
    own_piece = pltpu.make_async_copy(piece_of(h), wout_ref.at[h], load_sem.at[2])
    own_piece.start()

    g0.wait_recv()
    part_a = win_ref.at[x_peer, : n // 2]
    g2 = push(part_a, part_a, g_sems, 2, to_y)
    g1.wait_recv()
    part_b = win_ref.at[y_peer, n // 2 :]
    g3 = push(part_b, part_b, g_sems, 3, to_x)

    for copy in (d2, d3, d4, d5):
        copy.wait_recv()
    far_p[...] = (far_p[...].astype(F32) + y_f[...].astype(F32) + x_f[...].astype(F32)).astype(BF16)
    dn_out = pltpu.make_async_copy(far_p, dn_ref, out_sem.at[0])
    dn_out.start()
    dn_out.wait()
    own_win.wait()
    own_gate.wait()
    own_piece.wait()
    k2.wait_recv()
    k3.wait_recv()
    for copy in pieces:
        copy.wait_recv()
    g2.wait_recv()
    g3.wait_recv()
    for i in (2, 3):
        swap(i).wait_send()
    for copy in sent:
        if copy is not d0 and copy is not d1:
            copy.wait_send()
    for finish in closing:
        finish()


def finish_kernel(
    gate_ref, rest_ref, w_ref, dtw_ref, gain_ref, wog_ref, wo_ref, hid_ref, og_ref, dn_ref, br_ref,
    win_ref, wdt_ref, norm_ref, wout_ref, gg_ref, blk_ref, hg_ref, *, heads, wide,
):
    ranks = gate_ref.shape[0]
    wog = wog_ref[...].astype(F32)
    wout_ref[...] = wog
    step = pl.program_id(0)

    @pl.when(step == 0)
    def _():
        gg_ref[...] = jnp.zeros_like(gg_ref)
        norm_ref[...] = jnp.zeros_like(norm_ref)

    def lay(ref, col):
        shape = (col.shape[0], ref.shape[1])
        place = lax.broadcasted_iota(jnp.int32, shape, 0) + step * col.shape[0]
        there = lax.broadcasted_iota(jnp.int32, shape, 1) == place
        ref[...] += jnp.sum(jnp.where(there, col, 0.0), axis=0, keepdims=True)

    lay(gg_ref, jnp.sum(wog * wo_ref[...].astype(F32), axis=1, keepdims=True))
    h32 = hid_ref[...].astype(F32)
    blk_ref[...] = (h32 + br_ref[...].astype(F32)).astype(BF16)
    dn = dn_ref[...].astype(F32)
    count = h32.shape[1]
    r0 = lax.rsqrt(jnp.sum(h32 * h32, axis=1, keepdims=True) / count + EPS)
    mixed = jnp.sum(dn * h32, axis=1, keepdims=True) / count
    hg_ref[...] = og_ref[...].astype(F32) + dn - h32 * (r0 * r0 * mixed)

    gain = gain_ref[...].astype(F32)
    norm = None

    def piece(at, raw):
        to = slice(at, at + raw.shape[1])
        win_ref[:, to] = raw * gain
        return jnp.sum(raw * w_ref[:, to].astype(F32), axis=1, keepdims=True)

    shared = None
    dt_parts = []
    for k in range(ranks):
        here = piece(k * wide, gate_ref[k].astype(F32)) + piece(DI + k * wide, rest_ref[k, :, :wide].astype(F32))
        norm = here if norm is None else norm + here
        bc = rest_ref[k, :, wide : wide + 2 * STATE].astype(F32)
        shared = bc if shared is None else shared + bc
        dt_parts.append(rest_ref[k, :, wide + 2 * STATE : wide + 2 * STATE + heads].astype(F32))
    norm = norm + piece(2 * DI, shared)
    raw = jnp.concatenate(dt_parts, axis=1)
    wdt_ref[...] = raw * gain
    lay(norm_ref, norm + jnp.sum(raw * dtw_ref[...].astype(F32), axis=1, keepdims=True))


def local(hidden, lengths, out_grad, norm_gain, w_in, w_dt, conv_weight, conv_bias, dt_bias, a_log, skip_gain, gate_gain, w_out):
    ranks = lax.axis_size("seq")
    rank = lax.axis_index("seq")
    owners = lax.axis_size("head")
    owner = lax.axis_index("head")
    local_len, width = hidden.shape[1], hidden.shape[2]
    heads = HEADS // ranks
    wide = heads * HEAD_DIM
    chans = wide + 2 * STATE
    cols = wide + chans + LANES
    tokens = ranks * local_len
    chunk = min(CHUNK, local_len)
    steps = tokens // chunk
    shard = w_in.shape[0]

    gain_rows = norm_gain[:, None]

    def scaled(v):
        return (v.astype(F32) * gain_rows.astype(F32)).astype(BF16)

    spare = LANES // 2
    ring = owners == 2 * ranks

    def sds(shape, kind):
        return jax.ShapeDtypeStruct(shape, kind)

    hbm = pl.BlockSpec(memory_space=pl.ANY)
    vmem = pl.BlockSpec(memory_space=pltpu.VMEM)

    def dma(count):
        return pltpu.SemaphoreType.DMA((count,))

    def forth(size):
        return pl.BlockSpec((chunk, size), lambda j: (j, 0))

    def back(size):
        return pl.BlockSpec((chunk, size), lambda j: (steps - 1 - j, 0))

    def whole(a):
        return pl.BlockSpec(a.shape, lambda j: (0,) * a.ndim, pipeline_mode=pl.Buffered(1))

    params = pltpu.CompilerParams(
        dimension_semantics=("arbitrary",), vmem_limit_bytes=56 * 1024 * 1024
    )
    grid = (steps,)
    cs = CHANNELS // owners
    hs = HEADS // owners
    scan_out = [
        sds((tokens, chans), BF16),
        sds((tokens, chans), BF16),
        sds((tokens, LANES), F32),
        sds((tokens, wide), BF16),
        sds((tokens, wide), BF16),
        sds((steps, STATE, wide), F32),
        sds((8, tokens), F32),
    ]

    if ring:
        lanes = -(-max(cs, DI // owners) // LANES) * LANES

        (
            h_all, og_all, w_t, w_o, z, u, d0, act, slope, aux, y, gg, states, sums, cw, dtb, rowp, colp,
        ) = pl.pallas_call(
            functools.partial(gather_kernel, heads=heads, wide=wide),
            in_specs=[hbm] * 4 + [vmem] * 6,
            out_specs=[hbm] * 13 + [vmem] * 5,
            out_shape=[
                sds((tokens, width), BF16),
                sds((tokens, width), BF16),
                sds((width, cols), BF16),
                sds((wide, width), BF16),
                sds((tokens, wide), BF16),
                sds((tokens, chans), BF16),
                sds((tokens, wide), BF16),
            ]
            + scan_out
            + [sds((16, chans), F32), sds((8, LANES), F32), sds((8, wide), F32), sds((LANES, LANES), F32)],
            scratch_shapes=[
                pltpu.VMEM((tokens, width), BF16),
                pltpu.VMEM((tokens, width), BF16),
                pltpu.VMEM((width, cols), BF16),
                pltpu.VMEM((wide, width), BF16),
                pltpu.VMEM((shard, cols - LANES), BF16),
                pltpu.VMEM((tokens, wide), BF16),
                pltpu.VMEM((tokens, chans), BF16),
                pltpu.VMEM((tokens, LANES), F32),
                pltpu.VMEM((owners, 16, lanes), BF16),
                pltpu.VMEM((16, lanes), F32),
                pltpu.VMEM((STATE, wide), F32),
                pltpu.VMEM((16, chans), F32),
                pltpu.VMEM((2, STATE, wide), F32),
            ]
            + [dma(4)] * 9
            + [dma(8)] * 5
            + [dma(owners)] * 2
            + [dma(6), dma(22), pltpu.SemaphoreType.DMA((steps, 5)), dma(2)],
            compiler_params=pltpu.CompilerParams(
                collective_id=0, has_side_effects=True, vmem_limit_bytes=56 * 1024 * 1024
            ),
            cost_estimate=pl.CostEstimate(
                flops=2 * tokens * width * (cols + wide), bytes_accessed=4 * tokens * (width + cols), transcendentals=0
            ),
            name="gather_scan",
        )(
            hidden[0], out_grad[0], w_in, w_out, gain_rows, w_dt, conv_weight, conv_bias[None], gate_gain[None],
            jnp.concatenate([dt_bias, a_log, skip_gain])[None],
        )
    else:
        dt_block = jnp.pad(scaled(lax.dynamic_slice_in_dim(w_dt, rank * heads, heads, 1)), ((0, 0), (0, LANES - heads)))
        w_t = lax.all_gather(
            jnp.concatenate(
                [
                    scaled(lax.dynamic_slice_in_dim(w_in, rank * wide, wide, 1)),
                    scaled(lax.dynamic_slice_in_dim(w_in, DI + rank * wide, wide, 1)),
                    scaled(w_in[:, 2 * DI :]),
                    dt_block,
                ],
                axis=1,
            ),
            "head", axis=0, tiled=True,
        )
        w_o = lax.dynamic_slice_in_dim(lax.all_gather(w_out, "head", axis=0, tiled=True), rank * wide, wide, 0)
        h_all = lax.all_gather(hidden[0], "seq", axis=0, tiled=True)
        og_all = lax.all_gather(out_grad[0], "seq", axis=0, tiled=True)
        h32 = h_all.astype(F32)
        r0 = lax.rsqrt(jnp.mean(h32 * h32, axis=1, keepdims=True) + EPS)
        projected = dot(h_all, w_t) * r0
        z = projected[:, :wide].astype(BF16)
        u = projected[:, wide : wide + chans].astype(BF16)
        d_raw = jnp.concatenate([projected[:, wide + chans : cols - 1], r0], axis=1)
        d0 = dot_t(og_all, w_o).astype(BF16)

        def mine(v, size):
            return lax.dynamic_slice_in_dim(v, rank * size, size, v.ndim - 1)

        conv_w = lax.all_gather(conv_weight, "head", axis=1, tiled=True)
        conv_b = lax.all_gather(conv_bias, "head", axis=0, tiled=True)
        cw = jnp.concatenate([conv_w, conv_b[None]], axis=0)
        cw = jnp.concatenate([mine(cw[:, :DI], wide), cw[:, DI:]], axis=1).astype(F32)
        cw = jnp.pad(cw, ((0, 16 - KERNEL - 1), (0, 0)))
        rate = -jnp.exp(mine(lax.all_gather(a_log, "head", axis=0, tiled=True), heads).astype(F32))
        dtb = jnp.pad(mine(lax.all_gather(dt_bias, "head", axis=0, tiled=True), heads).astype(F32), (0, LANES - heads))
        dtb = jnp.broadcast_to(dtb[None], (8, LANES))
        rowp = jnp.stack(
            [
                jnp.repeat(rate, HEAD_DIM),
                jnp.repeat(mine(lax.all_gather(skip_gain, "head", axis=0, tiled=True), heads).astype(F32), HEAD_DIM),
                mine(lax.all_gather(gate_gain, "head", axis=0, tiled=True), wide).astype(F32),
                jnp.pad(rate, (0, wide - heads)),
            ]
            + [jnp.zeros((wide,), F32)] * 4
        )
        colp = jnp.broadcast_to(jnp.pad(rate, (0, LANES - heads))[:, None], (LANES, LANES))
        act, slope, aux, y, gg, states, sums = pl.pallas_call(
            functools.partial(scan_kernel, heads=heads),
            grid=grid,
            in_specs=[
                forth(chans), forth(LANES), forth(wide), forth(wide),
                whole(cw), whole(dtb), whole(rowp), whole(colp),
            ],
            out_specs=[
                forth(chans), forth(chans), forth(LANES), forth(wide), forth(wide),
                pl.BlockSpec((1, STATE, wide), lambda j: (j, 0, 0)),
                pl.BlockSpec((8, chunk), lambda j: (0, j)),
            ],
            out_shape=scan_out,
            scratch_shapes=[pltpu.VMEM((STATE, wide), F32), pltpu.VMEM((16, chans), F32)],
            compiler_params=params,
            name="scan",
        )(u, d_raw, z, d0, cw, dtb, rowp, colp)

    mask = (jnp.arange(tokens, dtype=jnp.int32) < lengths[0]).astype(F32)
    n_own = DI // owners
    piece = n_own // owners
    per = owners // ranks
    wog_shape = (per, piece, width) if ring else (wide, width)
    line_shape = (4, per, piece, width) if ring else (1, 1, 16, LANES)
    in_chunk = min(CHUNK, local_len)
    branch, wog, dy, dpg, wig_gate = pl.pallas_call(
        functools.partial(mid_kernel, ring=ring),
        in_specs=[hbm] * 9 + [vmem] * 3,
        out_specs=[hbm] * 5,
        out_shape=[
            sds((local_len, width), BF16),
            sds(wog_shape, BF16),
            sds((tokens, wide), BF16),
            sds((tokens, wide), BF16),
            sds((width, wide), BF16),
        ],
        scratch_shapes=[
            pltpu.VMEM((tokens, LANES), F32),
            pltpu.VMEM((tokens, wide), BF16),
            pltpu.VMEM((wide, width), BF16),
            pltpu.VMEM((tokens, width // 2), BF16),
        ]
        + [pltpu.VMEM((local_len, width), BF16)] * 4
        + [pltpu.VMEM((local_len // 2, width), BF16)] * 2
        + [pltpu.VMEM((local_len, width), BF16)] * 2
        + [pltpu.VMEM((ranks, 8, tokens), F32)]
        + [pltpu.VMEM(line_shape, BF16)] * 3
        + [pltpu.VMEM((3,) + line_shape[1:], BF16)] * 2
        + [pltpu.VMEM((256 // (2 * piece), 2, piece, width // 2) if ring else (16, LANES), BF16)]
        + [pltpu.VMEM((2, in_chunk, wide), BF16)] * 4
        + [
            pltpu.VMEM((2, in_chunk, LANES), F32),
            pltpu.VMEM((2, in_chunk, wide), BF16),
            pltpu.VMEM((2, tokens, 256), BF16),
            pltpu.VMEM((2, 256, wide), BF16),
        ]
        + [dma(3)]
        + [dma(6)] * 2
        + [dma(3)] * 2
        + [dma(1)] * 2
        + [dma(4)] * 4
        + [pltpu.SemaphoreType.DMA((2, 5)), dma(2), dma(2), dma(2), dma(3)],
        compiler_params=pltpu.CompilerParams(
            collective_id=3, has_side_effects=True, vmem_limit_bytes=56 * 1024 * 1024
        ),
        cost_estimate=pl.CostEstimate(
            flops=6 * tokens * wide * width, bytes_accessed=4 * tokens * (width + 5 * wide), transcendentals=0
        ),
        name="mid",
    )(gg, w_o, og_all, h_all, act, aux, z, d0, y, sums, jnp.broadcast_to(mask[None], (8, tokens)), rowp)
    own_gate = lax.psum_scatter(wig_gate, "head", scatter_dimension=0, tiled=True)

    rest = chans + LANES
    dp, sm, pieces = pl.pallas_call(
        functools.partial(back_kernel, heads=heads, wide=wide, ring=ring),
        grid=grid,
        in_specs=[
            back(chans), back(LANES), back(wide), back(wide),
            pl.BlockSpec((1, STATE, wide), lambda j: (steps - 1 - j, 0, 0)),
            back(chans), back(chans), hbm,
            whole(rowp), whole(colp), whole(cw),
        ],
        out_specs=[back(rest), pl.BlockSpec((8, chans), lambda j: (0, 0)), hbm],
        out_shape=[sds((tokens, rest), BF16), sds((8, chans), F32), sds((ranks,) + wog_shape, BF16)],
        scratch_shapes=[
            pltpu.VMEM((STATE, wide), F32),
            pltpu.VMEM((16, chans), F32),
            pltpu.VMEM((LANES, wide), BF16),
            pltpu.VMEM((wide, LANES), BF16),
        ]
        + [dma(4)] * 2
        + [dma(1)],
        compiler_params=pltpu.CompilerParams(
            dimension_semantics=("arbitrary",), collective_id=2, has_side_effects=True,
            vmem_limit_bytes=56 * 1024 * 1024,
        )
        if ring
        else params,
        cost_estimate=pl.CostEstimate(
            flops=2 * tokens * wide * 12 * chunk, bytes_accessed=tokens * wide * 24, transcendentals=tokens * chunk * heads
        ),
        name="scan_back",
    )(act, aux, dy, y, states, slope, u, wog, rowp, colp, cw)

    if ring:
        dn, gate_rows, rest_rows, w_out_grad = pl.pallas_call(
            grads_kernel,
            in_specs=[hbm] * 6 + [vmem],
            out_specs=[hbm] * 4,
            out_shape=[
                sds((local_len, width), BF16),
                sds((ranks, shard, wide), BF16),
                sds((ranks, shard, rest), BF16),
                sds((owners, piece, width), BF16),
            ],
            scratch_shapes=[
                pltpu.VMEM((tokens, cols), BF16),
                pltpu.VMEM((width, cols), BF16),
                pltpu.VMEM((2, tokens, shard), BF16),
                pltpu.VMEM((shard, spare), F32),
                pltpu.VMEM((shard, spare), BF16),
            ]
            + [pltpu.VMEM((local_len, width), BF16)] * 3
            + [pltpu.VMEM((local_len // 2, width), BF16)] * 2
            + [pltpu.VMEM((local_len, width), BF16)] * 2
            + [
                pltpu.VMEM((2, shard, rest), BF16),
                pltpu.VMEM((shard, rest), BF16),
                pltpu.VMEM((4, shard, rest), BF16),
                pltpu.VMEM((3, shard, rest), BF16),
                pltpu.VMEM((3, shard, rest), BF16),
            ]
            + [dma(6), dma(2)]
            + [dma(6)] * 2
            + [dma(4)] * 10
            + [dma(owners)] * 2
            + [dma(2)],
            compiler_params=pltpu.CompilerParams(
                collective_id=1, has_side_effects=True, vmem_limit_bytes=56 * 1024 * 1024
            ),
            cost_estimate=pl.CostEstimate(
                flops=4 * tokens * width * cols, bytes_accessed=8 * tokens * cols, transcendentals=0
            ),
            name="weight_grads",
        )(dpg, dp, w_t, h_all, own_gate, pieces, sm)
        w_out_grad = w_out_grad.reshape(n_own, width)
        groups = chans // spare
        tiny_all = rest_rows[:, : 8 * groups, rest - spare :].astype(F32).reshape(ranks, groups, 8, spare)
        tiny_all = tiny_all.swapaxes(1, 2).reshape(ranks, 8, chans)
    else:
        full = lax.all_gather(lax.psum(wog, "head"), "seq", axis=0, tiled=True)
        w_out_grad = lax.dynamic_slice_in_dim(full, owner * n_own, n_own, 0)
        wig = t_dot(h_all, dp).astype(BF16)
        dn = (dot_t(dp, w_t[:, wide:]) + dot_t(dpg, w_t[:, :wide])).astype(BF16)
        dn = lax.psum_scatter(dn, "seq", scatter_dimension=0, tiled=True)
        gate_rows = lax.all_gather(own_gate, "seq")
        rest_rows = lax.all_gather(lax.psum_scatter(wig, "head", scatter_dimension=0, tiled=True), "seq")
        tiny_all = lax.all_gather(lax.psum(sm, "head"), "seq")
    strips = min(4, shard // 16)

    def strip(total, size):
        return pl.BlockSpec((total // strips, size), lambda j: (j, 0))

    def ranks_strip(size):
        return pl.BlockSpec((ranks, shard // strips, size), lambda j: (0, j, 0))

    w_in_grad, w_dt_grad, norm_gain_grad, w_out_grad, gate_gain_grad, block_out, hidden_grad = pl.pallas_call(
        functools.partial(finish_kernel, heads=heads, wide=wide),
        grid=(strips,),
        in_specs=[
            ranks_strip(wide), ranks_strip(rest), strip(shard, PROJ), strip(shard, HEADS), strip(shard, 1),
            strip(n_own, width), strip(n_own, width),
            strip(local_len, width), strip(local_len, width), strip(local_len, width), strip(local_len, width),
        ],
        out_specs=[
            strip(shard, PROJ), strip(shard, HEADS), pl.BlockSpec((1, shard), lambda j: (0, 0)),
            strip(n_own, width), pl.BlockSpec((1, n_own), lambda j: (0, 0)),
            strip(local_len, width), strip(local_len, width),
        ],
        out_shape=[
            sds((shard, PROJ), F32),
            sds((shard, HEADS), F32),
            sds((1, shard), F32),
            sds((n_own, width), F32),
            sds((1, n_own), F32),
            sds((local_len, width), BF16),
            sds((local_len, width), F32),
        ],
        compiler_params=params,
        cost_estimate=pl.CostEstimate(flops=6 * shard * PROJ, bytes_accessed=16 * shard * PROJ, transcendentals=0),
        name="finish",
    )(
        gate_rows, rest_rows, w_in, w_dt, gain_rows, w_out_grad, w_out,
        hidden[0], out_grad[0], dn, branch,
    )

    conv_all = jnp.concatenate(
        [tiny_all[:, :5, :wide].swapaxes(0, 1).reshape(5, DI), jnp.sum(tiny_all[:, :5, wide:], axis=0)], axis=1
    )
    skip_all = jnp.sum(tiny_all[:, 5, :wide].reshape(ranks, heads, HEAD_DIM), axis=2)
    vec = jnp.stack([tiny_all[:, 6, :heads], tiny_all[:, 7, :heads], skip_all]).reshape(3, HEADS)
    conv_own = lax.dynamic_slice_in_dim(conv_all, owner * cs, cs, 1)
    vec_own = lax.dynamic_slice_in_dim(vec, owner * hs, hs, 1)

    return (
        block_out[None],
        hidden_grad[None],
        norm_gain_grad.reshape(shard),
        w_in_grad,
        w_dt_grad,
        conv_own[:KERNEL],
        conv_own[KERNEL],
        vec_own[0],
        vec_own[1],
        vec_own[2],
        gate_gain_grad.reshape(n_own) / gate_gain.astype(F32),
        w_out_grad,
    )


def solution(mesh):
    rows = P("head", "seq", None)
    return jax.shard_map(
        local,
        mesh=mesh,
        in_specs=(
            rows, P("head"), rows, P("head"), P("head", None), P("head", None), P(None, "head"),
            P("head"), P("head"), P("head"), P("head"), P("head"), P("head", None),
        ),
        out_specs=(
            rows, rows, P("head"), P("head", None), P("head", None), P(None, "head"),
            P("head"), P("head"), P("head"), P("head"), P("head"), P("head", None),
        ),
        check_vma=False,
    )
```
